32 devices in a mesh: ja: 8 (over z, y), ia: 4 (over x, core).
Axes of the slice: x: 2, y: 2, z: 4, core: 2. Of those that a mesh axis runs over, the one named last changes fastest.
Arguments:
- argo_value: float32 [32768, 150], P(('ja', 'ia')), may hold values from -6 to 6
- argo_owner: int32 [32768, 1], P(('ja', 'ia')), may hold values from 0 to 31; in each aligned block of 1024 rows (0 to 1023, 1024 to 2047, ...) at most 96 rows name the same one
- argo_cell: int32 [32768], P(('ja', 'ia')), may hold values from 0 to 8191
- alt_value: float32 [24576], P(('ja', 'ia')), may hold values from -6 to 6
- alt_owner: int32 [24576, 1], P(('ja', 'ia')), may hold values from 0 to 31; in each aligned block of 768 rows (0 to 767, 768 to 1535, ...) at most 72 rows name the same one
- alt_cell: int32 [24576], P(('ja', 'ia')), may hold values from 0 to 8191
- alt_profile: float32 [150], replicated, may hold values from -3 to 3
- land_mask: int32 [128, 2048], P('ja', 'ia'), may hold values 0 or 1
- coef_east: float32 [128, 2048], P('ja', 'ia'), may hold values from 0.05 to 0.24
- coef_north: float32 [128, 2048], P('ja', 'ia'), may hold values from 0.05 to 0.24
- mirror: int32 [2048], P('ia'), may hold values from 0 to 2047, as said below
- vinv: float32 [128, 2, 75, 75], P('ja'), may hold values from -1 to 1
Outputs:
- gradient: float32 [150, 128, 2048], P(None, 'ja', 'ia')
The draws below stay inside these ranges and needn't reach their ends.
Inputs may be any that keep to these rules, and one draw needn't show every extreme that they name: `argo_owner`: the rows of one device name one owner at most 96 times, a bound that some block reaches. `alt_owner`: the rows of one device name one owner at most 72 times, a bound that some block reaches. mirror[i] is 2047 - i or 2047 - (i XOR 1), and mirror[mirror[i]] = i.
All inputs are finite; a program needn't handle non-finite values. No bound on the sum of `land_mask` on one device may be relied on, other than what follows from the above.
Results may differ from the reference program's by a relative error of at most 0.0001.
Values sent between devices are 32-bit elements; how exact they have to be, the bound alone decides.
No kernel may reach another device: no remote copies, remote signals or barrier semaphores. Data moves between devices by JAX's collectives and lax.ppermute only.
A program may use at most 128 MiB of HBM per device.

```python
import math
import jax
import jax.numpy as jnp
import numpy as np
from jax import lax

K = 75
CJ = 16
CI = 512
OBS_DEV = 1024
ALT_DEV = 768
ITERS = 3
NJ = 128
NI = 2048
TOTAL_OBS = 32768
TOTAL_ALT = 24576
CAP = 96
CAPH = 72
N_IA = 4
DEVICES = 32


def draw_mirror(key, part):
    half_count = NI // 2
    flip_bits = jax.random.randint(key, (NI // 4,), 0, 2, dtype=jnp.int32)
    lower_half = jnp.arange(half_count, dtype=jnp.int32)
    lower_map = NI - 1 - jnp.bitwise_xor(lower_half, flip_bits[lower_half // 2])
    upper_half = jnp.arange(half_count, NI, dtype=jnp.int32)
    mirrored = NI - 1 - upper_half
    upper_map = jnp.bitwise_xor(mirrored, flip_bits[mirrored // 2])
    return jnp.concatenate([lower_map, upper_map]).astype(jnp.int32)


def draw_vinv(key, part):
    first_key, second_key = jax.random.split(jax.random.fold_in(key, 17))
    off_part = jnp.clip(jax.random.normal(first_key, (NJ, 2, K, K), jnp.float32), -4.0, 4.0) * (0.35 / K ** 0.5)
    diag_part = jax.random.uniform(second_key, (NJ, 2, K, 1), jnp.float32, 0.5, 1.0)
    identity = (jnp.arange(K)[:, None] == jnp.arange(K)[None, :]).astype(jnp.float32)
    return (off_part * (1.0 - identity) + diag_part * identity).astype(jnp.float32)


def plant(entries, key, least, largest):
    dims = entries.shape
    place = [jax.random.randint(jax.random.fold_in(key, axis), (), 0, dims[axis]) for axis in range(len(dims))]
    entries = entries.at[tuple(place)].set(least)
    longest = dims.index(max(dims))
    place[longest] = (place[longest] + 1) % dims[longest]
    return entries.at[tuple(place)].set(largest)


def levels(key, extent, shards, low, top_value):
    gain = 1.0
    for position, shards_of in shards:
        steps = jax.random.uniform(jax.random.fold_in(jax.random.fold_in(key, 6), position), (shards_of,), jnp.float32, low / len(shards), top_value / len(shards))
        gain = gain * jnp.repeat(jnp.exp(steps), extent[position] // shards_of).reshape((-1,) + (1,) * (len(extent) - 1 - position))
    return gain


def assign_block(key, own, number, rows, count, top, limit, slope):
    sequence = jax.random.permutation(key, count)
    crowded, ordinary = portions_of(count, rows * top, limit, slope, True), portions_of(count, rows * top, limit, slope, False)
    places = jnp.arange(count)

    def named(lengths, offset_by):
        used = int((lengths > 0).sum())
        fixed = max(1, used // 4)
        moved = fixed + (places - fixed + offset_by * (used - fixed)) % max(1, count - fixed)
        return jnp.zeros((count,), jnp.int32).at[sequence[jnp.where(places < fixed, places, moved)]].set(jnp.asarray(lengths, jnp.int32))

    lengths = jnp.where(number % 4 == 0, named(crowded, number // 4), named(ordinary, number - number // 4 - 1))
    mixed = jax.random.permutation(jax.random.fold_in(own, 3), count)
    donor, sink = mixed[0:count // 2 * 2:2], mixed[1:count // 2 * 2:2]
    room = jnp.minimum(lengths[donor] - 1, limit - lengths[sink]) // 2
    room = jnp.where((donor == sequence[0]) | (sink == sequence[0]) | (lengths[sink] == 0), 0, jnp.maximum(room, 0))
    moved = jax.random.randint(jax.random.fold_in(own, 4), (count // 2,), 0, 1 << 20) % (room + 1)
    lengths = lengths.at[donor].add(-moved).at[sink].add(moved)
    items = jnp.searchsorted(jnp.cumsum(lengths), jnp.arange(rows * top), side="right").astype(jnp.int32)
    listing = items.reshape(top, rows).T
    listing = listing[jax.random.permutation(jax.random.fold_in(own, 1), rows)]
    offset_by = jax.random.randint(jax.random.fold_in(own, 2), (rows, 1), 0, top)
    return jnp.take_along_axis(listing, (jnp.arange(top)[None, :] + offset_by) % top, axis=1)


def portions_of(count, total, most, slope, full):
    weights = [(1 << 20) // math.isqrt(standing ** slope) + 1 for standing in range(1, count + 1)]
    largest = most if full else min(most, max(-(-total // count), total * weights[0] // sum(weights)))
    least = 1 if total - largest >= count - 1 else 0
    given, spare = [largest] + [least] * (count - 1), total - largest - least * (count - 1)
    while spare > 0:
        free = [i for i in range(1, count) if given[i] < largest] or [i for i in range(1, count) if given[i] < most]
        mass, left = sum([weights[i] for i in free]), spare
        for i in free:
            addition = min(most - given[i], max(1, left * weights[i] // mass), spare)
            given[i] = given[i] + addition
            spare = spare - addition
    return np.array(given)


def normal_values(own_key, extent, spread, bound, cuts=(), kind=jnp.bfloat16):
    level = levels(own_key, extent, cuts, -0.22, 0.18) if cuts else 1.0
    values = jax.random.normal(own_key, extent, jnp.float32) * spread * level
    return jnp.minimum(jnp.maximum(values, -bound), bound).astype(kind)


def setup_inputs(seed: int = 0) -> dict:
    keys = jax.random.split(jax.random.key(seed), 13)
    argo_value = normal_values(keys[0], (TOTAL_OBS, 2 * K), 1.0, 6.0, ((0, 32),), jnp.float32)
    argo_owner_keys = jax.random.split(jax.random.fold_in(keys[1], 1), TOTAL_OBS // OBS_DEV)
    argo_owner_turns = jax.random.permutation(jax.random.fold_in(keys[1], 3), TOTAL_OBS // OBS_DEV)
    argo_owner = jax.vmap(lambda own, number: assign_block(jax.random.fold_in(keys[1], 2), own, number, OBS_DEV, DEVICES, 1, CAP, 2))(argo_owner_keys, argo_owner_turns).reshape((TOTAL_OBS, 1))
    argo_cell = plant(jax.random.randint(keys[2], (TOTAL_OBS,), 0, CJ * CI), jax.random.fold_in(keys[2], 1), 0, (CJ * CI) - 1).astype(jnp.int32)
    alt_value = normal_values(keys[3], (TOTAL_ALT,), 1.0, 6.0, ((0, 32),), jnp.float32)
    alt_owner_keys = jax.random.split(jax.random.fold_in(keys[4], 1), TOTAL_ALT // ALT_DEV)
    alt_owner_turns = jax.random.permutation(jax.random.fold_in(keys[4], 3), TOTAL_ALT // ALT_DEV)
    alt_owner = jax.vmap(lambda own, number: assign_block(jax.random.fold_in(keys[4], 2), own, number, ALT_DEV, DEVICES, 1, CAPH, 2))(alt_owner_keys, alt_owner_turns).reshape((TOTAL_ALT, 1))
    alt_cell = plant(jax.random.randint(keys[5], (TOTAL_ALT,), 0, CJ * CI), jax.random.fold_in(keys[5], 1), 0, (CJ * CI) - 1).astype(jnp.int32)
    alt_profile = normal_values(keys[6], (2 * K,), 0.5, 3.0, (), jnp.float32)
    land_mask = plant((jax.random.randint(keys[7], (NJ, NI), 0, 4) < 3).astype(jnp.int32), jax.random.fold_in(keys[7], 1), 0, 1)
    coef_east = jnp.clip(0.05 + 0.19 * jax.random.uniform(keys[8], (NJ, NI), jnp.float32) ** levels(keys[8], (NJ, NI), ((0, 8), (1, 4)), -0.2, 0.2), 0.05, 0.24)
    coef_north = jnp.clip(0.05 + 0.19 * jax.random.uniform(keys[9], (NJ, NI), jnp.float32) ** levels(keys[9], (NJ, NI), ((0, 8), (1, 4)), -0.2, 0.2), 0.05, 0.24)
    mirror = draw_mirror(jax.random.fold_in(keys[12], 71), 0)
    vinv = draw_vinv(jax.random.fold_in(keys[12], 71), 0)
    return {"argo_value": argo_value, "argo_owner": argo_owner, "argo_cell": argo_cell, "alt_value": alt_value, "alt_owner": alt_owner, "alt_cell": alt_cell, "alt_profile": alt_profile, "land_mask": land_mask, "coef_east": coef_east, "coef_north": coef_north, "mirror": mirror, "vinv": vinv}


def grid_place(owner_list, cell_list):
    target = owner_list[:, 0]
    row_index = (target // N_IA) * CJ + cell_list // CI
    col_index = (target % N_IA) * CI + cell_list % CI
    return row_index, col_index


def reference(argo_value, argo_owner, argo_cell, alt_value, alt_owner, alt_cell, alt_profile, land_mask, coef_east, coef_north, mirror, vinv):
    row_index, col_index = grid_place(argo_owner, argo_cell)
    forcing = jnp.zeros((2 * K, NJ, NI), jnp.float32).at[:, row_index, col_index].add(argo_value.T)
    alt_rows, alt_cols = grid_place(alt_owner, alt_cell)
    sea_level = jnp.zeros((NJ, NI), jnp.float32).at[alt_rows, alt_cols].add(alt_value)
    state_field = forcing + alt_profile[:, None, None] * sea_level[None]
    wet = land_mask.astype(jnp.float32)
    east_w = coef_east * wet * jnp.roll(wet, -1, 1)
    west_w = jnp.roll(east_w, 1, 1)
    north_w = jnp.concatenate([coef_north[:-1] * wet[:-1] * wet[1:], jnp.zeros((1, NI), jnp.float32)], 0)
    south_w = jnp.concatenate([jnp.zeros((1, NI), jnp.float32), north_w[:-1]], 0)
    fold_w = 0.5 * (coef_north[-1] + coef_north[-1][mirror]) * wet[-1] * wet[-1][mirror]

    def horizontal(level_plane):
        result = level_plane + east_w * (jnp.roll(level_plane, -1, 1) - level_plane) + west_w * (jnp.roll(level_plane, 1, 1) - level_plane)
        upward = jnp.concatenate([level_plane[1:], level_plane[-1:]], 0)
        downward = jnp.concatenate([level_plane[:1], level_plane[:-1]], 0)
        result = result + north_w * (upward - level_plane) + south_w * (downward - level_plane)
        top_term = fold_w * (level_plane[-1][mirror] - level_plane[-1])
        return result.at[-1].add(top_term)

    for sweep in range(ITERS):
        state_field = lax.map(horizontal, state_field)
        field_parts = state_field.reshape(2, K, NJ, NI)
        mixed = [jnp.einsum("jlk,lji->kji", vinv[:, which], field_parts[which], precision=lax.Precision.HIGHEST) for which in range(2)]
        state_field = jnp.stack(mixed).reshape(2 * K, NJ, NI)
    return state_field * wet[None]
```

```python
import jax
import jax.numpy as jnp
from jax import lax
from jax.experimental import pallas as pl
from jax.experimental.pallas import tpu as pltpu
from jax.sharding import PartitionSpec as P

ITERS = 3
LEVELS = 75
PAD = 80
LANES = 128
BF = jnp.bfloat16
F32 = jnp.float32
VMEM_LIMIT = 56 * 1024 * 1024


def round_up(value, unit):
    return (value + unit - 1) // unit * unit


def split_two(value):
    high = value.astype(BF)
    low = (value - high.astype(F32)).astype(BF)
    return high, low


def mm(left, right):
    return jnp.dot(left, right, preferred_element_type=F32)


def slot_positions(owner_row, cell_row, col_count, row_count, capacity):
    count = owner_row.shape[1]
    base = owner_row.astype(F32) * float(row_count * count)
    inside = (cell_row // col_count).astype(F32) * float(count)
    order = lax.broadcasted_iota(jnp.int32, (1, count), 1).astype(F32)
    key = base + inside + order
    key_col = jnp.broadcast_to(key, (8, count)).T[:, 0:1]
    rank = jnp.zeros((1, count), F32)
    for start in range(0, count, 128):
        part = key_col[start : start + 128]
        before = (part < key) & (part >= base)
        rank = rank + jnp.sum(jnp.where(before, 1.0, 0.0), axis=0, keepdims=True)
    return owner_row.astype(F32) * float(capacity) + rank


def table_kernel(
    devices,
    capacity,
    group,
    row_count,
    col_count,
    value_ref,
    owner_ref,
    cell_ref,
    alt_value_ref,
    alt_owner_ref,
    alt_cell_ref,
    first_ref,
    second_ref,
    level_ref,
    alt_ref,
    hi_ref,
    lo_ref,
    alt_all_ref,
):
    n_obs = value_ref.shape[1]
    n_alt = alt_value_ref.shape[1]
    position = slot_positions(owner_ref[...], cell_ref[...], col_count, row_count, capacity)
    alt_position = slot_positions(
        alt_owner_ref[...], alt_cell_ref[...], col_count, row_count, capacity
    )
    level_ref[...] = jnp.zeros(level_ref.shape, F32)
    level_ref[0:75, :] = value_ref[0:75, :]
    level_ref[75:76, :] = cell_ref[...].astype(F32) + 1.0
    level_ref[80:128, :] = value_ref[75:123, :]
    for lane_group in range(4):
        level_ref[128 + 32 * lane_group : 155 + 32 * lane_group, :] = value_ref[123:150, :]
    high, low = split_two(level_ref[...].T)
    hi_ref[...] = high
    lo_ref[...] = low
    alt_ref[...] = jnp.zeros(alt_ref.shape, F32)
    pair = jnp.concatenate([alt_value_ref[...], alt_cell_ref[...].astype(F32) + 1.0], axis=0)
    pair_high = pair.astype(BF).astype(F32)
    alt_ref[76:78, :] = pair_high
    alt_ref[78:80, :] = pair - pair_high
    alt_all_ref[...] = alt_ref[...].T.astype(BF)
    per_step = max(1, 768 // capacity)
    rows = per_step * capacity

    def step(index, carry):
        slot = (lax.broadcasted_iota(jnp.int32, (rows, 1), 0) + index * rows).astype(F32)
        chosen = jnp.where(slot == position, 1.0, 0.0).astype(BF)
        chosen_alt = jnp.where(slot == alt_position, 1.0, 0.0).astype(BF)
        table = mm(chosen, hi_ref[...]) + mm(chosen, lo_ref[...])
        lane = lax.broadcasted_iota(jnp.int32, (1, LANES), 1)
        extra = mm(chosen_alt, alt_all_ref[...])
        extra = jnp.where(lane < 78, extra + pltpu.roll(extra, LANES - 2, 1), 0.0)
        extra = jnp.where(lane >= 76, extra, 0.0)
        first = table[:, :LANES] + extra
        start = index * per_step
        first_ref[pl.ds(start, per_step)] = first.reshape(per_step, capacity, LANES)
        rest = table[:, LANES:].reshape(per_step, capacity, LANES)
        total = jnp.zeros((per_step, group, LANES), F32)
        for lane_group in range(4):
            low_slot = lane_group * group
            if low_slot >= capacity:
                continue
            piece = rest[:, low_slot : low_slot + group]
            here = (lane // 32 == lane_group).reshape(1, 1, LANES)
            total = jnp.where(here, piece, total)
        second_ref[pl.ds(start, per_step)] = total
        return carry

    lax.fori_loop(0, devices // per_step, step, 0)


def send_tables(devices, capacity, group, row_count, col_count, values, owner, cell, alt_value, alt_owner, alt_cell):
    n_obs = owner.shape[1]
    n_alt = alt_owner.shape[1]

    def kernel(*refs):
        table_kernel(devices, capacity, group, row_count, col_count, *refs)

    return pl.pallas_call(
        kernel,
        out_shape=(
            jax.ShapeDtypeStruct((devices, capacity, LANES), F32),
            jax.ShapeDtypeStruct((devices, group, LANES), F32),
        ),
        scratch_shapes=[
            pltpu.VMEM((2 * LANES, n_obs), F32),
            pltpu.VMEM((LANES, n_alt), F32),
            pltpu.VMEM((n_obs, 2 * LANES), BF),
            pltpu.VMEM((n_obs, 2 * LANES), BF),
            pltpu.VMEM((n_alt, LANES), BF),
        ],
        compiler_params=pltpu.CompilerParams(vmem_limit_bytes=VMEM_LIMIT),
        name="send_tables",
    )(values, owner, cell, alt_value, alt_owner, alt_cell)


def add_columns(cols, state_row, row, row_count, first):
    lane = lax.broadcasted_iota(jnp.int32, (1, LANES), 1)
    west = pltpu.roll(state_row[:, :LANES], row, 1)
    east = pltpu.roll(state_row[:, -LANES:], row_count + 1 + row, 1)
    cols = jnp.where(lane == row, west, cols)
    return jnp.where(lane == row_count + row, east, cols)


def forcing_kernel(which, capacity, group, row_count, col_count, *refs):
    if which == 0:
        first_ref, profile_ref, state_ref, low_ref, top_ref, side_ref, sea_ref = refs
    else:
        first_ref, second_ref, profile_ref, sea_ref, state_ref, low_ref, top_ref, side_ref = refs
    devices = first_ref.shape[0]
    block = min(32, devices)
    members = block * 8
    octets = capacity // 8
    per_group = group // 8
    col_iota = lax.broadcasted_iota(jnp.int32, (1, col_count), 1)
    row_iota = lax.broadcasted_iota(jnp.int32, (row_count, 1), 0)

    def chunk(index, octet):
        begin = pl.multiple_of(octet * 8, 8)
        return first_ref[pl.ds(index * block, block), pl.ds(begin, 8), :].reshape(members, LANES)

    if which == 0:
        sea_ref[...] = jnp.zeros(sea_ref.shape, F32)

        def sea_step(step, carry):
            table = chunk(step // octets, step % octets)
            cell = table[:, 77:78].astype(jnp.int32) - 1
            hot = jnp.where((cell & (col_count - 1)) == col_iota, 1.0, 0.0).astype(BF)
            turned = table.T
            value = turned[76:77, :]
            rows = lax.shift_right_arithmetic(
                turned[77:78, :].astype(jnp.int32) - 1, col_count.bit_length() - 1
            )
            weighted = jnp.where(rows == row_iota, value, 0.0)
            high, low = split_two(weighted)
            sea_ref[...] += mm(high, hot) + mm(low, hot)
            return carry

        lax.fori_loop(0, octets * (devices // block), sea_step, 0)

    profile = jnp.broadcast_to(profile_ref[...], (PAD, LANES))

    def init(row, carry):
        line = sea_ref[pl.ds(row, 1), :]
        for start in range(0, col_count, LANES):
            state_ref[row, :, start : start + LANES] = profile * line[:, start : start + LANES]
        return carry

    lax.fori_loop(0, row_count, init, 0)
    span = 4

    def step(number, carry):
        index = number // octets
        octet = number % octets
        table = chunk(index, octet)
        cell = table[:, 75:76].astype(jnp.int32) - 1
        hot = jnp.where((cell & (col_count - 1)) == col_iota, 1.0, 0.0).astype(BF)
        turned = table.T
        rows = lax.shift_right_arithmetic(
            turned[75:76, :].astype(jnp.int32) - 1, col_count.bit_length() - 1
        )
        if which == 0:
            levels = turned[0:PAD]
        else:
            begin = pl.multiple_of((octet % per_group) * 8, 8)
            rest = second_ref[pl.ds(index * block, block), pl.ds(begin, 8), :]
            rest = rest.reshape(members, LANES).T
            lane_group = octet // per_group
            tail = rest[0:32]
            for other in range(1, 4):
                tail = jnp.where(lane_group == other, rest[32 * other : 32 * other + 32], tail)
            levels = jnp.concatenate([turned[80:128], tail], axis=0)
        high, low = split_two(levels)
        both = jnp.concatenate([high, low], axis=0)
        least = jnp.min(jnp.where(rows >= 0, rows, row_count))
        most = jnp.max(rows)

        def rows_step(start, inner):
            base = start * span
            pieces = []
            for offset in range(span):
                mask = jnp.where(rows == base + offset, 1.0, 0.0).astype(BF)
                pieces.append(both * mask)
            product = mm(jnp.concatenate(pieces, axis=0), hot)
            for offset in range(span):
                at = 2 * PAD * offset
                state_ref[base + offset] += product[at : at + PAD] + product[at + PAD : at + 2 * PAD]
            return inner

        lax.fori_loop(least // span, most // span + 1, rows_step, 0)
        return carry

    lax.fori_loop(0, octets * (devices // block), step, 0)
    low_ref[...] = state_ref[0]
    top_ref[...] = state_ref[row_count - 1]
    side_ref[:, LANES:] = state_ref[row_count - 1]

    def sides(row, cols):
        return add_columns(cols, state_ref[row], row, row_count, False)

    side_ref[:, :LANES] = lax.fori_loop(0, row_count, sides, jnp.zeros((PAD, LANES), F32))


def state_shapes(row_count, col_count):
    return (
        jax.ShapeDtypeStruct((row_count, PAD, col_count), F32),
        jax.ShapeDtypeStruct((PAD, col_count), F32),
        jax.ShapeDtypeStruct((PAD, col_count), F32),
        jax.ShapeDtypeStruct((PAD, LANES + col_count), F32),
    )


def make_forcing(which, capacity, group, row_count, col_count, operands):
    def kernel(*refs):
        forcing_kernel(which, capacity, group, row_count, col_count, *refs)

    shapes = state_shapes(row_count, col_count)
    if which == 0:
        shapes = shapes + (jax.ShapeDtypeStruct((row_count, col_count), F32),)
    return pl.pallas_call(
        kernel,
        out_shape=shapes,
        compiler_params=pltpu.CompilerParams(vmem_limit_bytes=VMEM_LIMIT),
        cost_estimate=pl.CostEstimate(
            flops=5_000_000_000, bytes_accessed=6_000_000, transcendentals=0
        ),
        name="forcing_" + ("temperature", "salinity")[which],
    )(*operands)


def diffusion_kernel(
    row_count,
    col_count,
    step_rows,
    flag_ref,
    state_ref,
    below_ref,
    above_ref,
    south_ref,
    north_ref,
    from_west_ref,
    from_east_ref,
    mirror_ref,
    coef_ref,
    matrix_ref,
    out_ref,
    low_ref,
    top_ref,
    side_ref,
):
    step = pl.program_id(0)
    steps = pl.num_programs(0)
    lane = lax.broadcasted_iota(jnp.int32, (1, LANES), 1)
    chunks = col_count // LANES
    is_top = flag_ref[0] > 0
    odd = flag_ref[1] > 0
    first = step == 0
    last = step == steps - 1

    @pl.when(first)
    def _():
        side_ref[...] = jnp.zeros(side_ref.shape, F32)

    for offset in range(step_rows):
        row = step * step_rows + offset

        def piece(chunk):
            return slice(chunk * LANES, (chunk + 1) * LANES)

        centers = [state_ref[offset, :, piece(c)] for c in range(chunks)]
        to_left = [pltpu.roll(c, LANES - 1, 1) for c in centers]
        to_right = [pltpu.roll(c, 1, 1) for c in centers]
        west_halo = pltpu.roll(
            from_west_ref[:, :LANES], lax.rem(2 * LANES - row_count - row, LANES), 1
        )
        east_halo = pltpu.roll(from_east_ref[:, :LANES], LANES - 1 - row, 1)
        outputs = []
        highs = []
        lows = []
        for c in range(chunks):
            if offset > 0:
                south = state_ref[offset - 1, :, piece(c)]
            else:
                south = jnp.where(first, south_ref[:, piece(c)], below_ref[0, :, piece(c)])
            if offset < step_rows - 1:
                north = state_ref[offset + 1, :, piece(c)]
            else:
                mirrored = slice(
                    LANES + (chunks - 1 - c) * LANES, LANES + (chunks - c) * LANES
                )
                partner = jnp.where(odd, from_east_ref[:, mirrored], from_west_ref[:, mirrored])
                index = jnp.broadcast_to(mirror_ref[0:1, piece(c)], (PAD, LANES))
                folded = jnp.take_along_axis(partner, index, axis=1)
                north = jnp.where(is_top, folded, north_ref[:, piece(c)])
                north = jnp.where(last, north, above_ref[0, :, piece(c)])
            right = to_left[c + 1] if c + 1 < chunks else east_halo
            left = to_right[c - 1] if c > 0 else west_halo
            east = jnp.where(lane == LANES - 1, right, to_left[c])
            west = jnp.where(lane == 0, left, to_right[c])

            def coef(kind):
                return coef_ref[offset, kind : kind + 1, piece(c)]

            mixed = (
                coef(0) * centers[c]
                + coef(1) * east
                + coef(2) * west
                + coef(3) * north
                + coef(4) * south
            )
            high, low = split_two(mixed)
            highs.append(high)
            lows.append(low)
        high = jnp.concatenate(highs, axis=1)
        low = jnp.concatenate(lows, axis=1)
        result = mm(matrix_ref[offset], jnp.concatenate([high, low, high], axis=0))
        out_ref[offset] = result
        side_ref[:, :LANES] = add_columns(side_ref[:, :LANES], result, row, row_count, False)
        if offset == 0:

            @pl.when(first)
            def _():
                low_ref[...] = result

        if offset == step_rows - 1:

            @pl.when(last)
            def _():
                top_ref[...] = result
                side_ref[:, LANES:] = result


def diffuse(flags, state, south, north, from_west, from_east, mirror, coef, matrix):
    row_count, _, col_count = state.shape
    step_rows = 4
    steps = row_count // step_rows

    def kernel(*refs):
        diffusion_kernel(row_count, col_count, step_rows, *refs)

    def whole(array):
        return pl.BlockSpec(array.shape, lambda s: (0,) * array.ndim)

    shapes = state_shapes(row_count, col_count)
    one = (1, PAD, col_count)
    block = (step_rows, PAD, col_count)
    return pl.pallas_call(
        kernel,
        grid=(steps,),
        in_specs=[
            pl.BlockSpec(memory_space=pltpu.SMEM),
            pl.BlockSpec(block, lambda s: (s, 0, 0)),
            pl.BlockSpec(one, lambda s: (jnp.maximum(s * step_rows - 1, 0), 0, 0)),
            pl.BlockSpec(
                one, lambda s: (jnp.minimum(s * step_rows + step_rows, row_count - 1), 0, 0)
            ),
            whole(south),
            whole(north),
            whole(from_west),
            whole(from_east),
            whole(mirror),
            pl.BlockSpec((step_rows,) + coef.shape[1:], lambda s: (s, 0, 0)),
            pl.BlockSpec((step_rows,) + matrix.shape[1:], lambda s: (s, 0, 0)),
        ],
        out_specs=[
            pl.BlockSpec(block, lambda s: (s, 0, 0)),
            whole(shapes[1]),
            whole(shapes[2]),
            whole(shapes[3]),
        ],
        out_shape=shapes,
        compiler_params=pltpu.CompilerParams(vmem_limit_bytes=VMEM_LIMIT),
        cost_estimate=pl.CostEstimate(
            flops=3_000_000_000, bytes_accessed=8_000_000, transcendentals=0
        ),
        name="diffusion",
    )(flags, state, state, state, south, north, from_west, from_east, mirror, coef, matrix)


def with_halo(cells, sides, width):
    for axis, dim in sides:
        count = lax.axis_size(axis)
        head = lax.slice_in_dim(cells, 0, width, axis=dim)
        tail = lax.slice_in_dim(cells, cells.shape[dim] - width, cells.shape[dim], axis=dim)
        cells = jnp.concatenate(
            [
                lax.ppermute(tail, axis, [(i, (i + 1) % count) for i in range(count)]),
                cells,
                lax.ppermute(head, axis, [((i + 1) % count, i) for i in range(count)]),
            ],
            axis=dim,
        )
    return cells


def edge_coefficients(land_mask, coef_east, coef_north, fold_index):
    row_count, col_count = land_mask.shape
    count_ja = lax.axis_size("ja")
    count_ia = lax.axis_size("ia")
    wet = land_mask.astype(F32)
    coast = with_halo(jnp.stack([wet, coef_east, coef_north]), (("ja", 1), ("ia", 2)), 1)
    wet_pad, east_pad, north_pad = coast[0], coast[1], coast[2]
    ja_index = lax.axis_index("ja")
    row_index = ja_index * row_count + jnp.arange(row_count, dtype=jnp.int32)
    not_top = (row_index != row_count * count_ja - 1).astype(F32)[:, None]
    not_bottom = (row_index != 0).astype(F32)[:, None]
    east_w = east_pad[1:-1, 1:-1] * wet_pad[1:-1, 1:-1] * wet_pad[1:-1, 2:]
    west_w = east_pad[1:-1, :-2] * wet_pad[1:-1, :-2] * wet_pad[1:-1, 1:-1]
    north_w = north_pad[1:-1, 1:-1] * wet_pad[1:-1, 1:-1] * wet_pad[2:, 1:-1] * not_top
    south_w = north_pad[:-2, 1:-1] * wet_pad[:-2, 1:-1] * wet_pad[1:-1, 1:-1] * not_bottom
    top_rows = jnp.stack([wet[-1], coef_north[-1]])
    partner = lax.ppermute(top_rows, "ia", [(i, count_ia - 1 - i) for i in range(count_ia)])
    partner = jnp.take(partner, fold_index, axis=1)
    fold_w = 0.5 * (coef_north[-1] + partner[1]) * wet[-1] * partner[0]
    north_w = north_w + (1.0 - not_top) * fold_w[None, :]
    center = 1.0 - (east_w + west_w + north_w + south_w)
    return jnp.stack([center, east_w, west_w, north_w, south_w], axis=1)


def mixing_matrices(vinv):
    turned = jnp.transpose(vinv, (1, 0, 3, 2))
    turned = jnp.pad(turned, ((0, 0), (0, 0), (0, PAD - LEVELS), (0, PAD - LEVELS)))
    high = lax.reduce_precision(turned, 8, 7)
    low = (turned - high).astype(BF)
    high = high.astype(BF)
    return jnp.concatenate([high, high, low], axis=3)


def body(
    argo_value,
    argo_owner,
    argo_cell,
    alt_value,
    alt_owner,
    alt_cell,
    alt_profile,
    land_mask,
    coef_east,
    coef_north,
    mirror,
    vinv,
):
    row_count, col_count = land_mask.shape
    count_ja = lax.axis_size("ja")
    count_ia = lax.axis_size("ia")
    devices = count_ja * count_ia
    capacity = round_up(3 * argo_value.shape[0] // devices, 8)
    group = round_up(capacity // 4, 8)
    first, second = send_tables(
        devices,
        capacity,
        group,
        row_count,
        col_count,
        argo_value.T,
        argo_owner.reshape(1, -1),
        argo_cell.reshape(1, -1),
        alt_value.reshape(1, -1),
        alt_owner.reshape(1, -1),
        alt_cell.reshape(1, -1),
    )
    first = lax.all_to_all(first, ("ja", "ia"), split_axis=0, concat_axis=0, tiled=True)
    second = lax.all_to_all(second, ("ja", "ia"), split_axis=0, concat_axis=0, tiled=True)

    ia_index = lax.axis_index("ia")
    is_top = (lax.axis_index("ja") == count_ja - 1).astype(jnp.int32)
    flags = jnp.stack([is_top, ia_index % 2]).astype(jnp.int32)
    fold_index = mirror - (count_ia - 1 - ia_index) * col_count
    mirror_lane = jnp.broadcast_to((fold_index % LANES)[None, :], (8, col_count))
    coef = edge_coefficients(land_mask, coef_east, coef_north, fold_index)
    matrices = mixing_matrices(vinv)
    profiles = jnp.pad(alt_profile.reshape(2, LEVELS, 1), ((0, 0), (0, PAD - LEVELS), (0, 0)))

    *temperature, sea = make_forcing(
        0, capacity, group, row_count, col_count, (first, profiles[0])
    )
    salinity = make_forcing(
        1, capacity, group, row_count, col_count, (first, second, profiles[1], sea)
    )
    fields = [temperature, salinity]

    ring_east = [(i, (i + 1) % count_ia) for i in range(count_ia)]
    ring_west = [((i + 1) % count_ia, i) for i in range(count_ia)]
    upward = [(i, i + 1) for i in range(count_ja - 1)]
    downward = [(i + 1, i) for i in range(count_ja - 1)]
    for sweep in range(ITERS):
        for which in range(2):
            state, low, top, side = fields[which]
            south = lax.ppermute(top, "ja", upward)
            north = lax.ppermute(low, "ja", downward)
            from_west = lax.ppermute(side, "ia", ring_east)
            from_east = lax.ppermute(side, "ia", ring_west)
            fields[which] = diffuse(
                flags,
                state,
                south,
                north,
                from_west,
                from_east,
                mirror_lane,
                coef,
                matrices[which],
            )
    wet = land_mask.astype(F32)
    both = jnp.concatenate([fields[0][0][:, :LEVELS], fields[1][0][:, :LEVELS]], axis=1)
    return jnp.transpose(both * wet[:, None, :], (1, 0, 2))


def solution(mesh):
    in_specs = (
        P(("ja", "ia"), None),
        P(("ja", "ia"), None),
        P(("ja", "ia")),
        P(("ja", "ia")),
        P(("ja", "ia"), None),
        P(("ja", "ia")),
        P(),
        P("ja", "ia"),
        P("ja", "ia"),
        P("ja", "ia"),
        P("ia"),
        P("ja", None, None, None),
    )
    out_specs = P(None, "ja", "ia")
    return jax.shard_map(body, mesh=mesh, in_specs=in_specs, out_specs=out_specs, check_vma=False)
```

```python
import jax
import jax.numpy as jnp
from jax import lax
from jax.experimental import pallas as pl
from jax.experimental.pallas import tpu as pltpu
from jax.sharding import PartitionSpec as P

ITERS = 3
LEVELS = 75
PAD = 80
LANES = 128
BF = jnp.bfloat16
F32 = jnp.float32
MIB = 1024 * 1024


def round_up(value, unit):
    return (value + unit - 1) // unit * unit


def split_two(value):
    high = value.astype(BF)
    low = (value - high.astype(F32)).astype(BF)
    return high, low


def mm(left, right):
    return jnp.dot(left, right, preferred_element_type=F32)


def slot_positions(owner_row, cell_row, col_count, row_count, capacity):
    count = owner_row.shape[1]
    base = owner_row.astype(F32) * float(row_count * count)
    inside = (cell_row // col_count).astype(F32) * float(count)
    order = lax.broadcasted_iota(jnp.int32, (1, count), 1).astype(F32)
    key = base + inside + order
    key_col = jnp.broadcast_to(key, (8, count)).T[:, 0:1]
    rank = jnp.zeros((1, count), F32)
    for start in range(0, count, 128):
        part = key_col[start : start + 128]
        before = (part < key) & (part >= base)
        rank = rank + jnp.sum(jnp.where(before, 1.0, 0.0), axis=0, keepdims=True)
    return owner_row.astype(F32) * float(capacity) + rank


def table_kernel(
    devices,
    capacity,
    group,
    row_count,
    col_count,
    value_ref,
    owner_ref,
    cell_ref,
    alt_value_ref,
    alt_owner_ref,
    alt_cell_ref,
    message_ref,
    level_ref,
    alt_ref,
    hi_ref,
    lo_ref,
    alt_all_ref,
):
    position = slot_positions(owner_ref[...], cell_ref[...], col_count, row_count, capacity)
    alt_position = slot_positions(
        alt_owner_ref[...], alt_cell_ref[...], col_count, row_count, capacity
    )
    level_ref[...] = jnp.zeros(level_ref.shape, F32)
    level_ref[0:75, :] = value_ref[0:75, :]
    level_ref[75:76, :] = cell_ref[...].astype(F32) + 1.0
    level_ref[80:128, :] = value_ref[75:123, :]
    for lane_group in range(4):
        level_ref[128 + 32 * lane_group : 155 + 32 * lane_group, :] = value_ref[123:150, :]
    high, low = split_two(level_ref[...].T)
    hi_ref[...] = high
    lo_ref[...] = low
    alt_ref[...] = jnp.zeros(alt_ref.shape, F32)
    pair = jnp.concatenate([alt_value_ref[...], alt_cell_ref[...].astype(F32) + 1.0], axis=0)
    pair_high = pair.astype(BF).astype(F32)
    alt_ref[76:78, :] = pair_high
    alt_ref[78:80, :] = pair - pair_high
    alt_all_ref[...] = alt_ref[...].T.astype(BF)
    per_step = max(1, 768 // capacity)
    rows = per_step * capacity

    def step(index, carry):
        slot = (lax.broadcasted_iota(jnp.int32, (rows, 1), 0) + index * rows).astype(F32)
        chosen = jnp.where(slot == position, 1.0, 0.0).astype(BF)
        chosen_alt = jnp.where(slot == alt_position, 1.0, 0.0).astype(BF)
        table = mm(chosen, hi_ref[...]) + mm(chosen, lo_ref[...])
        lane = lax.broadcasted_iota(jnp.int32, (1, LANES), 1)
        extra = mm(chosen_alt, alt_all_ref[...])
        extra = jnp.where(lane < 78, extra + pltpu.roll(extra, LANES - 2, 1), 0.0)
        extra = jnp.where(lane >= 76, extra, 0.0)
        first = table[:, :LANES] + extra
        start = index * per_step
        message_ref[pl.ds(start, per_step), 0:capacity] = first.reshape(per_step, capacity, LANES)
        rest = table[:, LANES:].reshape(per_step, capacity, LANES)
        total = jnp.zeros((per_step, group, LANES), F32)
        for lane_group in range(4):
            low_slot = lane_group * group
            if low_slot >= capacity:
                continue
            piece = rest[:, low_slot : low_slot + group]
            here = (lane // 32 == lane_group).reshape(1, 1, LANES)
            total = jnp.where(here, piece, total)
        message_ref[pl.ds(start, per_step), capacity : capacity + group] = total
        return carry

    lax.fori_loop(0, devices // per_step, step, 0)


def send_tables(devices, capacity, group, row_count, col_count, values, owner, cell, alt_value, alt_owner, alt_cell):
    n_obs = owner.shape[1]
    n_alt = alt_owner.shape[1]

    def kernel(*refs):
        table_kernel(devices, capacity, group, row_count, col_count, *refs)

    return pl.pallas_call(
        kernel,
        out_shape=jax.ShapeDtypeStruct((devices, capacity + group, LANES), F32),
        scratch_shapes=[
            pltpu.VMEM((2 * LANES, n_obs), F32),
            pltpu.VMEM((LANES, n_alt), F32),
            pltpu.VMEM((n_obs, 2 * LANES), BF),
            pltpu.VMEM((n_obs, 2 * LANES), BF),
            pltpu.VMEM((n_alt, LANES), BF),
        ],
        compiler_params=pltpu.CompilerParams(vmem_limit_bytes=40 * MIB),
        name="send_tables",
    )(values, owner, cell, alt_value, alt_owner, alt_cell)


def add_columns(cols, state_row, row, row_count):
    lane = lax.broadcasted_iota(jnp.int32, (1, LANES), 1)
    west = pltpu.roll(state_row[:, :LANES], row, 1)
    east = pltpu.roll(state_row[:, -LANES:], row_count + 1 + row, 1)
    cols = jnp.where(lane == row, west, cols)
    return jnp.where(lane == row_count + row, east, cols)


def write_edge(edge, odd, even_ref, odd_ref, is_low):
    to_odd = jnp.logical_not(odd) if is_low else odd

    @pl.when(to_odd)
    def _():
        odd_ref[...] = edge

    @pl.when(jnp.logical_not(to_odd))
    def _():
        even_ref[...] = edge


def forcing_kernel(
    capacity,
    group,
    row_count,
    col_count,
    flag_ref,
    message_ref,
    profile_ref,
    state_t,
    even_t,
    odd_t,
    cols_t,
    state_s,
    even_s,
    odd_s,
    cols_s,
    left_ref,
    hot_ref,
    rows_ref,
    sea_ref,
):
    devices = message_ref.shape[0]
    block = min(32, devices)
    members = block * 8
    octets = capacity // 8
    per_group = group // 8
    shift = col_count.bit_length() - 1
    col_iota = lax.broadcasted_iota(jnp.int32, (1, col_count), 1)
    row_iota = lax.broadcasted_iota(jnp.int32, (row_count, 1), 0)
    odd = flag_ref[1] > 0

    def chunk(index, start):
        return message_ref[index * block : (index + 1) * block, start : start + 8, :].reshape(
            members, LANES
        )

    def hot_of(cell):
        return jnp.where(((cell - 1) & (col_count - 1)) == col_iota, 1.0, 0.0).astype(BF)

    def rows_of(cell):
        return lax.shift_right_arithmetic(cell - 1, shift)

    sea = jnp.zeros((row_count, col_count), F32)
    count = 0
    for index in range(devices // block):
        tails = [
            chunk(index, capacity + 8 * part).T for part in range(per_group)
        ]
        for octet in range(octets):
            table = chunk(index, 8 * octet)
            turned = table.T
            tail = tails[octet % per_group]
            begin = 32 * (octet // per_group)
            levels = jnp.concatenate([turned, tail[begin : begin + 32]], axis=0)
            high, low = split_two(levels)
            left_ref[count, :, 0:members] = high
            left_ref[count, :, members : 2 * members] = low
            hot = hot_of(table[:, 75:76].astype(jnp.int32))
            hot_ref[count, 0:members] = hot
            hot_ref[count, members : 2 * members] = hot
            rows_ref[count] = jnp.broadcast_to(rows_of(turned[75:76].astype(jnp.int32)), (8, members))
            alt_hot = hot_of(table[:, 77:78].astype(jnp.int32))
            alt_rows = rows_of(turned[77:78].astype(jnp.int32))
            weighted = jnp.where(alt_rows == row_iota, turned[76:77], 0.0)
            high, low = split_two(weighted)
            product = mm(jnp.concatenate([high, low], axis=0), alt_hot)
            sea = sea + product[:row_count] + product[row_count:]
            count += 1
    sea_ref[...] = sea
    for start in range(0, col_count, LANES):
        for field, state in ((0, state_t), (1, state_s)):
            profile = jnp.broadcast_to(profile_ref[field], (PAD, LANES))
            for row in range(row_count):
                state[row, :, start : start + LANES] = (
                    profile * sea_ref[row : row + 1, start : start + LANES]
                )
    span = 4

    def step(number, carry):
        rows = rows_ref[number][0:1]
        least = jnp.min(jnp.where(rows >= 0, rows, row_count))
        most = jnp.max(rows)

        def rows_step(start, inner):
            base = start * span
            pieces = []
            for offset in range(span):
                mask = jnp.where(rows == base + offset, 1.0, 0.0).astype(BF)
                pieces.append(left_ref[number] * jnp.concatenate([mask, mask], axis=1))
            product = mm(jnp.concatenate(pieces, axis=0), hot_ref[number])
            for offset in range(span):
                at = 2 * PAD * offset
                state_t[base + offset] += product[at : at + PAD]
                state_s[base + offset] += product[at + PAD : at + 2 * PAD]
            return inner

        lax.fori_loop(least // span, most // span + 1, rows_step, 0)
        return carry

    lax.fori_loop(0, count, step, 0)
    for state, even_ref, odd_ref, cols_ref in (
        (state_t, even_t, odd_t, cols_t),
        (state_s, even_s, odd_s, cols_s),
    ):
        cols = jnp.zeros((PAD, LANES), F32)
        for row in range(row_count):
            cols = add_columns(cols, state[row], row, row_count)
        cols_ref[...] = cols
        write_edge(state[0], odd, even_ref, odd_ref, True)
        write_edge(state[row_count - 1], odd, even_ref, odd_ref, False)


def field_shapes(row_count, col_count):
    return (
        jax.ShapeDtypeStruct((row_count, PAD, col_count), F32),
        jax.ShapeDtypeStruct((PAD, col_count), F32),
        jax.ShapeDtypeStruct((PAD, col_count), F32),
        jax.ShapeDtypeStruct((PAD, LANES), F32),
    )


def make_forcing(capacity, group, row_count, col_count, flags, message, profiles):
    def kernel(*refs):
        forcing_kernel(capacity, group, row_count, col_count, *refs)

    devices = message.shape[0]
    members = min(32, devices) * 8
    chunks = capacity // 8 * (devices // min(32, devices))
    results = pl.pallas_call(
        kernel,
        in_specs=[
            pl.BlockSpec(memory_space=pltpu.SMEM),
            pl.BlockSpec(memory_space=pltpu.VMEM),
            pl.BlockSpec(memory_space=pltpu.VMEM),
        ],
        out_shape=field_shapes(row_count, col_count) * 2,
        scratch_shapes=[
            pltpu.VMEM((chunks, 2 * PAD, 2 * members), BF),
            pltpu.VMEM((chunks, 2 * members, col_count), BF),
            pltpu.VMEM((chunks, 8, members), jnp.int32),
            pltpu.VMEM((row_count, col_count), F32),
        ],
        compiler_params=pltpu.CompilerParams(vmem_limit_bytes=48 * MIB),
        name="forcing",
    )(flags, message, profiles)
    return [list(results[:4]), list(results[4:])]


def diffusion_kernel(row_count, col_count, step_rows, final, *refs):
    (
        flag_ref,
        state_ref,
        below_ref,
        above_ref,
        even_in,
        odd_in,
        from_west_ref,
        from_east_ref,
        mirror_ref,
        coef_ref,
        matrix_ref,
    ) = refs[:11]
    if final:
        wet_ref = refs[11]
        out_ref, south_ref, north_ref, right_ref = refs[-4:]
    else:
        out_ref, even_ref, odd_ref, cols_ref, south_ref, north_ref, right_ref = refs[-7:]
    step = pl.program_id(0)
    lane = lax.broadcasted_iota(jnp.int32, (1, LANES), 1)
    chunks = col_count // LANES
    is_top = flag_ref[0] > 0
    odd = flag_ref[1] > 0
    even = jnp.logical_not(odd)
    first = step == 0
    last = step == pl.num_programs(0) - 1

    def piece(chunk):
        return slice(chunk * LANES, (chunk + 1) * LANES)

    @pl.when(jnp.logical_not(first))
    def _():
        south_ref[...] = below_ref[0]

    @pl.when(jnp.logical_not(last))
    def _():
        north_ref[...] = above_ref[0]

    @pl.when(first)
    def _():
        right_ref[:, 3 * PAD :, :] = jnp.zeros((step_rows, 16, col_count), BF)
        if not final:
            cols_ref[...] = jnp.zeros(cols_ref.shape, F32)

    @pl.when(first & even)
    def _():
        south_ref[...] = odd_in[...]

    @pl.when(first & odd)
    def _():
        south_ref[...] = even_in[...]

    @pl.when(last & even)
    def _():
        north_ref[...] = even_in[...]

    @pl.when(last & odd & jnp.logical_not(is_top))
    def _():
        north_ref[...] = odd_in[...]

    @pl.when(last & is_top)
    def _():
        for c in range(chunks):
            index = jnp.broadcast_to(mirror_ref[0:1, piece(c)], (PAD, LANES))
            north_ref[:, piece(c)] = jnp.take_along_axis(
                odd_in[:, piece(chunks - 1 - c)], index, axis=1
            )

    def mix(offset):
        row = step * step_rows + offset
        centers = [state_ref[offset, :, piece(c)] for c in range(chunks)]
        to_left = [pltpu.roll(c, LANES - 1, 1) for c in centers]
        to_right = [pltpu.roll(c, 1, 1) for c in centers]
        to_right.append(
            pltpu.roll(from_west_ref[...], lax.rem(2 * LANES - row_count - row, LANES), 1)
        )
        to_left.append(pltpu.roll(from_east_ref[...], LANES - 1 - row, 1))
        for c in range(chunks):
            south = state_ref[offset - 1, :, piece(c)] if offset > 0 else south_ref[:, piece(c)]
            if offset < step_rows - 1:
                north = state_ref[offset + 1, :, piece(c)]
            else:
                north = north_ref[:, piece(c)]
            east = jnp.where(lane == LANES - 1, to_left[c + 1], to_left[c])
            west = jnp.where(lane == 0, to_right[c - 1], to_right[c])

            def coef(kind):
                return coef_ref[offset, kind : kind + 1, piece(c)]

            mixed = (
                coef(0) * centers[c]
                + coef(1) * east
                + coef(2) * west
                + coef(3) * north
                + coef(4) * south
            )
            high, low = split_two(mixed)
            right_ref[offset, 0:PAD, piece(c)] = high
            right_ref[offset, PAD : 2 * PAD, piece(c)] = low
            right_ref[offset, 2 * PAD : 3 * PAD, piece(c)] = high

    def product(offset):
        result = mm(matrix_ref[offset], right_ref[offset])
        if final:
            return result * wet_ref[offset : offset + 1, :]
        out_ref[offset] = result
        return result

    results = []
    for offset in range(step_rows):
        mix(offset)
        if offset > 0:
            results.append(product(offset - 1))
    results.append(product(step_rows - 1))
    if final:
        turned = jnp.swapaxes(jnp.stack(results), 0, 1)
        out_ref[...] = turned[:LEVELS]
        return
    cols = cols_ref[...]
    for offset in range(step_rows):
        cols = add_columns(cols, results[offset], step * step_rows + offset, row_count)
    cols_ref[...] = cols

    @pl.when(first)
    def _():
        write_edge(out_ref[0], odd, even_ref, odd_ref, True)

    @pl.when(last)
    def _():
        write_edge(out_ref[step_rows - 1], odd, even_ref, odd_ref, False)


def diffuse(flags, state, received, mirror, coef, matrix, final=None):
    row_count, _, col_count = state.shape
    step_rows = 4 if final is None else 8
    steps = row_count // step_rows

    def kernel(*refs):
        diffusion_kernel(row_count, col_count, step_rows, final is not None, *refs)

    def whole(array):
        return pl.BlockSpec(array.shape, lambda s: (0,) * len(array.shape))

    one = (1, PAD, col_count)
    block = (step_rows, PAD, col_count)
    in_specs = [
        pl.BlockSpec(memory_space=pltpu.SMEM),
        pl.BlockSpec(block, lambda s: (s, 0, 0)),
        pl.BlockSpec(one, lambda s: (jnp.maximum(s * step_rows - 1, 0), 0, 0)),
        pl.BlockSpec(
            one, lambda s: (jnp.minimum(s * step_rows + step_rows, row_count - 1), 0, 0)
        ),
        *[whole(array) for array in received],
        whole(mirror),
        pl.BlockSpec((step_rows,) + coef.shape[1:], lambda s: (s, 0, 0)),
        pl.BlockSpec((step_rows,) + matrix.shape[1:], lambda s: (s, 0, 0)),
    ]
    operands = [flags, state, state, state, *received, mirror, coef, matrix]
    aliases = {}
    if final is None:
        shapes = field_shapes(row_count, col_count)
        out_specs = [pl.BlockSpec(block, lambda s: (s, 0, 0)), *[whole(x) for x in shapes[1:]]]
    else:
        which, wet, target = final
        shapes = jax.ShapeDtypeStruct((2 * LEVELS, row_count, col_count), F32)
        out_specs = pl.BlockSpec((LEVELS, step_rows, col_count), lambda s: (which, s, 0))
        in_specs.append(pl.BlockSpec((step_rows, col_count), lambda s: (s, 0)))
        operands.append(wet)
        if target is not None:
            in_specs.append(pl.BlockSpec(memory_space=pl.ANY))
            operands.append(target)
            aliases = {len(operands) - 1: 0}
    return pl.pallas_call(
        kernel,
        grid=(steps,),
        in_specs=in_specs,
        out_specs=out_specs,
        out_shape=shapes,
        input_output_aliases=aliases,
        scratch_shapes=[
            pltpu.VMEM((PAD, col_count), F32),
            pltpu.VMEM((PAD, col_count), F32),
            pltpu.VMEM((step_rows, 256, col_count), BF),
        ],
        compiler_params=pltpu.CompilerParams(vmem_limit_bytes=28 * MIB),
        cost_estimate=pl.CostEstimate(
            flops=3_000_000_000, bytes_accessed=8_000_000, transcendentals=0
        ),
        name="diffusion",
    )(*operands)


def with_halo(cells, sides, width):
    for axis, dim in sides:
        count = lax.axis_size(axis)
        head = lax.slice_in_dim(cells, 0, width, axis=dim)
        tail = lax.slice_in_dim(cells, cells.shape[dim] - width, cells.shape[dim], axis=dim)
        cells = jnp.concatenate(
            [
                lax.ppermute(tail, axis, [(i, (i + 1) % count) for i in range(count)]),
                cells,
                lax.ppermute(head, axis, [((i + 1) % count, i) for i in range(count)]),
            ],
            axis=dim,
        )
    return cells


def edge_coefficients(land_mask, coef_east, coef_north, fold_index):
    row_count, col_count = land_mask.shape
    count_ja = lax.axis_size("ja")
    count_ia = lax.axis_size("ia")
    wet = land_mask.astype(F32)
    coast = with_halo(jnp.stack([wet, coef_east, coef_north]), (("ja", 1), ("ia", 2)), 1)
    wet_pad, east_pad, north_pad = coast[0], coast[1], coast[2]
    ja_index = lax.axis_index("ja")
    row_index = ja_index * row_count + jnp.arange(row_count, dtype=jnp.int32)
    not_top = (row_index != row_count * count_ja - 1).astype(F32)[:, None]
    not_bottom = (row_index != 0).astype(F32)[:, None]
    east_w = east_pad[1:-1, 1:-1] * wet_pad[1:-1, 1:-1] * wet_pad[1:-1, 2:]
    west_w = east_pad[1:-1, :-2] * wet_pad[1:-1, :-2] * wet_pad[1:-1, 1:-1]
    north_w = north_pad[1:-1, 1:-1] * wet_pad[1:-1, 1:-1] * wet_pad[2:, 1:-1] * not_top
    south_w = north_pad[:-2, 1:-1] * wet_pad[:-2, 1:-1] * wet_pad[1:-1, 1:-1] * not_bottom
    top_rows = jnp.stack([wet[-1], coef_north[-1]])
    partner = lax.ppermute(top_rows, "ia", [(i, count_ia - 1 - i) for i in range(count_ia)])
    partner = jnp.take(partner, fold_index, axis=1)
    fold_w = 0.5 * (coef_north[-1] + partner[1]) * wet[-1] * partner[0]
    north_w = north_w + (1.0 - not_top) * fold_w[None, :]
    center = 1.0 - (east_w + west_w + north_w + south_w)
    return jnp.stack([center, east_w, west_w, north_w, south_w], axis=1)


def mixing_matrices(vinv):
    turned = jnp.transpose(vinv, (1, 0, 3, 2))
    turned = jnp.pad(turned, ((0, 0), (0, 0), (0, PAD - LEVELS), (0, PAD - LEVELS)))
    high = lax.reduce_precision(turned, 8, 7)
    low = (turned - high).astype(BF)
    high = high.astype(BF)
    rest = jnp.zeros(high.shape[:3] + (256 - 3 * PAD,), BF)
    return jnp.concatenate([high, high, low, rest], axis=3)


def body(
    argo_value,
    argo_owner,
    argo_cell,
    alt_value,
    alt_owner,
    alt_cell,
    alt_profile,
    land_mask,
    coef_east,
    coef_north,
    mirror,
    vinv,
):
    row_count, col_count = land_mask.shape
    count_ja = lax.axis_size("ja")
    count_ia = lax.axis_size("ia")
    devices = count_ja * count_ia
    capacity = round_up(3 * argo_value.shape[0] // devices, 8)
    group = round_up(capacity // 4, 8)
    message = send_tables(
        devices,
        capacity,
        group,
        row_count,
        col_count,
        argo_value.T,
        argo_owner.reshape(1, -1),
        argo_cell.reshape(1, -1),
        alt_value.reshape(1, -1),
        alt_owner.reshape(1, -1),
        alt_cell.reshape(1, -1),
    )
    message = lax.all_to_all(message, ("ja", "ia"), split_axis=0, concat_axis=0, tiled=True)

    ia_index = lax.axis_index("ia")
    ja_index = lax.axis_index("ja")
    is_top = (ja_index == count_ja - 1).astype(jnp.int32)
    flags = jnp.stack([is_top, ja_index % 2]).astype(jnp.int32)
    fold_index = mirror - (count_ia - 1 - ia_index) * col_count
    mirror_lane = jnp.broadcast_to((fold_index % LANES)[None, :], (8, col_count))
    coef = edge_coefficients(land_mask, coef_east, coef_north, fold_index)
    matrices = mixing_matrices(vinv)
    profiles = jnp.pad(alt_profile.reshape(2, LEVELS, 1), ((0, 0), (0, PAD - LEVELS), (0, 0)))
    wet = land_mask.astype(F32)

    fields = make_forcing(capacity, group, row_count, col_count, flags, message, profiles)

    ring_east = [(i, (i + 1) % count_ia) for i in range(count_ia)]
    ring_west = [((i + 1) % count_ia, i) for i in range(count_ia)]
    even_swap = [(i, i ^ 1) for i in range(count_ja)]
    odd_swap = []
    for ja in range(1, count_ja):
        for ia in range(count_ia):
            partner = ((ja - 1) ^ 1) + 1
            to = (partner, ia) if ja < count_ja - 1 else (ja, count_ia - 1 - ia)
            odd_swap.append((ja * count_ia + ia, to[0] * count_ia + to[1]))
    output = None
    for sweep in range(ITERS):
        for which in range(2):
            state, even_edge, odd_edge, cols = fields[which]
            received = (
                lax.ppermute(even_edge, "ja", even_swap),
                lax.ppermute(odd_edge, ("ja", "ia"), odd_swap),
                lax.ppermute(cols, "ia", ring_east),
                lax.ppermute(cols, "ia", ring_west),
            )
            final = (which, wet, output) if sweep == ITERS - 1 else None
            result = diffuse(flags, state, received, mirror_lane, coef, matrices[which], final)
            if final is None:
                fields[which] = result
            else:
                output = result
    return output


def solution(mesh):
    in_specs = (
        P(("ja", "ia"), None),
        P(("ja", "ia"), None),
        P(("ja", "ia")),
        P(("ja", "ia")),
        P(("ja", "ia"), None),
        P(("ja", "ia")),
        P(),
        P("ja", "ia"),
        P("ja", "ia"),
        P("ja", "ia"),
        P("ia"),
        P("ja", None, None, None),
    )
    out_specs = P(None, "ja", "ia")
    return jax.shard_map(body, mesh=mesh, in_specs=in_specs, out_specs=out_specs, check_vma=False)
```

```python
import jax
import jax.numpy as jnp
from jax import lax
from jax.experimental import pallas as pl
from jax.experimental.pallas import tpu as pltpu
from jax.sharding import PartitionSpec as P

ITERS = 3
LEVELS = 75
PAD = 80
LANES = 128
BF = jnp.bfloat16
F32 = jnp.float32
MIB = 1024 * 1024


def round_up(value, unit):
    return (value + unit - 1) // unit * unit


def split_two(value):
    high = value.astype(BF)
    low = (value - high.astype(F32)).astype(BF)
    return high, low


def mm(left, right):
    return jnp.dot(left, right, preferred_element_type=F32)


def slot_positions(owner_row, cell_row, col_count, row_count, capacity):
    count = owner_row.shape[1]
    base = owner_row.astype(F32) * float(row_count * count)
    inside = (cell_row // col_count).astype(F32) * float(count)
    order = lax.broadcasted_iota(jnp.int32, (1, count), 1).astype(F32)
    key = base + inside + order
    key_col = jnp.broadcast_to(key, (8, count)).T[:, 0:1]
    rank = jnp.zeros((1, count), F32)
    for start in range(0, count, 128):
        part = key_col[start : start + 128]
        before = (part < key) & (part >= base)
        rank = rank + jnp.sum(jnp.where(before, 1.0, 0.0), axis=0, keepdims=True)
    return owner_row.astype(F32) * float(capacity) + rank


def table_kernel(
    devices,
    capacity,
    group,
    row_count,
    col_count,
    value_ref,
    owner_ref,
    cell_ref,
    alt_value_ref,
    alt_owner_ref,
    alt_cell_ref,
    message_ref,
    level_ref,
    alt_ref,
    hi_ref,
    lo_ref,
    alt_all_ref,
):
    position = slot_positions(owner_ref[...], cell_ref[...], col_count, row_count, capacity)
    alt_position = slot_positions(
        alt_owner_ref[...], alt_cell_ref[...], col_count, row_count, capacity
    )
    level_ref[...] = jnp.zeros(level_ref.shape, F32)
    level_ref[0:75, :] = value_ref[0:75, :]
    level_ref[75:76, :] = cell_ref[...].astype(F32) + 1.0
    level_ref[80:128, :] = value_ref[75:123, :]
    for lane_group in range(4):
        level_ref[128 + 32 * lane_group : 155 + 32 * lane_group, :] = value_ref[123:150, :]
    high, low = split_two(level_ref[...].T)
    hi_ref[...] = high
    lo_ref[...] = low
    alt_ref[...] = jnp.zeros(alt_ref.shape, F32)
    pair = jnp.concatenate([alt_value_ref[...], alt_cell_ref[...].astype(F32) + 1.0], axis=0)
    pair_high = pair.astype(BF).astype(F32)
    alt_ref[76:78, :] = pair_high
    alt_ref[78:80, :] = pair - pair_high
    alt_all_ref[...] = alt_ref[...].T.astype(BF)
    per_step = max(1, 768 // capacity)
    rows = per_step * capacity

    def step(index, carry):
        slot = (lax.broadcasted_iota(jnp.int32, (rows, 1), 0) + index * rows).astype(F32)
        chosen = jnp.where(slot == position, 1.0, 0.0).astype(BF)
        chosen_alt = jnp.where(slot == alt_position, 1.0, 0.0).astype(BF)
        table = mm(chosen, hi_ref[...]) + mm(chosen, lo_ref[...])
        lane = lax.broadcasted_iota(jnp.int32, (1, LANES), 1)
        extra = mm(chosen_alt, alt_all_ref[...])
        extra = jnp.where(lane < 78, extra + pltpu.roll(extra, LANES - 2, 1), 0.0)
        extra = jnp.where(lane >= 76, extra, 0.0)
        first = table[:, :LANES] + extra
        start = index * per_step
        message_ref[pl.ds(start, per_step), 0:capacity] = first.reshape(per_step, capacity, LANES)
        rest = table[:, LANES:].reshape(per_step, capacity, LANES)
        total = jnp.zeros((per_step, group, LANES), F32)
        for lane_group in range(4):
            low_slot = lane_group * group
            if low_slot >= capacity:
                continue
            piece = rest[:, low_slot : low_slot + group]
            here = (lane // 32 == lane_group).reshape(1, 1, LANES)
            total = jnp.where(here, piece, total)
        message_ref[pl.ds(start, per_step), capacity : capacity + group] = total
        return carry

    lax.fori_loop(0, devices // per_step, step, 0)


def send_tables(devices, capacity, group, row_count, col_count, values, owner, cell, alt_value, alt_owner, alt_cell):
    n_obs = owner.shape[1]
    n_alt = alt_owner.shape[1]

    def kernel(*refs):
        table_kernel(devices, capacity, group, row_count, col_count, *refs)

    return pl.pallas_call(
        kernel,
        out_shape=jax.ShapeDtypeStruct((devices, capacity + group, LANES), F32),
        scratch_shapes=[
            pltpu.VMEM((2 * LANES, n_obs), F32),
            pltpu.VMEM((LANES, n_alt), F32),
            pltpu.VMEM((n_obs, 2 * LANES), BF),
            pltpu.VMEM((n_obs, 2 * LANES), BF),
            pltpu.VMEM((n_alt, LANES), BF),
        ],
        compiler_params=pltpu.CompilerParams(vmem_limit_bytes=40 * MIB),
        name="send_tables",
    )(values, owner, cell, alt_value, alt_owner, alt_cell)


def add_columns(cols, state_row, row, row_count):
    lane = lax.broadcasted_iota(jnp.int32, (1, LANES), 1)
    west = pltpu.roll(state_row[:, :LANES], row, 1)
    east = pltpu.roll(state_row[:, -LANES:], row_count + 1 + row, 1)
    cols = jnp.where(lane == row, west, cols)
    return jnp.where(lane == row_count + row, east, cols)


def write_edge(edge, odd, even_ref, odd_ref, is_low):
    to_odd = jnp.logical_not(odd) if is_low else odd

    @pl.when(to_odd)
    def _():
        odd_ref[...] = edge

    @pl.when(jnp.logical_not(to_odd))
    def _():
        even_ref[...] = edge


def forcing_kernel(
    capacity,
    group,
    row_count,
    col_count,
    flag_ref,
    message_ref,
    profile_ref,
    state_t,
    even_t,
    odd_t,
    cols_t,
    state_s,
    even_s,
    odd_s,
    cols_s,
    left_ref,
    hot_ref,
    rows_ref,
    sea_ref,
):
    devices = message_ref.shape[0]
    block = min(32, devices)
    members = block * 8
    octets = capacity // 8
    per_group = group // 8
    shift = col_count.bit_length() - 1
    col_iota = lax.broadcasted_iota(jnp.int32, (1, col_count), 1)
    row_iota = lax.broadcasted_iota(jnp.int32, (row_count, 1), 0)
    odd = flag_ref[1] > 0

    def chunk(index, start):
        return message_ref[index * block : (index + 1) * block, start : start + 8, :].reshape(
            members, LANES
        )

    def hot_of(cell):
        return jnp.where(((cell - 1) & (col_count - 1)) == col_iota, 1.0, 0.0).astype(BF)

    def rows_of(cell):
        return lax.shift_right_arithmetic(cell - 1, shift)

    sea = jnp.zeros((row_count, col_count), F32)
    count = 0
    for index in range(devices // block):
        tails = [
            chunk(index, capacity + 8 * part).T for part in range(per_group)
        ]
        for octet in range(octets):
            table = chunk(index, 8 * octet)
            turned = table.T
            tail = tails[octet % per_group]
            begin = 32 * (octet // per_group)
            levels = jnp.concatenate([turned, tail[begin : begin + 32]], axis=0)
            high, low = split_two(levels)
            left_ref[count, :, 0:members] = high
            left_ref[count, :, members : 2 * members] = low
            hot = hot_of(table[:, 75:76].astype(jnp.int32))
            hot_ref[count, 0:members] = hot
            hot_ref[count, members : 2 * members] = hot
            rows_ref[count] = jnp.broadcast_to(rows_of(turned[75:76].astype(jnp.int32)), (8, members))
            alt_hot = hot_of(table[:, 77:78].astype(jnp.int32))
            alt_rows = rows_of(turned[77:78].astype(jnp.int32))
            weighted = jnp.where(alt_rows == row_iota, turned[76:77], 0.0)
            high, low = split_two(weighted)
            product = mm(jnp.concatenate([high, low], axis=0), alt_hot)
            sea = sea + product[:row_count] + product[row_count:]
            count += 1
    sea_ref[...] = sea
    for start in range(0, col_count, LANES):
        for field, state in ((0, state_t), (1, state_s)):
            profile = jnp.broadcast_to(profile_ref[field], (PAD, LANES))
            for row in range(row_count):
                state[row, :, start : start + LANES] = (
                    profile * sea_ref[row : row + 1, start : start + LANES]
                )
    span = 4

    def step(number, carry):
        rows = rows_ref[number][0:1]
        least = jnp.min(jnp.where(rows >= 0, rows, row_count))
        most = jnp.max(rows)

        def rows_step(start, inner):
            base = start * span
            pieces = []
            for offset in range(span):
                mask = jnp.where(rows == base + offset, 1.0, 0.0).astype(BF)
                pieces.append(left_ref[number] * jnp.concatenate([mask, mask], axis=1))
            product = mm(jnp.concatenate(pieces, axis=0), hot_ref[number])
            for offset in range(span):
                at = 2 * PAD * offset
                state_t[base + offset] += product[at : at + PAD]
                state_s[base + offset] += product[at + PAD : at + 2 * PAD]
            return inner

        lax.fori_loop(least // span, most // span + 1, rows_step, 0)
        return carry

    lax.fori_loop(0, count, step, 0)
    for state, even_ref, odd_ref, cols_ref in (
        (state_t, even_t, odd_t, cols_t),
        (state_s, even_s, odd_s, cols_s),
    ):
        cols = jnp.zeros((PAD, LANES), F32)
        for row in range(row_count):
            cols = add_columns(cols, state[row], row, row_count)
        cols_ref[...] = cols
        write_edge(state[0], odd, even_ref, odd_ref, True)
        write_edge(state[row_count - 1], odd, even_ref, odd_ref, False)


def field_shapes(row_count, col_count):
    return (
        jax.ShapeDtypeStruct((row_count, PAD, col_count), F32),
        jax.ShapeDtypeStruct((PAD, col_count), F32),
        jax.ShapeDtypeStruct((PAD, col_count), F32),
        jax.ShapeDtypeStruct((PAD, LANES), F32),
    )


def make_forcing(capacity, group, row_count, col_count, flags, message, profiles):
    def kernel(*refs):
        forcing_kernel(capacity, group, row_count, col_count, *refs)

    devices = message.shape[0]
    members = min(32, devices) * 8
    chunks = capacity // 8 * (devices // min(32, devices))
    results = pl.pallas_call(
        kernel,
        in_specs=[
            pl.BlockSpec(memory_space=pltpu.SMEM),
            pl.BlockSpec(memory_space=pltpu.VMEM),
            pl.BlockSpec(memory_space=pltpu.VMEM),
        ],
        out_shape=field_shapes(row_count, col_count) * 2,
        scratch_shapes=[
            pltpu.VMEM((chunks, 2 * PAD, 2 * members), BF),
            pltpu.VMEM((chunks, 2 * members, col_count), BF),
            pltpu.VMEM((chunks, 8, members), jnp.int32),
            pltpu.VMEM((row_count, col_count), F32),
        ],
        compiler_params=pltpu.CompilerParams(vmem_limit_bytes=48 * MIB),
        name="forcing",
    )(flags, message, profiles)
    return [list(results[:4]), list(results[4:])]


def diffusion_kernel(row_count, col_count, step_rows, final, *refs):
    (
        flag_ref,
        state_ref,
        below_ref,
        above_ref,
        even_in,
        odd_in,
        from_west_ref,
        from_east_ref,
        mirror_ref,
        coef_ref,
        matrix_ref,
    ) = refs[:11]
    if final:
        wet_ref = refs[11]
        out_ref, south_ref, north_ref, right_ref = refs[-4:]
    else:
        out_ref, even_ref, odd_ref, cols_ref, south_ref, north_ref, right_ref = refs[-7:]
    step = pl.program_id(0)
    lane = lax.broadcasted_iota(jnp.int32, (1, LANES), 1)
    chunks = col_count // LANES
    is_top = flag_ref[0] > 0
    odd = flag_ref[1] > 0
    even = jnp.logical_not(odd)
    first = step == 0
    last = step == pl.num_programs(0) - 1

    def piece(chunk):
        return slice(chunk * LANES, (chunk + 1) * LANES)

    @pl.when(jnp.logical_not(first))
    def _():
        south_ref[...] = below_ref[0]

    @pl.when(jnp.logical_not(last))
    def _():
        north_ref[...] = above_ref[0]

    @pl.when(first)
    def _():
        right_ref[:, 3 * PAD :, :] = jnp.zeros((step_rows, 16, col_count), BF)
        if not final:
            cols_ref[...] = jnp.zeros(cols_ref.shape, F32)

    @pl.when(first & even)
    def _():
        south_ref[...] = odd_in[0]

    @pl.when(first & odd)
    def _():
        south_ref[...] = even_in[0]

    @pl.when(last & even)
    def _():
        north_ref[...] = even_in[0]

    @pl.when(last & odd & jnp.logical_not(is_top))
    def _():
        north_ref[...] = odd_in[0]

    @pl.when(last & is_top)
    def _():
        for c in range(chunks):
            index = jnp.broadcast_to(mirror_ref[0:1, piece(c)], (PAD, LANES))
            north_ref[:, piece(c)] = jnp.take_along_axis(
                odd_in[0, :, piece(chunks - 1 - c)], index, axis=1
            )

    def mix(offset):
        row = step * step_rows + offset
        centers = [state_ref[offset, :, piece(c)] for c in range(chunks)]
        to_left = [pltpu.roll(c, LANES - 1, 1) for c in centers]
        to_right = [pltpu.roll(c, 1, 1) for c in centers]
        to_right.append(
            pltpu.roll(from_west_ref[0], lax.rem(2 * LANES - row_count - row, LANES), 1)
        )
        to_left.append(pltpu.roll(from_east_ref[0], LANES - 1 - row, 1))
        for c in range(chunks):
            south = state_ref[offset - 1, :, piece(c)] if offset > 0 else south_ref[:, piece(c)]
            if offset < step_rows - 1:
                north = state_ref[offset + 1, :, piece(c)]
            else:
                north = north_ref[:, piece(c)]
            east = jnp.where(lane == LANES - 1, to_left[c + 1], to_left[c])
            west = jnp.where(lane == 0, to_right[c - 1], to_right[c])

            def coef(kind):
                return coef_ref[offset, kind : kind + 1, piece(c)]

            mixed = (
                coef(0) * centers[c]
                + coef(1) * east
                + coef(2) * west
                + coef(3) * north
                + coef(4) * south
            )
            high, low = split_two(mixed)
            right_ref[offset, 0:PAD, piece(c)] = high
            right_ref[offset, PAD : 2 * PAD, piece(c)] = low
            right_ref[offset, 2 * PAD : 3 * PAD, piece(c)] = high

    def product(offset):
        result = mm(matrix_ref[offset], right_ref[offset])
        if final:
            return result * wet_ref[offset : offset + 1, :]
        out_ref[offset] = result
        return result

    results = []
    for offset in range(step_rows):
        mix(offset)
        if offset > 0:
            results.append(product(offset - 1))
    results.append(product(step_rows - 1))
    if final:
        turned = jnp.swapaxes(jnp.stack(results), 0, 1)
        out_ref[...] = turned[:LEVELS]
        return
    cols = cols_ref[...]
    for offset in range(step_rows):
        cols = add_columns(cols, results[offset], step * step_rows + offset, row_count)
    cols_ref[...] = cols

    @pl.when(first)
    def _():
        write_edge(out_ref[0], odd, even_ref, odd_ref, True)

    @pl.when(last)
    def _():
        write_edge(out_ref[step_rows - 1], odd, even_ref, odd_ref, False)


def diffuse(flags, state, received, mirror, coef, matrix, final=None):
    row_count, _, col_count = state.shape
    step_rows = 4 if final is None else 8
    steps = row_count // step_rows

    def kernel(*refs):
        diffusion_kernel(row_count, col_count, step_rows, final is not None, *refs)

    def whole(array):
        return pl.BlockSpec(array.shape, lambda s, flags: (0,) * len(array.shape))

    def picked(array, flag):
        return pl.BlockSpec((1,) + array.shape[1:], lambda s, flags: (flags[flag], 0, 0))

    one = (1, PAD, col_count)
    block = (step_rows, PAD, col_count)
    even_rows, odd_rows, all_cols = received
    in_specs = [
        pl.BlockSpec(block, lambda s, flags: (s, 0, 0)),
        pl.BlockSpec(one, lambda s, flags: (jnp.maximum(s * step_rows - 1, 0), 0, 0)),
        pl.BlockSpec(
            one, lambda s, flags: (jnp.minimum(s * step_rows + step_rows, row_count - 1), 0, 0)
        ),
        picked(even_rows, 2),
        picked(odd_rows, 3),
        picked(all_cols, 4),
        picked(all_cols, 5),
        whole(mirror),
        pl.BlockSpec((step_rows,) + coef.shape[1:], lambda s, flags: (s, 0, 0)),
        pl.BlockSpec((step_rows,) + matrix.shape[1:], lambda s, flags: (s, 0, 0)),
    ]
    operands = [state, state, state, even_rows, odd_rows, all_cols, all_cols, mirror, coef, matrix]
    aliases = {}
    if final is None:
        shapes = field_shapes(row_count, col_count)
        out_specs = [pl.BlockSpec(block, lambda s, flags: (s, 0, 0)), *[whole(x) for x in shapes[1:]]]
    else:
        which, wet, target = final
        shapes = jax.ShapeDtypeStruct((2 * LEVELS, row_count, col_count), F32)
        out_specs = pl.BlockSpec((LEVELS, step_rows, col_count), lambda s, flags: (which, s, 0))
        in_specs.append(pl.BlockSpec((step_rows, col_count), lambda s, flags: (s, 0)))
        operands.append(wet)
        if target is not None:
            in_specs.append(pl.BlockSpec(memory_space=pl.ANY))
            operands.append(target)
            aliases = {len(operands): 0}
    return pl.pallas_call(
        kernel,
        grid_spec=pltpu.PrefetchScalarGridSpec(
            num_scalar_prefetch=1,
            grid=(steps,),
            in_specs=in_specs,
            out_specs=out_specs,
            scratch_shapes=[
                pltpu.VMEM((PAD, col_count), F32),
                pltpu.VMEM((PAD, col_count), F32),
                pltpu.VMEM((step_rows, 256, col_count), BF),
            ],
        ),
        out_shape=shapes,
        input_output_aliases=aliases,
        compiler_params=pltpu.CompilerParams(vmem_limit_bytes=28 * MIB),
        cost_estimate=pl.CostEstimate(
            flops=3_000_000_000, bytes_accessed=8_000_000, transcendentals=0
        ),
        name="diffusion",
    )(flags, *operands)


def with_halo(cells, sides, width):
    for axis, dim in sides:
        count = lax.axis_size(axis)
        head = lax.slice_in_dim(cells, 0, width, axis=dim)
        tail = lax.slice_in_dim(cells, cells.shape[dim] - width, cells.shape[dim], axis=dim)
        cells = jnp.concatenate(
            [
                lax.ppermute(tail, axis, [(i, (i + 1) % count) for i in range(count)]),
                cells,
                lax.ppermute(head, axis, [((i + 1) % count, i) for i in range(count)]),
            ],
            axis=dim,
        )
    return cells


def edge_coefficients(land_mask, coef_east, coef_north, fold_index):
    row_count, col_count = land_mask.shape
    count_ja = lax.axis_size("ja")
    count_ia = lax.axis_size("ia")
    wet = land_mask.astype(F32)
    coast = with_halo(jnp.stack([wet, coef_east, coef_north]), (("ja", 1), ("ia", 2)), 1)
    wet_pad, east_pad, north_pad = coast[0], coast[1], coast[2]
    ja_index = lax.axis_index("ja")
    row_index = ja_index * row_count + jnp.arange(row_count, dtype=jnp.int32)
    not_top = (row_index != row_count * count_ja - 1).astype(F32)[:, None]
    not_bottom = (row_index != 0).astype(F32)[:, None]
    east_w = east_pad[1:-1, 1:-1] * wet_pad[1:-1, 1:-1] * wet_pad[1:-1, 2:]
    west_w = east_pad[1:-1, :-2] * wet_pad[1:-1, :-2] * wet_pad[1:-1, 1:-1]
    north_w = north_pad[1:-1, 1:-1] * wet_pad[1:-1, 1:-1] * wet_pad[2:, 1:-1] * not_top
    south_w = north_pad[:-2, 1:-1] * wet_pad[:-2, 1:-1] * wet_pad[1:-1, 1:-1] * not_bottom
    top_rows = jnp.stack([wet[-1], coef_north[-1]])
    partner = lax.ppermute(top_rows, "ia", [(i, count_ia - 1 - i) for i in range(count_ia)])
    partner = jnp.take(partner, fold_index, axis=1)
    fold_w = 0.5 * (coef_north[-1] + partner[1]) * wet[-1] * partner[0]
    north_w = north_w + (1.0 - not_top) * fold_w[None, :]
    center = 1.0 - (east_w + west_w + north_w + south_w)
    return jnp.stack([center, east_w, west_w, north_w, south_w], axis=1)


def mixing_matrices(vinv):
    turned = jnp.transpose(vinv, (1, 0, 3, 2))
    turned = jnp.pad(turned, ((0, 0), (0, 0), (0, PAD - LEVELS), (0, PAD - LEVELS)))
    high = lax.reduce_precision(turned, 8, 7)
    low = (turned - high).astype(BF)
    high = high.astype(BF)
    rest = jnp.zeros(high.shape[:3] + (256 - 3 * PAD,), BF)
    return jnp.concatenate([high, high, low, rest], axis=3)


def body(
    argo_value,
    argo_owner,
    argo_cell,
    alt_value,
    alt_owner,
    alt_cell,
    alt_profile,
    land_mask,
    coef_east,
    coef_north,
    mirror,
    vinv,
):
    row_count, col_count = land_mask.shape
    count_ja = lax.axis_size("ja")
    count_ia = lax.axis_size("ia")
    devices = count_ja * count_ia
    capacity = round_up(3 * argo_value.shape[0] // devices, 8)
    group = round_up(capacity // 4, 8)
    message = send_tables(
        devices,
        capacity,
        group,
        row_count,
        col_count,
        argo_value.T,
        argo_owner.reshape(1, -1),
        argo_cell.reshape(1, -1),
        alt_value.reshape(1, -1),
        alt_owner.reshape(1, -1),
        alt_cell.reshape(1, -1),
    )
    message = lax.all_to_all(message, ("ja", "ia"), split_axis=0, concat_axis=0, tiled=True)

    ia_index = lax.axis_index("ia")
    ja_index = lax.axis_index("ja")
    is_top = (ja_index == count_ja - 1).astype(jnp.int32)
    parity = ja_index % 2
    fold_partner = (ia_index < count_ia // 2).astype(jnp.int32)
    flags = jnp.stack(
        [
            is_top,
            parity,
            1 - parity,
            jnp.where(is_top > 0, fold_partner, parity),
            (ia_index + count_ia - 1) % count_ia,
            (ia_index + 1) % count_ia,
        ]
    ).astype(jnp.int32)
    fold_index = mirror - (count_ia - 1 - ia_index) * col_count
    mirror_lane = jnp.broadcast_to((fold_index % LANES)[None, :], (8, col_count))
    coef = edge_coefficients(land_mask, coef_east, coef_north, fold_index)
    matrices = mixing_matrices(vinv)
    profiles = jnp.pad(alt_profile.reshape(2, LEVELS, 1), ((0, 0), (0, PAD - LEVELS), (0, 0)))
    wet = land_mask.astype(F32)

    fields = make_forcing(capacity, group, row_count, col_count, flags, message, profiles)

    even_pairs = []
    odd_pairs = []
    for ja in range(0, count_ja, 2):
        even_pairs += [[ja * count_ia + ia, (ja + 1) * count_ia + ia] for ia in range(count_ia)]
    for ja in range(1, count_ja - 1, 2):
        odd_pairs += [[ja * count_ia + ia, (ja + 1) * count_ia + ia] for ia in range(count_ia)]
    for ja in (0, count_ja - 1):
        for ia in range(count_ia // 2):
            odd_pairs.append([ja * count_ia + ia, (ja + 1) * count_ia - 1 - ia])
    output = None
    for sweep in range(ITERS):
        for which in range(2):
            state, even_edge, odd_edge, cols = fields[which]
            received = (
                lax.all_gather(even_edge, ("ja", "ia"), axis_index_groups=even_pairs),
                lax.all_gather(odd_edge, ("ja", "ia"), axis_index_groups=odd_pairs),
                lax.all_gather(cols, "ia"),
            )
            final = (which, wet, output) if sweep == ITERS - 1 else None
            result = diffuse(flags, state, received, mirror_lane, coef, matrices[which], final)
            if final is None:
                fields[which] = result
            else:
                output = result
    return output


def solution(mesh):
    in_specs = (
        P(("ja", "ia"), None),
        P(("ja", "ia"), None),
        P(("ja", "ia")),
        P(("ja", "ia")),
        P(("ja", "ia"), None),
        P(("ja", "ia")),
        P(),
        P("ja", "ia"),
        P("ja", "ia"),
        P("ja", "ia"),
        P("ia"),
        P("ja", None, None, None),
    )
    out_specs = P(None, "ja", "ia")
    return jax.shard_map(body, mesh=mesh, in_specs=in_specs, out_specs=out_specs, check_vma=False)
```

```python
import jax
import jax.numpy as jnp
from jax import lax
from jax.experimental import pallas as pl
from jax.experimental.pallas import tpu as pltpu
from jax.sharding import PartitionSpec as P

ITERS = 3
LEVELS = 75
PAD = 80
LANES = 128
BF = jnp.bfloat16
F32 = jnp.float32
MIB = 1024 * 1024


def round_up(value, unit):
    return (value + unit - 1) // unit * unit


def split_two(value):
    high = value.astype(BF)
    low = (value - high.astype(F32)).astype(BF)
    return high, low


def mm(left, right):
    return jnp.dot(left, right, preferred_element_type=F32)


def as_column(row):
    return jnp.broadcast_to(row, (8, row.shape[1])).T[:, 0:1]


def slot_positions(owner_row, cell_row, col_count, row_count, capacity, spread):
    count = owner_row.shape[1]
    base = owner_row.astype(F32) * float(row_count * count)
    inside = cell_row // col_count
    order = lax.broadcasted_iota(jnp.int32, (1, count), 1).astype(F32)
    key = base + inside.astype(F32) * float(count) + order
    key_col = as_column(key)
    rank = jnp.zeros((1, count), F32)
    total = jnp.zeros((1, count), F32)
    beyond = base + float(row_count * count)
    for start in range(0, count, 128):
        part = key_col[start : start + 128]
        own = jnp.where(part >= base, 1.0, 0.0)
        rank = rank + jnp.sum(jnp.where(part < key, own, 0.0), axis=0, keepdims=True)
        if spread:
            total = total + jnp.sum(jnp.where(part < beyond, own, 0.0), axis=0, keepdims=True)
    if spread:
        goal = (inside * capacity // row_count).astype(F32) - rank
        goal_col = as_column(goal)
        shift = jnp.zeros((1, count), F32)
        for start in range(0, count, 128):
            part = key_col[start : start + 128]
            own = jnp.where(part >= base, goal_col[start : start + 128], 0.0)
            shift = jnp.maximum(
                shift, jnp.max(jnp.where(part <= key, own, 0.0), axis=0, keepdims=True)
            )
        rank = rank + jnp.minimum(shift, float(capacity) - total)
    return owner_row.astype(F32) * float(capacity) + rank


def table_kernel(
    capacity,
    group,
    row_count,
    col_count,
    value_ref,
    owner_ref,
    cell_ref,
    alt_ref,
    alt_owner_ref,
    message_ref,
    level_ref,
    side_ref,
    hi_ref,
    lo_ref,
    alt_all_ref,
    place_ref,
    alt_place_ref,
):
    index = pl.program_id(0)

    @pl.when(index == 0)
    def _():
        place_ref[0:1] = slot_positions(
            owner_ref[...], cell_ref[...], col_count, row_count, capacity, True
        )
        alt_place_ref[0:1] = slot_positions(
            alt_owner_ref[...],
            alt_ref[1:2].astype(jnp.int32),
            col_count,
            row_count,
            capacity,
            False,
        )
        level_ref[...] = jnp.zeros(level_ref.shape, F32)
        level_ref[0:75, :] = value_ref[0:75, :]
        level_ref[75:76, :] = cell_ref[...].astype(F32) + 1.0
        level_ref[80:128, :] = value_ref[75:123, :]
        for lane_group in range(4):
            level_ref[128 + 32 * lane_group : 155 + 32 * lane_group, :] = value_ref[123:150, :]
        high, low = split_two(level_ref[...].T)
        hi_ref[...] = high
        lo_ref[...] = low
        side_ref[...] = jnp.zeros(side_ref.shape, F32)
        pair = alt_ref[0:2] + lax.broadcasted_iota(jnp.int32, (2, 1), 0).astype(F32)
        pair_high = pair.astype(BF).astype(F32)
        side_ref[76:78, :] = pair_high
        side_ref[78:80, :] = pair - pair_high
        alt_all_ref[...] = side_ref[...].T.astype(BF)

    per_step = message_ref.shape[0]
    rows = per_step * capacity
    slot = (lax.broadcasted_iota(jnp.int32, (rows, 1), 0) + index * rows).astype(F32)
    chosen = jnp.where(slot == place_ref[0:1], 1.0, 0.0).astype(BF)
    chosen_alt = jnp.where(slot == alt_place_ref[0:1], 1.0, 0.0).astype(BF)
    table = mm(chosen, hi_ref[...]) + mm(chosen, lo_ref[...])
    lane = lax.broadcasted_iota(jnp.int32, (1, LANES), 1)
    extra = mm(chosen_alt, alt_all_ref[...])
    extra = jnp.where(lane < 78, extra + pltpu.roll(extra, LANES - 2, 1), 0.0)
    extra = jnp.where(lane >= 76, extra, 0.0)
    first = table[:, :LANES] + extra
    message_ref[:, 0:capacity] = first.reshape(per_step, capacity, LANES)
    rest = table[:, LANES:].reshape(per_step, capacity, LANES)
    total = jnp.zeros((per_step, group, LANES), F32)
    for lane_group in range(4):
        low_slot = lane_group * group
        if low_slot >= capacity:
            continue
        piece = rest[:, low_slot : low_slot + group]
        here = (lane // 32 == lane_group).reshape(1, 1, LANES)
        total = jnp.where(here, piece, total)
    message_ref[:, capacity : capacity + group] = total


def send_tables(devices, capacity, group, row_count, col_count, values, owner, cell, alt, alt_owner):
    n_obs = owner.shape[1]
    n_alt = alt_owner.shape[1]
    per_step = max(1, 768 // capacity)

    def kernel(*refs):
        table_kernel(capacity, group, row_count, col_count, *refs)

    operands = (values, owner, cell, alt, alt_owner)
    return pl.pallas_call(
        kernel,
        grid=(devices // per_step,),
        in_specs=[pl.BlockSpec(x.shape, lambda s: (0, 0)) for x in operands],
        out_specs=pl.BlockSpec((per_step, capacity + group, LANES), lambda s: (s, 0, 0)),
        out_shape=jax.ShapeDtypeStruct((devices, capacity + group, LANES), F32),
        scratch_shapes=[
            pltpu.VMEM((2 * LANES, n_obs), F32),
            pltpu.VMEM((LANES, n_alt), F32),
            pltpu.VMEM((n_obs, 2 * LANES), BF),
            pltpu.VMEM((n_obs, 2 * LANES), BF),
            pltpu.VMEM((n_alt, LANES), BF),
            pltpu.VMEM((8, n_obs), F32),
            pltpu.VMEM((8, n_alt), F32),
        ],
        compiler_params=pltpu.CompilerParams(vmem_limit_bytes=56 * MIB),
        name="send_tables",
    )(*operands)


def add_columns(cols, state_row, row, row_count):
    lane = lax.broadcasted_iota(jnp.int32, (1, LANES), 1)
    west = pltpu.roll(state_row[:, :LANES], row, 1)
    east = pltpu.roll(state_row[:, -LANES:], row_count + 1 + row, 1)
    cols = jnp.where(lane == row, west, cols)
    return jnp.where(lane == row_count + row, east, cols)


def write_edge(edge, odd, even_ref, odd_ref, is_low):
    to_odd = jnp.logical_not(odd) if is_low else odd

    @pl.when(to_odd)
    def _():
        odd_ref[...] = edge

    @pl.when(jnp.logical_not(to_odd))
    def _():
        even_ref[...] = edge


def forcing_kernel(which, capacity, alt_capacity, group, row_count, col_count, *refs):
    if which == 0:
        flag_ref, message_ref, profile_ref, coast_ref = refs[:4]
        state, even_ref, odd_ref, cols_ref, sea_ref, left_ref, hot_ref, rows_ref = refs[4:]
    else:
        flag_ref, message_ref, profile_ref, sea_ref = refs[:4]
        state, even_ref, odd_ref, cols_ref, left_ref, hot_ref, rows_ref = refs[4:]
    devices = message_ref.shape[0]
    block = min(32, devices)
    members = block * 8
    octets = capacity // 8
    alt_octets = (alt_capacity + 7) // 8
    per_group = group // 8
    shift = col_count.bit_length() - 1
    col_iota = lax.broadcasted_iota(jnp.int32, (1, col_count), 1)
    row_iota = lax.broadcasted_iota(jnp.int32, (row_count, 1), 0)
    odd = flag_ref[1] > 0

    def chunk(index, start):
        return message_ref[index * block : (index + 1) * block, start : start + 8, :].reshape(
            members, LANES
        )

    def hot_of(cell):
        return jnp.where(((cell - 1) & (col_count - 1)) == col_iota, 1.0, 0.0).astype(BF)

    def rows_of(cell):
        return lax.shift_right_arithmetic(cell - 1, shift)

    sea = jnp.zeros((row_count, col_count), F32)
    count = 0
    for index in range(devices // block):
        if which == 1:
            tails = [chunk(index, capacity + 8 * part).T for part in range(per_group)]
        for octet in range(octets):
            table = chunk(index, 8 * octet)
            turned = table.T
            if which == 0:
                levels = turned[0:PAD]
            else:
                tail = tails[octet % per_group]
                begin = 32 * (octet // per_group)
                levels = jnp.concatenate([turned[80:128], tail[begin : begin + 32]], axis=0)
            high, low = split_two(levels)
            left_ref[count, :, 0:members] = high
            left_ref[count, :, members : 2 * members] = low
            hot = hot_of(table[:, 75:76].astype(jnp.int32))
            hot_ref[count, 0:members] = hot
            hot_ref[count, members : 2 * members] = hot
            rows_ref[count] = jnp.broadcast_to(rows_of(turned[75:76].astype(jnp.int32)), (8, members))
            count += 1
            if which == 1 or octet >= alt_octets:
                continue
            alt_hot = hot_of(table[:, 77:78].astype(jnp.int32))
            alt_rows = rows_of(turned[77:78].astype(jnp.int32))
            weighted = jnp.where(alt_rows == row_iota, turned[76:77], 0.0)
            high, low = split_two(weighted)
            product = mm(jnp.concatenate([high, low], axis=0), alt_hot)
            sea = sea + product[:row_count] + product[row_count:]
    if which == 0:
        sea_ref[...] = sea
    for start in range(0, col_count, LANES):
        profile = jnp.broadcast_to(profile_ref[...], (PAD, LANES))
        for row in range(row_count):
            state[row, :, start : start + LANES] = (
                profile * sea_ref[row : row + 1, start : start + LANES]
            )
    span = 4

    def step(number, carry):
        rows = rows_ref[number][0:1]
        least = jnp.min(jnp.where(rows >= 0, rows, row_count))
        most = jnp.max(rows)

        def rows_step(start, inner):
            base = start * span
            pieces = []
            for offset in range(span):
                mask = jnp.where(rows == base + offset, 1.0, 0.0).astype(BF)
                pieces.append(left_ref[number] * jnp.concatenate([mask, mask], axis=1))
            product = mm(jnp.concatenate(pieces, axis=0), hot_ref[number])
            for offset in range(span):
                state[base + offset] += product[PAD * offset : PAD * (offset + 1)]
            return inner

        lax.fori_loop(least // span, most // span + 1, rows_step, 0)
        return carry

    lax.fori_loop(0, count, step, 0)
    if which == 0:
        for row in range(row_count):
            for kind in range(3):
                state[row, LEVELS + kind : LEVELS + kind + 1, :] = coast_ref[kind, row : row + 1, :]
    cols = jnp.zeros((PAD, LANES), F32)
    for row in range(row_count):
        cols = add_columns(cols, state[row], row, row_count)
    cols_ref[...] = cols
    write_edge(state[0], odd, even_ref, odd_ref, True)
    write_edge(state[row_count - 1], odd, even_ref, odd_ref, False)


def field_shapes(row_count, col_count):
    return (
        jax.ShapeDtypeStruct((row_count, PAD, col_count), F32),
        jax.ShapeDtypeStruct((PAD, col_count), F32),
        jax.ShapeDtypeStruct((PAD, col_count), F32),
        jax.ShapeDtypeStruct((PAD, LANES), F32),
    )


def make_forcing(which, capacity, alt_capacity, group, row_count, col_count, operands):
    def kernel(*refs):
        forcing_kernel(which, capacity, alt_capacity, group, row_count, col_count, *refs)

    devices = operands[1].shape[0]
    members = min(32, devices) * 8
    chunks = capacity // 8 * (devices // min(32, devices))
    shapes = field_shapes(row_count, col_count)
    if which == 0:
        shapes += (jax.ShapeDtypeStruct((row_count, col_count), F32),)
    return pl.pallas_call(
        kernel,
        in_specs=[
            pl.BlockSpec(memory_space=pltpu.SMEM),
            pl.BlockSpec(memory_space=pltpu.VMEM),
            pl.BlockSpec(memory_space=pltpu.VMEM),
            pl.BlockSpec(memory_space=pltpu.VMEM),
        ],
        out_shape=shapes,
        scratch_shapes=[
            pltpu.VMEM((chunks, PAD, 2 * members), BF),
            pltpu.VMEM((chunks, 2 * members, col_count), BF),
            pltpu.VMEM((chunks, 8, members), jnp.int32),
        ],
        compiler_params=pltpu.CompilerParams(vmem_limit_bytes=36 * MIB),
        cost_estimate=pl.CostEstimate(
            flops=8_000_000_000, bytes_accessed=8_000_000, transcendentals=0
        ),
        name="forcing_" + ("temperature", "salinity")[which],
    )(*operands)


def weight_kernel(
    row_count,
    col_count,
    flag_ref,
    coast_ref,
    even_in,
    odd_in,
    from_west_ref,
    from_east_ref,
    mirror_ref,
    out_ref,
    fold_ref,
):
    is_top = flag_ref[0] > 0
    odd = flag_ref[1] > 0
    wet, north, east = coast_ref[0], coast_ref[1], coast_ref[2]
    chunks = col_count // LANES
    lane = lax.broadcasted_iota(jnp.int32, (1, col_count), 1)
    west_cols = from_west_ref[...].T[row_count : 2 * row_count]
    east_cols = from_east_ref[...].T[0:row_count]
    west_wet = jnp.where(lane == 0, west_cols[:, 3:4], pltpu.roll(wet, 1, 1))
    west_coef = jnp.where(lane == 0, west_cols[:, 5:6], pltpu.roll(east, 1, 1))
    east_wet = jnp.where(
        lane == col_count - 1, east_cols[:, 3:4], pltpu.roll(wet, col_count - 1, 1)
    )
    east_w = east * wet * east_wet
    west_w = west_coef * west_wet * wet
    for c in range(chunks):
        index = jnp.broadcast_to(mirror_ref[0:1, c * LANES : (c + 1) * LANES], (8, LANES))
        source = odd_in[:, (chunks - 1 - c) * LANES : (chunks - c) * LANES]
        fold_ref[:, c * LANES : (c + 1) * LANES] = jnp.take_along_axis(source, index, axis=1)
    above = jnp.where(odd, odd_in[...], even_in[...])
    below = jnp.where(odd, even_in[...], odd_in[...])
    last = row_count - 1
    plain = north[last:] * wet[last:] * above[3:4]
    fold = 0.5 * (north[last:] + fold_ref[4:5]) * wet[last:] * fold_ref[3:4]
    top_w = jnp.where(is_top, fold, plain)
    between = north[:last] * wet[:last] * wet[1:]
    bottom_w = below[4:5] * below[3:4] * wet[0:1]
    north_w = jnp.concatenate([between, top_w], axis=0)
    south_w = jnp.concatenate([bottom_w, between], axis=0)
    center = 1.0 - (east_w + west_w + north_w + south_w)
    for kind, weight in enumerate((center, east_w, west_w, north_w, south_w)):
        for row in range(row_count):
            out_ref[row, kind : kind + 1, :] = weight[row : row + 1]


def edge_weights(flags, coast, received, mirror):
    _, row_count, col_count = coast.shape

    def kernel(*refs):
        weight_kernel(row_count, col_count, *refs)

    def spare(width):
        return pl.BlockSpec((8, width), lambda s: (9, 0))

    return pl.pallas_call(
        kernel,
        grid=(1,),
        in_specs=[
            pl.BlockSpec(memory_space=pltpu.SMEM),
            pl.BlockSpec(coast.shape, lambda s: (0, 0, 0)),
            spare(col_count),
            spare(col_count),
            spare(LANES),
            spare(LANES),
            pl.BlockSpec(mirror.shape, lambda s: (0, 0)),
        ],
        out_specs=pl.BlockSpec((row_count, 8, col_count), lambda s: (0, 0, 0)),
        out_shape=jax.ShapeDtypeStruct((row_count, 8, col_count), F32),
        scratch_shapes=[pltpu.VMEM((8, col_count), F32)],
        compiler_params=pltpu.CompilerParams(vmem_limit_bytes=16 * MIB),
        name="edge_weights",
    )(flags, coast, *received, mirror)


def diffusion_kernel(row_count, col_count, step_rows, final, *refs):
    (
        flag_ref,
        state_ref,
        below_ref,
        above_ref,
        even_in,
        odd_in,
        from_west_ref,
        from_east_ref,
        mirror_ref,
        coef_ref,
        matrix_ref,
    ) = refs[:11]
    if final:
        wet_ref = refs[11]
        out_ref, south_ref, north_ref, right_ref = refs[-4:]
    else:
        out_ref, even_ref, odd_ref, cols_ref, south_ref, north_ref, right_ref = refs[-7:]
    step = pl.program_id(0)
    lane = lax.broadcasted_iota(jnp.int32, (1, LANES), 1)
    chunks = col_count // LANES
    is_top = flag_ref[0] > 0
    odd = flag_ref[1] > 0
    even = jnp.logical_not(odd)
    first = step == 0
    last = step == pl.num_programs(0) - 1

    def piece(chunk):
        return slice(chunk * LANES, (chunk + 1) * LANES)

    @pl.when(jnp.logical_not(first))
    def _():
        south_ref[...] = below_ref[0]

    @pl.when(jnp.logical_not(last))
    def _():
        north_ref[...] = above_ref[0]

    @pl.when(first)
    def _():
        right_ref[:, 3 * PAD :, :] = jnp.zeros((step_rows, 16, col_count), BF)
        if not final:
            cols_ref[...] = jnp.zeros(cols_ref.shape, F32)

    @pl.when(first & even)
    def _():
        south_ref[...] = odd_in[...]

    @pl.when(first & odd)
    def _():
        south_ref[...] = even_in[...]

    @pl.when(last & even)
    def _():
        north_ref[...] = even_in[...]

    @pl.when(last & odd & jnp.logical_not(is_top))
    def _():
        north_ref[...] = odd_in[...]

    @pl.when(last & is_top)
    def _():
        for c in range(chunks):
            index = jnp.broadcast_to(mirror_ref[0:1, piece(c)], (PAD, LANES))
            north_ref[:, piece(c)] = jnp.take_along_axis(
                odd_in[:, piece(chunks - 1 - c)], index, axis=1
            )

    def mix(offset):
        row = step * step_rows + offset
        centers = [state_ref[offset, :, piece(c)] for c in range(chunks)]
        to_left = [pltpu.roll(c, LANES - 1, 1) for c in centers]
        to_right = [pltpu.roll(c, 1, 1) for c in centers]
        to_right.append(
            pltpu.roll(from_west_ref[...], lax.rem(2 * LANES - row_count - row, LANES), 1)
        )
        to_left.append(pltpu.roll(from_east_ref[...], LANES - 1 - row, 1))
        for c in range(chunks):
            south = state_ref[offset - 1, :, piece(c)] if offset > 0 else south_ref[:, piece(c)]
            if offset < step_rows - 1:
                north = state_ref[offset + 1, :, piece(c)]
            else:
                north = north_ref[:, piece(c)]
            east = jnp.where(lane == LANES - 1, to_left[c + 1], to_left[c])
            west = jnp.where(lane == 0, to_right[c - 1], to_right[c])

            def coef(kind):
                return coef_ref[offset, kind : kind + 1, piece(c)]

            mixed = (
                coef(0) * centers[c]
                + coef(1) * east
                + coef(2) * west
                + coef(3) * north
                + coef(4) * south
            )
            high, low = split_two(mixed)
            right_ref[offset, 0:PAD, piece(c)] = high
            right_ref[offset, PAD : 2 * PAD, piece(c)] = low
            right_ref[offset, 2 * PAD : 3 * PAD, piece(c)] = high

    def product(offset):
        result = mm(matrix_ref[offset], right_ref[offset])
        if final:
            return result * wet_ref[offset : offset + 1, :]
        out_ref[offset] = result
        return result

    results = []
    for offset in range(step_rows):
        mix(offset)
        if offset > 0:
            results.append(product(offset - 1))
    results.append(product(step_rows - 1))
    if final:
        turned = jnp.swapaxes(jnp.stack(results), 0, 1)
        out_ref[...] = turned[:LEVELS]
        return
    cols = cols_ref[...]
    for offset in range(step_rows):
        cols = add_columns(cols, results[offset], step * step_rows + offset, row_count)
    cols_ref[...] = cols

    @pl.when(first)
    def _():
        write_edge(out_ref[0], odd, even_ref, odd_ref, True)

    @pl.when(last)
    def _():
        write_edge(out_ref[step_rows - 1], odd, even_ref, odd_ref, False)


def diffuse(flags, state, received, mirror, coef, matrix, final=None):
    row_count, _, col_count = state.shape
    step_rows = 4 if final is None else 8
    steps = row_count // step_rows

    def kernel(*refs):
        diffusion_kernel(row_count, col_count, step_rows, final is not None, *refs)

    def whole(array):
        return pl.BlockSpec(array.shape, lambda s: (0,) * len(array.shape))

    one = (1, PAD, col_count)
    block = (step_rows, PAD, col_count)
    in_specs = [
        pl.BlockSpec(memory_space=pltpu.SMEM),
        pl.BlockSpec(block, lambda s: (s, 0, 0)),
        pl.BlockSpec(one, lambda s: (jnp.maximum(s * step_rows - 1, 0), 0, 0)),
        pl.BlockSpec(
            one, lambda s: (jnp.minimum(s * step_rows + step_rows, row_count - 1), 0, 0)
        ),
        *[whole(array) for array in received],
        whole(mirror),
        pl.BlockSpec((step_rows,) + coef.shape[1:], lambda s: (s, 0, 0)),
        pl.BlockSpec((step_rows,) + matrix.shape[1:], lambda s: (s, 0, 0)),
    ]
    operands = [flags, state, state, state, *received, mirror, coef, matrix]
    aliases = {}
    if final is None:
        shapes = field_shapes(row_count, col_count)
        out_specs = [pl.BlockSpec(block, lambda s: (s, 0, 0)), *[whole(x) for x in shapes[1:]]]
    else:
        which, wet, target = final
        shapes = jax.ShapeDtypeStruct((2 * LEVELS, row_count, col_count), F32)
        out_specs = pl.BlockSpec((LEVELS, step_rows, col_count), lambda s: (which, s, 0))
        in_specs.append(pl.BlockSpec((step_rows, col_count), lambda s: (s, 0)))
        operands.append(wet)
        if target is not None:
            in_specs.append(pl.BlockSpec(memory_space=pl.ANY))
            operands.append(target)
            aliases = {len(operands) - 1: 0}
    return pl.pallas_call(
        kernel,
        grid=(steps,),
        in_specs=in_specs,
        out_specs=out_specs,
        out_shape=shapes,
        input_output_aliases=aliases,
        scratch_shapes=[
            pltpu.VMEM((PAD, col_count), F32),
            pltpu.VMEM((PAD, col_count), F32),
            pltpu.VMEM((step_rows, 256, col_count), BF),
        ],
        compiler_params=pltpu.CompilerParams(vmem_limit_bytes=28 * MIB),
        cost_estimate=pl.CostEstimate(
            flops=3_000_000_000, bytes_accessed=8_000_000, transcendentals=0
        ),
        name="diffusion",
    )(*operands)


def mixing_matrices(vinv):
    turned = jnp.transpose(vinv, (1, 0, 3, 2))
    turned = jnp.pad(turned, ((0, 0), (0, 0), (0, PAD - LEVELS), (0, PAD - LEVELS)))
    high = lax.reduce_precision(turned, 8, 7)
    low = (turned - high).astype(BF)
    high = high.astype(BF)
    rest = jnp.zeros(high.shape[:3] + (256 - 3 * PAD,), BF)
    return jnp.concatenate([high, high, low, rest], axis=3)


def body(
    argo_value,
    argo_owner,
    argo_cell,
    alt_value,
    alt_owner,
    alt_cell,
    alt_profile,
    land_mask,
    coef_east,
    coef_north,
    mirror,
    vinv,
):
    row_count, col_count = land_mask.shape
    count_ja = lax.axis_size("ja")
    count_ia = lax.axis_size("ia")
    devices = count_ja * count_ia
    capacity = round_up(3 * argo_value.shape[0] // devices, 8)
    group = round_up(capacity // 4, 8)
    message = send_tables(
        devices,
        capacity,
        group,
        row_count,
        col_count,
        argo_value.T,
        argo_owner.reshape(1, -1),
        argo_cell.reshape(1, -1),
        jnp.stack([alt_value, alt_cell.astype(F32)]),
        alt_owner.reshape(1, -1),
    )
    message = lax.all_to_all(message, ("ja", "ia"), split_axis=0, concat_axis=0, tiled=True)

    ia_index = lax.axis_index("ia")
    ja_index = lax.axis_index("ja")
    is_top = (ja_index == count_ja - 1).astype(jnp.int32)
    flags = jnp.stack([is_top, ja_index % 2]).astype(jnp.int32)
    fold_index = mirror - (count_ia - 1 - ia_index) * col_count
    mirror_lane = jnp.broadcast_to((fold_index % LANES)[None, :], (8, col_count))
    matrices = mixing_matrices(vinv)
    profiles = jnp.pad(alt_profile.reshape(2, LEVELS, 1), ((0, 0), (0, PAD - LEVELS), (0, 0)))
    wet = land_mask.astype(F32)
    coast = jnp.stack([wet, coef_north, coef_east])
    alt_capacity = max(2, 3 * alt_value.shape[0] // devices)
    sizes = (capacity, alt_capacity, group, row_count, col_count)
    *temperature, sea = make_forcing(0, *sizes, (flags, message, profiles[0], coast))
    salinity = make_forcing(1, *sizes, (flags, message, profiles[1], sea))
    fields = [temperature, salinity]
    coef = None

    ring_east = [(i, (i + 1) % count_ia) for i in range(count_ia)]
    ring_west = [((i + 1) % count_ia, i) for i in range(count_ia)]
    even_swap = [(i, i ^ 1) for i in range(count_ja)]
    odd_swap = []
    for ja in range(1, count_ja):
        for ia in range(count_ia):
            partner = ((ja - 1) ^ 1) + 1
            to = (partner, ia) if ja < count_ja - 1 else (ja, count_ia - 1 - ia)
            odd_swap.append((ja * count_ia + ia, to[0] * count_ia + to[1]))
    output = None
    for sweep in range(ITERS):
        for which in range(2):
            state, even_edge, odd_edge, cols = fields[which]
            received = (
                lax.ppermute(even_edge, "ja", even_swap),
                lax.ppermute(odd_edge, ("ja", "ia"), odd_swap),
                lax.ppermute(cols, "ia", ring_east),
                lax.ppermute(cols, "ia", ring_west),
            )
            if coef is None:
                coef = edge_weights(flags, coast, received, mirror_lane)
            final = (which, wet, output) if sweep == ITERS - 1 else None
            result = diffuse(flags, state, received, mirror_lane, coef, matrices[which], final)
            if final is None:
                fields[which] = result
            else:
                output = result
    return output


def solution(mesh):
    in_specs = (
        P(("ja", "ia"), None),
        P(("ja", "ia"), None),
        P(("ja", "ia")),
        P(("ja", "ia")),
        P(("ja", "ia"), None),
        P(("ja", "ia")),
        P(),
        P("ja", "ia"),
        P("ja", "ia"),
        P("ja", "ia"),
        P("ia"),
        P("ja", None, None, None),
    )
    out_specs = P(None, "ja", "ia")
    return jax.shard_map(body, mesh=mesh, in_specs=in_specs, out_specs=out_specs, check_vma=False)
```

```python
import jax
import jax.numpy as jnp
from jax import lax
from jax.experimental import pallas as pl
from jax.experimental.pallas import tpu as pltpu
from jax.sharding import PartitionSpec as P

ITERS = 3
LEVELS = 75
PAD = 80
LANES = 128
NEAR, FAR, TOP = 0, 1, 2
BF = jnp.bfloat16
F32 = jnp.float32
MIB = 1024 * 1024


def round_up(value, unit):
    return (value + unit - 1) // unit * unit


def split_two(value):
    high = value.astype(BF)
    low = (value - high.astype(F32)).astype(BF)
    return high, low


def mm(left, right):
    return jnp.dot(left, right, preferred_element_type=F32)


def as_column(row):
    return jnp.broadcast_to(row, (8, row.shape[1])).T[:, 0:1]


def slot_positions(owner_row, cell_row, col_count, row_count, capacity, spread):
    count = owner_row.shape[1]
    base = owner_row.astype(F32) * float(row_count * count)
    inside = cell_row // col_count
    order = lax.broadcasted_iota(jnp.int32, (1, count), 1).astype(F32)
    key = base + inside.astype(F32) * float(count) + order
    key_col = as_column(key)
    rank = jnp.zeros((1, count), F32)
    total = jnp.zeros((1, count), F32)
    beyond = base + float(row_count * count)
    for start in range(0, count, 128):
        part = key_col[start : start + 128]
        own = jnp.where(part >= base, 1.0, 0.0)
        rank = rank + jnp.sum(jnp.where(part < key, own, 0.0), axis=0, keepdims=True)
        if spread:
            total = total + jnp.sum(jnp.where(part < beyond, own, 0.0), axis=0, keepdims=True)
    if spread:
        goal = (inside * capacity // row_count).astype(F32) - rank
        goal_col = as_column(goal)
        shift = jnp.zeros((1, count), F32)
        for start in range(0, count, 128):
            part = key_col[start : start + 128]
            own = jnp.where(part >= base, goal_col[start : start + 128], 0.0)
            shift = jnp.maximum(
                shift, jnp.max(jnp.where(part <= key, own, 0.0), axis=0, keepdims=True)
            )
        rank = rank + jnp.minimum(shift, float(capacity) - total)
    return owner_row.astype(F32) * float(capacity) + rank


def table_kernel(
    capacity,
    group,
    row_count,
    col_count,
    value_ref,
    owner_ref,
    cell_ref,
    alt_ref,
    alt_owner_ref,
    message_ref,
    level_ref,
    side_ref,
    hi_ref,
    lo_ref,
    alt_all_ref,
    place_ref,
    alt_place_ref,
):
    index = pl.program_id(0)

    @pl.when(index == 0)
    def _():
        place_ref[0:1] = slot_positions(
            owner_ref[...], cell_ref[...], col_count, row_count, capacity, True
        )
        alt_place_ref[0:1] = slot_positions(
            alt_owner_ref[...],
            alt_ref[1:2].astype(jnp.int32),
            col_count,
            row_count,
            capacity,
            False,
        )
        level_ref[...] = jnp.zeros(level_ref.shape, F32)
        level_ref[0:75, :] = value_ref[0:75, :]
        level_ref[75:76, :] = cell_ref[...].astype(F32) + 1.0
        level_ref[80:128, :] = value_ref[75:123, :]
        for lane_group in range(4):
            level_ref[128 + 32 * lane_group : 155 + 32 * lane_group, :] = value_ref[123:150, :]
        high, low = split_two(level_ref[...].T)
        hi_ref[...] = high
        lo_ref[...] = low
        side_ref[...] = jnp.zeros(side_ref.shape, F32)
        pair = alt_ref[0:2] + lax.broadcasted_iota(jnp.int32, (2, 1), 0).astype(F32)
        pair_high = pair.astype(BF).astype(F32)
        side_ref[76:78, :] = pair_high
        side_ref[78:80, :] = pair - pair_high
        alt_all_ref[...] = side_ref[...].T.astype(BF)

    per_step = message_ref.shape[0]
    rows = per_step * capacity
    slot = (lax.broadcasted_iota(jnp.int32, (rows, 1), 0) + index * rows).astype(F32)
    chosen = jnp.where(slot == place_ref[0:1], 1.0, 0.0).astype(BF)
    chosen_alt = jnp.where(slot == alt_place_ref[0:1], 1.0, 0.0).astype(BF)
    table = mm(chosen, hi_ref[...]) + mm(chosen, lo_ref[...])
    lane = lax.broadcasted_iota(jnp.int32, (1, LANES), 1)
    extra = mm(chosen_alt, alt_all_ref[...])
    extra = jnp.where(lane < 78, extra + pltpu.roll(extra, LANES - 2, 1), 0.0)
    extra = jnp.where(lane >= 76, extra, 0.0)
    first = table[:, :LANES] + extra
    message_ref[:, 0:capacity] = first.reshape(per_step, capacity, LANES)
    rest = table[:, LANES:].reshape(per_step, capacity, LANES)
    total = jnp.zeros((per_step, group, LANES), F32)
    for lane_group in range(4):
        low_slot = lane_group * group
        if low_slot >= capacity:
            continue
        piece = rest[:, low_slot : low_slot + group]
        here = (lane // 32 == lane_group).reshape(1, 1, LANES)
        total = jnp.where(here, piece, total)
    message_ref[:, capacity : capacity + group] = total


def send_tables(devices, capacity, group, row_count, col_count, values, owner, cell, alt, alt_owner):
    n_obs = owner.shape[1]
    n_alt = alt_owner.shape[1]
    per_step = max(1, 768 // capacity)

    def kernel(*refs):
        table_kernel(capacity, group, row_count, col_count, *refs)

    operands = (values, owner, cell, alt, alt_owner)
    return pl.pallas_call(
        kernel,
        grid=(devices // per_step,),
        in_specs=[pl.BlockSpec(x.shape, lambda s: (0, 0)) for x in operands],
        out_specs=pl.BlockSpec((per_step, capacity + group, LANES), lambda s: (s, 0, 0)),
        out_shape=jax.ShapeDtypeStruct((devices, capacity + group, LANES), F32),
        scratch_shapes=[
            pltpu.VMEM((2 * LANES, n_obs), F32),
            pltpu.VMEM((LANES, n_alt), F32),
            pltpu.VMEM((n_obs, 2 * LANES), BF),
            pltpu.VMEM((n_obs, 2 * LANES), BF),
            pltpu.VMEM((n_alt, LANES), BF),
            pltpu.VMEM((8, n_obs), F32),
            pltpu.VMEM((8, n_alt), F32),
        ],
        compiler_params=pltpu.CompilerParams(vmem_limit_bytes=56 * MIB),
        name="send_tables",
    )(*operands)


def add_columns(cols, pair, row, rows):
    lane = lax.broadcasted_iota(jnp.int32, (1, LANES), 1)
    for field in range(2):
        part = pair[field * PAD : (field + 1) * PAD]
        at = 2 * rows * field + row
        cols = jnp.where(lane == at, pltpu.roll(part[:, :LANES], at, 1), cols)
        at = at + rows
        cols = jnp.where(lane == at, pltpu.roll(part[:, -LANES:], at + 1, 1), cols)
    return cols


def write_messages(is_upper, state_ref, edge_ref, cols_ref):
    rows = state_ref.shape[0]
    cols = jnp.zeros((PAD, LANES), F32)
    for row in range(rows):
        cols = add_columns(cols, state_ref[row], row, rows)
    cols_ref[...] = cols
    edge_ref[...] = state_ref[jnp.where(is_upper, rows - 1, 0)]


def prepare(capacity, alt_capacity, group, col_count, message_ref, sea_ref, left_ref, hot_ref, rows_ref):
    row_count = sea_ref.shape[0]
    devices = message_ref.shape[0]
    block = min(32, devices)
    members = block * 8
    octets = capacity // 8
    alt_octets = (alt_capacity + 7) // 8
    per_group = group // 8
    shift = col_count.bit_length() - 1
    col_iota = lax.broadcasted_iota(jnp.int32, (1, col_count), 1)
    row_iota = lax.broadcasted_iota(jnp.int32, (row_count, 1), 0)

    def chunk(index, start):
        return message_ref[index * block : (index + 1) * block, start : start + 8, :].reshape(
            members, LANES
        )

    def hot_of(cell):
        return jnp.where(((cell - 1) & (col_count - 1)) == col_iota, 1.0, 0.0).astype(BF)

    def rows_of(cell):
        return lax.shift_right_arithmetic(cell - 1, shift)

    sea = jnp.zeros((row_count, col_count), F32)
    count = 0
    for index in range(devices // block):
        tails = [chunk(index, capacity + 8 * part).T for part in range(per_group)]
        for octet in range(octets):
            table = chunk(index, 8 * octet)
            turned = table.T
            tail = tails[octet % per_group]
            begin = 32 * (octet // per_group)
            levels = jnp.concatenate([turned, tail[begin : begin + 32]], axis=0)
            high, low = split_two(levels)
            left_ref[count, :, 0:members] = high
            left_ref[count, :, members : 2 * members] = low
            hot = hot_of(table[:, 75:76].astype(jnp.int32))
            hot_ref[count, 0:members] = hot
            hot_ref[count, members : 2 * members] = hot
            rows_ref[count] = jnp.broadcast_to(rows_of(turned[75:76].astype(jnp.int32)), (8, members))
            count += 1
            if octet >= alt_octets:
                continue
            alt_hot = hot_of(table[:, 77:78].astype(jnp.int32))
            alt_rows = rows_of(turned[77:78].astype(jnp.int32))
            weighted = jnp.where(alt_rows == row_iota, turned[76:77], 0.0)
            high, low = split_two(weighted)
            product = mm(jnp.concatenate([high, low], axis=0), alt_hot)
            sea = sea + product[:row_count] + product[row_count:]
    sea_ref[...] = sea


def half_forcing(is_upper, profile_ref, coast_refs, sea_ref, left_ref, hot_ref, rows_ref, outputs):
    state, edge_ref, cols_ref = outputs
    rows, _, col_count = state.shape
    count = left_ref.shape[0]
    first_row = jnp.where(is_upper, rows, 0)
    aligned = pl.multiple_of(first_row, 8)
    sea = sea_ref[pl.ds(aligned, rows), :]
    for start in range(0, col_count, LANES):
        profile = jnp.broadcast_to(profile_ref[...], (2 * PAD, LANES))
        for row in range(rows):
            state[row, :, start : start + LANES] = profile * sea[row : row + 1, start : start + LANES]
    span = 4

    def step(number, carry):
        here = rows_ref[number][0:1] - first_row
        inside = (here >= 0) & (here < rows)
        least = jnp.min(jnp.where(inside, here, rows))
        most = jnp.max(jnp.where(inside, here, -1))

        def rows_step(start, inner):
            base = start * span
            pieces = []
            for offset in range(span):
                mask = jnp.where(here == base + offset, 1.0, 0.0).astype(BF)
                pieces.append(left_ref[number] * jnp.concatenate([mask, mask], axis=1))
            product = mm(jnp.concatenate(pieces, axis=0), hot_ref[number])
            for offset in range(span):
                state[base + offset] += product[2 * PAD * offset : 2 * PAD * (offset + 1)]
            return inner

        lax.fori_loop(least // span, (most + span) // span, rows_step, 0)
        return carry

    lax.fori_loop(0, count, step, 0)
    for kind, coast_ref in enumerate(coast_refs):
        coast = coast_ref[pl.ds(aligned, rows), :].astype(F32)
        for row in range(rows):
            state[row, LEVELS + kind : LEVELS + kind + 1, :] = coast[row : row + 1, :]
    write_messages(is_upper, state, edge_ref, cols_ref)


def half_shapes(row_count, col_count):
    return (
        jax.ShapeDtypeStruct((row_count // 2, 2 * PAD, col_count), F32),
        jax.ShapeDtypeStruct((2 * PAD, col_count), F32),
        jax.ShapeDtypeStruct((PAD, LANES), F32),
    )


def in_place(count):
    return [pl.BlockSpec(memory_space=pltpu.SMEM)] + [pl.BlockSpec(memory_space=pltpu.VMEM)] * count


def near_forcing(capacity, alt_capacity, group, flags, message, profile, coast):
    row_count, col_count = coast[0].shape
    devices = message.shape[0]
    members = min(32, devices) * 8
    chunks = capacity // 8 * (devices // min(32, devices))

    def kernel(flag_ref, message_ref, profile_ref, wet, north, east, *outs):
        prepare(capacity, alt_capacity, group, col_count, message_ref, *outs[3:])
        half_forcing(flag_ref[NEAR] > 0, profile_ref, (wet, north, east), *outs[3:], outs[:3])

    return pl.pallas_call(
        kernel,
        in_specs=in_place(5),
        out_shape=half_shapes(row_count, col_count)
        + (
            jax.ShapeDtypeStruct((row_count, col_count), F32),
            jax.ShapeDtypeStruct((chunks, 2 * PAD, 2 * members), BF),
            jax.ShapeDtypeStruct((chunks, 2 * members, col_count), BF),
            jax.ShapeDtypeStruct((chunks, 8, members), jnp.int32),
        ),
        compiler_params=pltpu.CompilerParams(vmem_limit_bytes=30 * MIB),
        cost_estimate=pl.CostEstimate(
            flops=9_000_000_000, bytes_accessed=8_000_000, transcendentals=0
        ),
        name="forcing_near",
    )(flags, message, profile, *coast)


def far_forcing(flags, profile, coast, prepared):
    row_count, col_count = coast[0].shape

    def kernel(flag_ref, profile_ref, wet, north, east, sea, left, hot, rows, *outs):
        half_forcing(
            flag_ref[FAR] > 0, profile_ref, (wet, north, east), sea, left, hot, rows, outs
        )

    return pl.pallas_call(
        kernel,
        in_specs=in_place(8),
        out_shape=half_shapes(row_count, col_count),
        compiler_params=pltpu.CompilerParams(vmem_limit_bytes=30 * MIB),
        cost_estimate=pl.CostEstimate(
            flops=4_000_000_000, bytes_accessed=8_000_000, transcendentals=0
        ),
        name="forcing_far",
    )(flags, profile, *coast, *prepared)


def fold_row(row_ref, mirror_ref, piece, chunk, chunks, rows):
    index = jnp.broadcast_to(mirror_ref[0:1, piece(chunk)], (rows, LANES))
    return jnp.take_along_axis(row_ref[:, piece(chunks - 1 - chunk)], index, axis=1)


def weight_kernel(which, flag_ref, wet_ref, north_ref, east_ref, edge_in, west_in, east_in, mirror_ref, out_ref, fold_ref):
    row_count, col_count = wet_ref.shape
    rows = row_count // 2
    is_upper = flag_ref[which] > 0
    at = pl.multiple_of(jnp.where(is_upper, rows, 0), 8)
    wet = wet_ref[pl.ds(at, rows), :].astype(F32)
    north = north_ref[pl.ds(at, rows), :]
    east = east_ref[pl.ds(at, rows), :]
    chunks = col_count // LANES
    lane = lax.broadcasted_iota(jnp.int32, (1, col_count), 1)
    west_cols = west_in[72:80, :].T[rows : 2 * rows]
    east_cols = east_in[72:80, :].T[0:rows]
    west_wet = jnp.where(lane == 0, west_cols[:, 3:4], pltpu.roll(wet, 1, 1))
    west_coef = jnp.where(lane == 0, west_cols[:, 5:6], pltpu.roll(east, 1, 1))
    east_wet = jnp.where(
        lane == col_count - 1, east_cols[:, 3:4], pltpu.roll(wet, col_count - 1, 1)
    )
    east_w = east * wet * east_wet
    west_w = west_coef * west_wet * wet

    def piece(c):
        return slice(c * LANES, (c + 1) * LANES)

    spare_ref = edge_in.at[72:80]
    if which == FAR:
        for c in range(chunks):
            fold_ref[:, piece(c)] = fold_row(spare_ref, mirror_ref, piece, c, chunks, 8)
    spare = spare_ref[...]
    last = rows - 1
    inner_wet = jnp.where(
        is_upper, wet_ref[rows - 1 : rows, :], wet_ref[rows : rows + 1, :]
    ).astype(F32)
    above = jnp.where(is_upper, spare[3:4], inner_wet)
    top_w = north[last:] * wet[last:] * above
    if which == FAR:
        fold = 0.5 * (north[last:] + fold_ref[4:5]) * wet[last:] * fold_ref[3:4]
        top_w = jnp.where(flag_ref[TOP] > 0, fold, top_w)
    below = jnp.where(is_upper, north_ref[rows - 1 : rows, :] * inner_wet, spare[4:5] * spare[3:4])
    between = north[:last] * wet[:last] * wet[1:]
    north_w = jnp.concatenate([between, top_w], axis=0)
    south_w = jnp.concatenate([below * wet[0:1], between], axis=0)
    center = 1.0 - (east_w + west_w + north_w + south_w)
    for kind, weight in enumerate((center, east_w, west_w, north_w, south_w)):
        for row in range(rows):
            out_ref[row, kind : kind + 1, :] = weight[row : row + 1]


def edge_weights(which, flags, coast, received, mirror):
    row_count, col_count = coast[0].shape

    def kernel(*refs):
        weight_kernel(which, *refs)

    return pl.pallas_call(
        kernel,
        in_specs=in_place(7),
        out_shape=jax.ShapeDtypeStruct((row_count // 2, 8, col_count), F32),
        scratch_shapes=[pltpu.VMEM((8, col_count), F32)],
        compiler_params=pltpu.CompilerParams(vmem_limit_bytes=16 * MIB),
        name="edge_weights",
    )(flags, *coast, *received, mirror)


def set_outer_rows(which, flag_ref, edge_in, inner, mirror_ref, south_ref, north_ref):
    levels, col_count = edge_in.shape
    is_upper = flag_ref[which] > 0
    is_top = flag_ref[TOP] > 0
    chunks = col_count // LANES

    def piece(c):
        return slice(c * LANES, (c + 1) * LANES)

    @pl.when(is_upper)
    def _():
        south_ref[...] = inner[...]

    @pl.when(jnp.logical_not(is_upper))
    def _():
        south_ref[...] = edge_in[...]
        north_ref[...] = inner[...]

    if which == NEAR:

        @pl.when(is_upper)
        def _():
            north_ref[...] = edge_in[...]

        return

    @pl.when(is_upper & jnp.logical_not(is_top))
    def _():
        north_ref[...] = edge_in[...]

    @pl.when(is_top)
    def _():
        for c in range(chunks):
            north_ref[:, piece(c)] = fold_row(edge_in, mirror_ref, piece, c, chunks, levels)


def mix_row(row, rows, field, at, state_ref, south_ref, north_ref, west_in, east_in, coef_ref, right_ref, slot):
    col_count = state_ref.shape[2]
    chunks = col_count // LANES
    lane = lax.broadcasted_iota(jnp.int32, (1, LANES), 1)
    levels = slice(at, at + PAD)

    def piece(chunk):
        return slice(chunk * LANES, (chunk + 1) * LANES)

    west_lane = 2 * rows * field + rows + row
    east_lane = 2 * rows * field + row
    centers = [state_ref[row, levels, piece(c)] for c in range(chunks)]
    to_left = [pltpu.roll(c, LANES - 1, 1) for c in centers]
    to_right = [pltpu.roll(c, 1, 1) for c in centers]
    to_right.append(pltpu.roll(west_in[...], LANES - west_lane, 1))
    to_left.append(pltpu.roll(east_in[...], LANES - 1 - east_lane, 1))
    for c in range(chunks):
        south = state_ref[row - 1, levels, piece(c)] if row > 0 else south_ref[levels, piece(c)]
        if row < rows - 1:
            north = state_ref[row + 1, levels, piece(c)]
        else:
            north = north_ref[levels, piece(c)]
        east = jnp.where(lane == LANES - 1, to_left[c + 1], to_left[c])
        west = jnp.where(lane == 0, to_right[c - 1], to_right[c])

        def coef(kind):
            return coef_ref[row, kind : kind + 1, piece(c)]

        mixed = (
            coef(0) * centers[c]
            + coef(1) * east
            + coef(2) * west
            + coef(3) * north
            + coef(4) * south
        )
        high, low = split_two(mixed)
        right_ref[slot, 0:PAD, piece(c)] = high
        right_ref[slot, PAD : 2 * PAD, piece(c)] = low
        right_ref[slot, 2 * PAD : 3 * PAD, piece(c)] = high


def diffuse(which, flags, state, other, received, mirror, coef, matrix):
    rows, _, col_count = state.shape
    slots = 4

    def kernel(flag_ref, state_ref, other_ref, edge_in, west_in, east_in, mirror_ref, coef_ref, matrix_ref, out_ref, edge_ref, cols_ref, south_ref, north_ref, right_ref):
        is_upper = flag_ref[which] > 0
        inner = other_ref.at[jnp.where(is_upper, rows - 1, 0)]
        set_outer_rows(which, flag_ref, edge_in, inner, mirror_ref, south_ref, north_ref)
        right_ref[:, 3 * PAD :, :] = jnp.zeros((slots, 16, col_count), BF)
        units = [(row, field) for row in range(rows) for field in range(2)]

        def product(number):
            row, field = units[number]
            result = mm(matrix_ref[field, row], right_ref[number % slots])
            out_ref[row, field * PAD : (field + 1) * PAD] = result

        for number, (row, field) in enumerate(units):
            mix_row(row, rows, field, field * PAD, state_ref, south_ref, north_ref, west_in, east_in, coef_ref, right_ref, number % slots)
            if number > 0:
                product(number - 1)
        product(len(units) - 1)
        write_messages(is_upper, out_ref, edge_ref, cols_ref)

    return pl.pallas_call(
        kernel,
        in_specs=in_place(8),
        out_shape=half_shapes(2 * rows, col_count),
        scratch_shapes=[
            pltpu.VMEM((2 * PAD, col_count), F32),
            pltpu.VMEM((2 * PAD, col_count), F32),
            pltpu.VMEM((slots, 256, col_count), BF),
        ],
        compiler_params=pltpu.CompilerParams(vmem_limit_bytes=24 * MIB),
        cost_estimate=pl.CostEstimate(
            flops=3_000_000_000, bytes_accessed=8_000_000, transcendentals=0
        ),
        name="diffusion_" + ("near", "far")[which],
    )(flags, state, other, *received, mirror, coef, matrix)


def diffuse_last(which, flags, state, other, received, mirror, coef, matrix, mask, target):
    rows, _, col_count = state.shape
    slots = 4

    def kernel(flag_ref, state_ref, other_ref, edge_in, west_in, east_in, mirror_ref, coef_ref, matrix_ref, mask_ref, *refs):
        out_ref, south_ref, north_ref, right_ref = refs[-4:]
        field = pl.program_id(0)
        set_outer_rows(which, flag_ref, edge_in, other_ref.at[0], mirror_ref, south_ref, north_ref)
        right_ref[:, 3 * PAD :, :] = jnp.zeros((slots, 16, col_count), BF)
        wet = mask_ref[...].astype(F32)
        results = []

        def product(row):
            result = mm(matrix_ref[0, row], right_ref[row % slots])
            results.append(result * wet[row : row + 1])

        for row in range(rows):
            mix_row(row, rows, field, 0, state_ref, south_ref, north_ref, west_in, east_in, coef_ref, right_ref, row % slots)
            if row > 0:
                product(row - 1)
        product(rows - 1)
        out_ref[...] = jnp.swapaxes(jnp.stack(results), 0, 1)[:LEVELS]

    def whole(array):
        return pl.BlockSpec(array.shape, lambda f, flags: (0,) * len(array.shape))

    edge_in, west_in, east_in = received
    in_specs = [
        pl.BlockSpec((rows, PAD, col_count), lambda f, flags: (0, f, 0)),
        pl.BlockSpec((1, PAD, col_count), lambda f, flags: (flags[which] * (rows - 1), f, 0)),
        pl.BlockSpec((PAD, col_count), lambda f, flags: (f, 0)),
        whole(west_in),
        whole(east_in),
        whole(mirror),
        whole(coef),
        pl.BlockSpec((1, rows) + matrix.shape[2:], lambda f, flags: (f, 0, 0, 0)),
        pl.BlockSpec((rows, col_count), lambda f, flags: (flags[which], 0)),
    ]
    operands = [state, other, edge_in, west_in, east_in, mirror, coef, matrix, mask]
    aliases = {}
    if target is not None:
        in_specs.append(pl.BlockSpec(memory_space=pl.ANY))
        operands.append(target)
        aliases = {len(operands): 0}
    return pl.pallas_call(
        kernel,
        grid_spec=pltpu.PrefetchScalarGridSpec(
            num_scalar_prefetch=1,
            grid=(2,),
            in_specs=in_specs,
            out_specs=pl.BlockSpec((LEVELS, rows, col_count), lambda f, flags: (f, flags[which], 0)),
            scratch_shapes=[
                pltpu.VMEM((PAD, col_count), F32),
                pltpu.VMEM((PAD, col_count), F32),
                pltpu.VMEM((slots, 256, col_count), BF),
            ],
        ),
        out_shape=jax.ShapeDtypeStruct((2 * LEVELS, 2 * rows, col_count), F32),
        input_output_aliases=aliases,
        compiler_params=pltpu.CompilerParams(vmem_limit_bytes=28 * MIB),
        cost_estimate=pl.CostEstimate(
            flops=3_000_000_000, bytes_accessed=8_000_000, transcendentals=0
        ),
        name="diffusion_last",
    )(flags, *operands)


def mixing_matrices(vinv):
    turned = jnp.transpose(vinv, (1, 0, 3, 2))
    turned = jnp.pad(turned, ((0, 0), (0, 0), (0, PAD - LEVELS), (0, PAD - LEVELS)))
    high = lax.reduce_precision(turned, 8, 7)
    low = (turned - high).astype(BF)
    high = high.astype(BF)
    rest = jnp.zeros(high.shape[:3] + (256 - 3 * PAD,), BF)
    return jnp.concatenate([high, high, low, rest], axis=3)


def body(
    argo_value,
    argo_owner,
    argo_cell,
    alt_value,
    alt_owner,
    alt_cell,
    alt_profile,
    land_mask,
    coef_east,
    coef_north,
    mirror,
    vinv,
):
    row_count, col_count = land_mask.shape
    count_ja = lax.axis_size("ja")
    count_ia = lax.axis_size("ia")
    devices = count_ja * count_ia
    capacity = round_up(3 * argo_value.shape[0] // devices, 8)
    group = round_up(capacity // 4, 8)
    message = send_tables(
        devices,
        capacity,
        group,
        row_count,
        col_count,
        argo_value.T,
        argo_owner.reshape(1, -1),
        argo_cell.reshape(1, -1),
        jnp.stack([alt_value, alt_cell.astype(F32)]),
        alt_owner.reshape(1, -1),
    )
    message = lax.all_to_all(message, ("ja", "ia"), split_axis=0, concat_axis=0, tiled=True)

    ia_index = lax.axis_index("ia")
    ja_index = lax.axis_index("ja")
    is_top = (ja_index == count_ja - 1).astype(jnp.int32)
    parity = ja_index % 2
    flags = jnp.stack([1 - parity, parity, is_top]).astype(jnp.int32)
    fold_index = mirror - (count_ia - 1 - ia_index) * col_count
    mirror_lane = jnp.broadcast_to((fold_index % LANES)[None, :], (8, col_count))
    matrices = mixing_matrices(vinv)
    profile = jnp.pad(alt_profile.reshape(2, LEVELS, 1), ((0, 0), (0, PAD - LEVELS), (0, 0)))
    profile = profile.reshape(2 * PAD, 1)
    alt_capacity = max(2, 3 * alt_value.shape[0] // devices)
    coast = (land_mask, coef_north, coef_east)
    rows = row_count // 2
    lower = [matrices[:, :rows], matrices[:, rows:]]
    odd_device = parity == 1
    half_matrices = [
        jnp.where(odd_device, lower[0], lower[1]),
        jnp.where(odd_device, lower[1], lower[0]),
    ]

    ring_east = [(i, (i + 1) % count_ia) for i in range(count_ia)]
    ring_west = [((i + 1) % count_ia, i) for i in range(count_ia)]
    even_swap = []
    odd_swap = []
    for ja in range(count_ja):
        for ia in range(count_ia):
            here = ja * count_ia + ia
            even_swap.append((here, (ja ^ 1) * count_ia + ia))
            if ja == count_ja - 1:
                odd_swap.append((here, ja * count_ia + count_ia - 1 - ia))
            elif ja > 0:
                odd_swap.append((here, (((ja - 1) ^ 1) + 1) * count_ia + ia))
    swaps = (even_swap, odd_swap)

    def exchange(which, edge, cols):
        return (
            lax.ppermute(edge, ("ja", "ia"), swaps[which]),
            lax.ppermute(cols, "ia", ring_east),
            lax.ppermute(cols, "ia", ring_west),
        )

    near, edge, cols, *prepared = near_forcing(
        capacity, alt_capacity, group, flags, message, profile, coast
    )
    near_in = exchange(NEAR, edge, cols)
    far, edge, cols = far_forcing(flags, profile, coast, prepared)
    far_in = exchange(FAR, edge, cols)
    near_coef = edge_weights(NEAR, flags, coast, near_in, mirror_lane)
    far_coef = None
    for sweep in range(ITERS - 1):
        old_near = near
        near, edge, cols = diffuse(
            NEAR, flags, near, far, near_in, mirror_lane, near_coef, half_matrices[NEAR]
        )
        near_in = exchange(NEAR, edge, cols)
        if far_coef is None:
            far_coef = edge_weights(FAR, flags, coast, far_in, mirror_lane)
        far, edge, cols = diffuse(
            FAR, flags, far, old_near, far_in, mirror_lane, far_coef, half_matrices[FAR]
        )
        far_in = exchange(FAR, edge, cols)
    output = diffuse_last(
        NEAR, flags, near, far, near_in, mirror_lane, near_coef, half_matrices[NEAR], land_mask, None
    )
    return diffuse_last(
        FAR, flags, far, near, far_in, mirror_lane, far_coef, half_matrices[FAR], land_mask, output
    )


def solution(mesh):
    in_specs = (
        P(("ja", "ia"), None),
        P(("ja", "ia"), None),
        P(("ja", "ia")),
        P(("ja", "ia")),
        P(("ja", "ia"), None),
        P(("ja", "ia")),
        P(),
        P("ja", "ia"),
        P("ja", "ia"),
        P("ja", "ia"),
        P("ia"),
        P("ja", None, None, None),
    )
    out_specs = P(None, "ja", "ia")
    return jax.shard_map(body, mesh=mesh, in_specs=in_specs, out_specs=out_specs, check_vma=False)
```

```python
import jax
import jax.numpy as jnp
from jax import lax
from jax.experimental import pallas as pl
from jax.experimental.pallas import tpu as pltpu
from jax.sharding import PartitionSpec as P

ITERS = 3
LEVELS = 75
PAD = 80
LANES = 128
NEAR, FAR, TOP = 0, 1, 2
BF = jnp.bfloat16
F32 = jnp.float32
MIB = 1024 * 1024


def round_up(value, unit):
    return (value + unit - 1) // unit * unit


def split_two(value):
    high = value.astype(BF)
    low = (value - high.astype(F32)).astype(BF)
    return high, low


def mm(left, right):
    return jnp.dot(left, right, preferred_element_type=F32)


def as_column(row):
    return jnp.broadcast_to(row, (8, row.shape[1])).T[:, 0:1]


def slot_ranks(owner_row, cell_row, devices, col_count, row_count, capacity, spread):
    count = owner_row.shape[1]
    base = owner_row.astype(F32) * float(row_count * count)
    inside = cell_row // col_count
    order = lax.broadcasted_iota(jnp.int32, (1, count), 1).astype(F32)
    key = base + inside.astype(F32) * float(count) + order
    key_col = as_column(key)
    rank = jnp.zeros((1, count), F32)
    for start in range(0, count, 128):
        part = key_col[start : start + 128]
        before = (part < key) & (part >= base)
        rank = rank + jnp.sum(jnp.where(before, 1.0, 0.0), axis=0, keepdims=True)
    if spread:
        owners = lax.broadcasted_iota(jnp.int32, (devices, 1), 0) == owner_row
        totals = jnp.sum(jnp.where(owners, 1.0, 0.0), axis=1, keepdims=True)
        total = jnp.sum(jnp.where(owners, totals, 0.0), axis=0, keepdims=True)
        goal = (inside * capacity // row_count).astype(F32) - rank
        goal_col = as_column(goal)
        shift = jnp.zeros((1, count), F32)
        for start in range(0, count, 128):
            part = key_col[start : start + 128]
            within = (part <= key) & (part >= base)
            shift = jnp.maximum(
                shift,
                jnp.max(
                    jnp.where(within, goal_col[start : start + 128], 0.0), axis=0, keepdims=True
                ),
            )
        rank = rank + jnp.minimum(shift, float(capacity) - total)
    return rank


def table_kernel(
    devices,
    capacity,
    group,
    row_count,
    col_count,
    value_ref,
    owner_ref,
    cell_ref,
    alt_value_ref,
    alt_cell_ref,
    alt_owner_ref,
    message_ref,
    level_ref,
    side_ref,
    hi_ref,
    lo_ref,
    alt_all_ref,
    rank_hot_ref,
    alt_rank_hot_ref,
):
    index = pl.program_id(0)
    n_obs = owner_ref.shape[1]
    n_alt = alt_owner_ref.shape[1]

    @pl.when(index == 0)
    def _():
        slot = lax.broadcasted_iota(jnp.int32, (capacity, 1), 0).astype(F32)
        alt_cell = alt_cell_ref[...].reshape(1, n_alt)
        rank = slot_ranks(
            owner_ref[...], cell_ref[...], devices, col_count, row_count, capacity, True
        )
        rank_hot_ref[...] = jnp.where(slot == rank, 1.0, 0.0).astype(BF)
        rank = slot_ranks(
            alt_owner_ref[...], alt_cell, devices, col_count, row_count, capacity, False
        )
        alt_rank_hot_ref[...] = jnp.where(slot == rank, 1.0, 0.0).astype(BF)
        level_ref[...] = jnp.zeros(level_ref.shape, F32)
        level_ref[0:75, :] = value_ref[0:75, :]
        level_ref[75:76, :] = cell_ref[...].astype(F32) + 1.0
        level_ref[80:128, :] = value_ref[75:123, :]
        for lane_group in range(4):
            level_ref[128 + 32 * lane_group : 155 + 32 * lane_group, :] = value_ref[123:150, :]
        high, low = split_two(level_ref[...].T)
        hi_ref[...] = high
        lo_ref[...] = low
        side_ref[...] = jnp.zeros(side_ref.shape, F32)
        pair = jnp.concatenate(
            [alt_value_ref[...].reshape(1, n_alt), alt_cell.astype(F32) + 1.0], axis=0
        )
        pair_high = pair.astype(BF).astype(F32)
        side_ref[76:78, :] = pair_high
        side_ref[78:80, :] = pair - pair_high
        alt_all_ref[...] = side_ref[...].T.astype(BF)

    per_step = message_ref.shape[0]
    chosen = []
    chosen_alt = []
    for member in range(per_step):
        device = index * per_step + member
        mask = jnp.where(owner_ref[...] == device, 1.0, 0.0).astype(BF)
        chosen.append(rank_hot_ref[...] * mask)
        mask = jnp.where(alt_owner_ref[...] == device, 1.0, 0.0).astype(BF)
        chosen_alt.append(alt_rank_hot_ref[...] * mask)
    chosen = jnp.concatenate(chosen, axis=0)
    chosen_alt = jnp.concatenate(chosen_alt, axis=0)
    table = mm(chosen, hi_ref[...]) + mm(chosen, lo_ref[...])
    lane = lax.broadcasted_iota(jnp.int32, (1, LANES), 1)
    extra = mm(chosen_alt, alt_all_ref[...])
    extra = jnp.where(lane < 78, extra + pltpu.roll(extra, LANES - 2, 1), 0.0)
    extra = jnp.where(lane >= 76, extra, 0.0)
    first = table[:, :LANES] + extra
    message_ref[:, 0:capacity] = first.reshape(per_step, capacity, LANES)
    rest = table[:, LANES:].reshape(per_step, capacity, LANES)
    total = jnp.zeros((per_step, group, LANES), F32)
    for lane_group in range(4):
        low_slot = lane_group * group
        if low_slot >= capacity:
            continue
        piece = rest[:, low_slot : low_slot + group]
        here = (lane // 32 == lane_group).reshape(1, 1, LANES)
        total = jnp.where(here, piece, total)
    message_ref[:, capacity : capacity + group] = total


def send_tables(devices, capacity, group, row_count, col_count, operands):
    n_obs = operands[1].shape[1]
    n_alt = operands[5].shape[1]
    per_step = max(1, 768 // capacity)

    def kernel(*refs):
        table_kernel(devices, capacity, group, row_count, col_count, *refs)

    def whole(array):
        return pl.BlockSpec(array.shape, lambda s: (0,) * len(array.shape))

    return pl.pallas_call(
        kernel,
        grid=(devices // per_step,),
        in_specs=[whole(x) for x in operands],
        out_specs=pl.BlockSpec((per_step, capacity + group, LANES), lambda s: (s, 0, 0)),
        out_shape=jax.ShapeDtypeStruct((devices, capacity + group, LANES), F32),
        scratch_shapes=[
            pltpu.VMEM((2 * LANES, n_obs), F32),
            pltpu.VMEM((LANES, n_alt), F32),
            pltpu.VMEM((n_obs, 2 * LANES), BF),
            pltpu.VMEM((n_obs, 2 * LANES), BF),
            pltpu.VMEM((n_alt, LANES), BF),
            pltpu.VMEM((capacity, n_obs), BF),
            pltpu.VMEM((capacity, n_alt), BF),
        ],
        compiler_params=pltpu.CompilerParams(vmem_limit_bytes=56 * MIB),
        name="send_tables",
    )(*operands)


def column_lane(which, rows, field, east, row):
    return (4 * which + 2 * field + east) * rows + row


def columns_of(which, state_ref, cols):
    rows = state_ref.shape[0]
    lane = lax.broadcasted_iota(jnp.int32, (1, LANES), 1)
    for row in range(rows):
        for field in range(2):
            part = state_ref[row, field * PAD : (field + 1) * PAD, :]
            at = column_lane(which, rows, field, 0, row)
            cols = jnp.where(lane == at, pltpu.roll(part[:, :LANES], at, 1), cols)
            at = column_lane(which, rows, field, 1, row)
            cols = jnp.where(lane == at, pltpu.roll(part[:, -LANES:], at + 1, 1), cols)
    return cols


def add_far_columns(near_cols_ref, state_ref, cols_ref):
    cols_ref[...] = columns_of(FAR, state_ref, near_cols_ref[...])


def write_edge(is_upper, state_ref, edge_ref):
    edge_ref[...] = state_ref[jnp.where(is_upper, state_ref.shape[0] - 1, 0)]


def prepare(capacity, alt_capacity, group, col_count, message_ref, sea_ref, left_ref, hot_ref, rows_ref, bound_ref):
    row_count = sea_ref.shape[0]
    devices = message_ref.shape[0]
    block = min(32, devices)
    members = block * 8
    octets = capacity // 8
    alt_octets = (alt_capacity + 7) // 8
    per_group = group // 8
    shift = col_count.bit_length() - 1
    col_iota = lax.broadcasted_iota(jnp.int32, (1, col_count), 1)
    row_iota = lax.broadcasted_iota(jnp.int32, (row_count, 1), 0)

    def chunk(index, start):
        return message_ref[index * block : (index + 1) * block, start : start + 8, :].reshape(
            members, LANES
        )

    def hot_of(cell):
        return jnp.where(((cell - 1) & (col_count - 1)) == col_iota, 1.0, 0.0).astype(BF)

    def rows_of(cell):
        return lax.shift_right_arithmetic(cell - 1, shift)

    sea = jnp.zeros((row_count, col_count), F32)
    count = 0
    for index in range(devices // block):
        tails = [chunk(index, capacity + 8 * part).T for part in range(per_group)]
        for octet in range(octets):
            table = chunk(index, 8 * octet)
            turned = table.T
            tail = tails[octet % per_group]
            begin = 32 * (octet // per_group)
            levels = jnp.concatenate([turned, tail[begin : begin + 32]], axis=0)
            high, low = split_two(levels)
            left_ref[count, :, 0:members] = high
            left_ref[count, :, members : 2 * members] = low
            hot = hot_of(table[:, 75:76].astype(jnp.int32))
            hot_ref[count, 0:members] = hot
            hot_ref[count, members : 2 * members] = hot
            rows = rows_of(turned[75:76].astype(jnp.int32))
            rows_ref[count] = jnp.broadcast_to(rows, (8, members))
            bound_ref[2 * count] = jnp.min(jnp.where(rows >= 0, rows, row_count))
            bound_ref[2 * count + 1] = jnp.max(rows)
            count += 1
            if octet >= alt_octets:
                continue
            alt_hot = hot_of(table[:, 77:78].astype(jnp.int32))
            alt_rows = rows_of(turned[77:78].astype(jnp.int32))
            weighted = jnp.where(alt_rows == row_iota, turned[76:77], 0.0)
            high, low = split_two(weighted)
            product = mm(jnp.concatenate([high, low], axis=0), alt_hot)
            sea = sea + product[:row_count] + product[row_count:]
    sea_ref[...] = sea


def half_forcing(is_upper, profile_ref, coast_refs, sea_ref, left_ref, hot_ref, rows_ref, bound_ref, outputs):
    state, edge_ref, cols_ref = outputs
    rows, _, col_count = state.shape
    count = left_ref.shape[0]
    first_row = jnp.where(is_upper, rows, 0)
    aligned = pl.multiple_of(first_row, 8)
    sea = sea_ref[pl.ds(aligned, rows), :]
    for start in range(0, col_count, LANES):
        profile = jnp.broadcast_to(profile_ref[...], (2 * PAD, LANES))
        for row in range(rows):
            state[row, :, start : start + LANES] = profile * sea[row : row + 1, start : start + LANES]
    span = 2

    def step(number, carry):
        here = rows_ref[number][0:1] - first_row
        least = jnp.maximum(bound_ref[2 * number] - first_row, 0)
        most = jnp.minimum(bound_ref[2 * number + 1] - first_row, rows - 1)

        def rows_step(start, inner):
            base = start * span
            pieces = []
            for offset in range(span):
                mask = jnp.where(here == base + offset, 1.0, 0.0).astype(BF)
                pieces.append(left_ref[number] * jnp.concatenate([mask, mask], axis=1))
            product = mm(jnp.concatenate(pieces, axis=0), hot_ref[number])
            for offset in range(span):
                state[base + offset] += product[2 * PAD * offset : 2 * PAD * (offset + 1)]
            return inner

        lax.fori_loop(least // span, (most + span) // span, rows_step, 0)
        return carry

    lax.fori_loop(0, count, step, 0)
    for kind, coast_ref in enumerate(coast_refs):
        coast = coast_ref[pl.ds(aligned, rows), :].astype(F32)
        for row in range(rows):
            state[row, LEVELS + kind : LEVELS + kind + 1, :] = coast[row : row + 1, :]
    write_edge(is_upper, state, edge_ref)


def half_shapes(row_count, col_count):
    return (
        jax.ShapeDtypeStruct((row_count // 2, 2 * PAD, col_count), F32),
        jax.ShapeDtypeStruct((2 * PAD, col_count), F32),
        jax.ShapeDtypeStruct((PAD, LANES), F32),
    )


def in_place(count):
    return [pl.BlockSpec(memory_space=pltpu.SMEM)] + [pl.BlockSpec(memory_space=pltpu.VMEM)] * count


def near_forcing(capacity, alt_capacity, group, flags, message, profile, coast):
    row_count, col_count = coast[0].shape
    devices = message.shape[0]
    members = min(32, devices) * 8
    chunks = capacity // 8 * (devices // min(32, devices))

    def kernel(flag_ref, message_ref, profile_ref, wet, north, east, *outs):
        prepare(capacity, alt_capacity, group, col_count, message_ref, *outs[3:])
        half_forcing(flag_ref[NEAR] > 0, profile_ref, (wet, north, east), *outs[3:], outs[:3])
        outs[2][...] = columns_of(NEAR, outs[0], jnp.zeros((PAD, LANES), F32))

    return pl.pallas_call(
        kernel,
        in_specs=in_place(5),
        out_shape=half_shapes(row_count, col_count)
        + (
            jax.ShapeDtypeStruct((row_count, col_count), F32),
            jax.ShapeDtypeStruct((chunks, 2 * PAD, 2 * members), BF),
            jax.ShapeDtypeStruct((chunks, 2 * members, col_count), BF),
            jax.ShapeDtypeStruct((chunks, 8, members), jnp.int32),
            jax.ShapeDtypeStruct((2 * chunks,), jnp.int32),
        ),
        out_specs=[pl.BlockSpec(memory_space=pltpu.VMEM)] * 7
        + [pl.BlockSpec(memory_space=pltpu.SMEM)],
        compiler_params=pltpu.CompilerParams(vmem_limit_bytes=30 * MIB),
        cost_estimate=pl.CostEstimate(
            flops=9_000_000_000, bytes_accessed=8_000_000, transcendentals=0
        ),
        name="forcing_near",
    )(flags, message, profile, *coast)


def far_forcing(flags, profile, coast, prepared, near_cols):
    row_count, col_count = coast[0].shape

    def kernel(flag_ref, profile_ref, wet, north, east, sea, left, hot, rows, bound, cols, *outs):
        half_forcing(
            flag_ref[FAR] > 0, profile_ref, (wet, north, east), sea, left, hot, rows, bound, outs
        )
        add_far_columns(cols, outs[0], outs[2])

    return pl.pallas_call(
        kernel,
        in_specs=in_place(8)
        + [pl.BlockSpec(memory_space=pltpu.SMEM), pl.BlockSpec(memory_space=pltpu.VMEM)],
        out_shape=half_shapes(row_count, col_count),
        compiler_params=pltpu.CompilerParams(vmem_limit_bytes=30 * MIB),
        cost_estimate=pl.CostEstimate(
            flops=4_000_000_000, bytes_accessed=8_000_000, transcendentals=0
        ),
        name="forcing_far",
    )(flags, profile, *coast, *prepared, near_cols)


def fold_row(row_ref, mirror_ref, piece, chunk, chunks, rows):
    index = jnp.broadcast_to(mirror_ref[0:1, piece(chunk)], (rows, LANES))
    return jnp.take_along_axis(row_ref[:, piece(chunks - 1 - chunk)], index, axis=1)


def weight_kernel(which, flag_ref, wet_ref, north_ref, east_ref, edge_in, west_in, east_in, mirror_ref, out_ref, fold_ref):
    row_count, col_count = wet_ref.shape
    rows = row_count // 2
    is_upper = flag_ref[which] > 0
    at = pl.multiple_of(jnp.where(is_upper, rows, 0), 8)
    wet = wet_ref[pl.ds(at, rows), :].astype(F32)
    north = north_ref[pl.ds(at, rows), :]
    east = east_ref[pl.ds(at, rows), :]
    chunks = col_count // LANES
    lane = lax.broadcasted_iota(jnp.int32, (1, col_count), 1)
    start = column_lane(which, rows, 0, 1, 0)
    west_cols = west_in[72:80, :].T[start : start + rows]
    start = column_lane(which, rows, 0, 0, 0)
    east_cols = east_in[72:80, :].T[start : start + rows]
    west_wet = jnp.where(lane == 0, west_cols[:, 3:4], pltpu.roll(wet, 1, 1))
    west_coef = jnp.where(lane == 0, west_cols[:, 5:6], pltpu.roll(east, 1, 1))
    east_wet = jnp.where(
        lane == col_count - 1, east_cols[:, 3:4], pltpu.roll(wet, col_count - 1, 1)
    )
    east_w = east * wet * east_wet
    west_w = west_coef * west_wet * wet

    def piece(c):
        return slice(c * LANES, (c + 1) * LANES)

    spare_ref = edge_in.at[72:80]
    if which == FAR:
        for c in range(chunks):
            fold_ref[:, piece(c)] = fold_row(spare_ref, mirror_ref, piece, c, chunks, 8)
    spare = spare_ref[...]
    last = rows - 1
    inner_wet = jnp.where(
        is_upper, wet_ref[rows - 1 : rows, :], wet_ref[rows : rows + 1, :]
    ).astype(F32)
    above = jnp.where(is_upper, spare[3:4], inner_wet)
    top_w = north[last:] * wet[last:] * above
    if which == FAR:
        fold = 0.5 * (north[last:] + fold_ref[4:5]) * wet[last:] * fold_ref[3:4]
        top_w = jnp.where(flag_ref[TOP] > 0, fold, top_w)
    below = jnp.where(is_upper, north_ref[rows - 1 : rows, :] * inner_wet, spare[4:5] * spare[3:4])
    between = north[:last] * wet[:last] * wet[1:]
    north_w = jnp.concatenate([between, top_w], axis=0)
    south_w = jnp.concatenate([below * wet[0:1], between], axis=0)
    center = 1.0 - (east_w + west_w + north_w + south_w)
    for kind, weight in enumerate((center, east_w, west_w, north_w, south_w)):
        for row in range(rows):
            out_ref[row, kind : kind + 1, :] = weight[row : row + 1]


def edge_weights(which, flags, coast, received, mirror):
    row_count, col_count = coast[0].shape

    def kernel(*refs):
        weight_kernel(which, *refs)

    return pl.pallas_call(
        kernel,
        in_specs=in_place(7),
        out_shape=jax.ShapeDtypeStruct((row_count // 2, 8, col_count), F32),
        scratch_shapes=[pltpu.VMEM((8, col_count), F32)],
        compiler_params=pltpu.CompilerParams(vmem_limit_bytes=16 * MIB),
        name="edge_weights",
    )(flags, *coast, *received, mirror)


def set_outer_rows(which, flag_ref, edge_in, inner, mirror_ref, south_ref, north_ref):
    levels, col_count = edge_in.shape
    is_upper = flag_ref[which] > 0
    is_top = flag_ref[TOP] > 0
    chunks = col_count // LANES

    def piece(c):
        return slice(c * LANES, (c + 1) * LANES)

    @pl.when(is_upper)
    def _():
        south_ref[...] = inner[...]

    @pl.when(jnp.logical_not(is_upper))
    def _():
        south_ref[...] = edge_in[...]
        north_ref[...] = inner[...]

    if which == NEAR:

        @pl.when(is_upper)
        def _():
            north_ref[...] = edge_in[...]

        return

    @pl.when(is_upper & jnp.logical_not(is_top))
    def _():
        north_ref[...] = edge_in[...]

    @pl.when(is_top)
    def _():
        for c in range(chunks):
            north_ref[:, piece(c)] = fold_row(edge_in, mirror_ref, piece, c, chunks, levels)


def mix_row(which, row, rows, field, at, state_ref, south_ref, north_ref, west_in, east_in, coef_ref, right_ref, slot):
    col_count = state_ref.shape[2]
    chunks = col_count // LANES
    lane = lax.broadcasted_iota(jnp.int32, (1, LANES), 1)
    levels = slice(at, at + PAD)

    def piece(chunk):
        return slice(chunk * LANES, (chunk + 1) * LANES)

    west_lane = column_lane(which, rows, field, 1, row)
    east_lane = column_lane(which, rows, field, 0, row)
    centers = [state_ref[row, levels, piece(c)] for c in range(chunks)]
    to_left = [pltpu.roll(c, LANES - 1, 1) for c in centers]
    to_right = [pltpu.roll(c, 1, 1) for c in centers]
    to_right.append(pltpu.roll(west_in[...], LANES - west_lane, 1))
    to_left.append(pltpu.roll(east_in[...], LANES - 1 - east_lane, 1))
    for c in range(chunks):
        south = state_ref[row - 1, levels, piece(c)] if row > 0 else south_ref[levels, piece(c)]
        if row < rows - 1:
            north = state_ref[row + 1, levels, piece(c)]
        else:
            north = north_ref[levels, piece(c)]
        east = jnp.where(lane == LANES - 1, to_left[c + 1], to_left[c])
        west = jnp.where(lane == 0, to_right[c - 1], to_right[c])

        def coef(kind):
            return coef_ref[row, kind : kind + 1, piece(c)]

        mixed = (
            coef(0) * centers[c]
            + coef(1) * east
            + coef(2) * west
            + coef(3) * north
            + coef(4) * south
        )
        high, low = split_two(mixed)
        right_ref[slot, 0:PAD, piece(c)] = high
        right_ref[slot, PAD : 2 * PAD, piece(c)] = low
        right_ref[slot, 2 * PAD : 3 * PAD, piece(c)] = high


def diffuse(which, flags, state, other, received, mirror, coef, matrix, *near_cols):
    rows, _, col_count = state.shape
    slots = 4

    def kernel(flag_ref, state_ref, other_ref, edge_in, west_in, east_in, mirror_ref, coef_ref, matrix_ref, *refs):
        out_ref, edge_ref, cols_ref, south_ref, north_ref, right_ref = refs[-6:]
        is_upper = flag_ref[which] > 0
        inner = other_ref.at[jnp.where(is_upper, rows - 1, 0)]
        set_outer_rows(which, flag_ref, edge_in, inner, mirror_ref, south_ref, north_ref)
        right_ref[:, 3 * PAD :, :] = jnp.zeros((slots, 16, col_count), BF)
        units = [(row, field) for row in range(rows) for field in range(2)]

        def product(number):
            row, field = units[number]
            result = mm(matrix_ref[field, row], right_ref[number % slots])
            out_ref[row, field * PAD : (field + 1) * PAD] = result

        for number, (row, field) in enumerate(units):
            mix_row(which, row, rows, field, field * PAD, state_ref, south_ref, north_ref, west_in, east_in, coef_ref, right_ref, number % slots)
            if number > 0:
                product(number - 1)
        product(len(units) - 1)
        write_edge(is_upper, out_ref, edge_ref)
        if which == NEAR:
            cols_ref[...] = columns_of(NEAR, out_ref, jnp.zeros((PAD, LANES), F32))
        else:
            add_far_columns(refs[0], out_ref, cols_ref)

    return pl.pallas_call(
        kernel,
        in_specs=in_place(8 + len(near_cols)),
        out_shape=half_shapes(2 * rows, col_count),
        scratch_shapes=[
            pltpu.VMEM((2 * PAD, col_count), F32),
            pltpu.VMEM((2 * PAD, col_count), F32),
            pltpu.VMEM((slots, 256, col_count), BF),
        ],
        compiler_params=pltpu.CompilerParams(vmem_limit_bytes=24 * MIB),
        cost_estimate=pl.CostEstimate(
            flops=3_000_000_000, bytes_accessed=8_000_000, transcendentals=0
        ),
        name="diffusion_" + ("near", "far")[which],
    )(flags, state, other, *received, mirror, coef, matrix, *near_cols)


def diffuse_last(which, flags, state, other, received, mirror, coef, matrix, mask, target):
    rows, _, col_count = state.shape
    slots = 4

    def kernel(flag_ref, state_ref, other_ref, edge_in, west_in, east_in, mirror_ref, coef_ref, matrix_ref, mask_ref, *refs):
        out_ref, south_ref, north_ref, right_ref = refs[-4:]
        field = pl.program_id(0)
        set_outer_rows(which, flag_ref, edge_in, other_ref.at[0], mirror_ref, south_ref, north_ref)
        right_ref[:, 3 * PAD :, :] = jnp.zeros((slots, 16, col_count), BF)
        wet = mask_ref[...].astype(F32)
        results = []

        def product(row):
            result = mm(matrix_ref[0, row], right_ref[row % slots])
            results.append(result * wet[row : row + 1])

        for row in range(rows):
            mix_row(which, row, rows, field, 0, state_ref, south_ref, north_ref, west_in, east_in, coef_ref, right_ref, row % slots)
            if row > 0:
                product(row - 1)
        product(rows - 1)
        out_ref[...] = jnp.swapaxes(jnp.stack(results), 0, 1)[:LEVELS]

    def whole(array):
        return pl.BlockSpec(array.shape, lambda f, flags: (0,) * len(array.shape))

    edge_in, west_in, east_in = received
    in_specs = [
        pl.BlockSpec((rows, PAD, col_count), lambda f, flags: (0, f, 0)),
        pl.BlockSpec((1, PAD, col_count), lambda f, flags: (flags[which] * (rows - 1), f, 0)),
        pl.BlockSpec((PAD, col_count), lambda f, flags: (f, 0)),
        whole(west_in),
        whole(east_in),
        whole(mirror),
        whole(coef),
        pl.BlockSpec((1, rows) + matrix.shape[2:], lambda f, flags: (f, 0, 0, 0)),
        pl.BlockSpec((rows, col_count), lambda f, flags: (flags[which], 0)),
    ]
    operands = [state, other, edge_in, west_in, east_in, mirror, coef, matrix, mask]
    aliases = {}
    if target is not None:
        in_specs.append(pl.BlockSpec(memory_space=pl.ANY))
        operands.append(target)
        aliases = {len(operands): 0}
    return pl.pallas_call(
        kernel,
        grid_spec=pltpu.PrefetchScalarGridSpec(
            num_scalar_prefetch=1,
            grid=(2,),
            in_specs=in_specs,
            out_specs=pl.BlockSpec((LEVELS, rows, col_count), lambda f, flags: (f, flags[which], 0)),
            scratch_shapes=[
                pltpu.VMEM((PAD, col_count), F32),
                pltpu.VMEM((PAD, col_count), F32),
                pltpu.VMEM((slots, 256, col_count), BF),
            ],
        ),
        out_shape=jax.ShapeDtypeStruct((2 * LEVELS, 2 * rows, col_count), F32),
        input_output_aliases=aliases,
        compiler_params=pltpu.CompilerParams(vmem_limit_bytes=28 * MIB),
        cost_estimate=pl.CostEstimate(
            flops=3_000_000_000, bytes_accessed=8_000_000, transcendentals=0
        ),
        name="diffusion_last",
    )(flags, *operands)


def mixing_matrices(vinv):
    turned = jnp.transpose(vinv, (1, 0, 3, 2))
    turned = jnp.pad(turned, ((0, 0), (0, 0), (0, PAD - LEVELS), (0, PAD - LEVELS)))
    high = lax.reduce_precision(turned, 8, 7)
    low = (turned - high).astype(BF)
    high = high.astype(BF)
    rest = jnp.zeros(high.shape[:3] + (256 - 3 * PAD,), BF)
    return jnp.concatenate([high, high, low, rest], axis=3)


def body(
    argo_value,
    argo_owner,
    argo_cell,
    alt_value,
    alt_owner,
    alt_cell,
    alt_profile,
    land_mask,
    coef_east,
    coef_north,
    mirror,
    vinv,
):
    row_count, col_count = land_mask.shape
    count_ja = lax.axis_size("ja")
    count_ia = lax.axis_size("ia")
    devices = count_ja * count_ia
    capacity = round_up(3 * argo_value.shape[0] // devices, 8)
    group = round_up(capacity // 4, 8)
    message = send_tables(
        devices,
        capacity,
        group,
        row_count,
        col_count,
        (
            argo_value.T,
            argo_owner.reshape(1, -1),
            argo_cell.reshape(1, -1),
            alt_value,
            alt_cell,
            alt_owner.reshape(1, -1),
        ),
    )
    message, ja_index = lax.optimization_barrier((message, lax.axis_index("ja")))
    message = lax.all_to_all(message, ("ja", "ia"), split_axis=0, concat_axis=0, tiled=True)

    ia_index = lax.axis_index("ia")
    is_top = (ja_index == count_ja - 1).astype(jnp.int32)
    parity = ja_index % 2
    flags = jnp.stack([1 - parity, parity, is_top]).astype(jnp.int32)
    fold_index = mirror - (count_ia - 1 - ia_index) * col_count
    mirror_lane = jnp.broadcast_to((fold_index % LANES)[None, :], (8, col_count))
    matrices = mixing_matrices(vinv)
    profile = jnp.pad(alt_profile.reshape(2, LEVELS, 1), ((0, 0), (0, PAD - LEVELS), (0, 0)))
    profile = profile.reshape(2 * PAD, 1)
    alt_capacity = max(2, 3 * alt_value.shape[0] // devices)
    coast = (land_mask, coef_north, coef_east)
    rows = row_count // 2
    lower = [matrices[:, :rows], matrices[:, rows:]]
    odd_device = parity == 1
    half_matrices = [
        jnp.where(odd_device, lower[0], lower[1]),
        jnp.where(odd_device, lower[1], lower[0]),
    ]

    ring_east = [(i, (i + 1) % count_ia) for i in range(count_ia)]
    ring_west = [((i + 1) % count_ia, i) for i in range(count_ia)]
    even_swap = []
    odd_swap = []
    for ja in range(count_ja):
        for ia in range(count_ia):
            here = ja * count_ia + ia
            even_swap.append((here, (ja ^ 1) * count_ia + ia))
            if ja == count_ja - 1:
                odd_swap.append((here, ja * count_ia + count_ia - 1 - ia))
            elif ja > 0:
                odd_swap.append((here, (((ja - 1) ^ 1) + 1) * count_ia + ia))
    swaps = (even_swap, odd_swap)

    def swap(which, edge):
        return lax.ppermute(edge, ("ja", "ia"), swaps[which])

    def pass_columns(cols):
        return lax.ppermute(cols, "ia", ring_east), lax.ppermute(cols, "ia", ring_west)

    near, near_edge, cols, *prepared = near_forcing(
        capacity, alt_capacity, group, flags, message, profile, coast
    )
    near_edge = swap(NEAR, near_edge)
    far, far_edge, cols = far_forcing(flags, profile, coast, prepared, cols)
    sides = pass_columns(cols)
    far_edge = swap(FAR, far_edge)
    near_coef = edge_weights(NEAR, flags, coast, (near_edge, *sides), mirror_lane)
    far_coef = None
    for sweep in range(ITERS - 1):
        new_near, new_edge, cols = diffuse(
            NEAR, flags, near, far, (near_edge, *sides), mirror_lane, near_coef, half_matrices[NEAR]
        )
        near_edge = swap(NEAR, new_edge)
        if far_coef is None:
            far_coef = edge_weights(FAR, flags, coast, (far_edge, *sides), mirror_lane)
        far, new_edge, cols = diffuse(
            FAR, flags, far, near, (far_edge, *sides), mirror_lane, far_coef, half_matrices[FAR], cols
        )
        near = new_near
        sides = pass_columns(cols)
        far_edge = swap(FAR, new_edge)
    output = diffuse_last(
        NEAR, flags, near, far, (near_edge, *sides), mirror_lane, near_coef, half_matrices[NEAR], land_mask, None
    )
    return diffuse_last(
        FAR, flags, far, near, (far_edge, *sides), mirror_lane, far_coef, half_matrices[FAR], land_mask, output
    )


def solution(mesh):
    in_specs = (
        P(("ja", "ia"), None),
        P(("ja", "ia"), None),
        P(("ja", "ia")),
        P(("ja", "ia")),
        P(("ja", "ia"), None),
        P(("ja", "ia")),
        P(),
        P("ja", "ia"),
        P("ja", "ia"),
        P("ja", "ia"),
        P("ia"),
        P("ja", None, None, None),
    )
    out_specs = P(None, "ja", "ia")
    return jax.shard_map(body, mesh=mesh, in_specs=in_specs, out_specs=out_specs, check_vma=False)
```

```python
import jax
import jax.numpy as jnp
from jax import lax
from jax.experimental import pallas as pl
from jax.experimental.pallas import tpu as pltpu
from jax.sharding import PartitionSpec as P

ITERS = 3
LEVELS = 75
PAD = 80
LANES = 128
NEAR, FAR, TOP = 0, 1, 2
BF = jnp.bfloat16
F32 = jnp.float32
MIB = 1024 * 1024


def round_up(value, unit):
    return (value + unit - 1) // unit * unit


def split_two(value):
    high = value.astype(BF)
    low = (value - high.astype(F32)).astype(BF)
    return high, low


def mm(left, right):
    return jnp.dot(left, right, preferred_element_type=F32)


def as_column(row):
    return jnp.broadcast_to(row, (8, row.shape[1])).T[:, 0:1]


def slot_ranks(owner_row, cell_row, devices, col_count, row_count, capacity, spread):
    count = owner_row.shape[1]
    owner = owner_row.astype(F32)
    inside = cell_row // col_count
    order = lax.broadcasted_iota(jnp.int32, (1, count), 1).astype(F32)
    key = (owner * float(row_count) + inside.astype(F32)) * float(count) + order
    key_col = as_column(key)
    device = lax.broadcasted_iota(jnp.int32, (devices, 1), 0)
    mine = device == owner_row
    totals = jnp.sum(jnp.where(mine, 1.0, 0.0), axis=1, keepdims=True)
    rank = -jnp.sum(jnp.where(device < owner_row, totals, 0.0), axis=0, keepdims=True)
    for start in range(0, count, 128):
        before = jnp.where(key_col[start : start + 128] < key, 1.0, 0.0)
        rank = rank + jnp.sum(before, axis=0, keepdims=True)
    if spread:
        total = jnp.sum(jnp.where(mine, totals, 0.0), axis=0, keepdims=True)
        offset = owner * 1024.0
        goal = (inside * capacity // row_count).astype(F32) - rank + offset
        goal_col = as_column(goal)
        shift = offset
        for start in range(0, count, 128):
            within = key_col[start : start + 128] <= key
            reached = jnp.where(within, goal_col[start : start + 128], 0.0)
            shift = jnp.maximum(shift, jnp.max(reached, axis=0, keepdims=True))
        rank = rank + jnp.minimum(shift - offset, float(capacity) - total)
    return rank


def table_kernel(
    devices,
    capacity,
    group,
    row_count,
    col_count,
    value_ref,
    owner_ref,
    cell_ref,
    alt_value_ref,
    alt_cell_ref,
    alt_owner_ref,
    message_ref,
    level_ref,
    side_ref,
    hi_ref,
    lo_ref,
    alt_all_ref,
    rank_hot_ref,
    alt_rank_hot_ref,
):
    index = pl.program_id(0)
    n_obs = owner_ref.shape[1]
    n_alt = alt_owner_ref.shape[1]

    @pl.when(index == 0)
    def _():
        slot = lax.broadcasted_iota(jnp.int32, (capacity, 1), 0).astype(F32)
        alt_cell = alt_cell_ref[...].reshape(1, n_alt)
        rank = slot_ranks(
            owner_ref[...], cell_ref[...], devices, col_count, row_count, capacity, True
        )
        rank_hot_ref[...] = jnp.where(slot == rank, 1.0, 0.0).astype(BF)
        rank = slot_ranks(
            alt_owner_ref[...], alt_cell, devices, col_count, row_count, capacity, False
        )
        alt_rank_hot_ref[...] = jnp.where(slot == rank, 1.0, 0.0).astype(BF)
        level_ref[...] = jnp.zeros(level_ref.shape, F32)
        level_ref[0:75, :] = value_ref[0:75, :]
        level_ref[75:76, :] = cell_ref[...].astype(F32) + 1.0
        level_ref[80:128, :] = value_ref[75:123, :]
        for lane_group in range(4):
            level_ref[128 + 32 * lane_group : 155 + 32 * lane_group, :] = value_ref[123:150, :]
        high, low = split_two(level_ref[...].T)
        hi_ref[...] = high
        lo_ref[...] = low
        side_ref[...] = jnp.zeros(side_ref.shape, F32)
        pair = jnp.concatenate(
            [alt_value_ref[...].reshape(1, n_alt), alt_cell.astype(F32) + 1.0], axis=0
        )
        pair_high = pair.astype(BF).astype(F32)
        side_ref[76:78, :] = pair_high
        side_ref[78:80, :] = pair - pair_high
        alt_all_ref[...] = side_ref[...].T.astype(BF)

    per_step = message_ref.shape[0]
    chosen = []
    chosen_alt = []
    for member in range(per_step):
        device = index * per_step + member
        mask = jnp.where(owner_ref[...] == device, 1.0, 0.0).astype(BF)
        chosen.append(rank_hot_ref[...] * mask)
        mask = jnp.where(alt_owner_ref[...] == device, 1.0, 0.0).astype(BF)
        chosen_alt.append(alt_rank_hot_ref[...] * mask)
    chosen = jnp.concatenate(chosen, axis=0)
    chosen_alt = jnp.concatenate(chosen_alt, axis=0)
    table = mm(chosen, hi_ref[...]) + mm(chosen, lo_ref[...])
    lane = lax.broadcasted_iota(jnp.int32, (1, LANES), 1)
    extra = mm(chosen_alt, alt_all_ref[...])
    extra = jnp.where(lane < 78, extra + pltpu.roll(extra, LANES - 2, 1), 0.0)
    extra = jnp.where(lane >= 76, extra, 0.0)
    first = table[:, :LANES] + extra
    message_ref[:, 0:capacity] = first.reshape(per_step, capacity, LANES)
    rest = table[:, LANES:].reshape(per_step, capacity, LANES)
    total = jnp.zeros((per_step, group, LANES), F32)
    for lane_group in range(4):
        low_slot = lane_group * group
        if low_slot >= capacity:
            continue
        piece = rest[:, low_slot : low_slot + group]
        here = (lane // 32 == lane_group).reshape(1, 1, LANES)
        total = jnp.where(here, piece, total)
    message_ref[:, capacity : capacity + group] = total


def send_tables(devices, capacity, group, row_count, col_count, operands):
    n_obs = operands[1].shape[1]
    n_alt = operands[5].shape[1]
    per_step = max(1, 768 // capacity)

    def kernel(*refs):
        table_kernel(devices, capacity, group, row_count, col_count, *refs)

    def whole(array):
        return pl.BlockSpec(array.shape, lambda s: (0,) * len(array.shape))

    return pl.pallas_call(
        kernel,
        grid=(devices // per_step,),
        in_specs=[whole(x) for x in operands],
        out_specs=pl.BlockSpec((per_step, capacity + group, LANES), lambda s: (s, 0, 0)),
        out_shape=jax.ShapeDtypeStruct((devices, capacity + group, LANES), F32),
        scratch_shapes=[
            pltpu.VMEM((2 * LANES, n_obs), F32),
            pltpu.VMEM((LANES, n_alt), F32),
            pltpu.VMEM((n_obs, 2 * LANES), BF),
            pltpu.VMEM((n_obs, 2 * LANES), BF),
            pltpu.VMEM((n_alt, LANES), BF),
            pltpu.VMEM((capacity, n_obs), BF),
            pltpu.VMEM((capacity, n_alt), BF),
        ],
        compiler_params=pltpu.CompilerParams(vmem_limit_bytes=56 * MIB),
        name="send_tables",
    )(*operands)


def column_lane(which, rows, field, east, row):
    return (4 * which + 2 * field + east) * rows + row


def columns_of(which, state_ref, cols):
    rows = state_ref.shape[0]
    lane = lax.broadcasted_iota(jnp.int32, (1, LANES), 1)
    for row in range(rows):
        for field in range(2):
            part = state_ref[row, field * PAD : (field + 1) * PAD, :]
            at = column_lane(which, rows, field, 0, row)
            cols = jnp.where(lane == at, pltpu.roll(part[:, :LANES], at, 1), cols)
            at = column_lane(which, rows, field, 1, row)
            cols = jnp.where(lane == at, pltpu.roll(part[:, -LANES:], at + 1, 1), cols)
    return cols


def add_far_columns(near_cols_ref, state_ref, cols_ref):
    cols_ref[...] = columns_of(FAR, state_ref, near_cols_ref[...])


def write_edge(is_upper, state_ref, edge_ref):
    edge_ref[...] = state_ref[jnp.where(is_upper, state_ref.shape[0] - 1, 0)]


def prepare(capacity, alt_capacity, group, col_count, message_ref, sea_ref, left_ref, hot_ref, rows_ref, bound_ref):
    row_count = sea_ref.shape[0]
    devices = message_ref.shape[0]
    block = min(32, devices)
    members = block * 8
    octets = capacity // 8
    alt_octets = (alt_capacity + 7) // 8
    per_group = group // 8
    shift = col_count.bit_length() - 1
    col_iota = lax.broadcasted_iota(jnp.int32, (1, col_count), 1)
    row_iota = lax.broadcasted_iota(jnp.int32, (row_count, 1), 0)

    def chunk(index, start):
        return message_ref[index * block : (index + 1) * block, start : start + 8, :].reshape(
            members, LANES
        )

    def hot_of(cell):
        return jnp.where(((cell - 1) & (col_count - 1)) == col_iota, 1.0, 0.0).astype(BF)

    def rows_of(cell):
        return lax.shift_right_arithmetic(cell - 1, shift)

    sea = jnp.zeros((row_count, col_count), F32)
    count = 0
    for index in range(devices // block):
        tails = [chunk(index, capacity + 8 * part).T for part in range(per_group)]
        for octet in range(octets):
            table = chunk(index, 8 * octet)
            turned = table.T
            tail = tails[octet % per_group]
            begin = 32 * (octet // per_group)
            levels = jnp.concatenate([turned, tail[begin : begin + 32]], axis=0)
            high, low = split_two(levels)
            left_ref[count, :, 0:members] = high
            left_ref[count, :, members : 2 * members] = low
            hot = hot_of(table[:, 75:76].astype(jnp.int32))
            hot_ref[count, 0:members] = hot
            hot_ref[count, members : 2 * members] = hot
            rows = rows_of(turned[75:76].astype(jnp.int32))
            rows_ref[count] = jnp.broadcast_to(rows, (8, members))
            bound_ref[2 * count] = jnp.min(jnp.where(rows >= 0, rows, row_count))
            bound_ref[2 * count + 1] = jnp.max(rows)
            count += 1
            if octet >= alt_octets:
                continue
            alt_hot = hot_of(table[:, 77:78].astype(jnp.int32))
            alt_rows = rows_of(turned[77:78].astype(jnp.int32))
            weighted = jnp.where(alt_rows == row_iota, turned[76:77], 0.0)
            high, low = split_two(weighted)
            product = mm(jnp.concatenate([high, low], axis=0), alt_hot)
            sea = sea + product[:row_count] + product[row_count:]
    sea_ref[...] = sea


def half_forcing(is_upper, profile_ref, coast_refs, sea_ref, left_ref, hot_ref, rows_ref, bound_ref, outputs):
    state, edge_ref, cols_ref = outputs
    rows, _, col_count = state.shape
    count = left_ref.shape[0]
    first_row = jnp.where(is_upper, rows, 0)
    aligned = pl.multiple_of(first_row, 8)
    sea = sea_ref[pl.ds(aligned, rows), :]
    for start in range(0, col_count, LANES):
        profile = jnp.broadcast_to(profile_ref[...], (2 * PAD, LANES))
        for row in range(rows):
            state[row, :, start : start + LANES] = profile * sea[row : row + 1, start : start + LANES]
    span = 2

    def step(number, carry):
        here = rows_ref[number][0:1] - first_row
        least = jnp.maximum(bound_ref[2 * number] - first_row, 0)
        most = jnp.minimum(bound_ref[2 * number + 1] - first_row, rows - 1)

        def rows_step(start, inner):
            base = start * span
            pieces = []
            for offset in range(span):
                mask = jnp.where(here == base + offset, 1.0, 0.0).astype(BF)
                pieces.append(left_ref[number] * jnp.concatenate([mask, mask], axis=1))
            product = mm(jnp.concatenate(pieces, axis=0), hot_ref[number])
            for offset in range(span):
                state[base + offset] += product[2 * PAD * offset : 2 * PAD * (offset + 1)]
            return inner

        lax.fori_loop(least // span, (most + span) // span, rows_step, 0)
        return carry

    lax.fori_loop(0, count, step, 0)
    for kind, coast_ref in enumerate(coast_refs):
        coast = coast_ref[pl.ds(aligned, rows), :].astype(F32)
        for row in range(rows):
            state[row, LEVELS + kind : LEVELS + kind + 1, :] = coast[row : row + 1, :]
    write_edge(is_upper, state, edge_ref)


def half_shapes(row_count, col_count):
    return (
        jax.ShapeDtypeStruct((row_count // 2, 2 * PAD, col_count), F32),
        jax.ShapeDtypeStruct((2 * PAD, col_count), F32),
        jax.ShapeDtypeStruct((PAD, LANES), F32),
    )


def in_place(count):
    return [pl.BlockSpec(memory_space=pltpu.SMEM)] + [pl.BlockSpec(memory_space=pltpu.VMEM)] * count


def near_forcing(capacity, alt_capacity, group, flags, message, profile, coast):
    row_count, col_count = coast[0].shape
    devices = message.shape[0]
    members = min(32, devices) * 8
    chunks = capacity // 8 * (devices // min(32, devices))

    def kernel(flag_ref, message_ref, profile_ref, wet, north, east, *outs):
        prepare(capacity, alt_capacity, group, col_count, message_ref, *outs[3:])
        half_forcing(flag_ref[NEAR] > 0, profile_ref, (wet, north, east), *outs[3:], outs[:3])
        outs[2][...] = columns_of(NEAR, outs[0], jnp.zeros((PAD, LANES), F32))

    return pl.pallas_call(
        kernel,
        in_specs=in_place(5),
        out_shape=half_shapes(row_count, col_count)
        + (
            jax.ShapeDtypeStruct((row_count, col_count), F32),
            jax.ShapeDtypeStruct((chunks, 2 * PAD, 2 * members), BF),
            jax.ShapeDtypeStruct((chunks, 2 * members, col_count), BF),
            jax.ShapeDtypeStruct((chunks, 8, members), jnp.int32),
            jax.ShapeDtypeStruct((2 * chunks,), jnp.int32),
        ),
        out_specs=[pl.BlockSpec(memory_space=pltpu.VMEM)] * 7
        + [pl.BlockSpec(memory_space=pltpu.SMEM)],
        compiler_params=pltpu.CompilerParams(vmem_limit_bytes=30 * MIB),
        cost_estimate=pl.CostEstimate(
            flops=9_000_000_000, bytes_accessed=8_000_000, transcendentals=0
        ),
        name="forcing_near",
    )(flags, message, profile, *coast)


def far_forcing(flags, profile, coast, prepared, near_cols):
    row_count, col_count = coast[0].shape

    def kernel(flag_ref, profile_ref, wet, north, east, sea, left, hot, rows, bound, cols, *outs):
        half_forcing(
            flag_ref[FAR] > 0, profile_ref, (wet, north, east), sea, left, hot, rows, bound, outs
        )
        add_far_columns(cols, outs[0], outs[2])

    return pl.pallas_call(
        kernel,
        in_specs=in_place(8)
        + [pl.BlockSpec(memory_space=pltpu.SMEM), pl.BlockSpec(memory_space=pltpu.VMEM)],
        out_shape=half_shapes(row_count, col_count),
        compiler_params=pltpu.CompilerParams(vmem_limit_bytes=30 * MIB),
        cost_estimate=pl.CostEstimate(
            flops=4_000_000_000, bytes_accessed=8_000_000, transcendentals=0
        ),
        name="forcing_far",
    )(flags, profile, *coast, *prepared, near_cols)


def fold_row(row_ref, mirror_ref, piece, chunk, chunks, rows):
    index = jnp.broadcast_to(mirror_ref[0:1, piece(chunk)], (rows, LANES))
    return jnp.take_along_axis(row_ref[:, piece(chunks - 1 - chunk)], index, axis=1)


def weight_kernel(which, flag_ref, wet_ref, north_ref, east_ref, edge_in, west_in, east_in, mirror_ref, out_ref, fold_ref):
    row_count, col_count = wet_ref.shape
    rows = row_count // 2
    is_upper = flag_ref[which] > 0
    at = pl.multiple_of(jnp.where(is_upper, rows, 0), 8)
    wet = wet_ref[pl.ds(at, rows), :].astype(F32)
    north = north_ref[pl.ds(at, rows), :]
    east = east_ref[pl.ds(at, rows), :]
    chunks = col_count // LANES
    lane = lax.broadcasted_iota(jnp.int32, (1, col_count), 1)
    start = column_lane(which, rows, 0, 1, 0)
    west_cols = west_in[72:80, :].T[start : start + rows]
    start = column_lane(which, rows, 0, 0, 0)
    east_cols = east_in[72:80, :].T[start : start + rows]
    west_wet = jnp.where(lane == 0, west_cols[:, 3:4], pltpu.roll(wet, 1, 1))
    west_coef = jnp.where(lane == 0, west_cols[:, 5:6], pltpu.roll(east, 1, 1))
    east_wet = jnp.where(
        lane == col_count - 1, east_cols[:, 3:4], pltpu.roll(wet, col_count - 1, 1)
    )
    east_w = east * wet * east_wet
    west_w = west_coef * west_wet * wet

    def piece(c):
        return slice(c * LANES, (c + 1) * LANES)

    spare_ref = edge_in.at[72:80]
    if which == FAR:
        for c in range(chunks):
            fold_ref[:, piece(c)] = fold_row(spare_ref, mirror_ref, piece, c, chunks, 8)
    spare = spare_ref[...]
    last = rows - 1
    inner_wet = jnp.where(
        is_upper, wet_ref[rows - 1 : rows, :], wet_ref[rows : rows + 1, :]
    ).astype(F32)
    above = jnp.where(is_upper, spare[3:4], inner_wet)
    top_w = north[last:] * wet[last:] * above
    if which == FAR:
        fold = 0.5 * (north[last:] + fold_ref[4:5]) * wet[last:] * fold_ref[3:4]
        top_w = jnp.where(flag_ref[TOP] > 0, fold, top_w)
    below = jnp.where(is_upper, north_ref[rows - 1 : rows, :] * inner_wet, spare[4:5] * spare[3:4])
    between = north[:last] * wet[:last] * wet[1:]
    north_w = jnp.concatenate([between, top_w], axis=0)
    south_w = jnp.concatenate([below * wet[0:1], between], axis=0)
    center = 1.0 - (east_w + west_w + north_w + south_w)
    for kind, weight in enumerate((center, east_w, west_w, north_w, south_w)):
        for row in range(rows):
            out_ref[row, kind : kind + 1, :] = weight[row : row + 1]


def edge_weights(which, flags, coast, received, mirror):
    row_count, col_count = coast[0].shape

    def kernel(*refs):
        weight_kernel(which, *refs)

    return pl.pallas_call(
        kernel,
        in_specs=in_place(7),
        out_shape=jax.ShapeDtypeStruct((row_count // 2, 8, col_count), F32),
        scratch_shapes=[pltpu.VMEM((8, col_count), F32)],
        compiler_params=pltpu.CompilerParams(vmem_limit_bytes=16 * MIB),
        name="edge_weights",
    )(flags, *coast, *received, mirror)


def set_outer_rows(which, flag_ref, edge_in, inner, mirror_ref, south_ref, north_ref):
    levels, col_count = edge_in.shape
    is_upper = flag_ref[which] > 0
    is_top = flag_ref[TOP] > 0
    chunks = col_count // LANES

    def piece(c):
        return slice(c * LANES, (c + 1) * LANES)

    @pl.when(is_upper)
    def _():
        south_ref[...] = inner[...]

    @pl.when(jnp.logical_not(is_upper))
    def _():
        south_ref[...] = edge_in[...]
        north_ref[...] = inner[...]

    if which == NEAR:

        @pl.when(is_upper)
        def _():
            north_ref[...] = edge_in[...]

        return

    @pl.when(is_upper & jnp.logical_not(is_top))
    def _():
        north_ref[...] = edge_in[...]

    @pl.when(is_top)
    def _():
        for c in range(chunks):
            north_ref[:, piece(c)] = fold_row(edge_in, mirror_ref, piece, c, chunks, levels)


def mix_row(which, row, rows, field, at, state_ref, south_ref, north_ref, west_in, east_in, coef_ref, right_ref, slot):
    col_count = state_ref.shape[2]
    chunks = col_count // LANES
    lane = lax.broadcasted_iota(jnp.int32, (1, LANES), 1)
    levels = slice(at, at + PAD)

    def piece(chunk):
        return slice(chunk * LANES, (chunk + 1) * LANES)

    west_lane = column_lane(which, rows, field, 1, row)
    east_lane = column_lane(which, rows, field, 0, row)
    centers = [state_ref[row, levels, piece(c)] for c in range(chunks)]
    to_left = [pltpu.roll(c, LANES - 1, 1) for c in centers]
    to_right = [pltpu.roll(c, 1, 1) for c in centers]
    to_right.append(pltpu.roll(west_in[...], LANES - west_lane, 1))
    to_left.append(pltpu.roll(east_in[...], LANES - 1 - east_lane, 1))
    for c in range(chunks):
        south = state_ref[row - 1, levels, piece(c)] if row > 0 else south_ref[levels, piece(c)]
        if row < rows - 1:
            north = state_ref[row + 1, levels, piece(c)]
        else:
            north = north_ref[levels, piece(c)]
        east = jnp.where(lane == LANES - 1, to_left[c + 1], to_left[c])
        west = jnp.where(lane == 0, to_right[c - 1], to_right[c])

        def coef(kind):
            return coef_ref[row, kind : kind + 1, piece(c)]

        mixed = (
            coef(0) * centers[c]
            + coef(1) * east
            + coef(2) * west
            + coef(3) * north
            + coef(4) * south
        )
        high, low = split_two(mixed)
        right_ref[slot, 0:PAD, piece(c)] = high
        right_ref[slot, PAD : 2 * PAD, piece(c)] = low
        right_ref[slot, 2 * PAD : 3 * PAD, piece(c)] = high


def diffuse(which, flags, state, other, received, mirror, coef, matrix, *near_cols):
    rows, _, col_count = state.shape
    slots = 4

    def kernel(flag_ref, state_ref, other_ref, edge_in, west_in, east_in, mirror_ref, coef_ref, matrix_ref, *refs):
        out_ref, edge_ref, cols_ref, south_ref, north_ref, right_ref = refs[-6:]
        is_upper = flag_ref[which] > 0
        inner = other_ref.at[jnp.where(is_upper, rows - 1, 0)]
        set_outer_rows(which, flag_ref, edge_in, inner, mirror_ref, south_ref, north_ref)
        right_ref[:, 3 * PAD :, :] = jnp.zeros((slots, 16, col_count), BF)
        units = [(row, field) for row in range(rows) for field in range(2)]

        def product(number):
            row, field = units[number]
            result = mm(matrix_ref[field, row], right_ref[number % slots])
            out_ref[row, field * PAD : (field + 1) * PAD] = result

        for number, (row, field) in enumerate(units):
            mix_row(which, row, rows, field, field * PAD, state_ref, south_ref, north_ref, west_in, east_in, coef_ref, right_ref, number % slots)
            if number > 0:
                product(number - 1)
        product(len(units) - 1)
        write_edge(is_upper, out_ref, edge_ref)
        if which == NEAR:
            cols_ref[...] = columns_of(NEAR, out_ref, jnp.zeros((PAD, LANES), F32))
        else:
            add_far_columns(refs[0], out_ref, cols_ref)

    return pl.pallas_call(
        kernel,
        in_specs=in_place(8 + len(near_cols)),
        out_shape=half_shapes(2 * rows, col_count),
        scratch_shapes=[
            pltpu.VMEM((2 * PAD, col_count), F32),
            pltpu.VMEM((2 * PAD, col_count), F32),
            pltpu.VMEM((slots, 256, col_count), BF),
        ],
        compiler_params=pltpu.CompilerParams(vmem_limit_bytes=24 * MIB),
        cost_estimate=pl.CostEstimate(
            flops=3_000_000_000, bytes_accessed=8_000_000, transcendentals=0
        ),
        name="diffusion_" + ("near", "far")[which],
    )(flags, state, other, *received, mirror, coef, matrix, *near_cols)


def diffuse_last(which, flags, state, other, received, mirror, coef, matrix, mask, target):
    rows, _, col_count = state.shape
    slots = 4

    def kernel(flag_ref, state_ref, other_ref, edge_in, west_in, east_in, mirror_ref, coef_ref, matrix_ref, mask_ref, *refs):
        out_ref, south_ref, north_ref, right_ref, stage_ref, sems = refs[-6:]
        is_upper = flag_ref[which] > 0
        inner = other_ref.at[jnp.where(is_upper, rows - 1, 0)]
        set_outer_rows(which, flag_ref, edge_in, inner, mirror_ref, south_ref, north_ref)
        right_ref[:, 3 * PAD :, :] = jnp.zeros((slots, 16, col_count), BF)
        at = pl.multiple_of(jnp.where(is_upper, rows, 0), 8)
        wet = mask_ref[pl.ds(at, rows), :].astype(F32)
        copies = []
        for field in range(2):
            results = []

            def product(row):
                result = mm(matrix_ref[field, row], right_ref[row % slots])
                results.append(result * wet[row : row + 1])

            for row in range(rows):
                mix_row(which, row, rows, field, field * PAD, state_ref, south_ref, north_ref, west_in, east_in, coef_ref, right_ref, row % slots)
                if row > 0:
                    product(row - 1)
            product(rows - 1)
            stage_ref[field] = jnp.swapaxes(jnp.stack(results), 0, 1)[:LEVELS]
            copy = pltpu.make_async_copy(
                stage_ref.at[field],
                out_ref.at[pl.ds(field * LEVELS, LEVELS), pl.ds(at, rows), :],
                sems.at[field],
            )
            copy.start()
            copies.append(copy)
        for copy in copies:
            copy.wait()

    in_specs = in_place(9)
    operands = [flags, state, other, *received, mirror, coef, matrix, mask]
    aliases = {}
    if target is not None:
        in_specs.append(pl.BlockSpec(memory_space=pl.ANY))
        aliases = {len(operands): 0}
        operands.append(target)
    return pl.pallas_call(
        kernel,
        in_specs=in_specs,
        out_specs=pl.BlockSpec(memory_space=pl.ANY),
        out_shape=jax.ShapeDtypeStruct((2 * LEVELS, 2 * rows, col_count), F32),
        input_output_aliases=aliases,
        scratch_shapes=[
            pltpu.VMEM((2 * PAD, col_count), F32),
            pltpu.VMEM((2 * PAD, col_count), F32),
            pltpu.VMEM((slots, 256, col_count), BF),
            pltpu.VMEM((2, LEVELS, rows, col_count), F32),
            pltpu.SemaphoreType.DMA((2,)),
        ],
        compiler_params=pltpu.CompilerParams(vmem_limit_bytes=24 * MIB),
        cost_estimate=pl.CostEstimate(
            flops=3_000_000_000, bytes_accessed=8_000_000, transcendentals=0
        ),
        name="diffusion_last",
    )(*operands)


def mixing_matrices(vinv):
    turned = jnp.transpose(vinv, (1, 0, 3, 2))
    turned = jnp.pad(turned, ((0, 0), (0, 0), (0, PAD - LEVELS), (0, PAD - LEVELS)))
    high = lax.reduce_precision(turned, 8, 7)
    low = (turned - high).astype(BF)
    high = high.astype(BF)
    rest = jnp.zeros(high.shape[:3] + (256 - 3 * PAD,), BF)
    return jnp.concatenate([high, high, low, rest], axis=3)


def body(
    argo_value,
    argo_owner,
    argo_cell,
    alt_value,
    alt_owner,
    alt_cell,
    alt_profile,
    land_mask,
    coef_east,
    coef_north,
    mirror,
    vinv,
):
    row_count, col_count = land_mask.shape
    count_ja = lax.axis_size("ja")
    count_ia = lax.axis_size("ia")
    devices = count_ja * count_ia
    capacity = round_up(3 * argo_value.shape[0] // devices, 8)
    group = round_up(capacity // 4, 8)
    message = send_tables(
        devices,
        capacity,
        group,
        row_count,
        col_count,
        (
            argo_value.T,
            argo_owner.reshape(1, -1),
            argo_cell.reshape(1, -1),
            alt_value,
            alt_cell,
            alt_owner.reshape(1, -1),
        ),
    )
    message, ja_index = lax.optimization_barrier((message, lax.axis_index("ja")))
    message = lax.all_to_all(message, ("ja", "ia"), split_axis=0, concat_axis=0, tiled=True)

    ia_index = lax.axis_index("ia")
    is_top = (ja_index == count_ja - 1).astype(jnp.int32)
    parity = ja_index % 2
    flags = jnp.stack([1 - parity, parity, is_top]).astype(jnp.int32)
    fold_index = mirror - (count_ia - 1 - ia_index) * col_count
    mirror_lane = jnp.broadcast_to((fold_index % LANES)[None, :], (8, col_count))
    matrices = mixing_matrices(vinv)
    profile = jnp.pad(alt_profile.reshape(2, LEVELS, 1), ((0, 0), (0, PAD - LEVELS), (0, 0)))
    profile = profile.reshape(2 * PAD, 1)
    alt_capacity = max(2, 3 * alt_value.shape[0] // devices)
    coast = (land_mask, coef_north, coef_east)
    rows = row_count // 2
    lower = [matrices[:, :rows], matrices[:, rows:]]
    odd_device = parity == 1
    half_matrices = [
        jnp.where(odd_device, lower[0], lower[1]),
        jnp.where(odd_device, lower[1], lower[0]),
    ]

    ring_east = [(i, (i + 1) % count_ia) for i in range(count_ia)]
    ring_west = [((i + 1) % count_ia, i) for i in range(count_ia)]
    even_swap = []
    odd_swap = []
    for ja in range(count_ja):
        for ia in range(count_ia):
            here = ja * count_ia + ia
            even_swap.append((here, (ja ^ 1) * count_ia + ia))
            if ja == count_ja - 1:
                odd_swap.append((here, ja * count_ia + count_ia - 1 - ia))
            elif ja > 0:
                odd_swap.append((here, (((ja - 1) ^ 1) + 1) * count_ia + ia))
    swaps = (even_swap, odd_swap)

    def swap(which, edge):
        return lax.ppermute(edge, ("ja", "ia"), swaps[which])

    def columns_then_rows(cols, edge):
        from_west = lax.ppermute(cols, "ia", ring_east)
        from_east = lax.ppermute(cols, "ia", ring_west)
        from_west, from_east, edge = lax.optimization_barrier((from_west, from_east, edge))
        return (from_west, from_east), swap(FAR, edge)

    near, near_edge, cols, *prepared = near_forcing(
        capacity, alt_capacity, group, flags, message, profile, coast
    )
    near_edge = swap(NEAR, near_edge)
    far, far_edge, cols = far_forcing(flags, profile, coast, prepared, cols)
    sides, far_edge = columns_then_rows(cols, far_edge)
    near_coef = edge_weights(NEAR, flags, coast, (near_edge, *sides), mirror_lane)
    far_coef = None
    for sweep in range(ITERS - 1):
        new_near, new_edge, cols = diffuse(
            NEAR, flags, near, far, (near_edge, *sides), mirror_lane, near_coef, half_matrices[NEAR]
        )
        near_edge = swap(NEAR, new_edge)
        if far_coef is None:
            far_coef = edge_weights(FAR, flags, coast, (far_edge, *sides), mirror_lane)
        far, new_edge, cols = diffuse(
            FAR, flags, far, near, (far_edge, *sides), mirror_lane, far_coef, half_matrices[FAR], cols
        )
        near = new_near
        sides, far_edge = columns_then_rows(cols, new_edge)
    output = diffuse_last(
        NEAR, flags, near, far, (near_edge, *sides), mirror_lane, near_coef, half_matrices[NEAR], land_mask, None
    )
    return diffuse_last(
        FAR, flags, far, near, (far_edge, *sides), mirror_lane, far_coef, half_matrices[FAR], land_mask, output
    )


def solution(mesh):
    in_specs = (
        P(("ja", "ia"), None),
        P(("ja", "ia"), None),
        P(("ja", "ia")),
        P(("ja", "ia")),
        P(("ja", "ia"), None),
        P(("ja", "ia")),
        P(),
        P("ja", "ia"),
        P("ja", "ia"),
        P("ja", "ia"),
        P("ia"),
        P("ja", None, None, None),
    )
    out_specs = P(None, "ja", "ia")
    return jax.shard_map(body, mesh=mesh, in_specs=in_specs, out_specs=out_specs, check_vma=False)
```

```python
import jax
import jax.numpy as jnp
from jax import lax
from jax.experimental import pallas as pl
from jax.experimental.pallas import tpu as pltpu
from jax.sharding import PartitionSpec as P

ITERS = 3
LEVELS = 75
PAD = 80
LANES = 128
NEAR, FAR, TOP = 0, 1, 2
BF = jnp.bfloat16
F32 = jnp.float32
MIB = 1024 * 1024


def round_up(value, unit):
    return (value + unit - 1) // unit * unit


def split_two(value):
    high = value.astype(BF)
    low = (value - high.astype(F32)).astype(BF)
    return high, low


def mm(left, right):
    return jnp.dot(left, right, preferred_element_type=F32)


def as_column(row):
    return jnp.broadcast_to(row, (8, row.shape[1])).T[:, 0:1]


def slot_ranks(owner_row, cell_row, devices, col_count, row_count, capacity, spread):
    count = owner_row.shape[1]
    owner = owner_row.astype(F32)
    inside = cell_row // col_count
    order = lax.broadcasted_iota(jnp.int32, (1, count), 1).astype(F32)
    key = (owner * float(row_count) + inside.astype(F32)) * float(count) + order
    key_col = as_column(key)
    device = lax.broadcasted_iota(jnp.int32, (devices, 1), 0)
    mine = device == owner_row
    totals = jnp.sum(jnp.where(mine, 1.0, 0.0), axis=1, keepdims=True)
    rank = -jnp.sum(jnp.where(device < owner_row, totals, 0.0), axis=0, keepdims=True)
    for start in range(0, count, 128):
        before = jnp.where(key_col[start : start + 128] < key, 1.0, 0.0)
        rank = rank + jnp.sum(before, axis=0, keepdims=True)
    if spread:
        total = jnp.sum(jnp.where(mine, totals, 0.0), axis=0, keepdims=True)
        offset = owner * 1024.0
        goal = (inside * capacity // row_count).astype(F32) - rank + offset
        goal_col = as_column(goal)
        shift = offset
        for start in range(0, count, 128):
            within = key_col[start : start + 128] <= key
            reached = jnp.where(within, goal_col[start : start + 128], 0.0)
            shift = jnp.maximum(shift, jnp.max(reached, axis=0, keepdims=True))
        rank = rank + jnp.minimum(shift - offset, float(capacity) - total)
    return rank


def table_kernel(
    devices,
    capacity,
    group,
    row_count,
    col_count,
    value_ref,
    owner_ref,
    cell_ref,
    alt_value_ref,
    alt_cell_ref,
    alt_owner_ref,
    message_ref,
    level_ref,
    side_ref,
    hi_ref,
    lo_ref,
    alt_all_ref,
    rank_hot_ref,
    alt_rank_hot_ref,
):
    index = pl.program_id(0)
    n_obs = owner_ref.shape[1]
    n_alt = alt_owner_ref.shape[1]

    @pl.when(index == 0)
    def _():
        slot = lax.broadcasted_iota(jnp.int32, (capacity, 1), 0).astype(F32)
        alt_cell = alt_cell_ref[...].reshape(1, n_alt)
        rank = slot_ranks(
            owner_ref[...], cell_ref[...], devices, col_count, row_count, capacity, True
        )
        rank_hot_ref[...] = jnp.where(slot == rank, 1.0, 0.0).astype(BF)
        rank = slot_ranks(
            alt_owner_ref[...], alt_cell, devices, col_count, row_count, capacity, False
        )
        alt_rank_hot_ref[...] = jnp.where(slot == rank, 1.0, 0.0).astype(BF)
        level_ref[...] = jnp.zeros(level_ref.shape, F32)
        level_ref[0:75, :] = value_ref[0:75, :]
        level_ref[75:76, :] = cell_ref[...].astype(F32) + 1.0
        level_ref[80:128, :] = value_ref[75:123, :]
        for lane_group in range(4):
            level_ref[128 + 32 * lane_group : 155 + 32 * lane_group, :] = value_ref[123:150, :]
        high, low = split_two(level_ref[...].T)
        hi_ref[...] = high
        lo_ref[...] = low
        side_ref[...] = jnp.zeros(side_ref.shape, F32)
        pair = jnp.concatenate(
            [alt_value_ref[...].reshape(1, n_alt), alt_cell.astype(F32) + 1.0], axis=0
        )
        pair_high = pair.astype(BF).astype(F32)
        side_ref[76:78, :] = pair_high
        side_ref[78:80, :] = pair - pair_high
        alt_all_ref[...] = side_ref[...].T.astype(BF)

    per_step = message_ref.shape[0]
    chosen = []
    chosen_alt = []
    for member in range(per_step):
        device = index * per_step + member
        mask = jnp.where(owner_ref[...] == device, 1.0, 0.0).astype(BF)
        chosen.append(rank_hot_ref[...] * mask)
        mask = jnp.where(alt_owner_ref[...] == device, 1.0, 0.0).astype(BF)
        chosen_alt.append(alt_rank_hot_ref[...] * mask)
    chosen = jnp.concatenate(chosen, axis=0)
    chosen_alt = jnp.concatenate(chosen_alt, axis=0)
    table = mm(chosen, hi_ref[...]) + mm(chosen, lo_ref[...])
    lane = lax.broadcasted_iota(jnp.int32, (1, LANES), 1)
    extra = mm(chosen_alt, alt_all_ref[...])
    extra = jnp.where(lane < 78, extra + pltpu.roll(extra, LANES - 2, 1), 0.0)
    extra = jnp.where(lane >= 76, extra, 0.0)
    first = table[:, :LANES] + extra
    message_ref[:, 0:capacity] = first.reshape(per_step, capacity, LANES)
    rest = table[:, LANES:].reshape(per_step, capacity, LANES)
    total = jnp.zeros((per_step, group, LANES), F32)
    for lane_group in range(4):
        low_slot = lane_group * group
        if low_slot >= capacity:
            continue
        piece = rest[:, low_slot : low_slot + group]
        here = (lane // 32 == lane_group).reshape(1, 1, LANES)
        total = jnp.where(here, piece, total)
    message_ref[:, capacity : capacity + group] = total


def send_tables(devices, capacity, group, row_count, col_count, operands):
    n_obs = operands[1].shape[1]
    n_alt = operands[5].shape[1]
    per_step = max(1, 768 // capacity)

    def kernel(*refs):
        table_kernel(devices, capacity, group, row_count, col_count, *refs)

    def whole(array):
        return pl.BlockSpec(array.shape, lambda s: (0,) * len(array.shape))

    return pl.pallas_call(
        kernel,
        grid=(devices // per_step,),
        in_specs=[whole(x) for x in operands],
        out_specs=pl.BlockSpec((per_step, capacity + group, LANES), lambda s: (s, 0, 0)),
        out_shape=jax.ShapeDtypeStruct((devices, capacity + group, LANES), F32),
        scratch_shapes=[
            pltpu.VMEM((2 * LANES, n_obs), F32),
            pltpu.VMEM((LANES, n_alt), F32),
            pltpu.VMEM((n_obs, 2 * LANES), BF),
            pltpu.VMEM((n_obs, 2 * LANES), BF),
            pltpu.VMEM((n_alt, LANES), BF),
            pltpu.VMEM((capacity, n_obs), BF),
            pltpu.VMEM((capacity, n_alt), BF),
        ],
        compiler_params=pltpu.CompilerParams(vmem_limit_bytes=56 * MIB),
        name="send_tables",
    )(*operands)


def column_lane(which, rows, field, east, row):
    return (4 * which + 2 * field + east) * rows + row


def columns_of(which, state_ref, cols):
    rows = state_ref.shape[0]
    lane = lax.broadcasted_iota(jnp.int32, (1, LANES), 1)
    for row in range(rows):
        for field in range(2):
            part = state_ref[row, field * PAD : (field + 1) * PAD, :]
            at = column_lane(which, rows, field, 0, row)
            cols = jnp.where(lane == at, pltpu.roll(part[:, :LANES], at, 1), cols)
            at = column_lane(which, rows, field, 1, row)
            cols = jnp.where(lane == at, pltpu.roll(part[:, -LANES:], at + 1, 1), cols)
    return cols


def add_far_columns(near_cols_ref, state_ref, cols_ref):
    cols_ref[...] = columns_of(FAR, state_ref, near_cols_ref[...])


def write_edge(is_upper, state_ref, edge_ref):
    edge_ref[...] = state_ref[jnp.where(is_upper, state_ref.shape[0] - 1, 0)]


def prepare(capacity, alt_capacity, group, col_count, message_ref, sea_ref, left_ref, hot_ref, rows_ref, bound_ref):
    row_count = sea_ref.shape[0]
    devices = message_ref.shape[0]
    block = min(32, devices)
    members = block * 8
    octets = capacity // 8
    alt_octets = (alt_capacity + 7) // 8
    per_group = group // 8
    shift = col_count.bit_length() - 1
    col_iota = lax.broadcasted_iota(jnp.int32, (1, col_count), 1)
    row_iota = lax.broadcasted_iota(jnp.int32, (row_count, 1), 0)

    def chunk(index, start):
        return message_ref[index * block : (index + 1) * block, start : start + 8, :].reshape(
            members, LANES
        )

    def hot_of(cell):
        return jnp.where(((cell - 1) & (col_count - 1)) == col_iota, 1.0, 0.0).astype(BF)

    def rows_of(cell):
        return lax.shift_right_arithmetic(cell - 1, shift)

    sea = jnp.zeros((row_count, col_count), F32)
    count = 0
    for index in range(devices // block):
        tails = [chunk(index, capacity + 8 * part).T for part in range(per_group)]
        for octet in range(octets):
            table = chunk(index, 8 * octet)
            turned = table.T
            tail = tails[octet % per_group]
            begin = 32 * (octet // per_group)
            levels = jnp.concatenate([turned, tail[begin : begin + 32]], axis=0)
            high, low = split_two(levels)
            left_ref[count, :, 0:members] = high
            left_ref[count, :, members : 2 * members] = low
            hot = hot_of(table[:, 75:76].astype(jnp.int32))
            hot_ref[count] = hot
            rows = rows_of(turned[75:76].astype(jnp.int32))
            rows_ref[count] = jnp.broadcast_to(rows, (8, members))
            bound_ref[2 * count] = jnp.min(jnp.where(rows >= 0, rows, row_count))
            bound_ref[2 * count + 1] = jnp.max(rows)
            count += 1
            if octet >= alt_octets:
                continue
            alt_hot = hot_of(table[:, 77:78].astype(jnp.int32))
            alt_rows = rows_of(turned[77:78].astype(jnp.int32))
            weighted = jnp.where(alt_rows == row_iota, turned[76:77], 0.0)
            high, low = split_two(weighted)
            product = mm(jnp.concatenate([high, low], axis=0), alt_hot)
            sea = sea + product[:row_count] + product[row_count:]
    sea_ref[...] = sea


def chosen_rows(number, row, span, left_ref, hot_ref, rows_ref):
    here = rows_ref[number][0:1]
    pieces = []
    for offset in range(span):
        mask = jnp.where(here == row + offset, 1.0, 0.0).astype(BF)
        pieces.append(left_ref[number] * jnp.concatenate([mask, mask], axis=1))
    hot = hot_ref[number]
    return mm(jnp.concatenate(pieces, axis=0), jnp.concatenate([hot, hot], axis=0))


def outer_forcing(row, is_upper, profile_ref, coast_refs, sea_ref, left_ref, hot_ref, rows_ref, bound_ref, edge_ref):
    row_count, col_count = sea_ref.shape
    last = row_count - 1
    profile = jnp.broadcast_to(profile_ref[...], (2 * PAD, LANES))
    sea = jnp.where(is_upper, sea_ref[last : last + 1, :], sea_ref[0:1, :])
    for start in range(0, col_count, LANES):
        edge_ref[:, start : start + LANES] = profile * sea[:, start : start + LANES]

    def step(number, carry):
        @pl.when((bound_ref[2 * number] <= row) & (row <= bound_ref[2 * number + 1]))
        def _():
            edge_ref[...] += chosen_rows(number, row, 1, left_ref, hot_ref, rows_ref)

        return carry

    lax.fori_loop(0, left_ref.shape[0], step, 0)
    for kind, coast_ref in enumerate(coast_refs):
        coast = jnp.where(is_upper, coast_ref[last : last + 1, :], coast_ref[0:1, :])
        edge_ref[LEVELS + kind : LEVELS + kind + 1, :] = coast.astype(F32)


def half_forcing(is_upper, profile_ref, coast_refs, sea_ref, left_ref, hot_ref, rows_ref, bound_ref, state):
    rows, _, col_count = state.shape
    first_row = jnp.where(is_upper, rows, 0)
    aligned = pl.multiple_of(first_row, 8)
    sea = sea_ref[pl.ds(aligned, rows), :]
    for start in range(0, col_count, LANES):
        profile = jnp.broadcast_to(profile_ref[...], (2 * PAD, LANES))
        for row in range(rows):
            state[row, :, start : start + LANES] = profile * sea[row : row + 1, start : start + LANES]
    span = 2

    def step(number, carry):
        least = jnp.maximum(bound_ref[2 * number] - first_row, 0)
        most = jnp.minimum(bound_ref[2 * number + 1] - first_row, rows - 1)

        def rows_step(start, inner):
            base = start * span
            product = chosen_rows(number, first_row + base, span, left_ref, hot_ref, rows_ref)
            for offset in range(span):
                state[base + offset] += product[2 * PAD * offset : 2 * PAD * (offset + 1)]
            return inner

        lax.fori_loop(least // span, (most + span) // span, rows_step, 0)
        return carry

    lax.fori_loop(0, left_ref.shape[0], step, 0)
    for kind, coast_ref in enumerate(coast_refs):
        coast = coast_ref[pl.ds(aligned, rows), :].astype(F32)
        for row in range(rows):
            state[row, LEVELS + kind : LEVELS + kind + 1, :] = coast[row : row + 1, :]


def half_shapes(row_count, col_count):
    return (
        jax.ShapeDtypeStruct((row_count // 2, 2 * PAD, col_count), F32),
        jax.ShapeDtypeStruct((2 * PAD, col_count), F32),
        jax.ShapeDtypeStruct((PAD, LANES), F32),
    )


def in_place(count):
    return [pl.BlockSpec(memory_space=pltpu.SMEM)] + [pl.BlockSpec(memory_space=pltpu.VMEM)] * count


def first_forcing(capacity, alt_capacity, group, flags, message, profile, coast):
    row_count, col_count = coast[0].shape
    devices = message.shape[0]
    members = min(32, devices) * 8
    chunks = capacity // 8 * (devices // min(32, devices))

    def kernel(flag_ref, message_ref, profile_ref, wet, north, east, edge_ref, *outs):
        prepare(capacity, alt_capacity, group, col_count, message_ref, *outs)
        is_upper = flag_ref[NEAR] > 0
        row = jnp.where(is_upper, row_count - 1, 0)
        outer_forcing(row, is_upper, profile_ref, (wet, north, east), *outs, edge_ref)

    return pl.pallas_call(
        kernel,
        in_specs=in_place(5),
        out_shape=(
            half_shapes(row_count, col_count)[1],
            jax.ShapeDtypeStruct((row_count, col_count), F32),
            jax.ShapeDtypeStruct((chunks, 2 * PAD, 2 * members), BF),
            jax.ShapeDtypeStruct((chunks, members, col_count), BF),
            jax.ShapeDtypeStruct((chunks, 8, members), jnp.int32),
            jax.ShapeDtypeStruct((2 * chunks,), jnp.int32),
        ),
        out_specs=[pl.BlockSpec(memory_space=pltpu.VMEM)] * 5
        + [pl.BlockSpec(memory_space=pltpu.SMEM)],
        compiler_params=pltpu.CompilerParams(vmem_limit_bytes=24 * MIB),
        cost_estimate=pl.CostEstimate(
            flops=6_000_000_000, bytes_accessed=8_000_000, transcendentals=0
        ),
        name="forcing_first",
    )(flags, message, profile, *coast)


def rest_forcing(flags, profile, coast, prepared):
    row_count, col_count = coast[0].shape

    def kernel(flag_ref, profile_ref, wet, north, east, sea, left, hot, rows, bound, near, far, edge_ref, cols_ref):
        coast_refs = (wet, north, east)
        operands = (sea, left, hot, rows, bound)
        half_forcing(flag_ref[FAR] > 0, profile_ref, coast_refs, *operands, far)
        half_forcing(flag_ref[NEAR] > 0, profile_ref, coast_refs, *operands, near)
        write_edge(flag_ref[FAR] > 0, far, edge_ref)
        cols = columns_of(NEAR, near, jnp.zeros((PAD, LANES), F32))
        cols_ref[...] = columns_of(FAR, far, cols)

    state, edge, cols = half_shapes(row_count, col_count)
    return pl.pallas_call(
        kernel,
        in_specs=in_place(8) + [pl.BlockSpec(memory_space=pltpu.SMEM)],
        out_shape=(state, state, edge, cols),
        compiler_params=pltpu.CompilerParams(vmem_limit_bytes=20 * MIB),
        cost_estimate=pl.CostEstimate(
            flops=6_000_000_000, bytes_accessed=8_000_000, transcendentals=0
        ),
        name="forcing_rest",
    )(flags, profile, *coast, *prepared)


def fold_row(row_ref, mirror_ref, piece, chunk, chunks, rows):
    index = jnp.broadcast_to(mirror_ref[0:1, piece(chunk)], (rows, LANES))
    return jnp.take_along_axis(row_ref[:, piece(chunks - 1 - chunk)], index, axis=1)


def weight_kernel(which, flag_ref, wet_ref, north_ref, east_ref, edge_in, west_in, east_in, mirror_ref, out_ref, fold_ref):
    row_count, col_count = wet_ref.shape
    rows = row_count // 2
    is_upper = flag_ref[which] > 0
    at = pl.multiple_of(jnp.where(is_upper, rows, 0), 8)
    wet = wet_ref[pl.ds(at, rows), :].astype(F32)
    north = north_ref[pl.ds(at, rows), :]
    east = east_ref[pl.ds(at, rows), :]
    chunks = col_count // LANES
    lane = lax.broadcasted_iota(jnp.int32, (1, col_count), 1)
    start = column_lane(which, rows, 0, 1, 0)
    west_cols = west_in[72:80, :].T[start : start + rows]
    start = column_lane(which, rows, 0, 0, 0)
    east_cols = east_in[72:80, :].T[start : start + rows]
    west_wet = jnp.where(lane == 0, west_cols[:, 3:4], pltpu.roll(wet, 1, 1))
    west_coef = jnp.where(lane == 0, west_cols[:, 5:6], pltpu.roll(east, 1, 1))
    east_wet = jnp.where(
        lane == col_count - 1, east_cols[:, 3:4], pltpu.roll(wet, col_count - 1, 1)
    )
    east_w = east * wet * east_wet
    west_w = west_coef * west_wet * wet

    def piece(c):
        return slice(c * LANES, (c + 1) * LANES)

    spare_ref = edge_in.at[72:80]
    if which == FAR:
        for c in range(chunks):
            fold_ref[:, piece(c)] = fold_row(spare_ref, mirror_ref, piece, c, chunks, 8)
    spare = spare_ref[...]
    last = rows - 1
    inner_wet = jnp.where(
        is_upper, wet_ref[rows - 1 : rows, :], wet_ref[rows : rows + 1, :]
    ).astype(F32)
    above = jnp.where(is_upper, spare[3:4], inner_wet)
    top_w = north[last:] * wet[last:] * above
    if which == FAR:
        fold = 0.5 * (north[last:] + fold_ref[4:5]) * wet[last:] * fold_ref[3:4]
        top_w = jnp.where(flag_ref[TOP] > 0, fold, top_w)
    below = jnp.where(is_upper, north_ref[rows - 1 : rows, :] * inner_wet, spare[4:5] * spare[3:4])
    between = north[:last] * wet[:last] * wet[1:]
    north_w = jnp.concatenate([between, top_w], axis=0)
    south_w = jnp.concatenate([below * wet[0:1], between], axis=0)
    center = 1.0 - (east_w + west_w + north_w + south_w)
    for kind, weight in enumerate((center, east_w, west_w, north_w, south_w)):
        for row in range(rows):
            out_ref[row, kind : kind + 1, :] = weight[row : row + 1]


def edge_weights(which, flags, coast, received, mirror):
    row_count, col_count = coast[0].shape

    def kernel(*refs):
        weight_kernel(which, *refs)

    return pl.pallas_call(
        kernel,
        in_specs=in_place(7),
        out_shape=jax.ShapeDtypeStruct((row_count // 2, 8, col_count), F32),
        scratch_shapes=[pltpu.VMEM((8, col_count), F32)],
        compiler_params=pltpu.CompilerParams(vmem_limit_bytes=16 * MIB),
        name="edge_weights",
    )(flags, *coast, *received, mirror)


def set_outer_rows(which, flag_ref, edge_in, inner, mirror_ref, south_ref, north_ref):
    levels, col_count = edge_in.shape
    is_upper = flag_ref[which] > 0
    is_top = flag_ref[TOP] > 0
    chunks = col_count // LANES

    def piece(c):
        return slice(c * LANES, (c + 1) * LANES)

    @pl.when(is_upper)
    def _():
        south_ref[...] = inner[...]

    @pl.when(jnp.logical_not(is_upper))
    def _():
        south_ref[...] = edge_in[...]
        north_ref[...] = inner[...]

    if which == NEAR:

        @pl.when(is_upper)
        def _():
            north_ref[...] = edge_in[...]

        return

    @pl.when(is_upper & jnp.logical_not(is_top))
    def _():
        north_ref[...] = edge_in[...]

    @pl.when(is_top)
    def _():
        for c in range(chunks):
            north_ref[:, piece(c)] = fold_row(edge_in, mirror_ref, piece, c, chunks, levels)


def mix_row(which, row, rows, field, at, state_ref, south_ref, north_ref, west_in, east_in, coef_ref, right_ref, slot):
    col_count = state_ref.shape[2]
    chunks = col_count // LANES
    lane = lax.broadcasted_iota(jnp.int32, (1, LANES), 1)
    levels = slice(at, at + PAD)

    def piece(chunk):
        return slice(chunk * LANES, (chunk + 1) * LANES)

    west_lane = column_lane(which, rows, field, 1, row)
    east_lane = column_lane(which, rows, field, 0, row)
    centers = [state_ref[row, levels, piece(c)] for c in range(chunks)]
    to_left = [pltpu.roll(c, LANES - 1, 1) for c in centers]
    to_right = [pltpu.roll(c, 1, 1) for c in centers]
    to_right.append(pltpu.roll(west_in[...], LANES - west_lane, 1))
    to_left.append(pltpu.roll(east_in[...], LANES - 1 - east_lane, 1))
    for c in range(chunks):
        south = state_ref[row - 1, levels, piece(c)] if row > 0 else south_ref[levels, piece(c)]
        if row < rows - 1:
            north = state_ref[row + 1, levels, piece(c)]
        else:
            north = north_ref[levels, piece(c)]
        east = jnp.where(lane == LANES - 1, to_left[c + 1], to_left[c])
        west = jnp.where(lane == 0, to_right[c - 1], to_right[c])

        def coef(kind):
            return coef_ref[row, kind : kind + 1, piece(c)]

        mixed = (
            coef(0) * centers[c]
            + coef(1) * east
            + coef(2) * west
            + coef(3) * north
            + coef(4) * south
        )
        high, low = split_two(mixed)
        right_ref[slot, 0:PAD, piece(c)] = high
        right_ref[slot, PAD : 2 * PAD, piece(c)] = low
        right_ref[slot, 2 * PAD : 3 * PAD, piece(c)] = high


def diffuse(which, flags, state, other, received, mirror, coef, matrix, *near_cols):
    rows, _, col_count = state.shape
    slots = 4

    def kernel(flag_ref, state_ref, other_ref, edge_in, west_in, east_in, mirror_ref, coef_ref, matrix_ref, *refs):
        out_ref, edge_ref, cols_ref, south_ref, north_ref, right_ref = refs[-6:]
        is_upper = flag_ref[which] > 0
        inner = other_ref.at[jnp.where(is_upper, rows - 1, 0)]
        set_outer_rows(which, flag_ref, edge_in, inner, mirror_ref, south_ref, north_ref)
        right_ref[:, 3 * PAD :, :] = jnp.zeros((slots, 16, col_count), BF)
        units = [(row, field) for row in range(rows) for field in range(2)]

        def product(number):
            row, field = units[number]
            result = mm(matrix_ref[field, row], right_ref[number % slots])
            out_ref[row, field * PAD : (field + 1) * PAD] = result

        for number, (row, field) in enumerate(units):
            mix_row(which, row, rows, field, field * PAD, state_ref, south_ref, north_ref, west_in, east_in, coef_ref, right_ref, number % slots)
            if number > 0:
                product(number - 1)
        product(len(units) - 1)
        write_edge(is_upper, out_ref, edge_ref)
        if which == NEAR:
            cols_ref[...] = columns_of(NEAR, out_ref, jnp.zeros((PAD, LANES), F32))
        else:
            add_far_columns(refs[0], out_ref, cols_ref)

    return pl.pallas_call(
        kernel,
        in_specs=in_place(8 + len(near_cols)),
        out_shape=half_shapes(2 * rows, col_count),
        scratch_shapes=[
            pltpu.VMEM((2 * PAD, col_count), F32),
            pltpu.VMEM((2 * PAD, col_count), F32),
            pltpu.VMEM((slots, 256, col_count), BF),
        ],
        compiler_params=pltpu.CompilerParams(vmem_limit_bytes=16 * MIB),
        cost_estimate=pl.CostEstimate(
            flops=3_000_000_000, bytes_accessed=8_000_000, transcendentals=0
        ),
        name="diffusion_" + ("near", "far")[which],
    )(flags, state, other, *received, mirror, coef, matrix, *near_cols)


def diffuse_last(which, flags, state, other, received, mirror, coef, matrix, mask, target):
    rows, _, col_count = state.shape
    slots = 4

    def kernel(flag_ref, state_ref, other_ref, edge_in, west_in, east_in, mirror_ref, coef_ref, matrix_ref, mask_ref, *refs):
        out_ref, south_ref, north_ref, right_ref = refs[-4:]
        field = pl.program_id(0)
        set_outer_rows(which, flag_ref, edge_in, other_ref.at[0], mirror_ref, south_ref, north_ref)
        right_ref[:, 3 * PAD :, :] = jnp.zeros((slots, 16, col_count), BF)
        wet = mask_ref[...].astype(F32)
        results = []

        def product(row):
            result = mm(matrix_ref[0, row], right_ref[row % slots])
            results.append(result * wet[row : row + 1])

        for row in range(rows):
            mix_row(which, row, rows, field, 0, state_ref, south_ref, north_ref, west_in, east_in, coef_ref, right_ref, row % slots)
            if row > 0:
                product(row - 1)
        product(rows - 1)
        out_ref[...] = jnp.swapaxes(jnp.stack(results), 0, 1)[:LEVELS]

    def whole(array):
        return pl.BlockSpec(array.shape, lambda f, flags: (0,) * len(array.shape))

    edge_in, west_in, east_in = received
    in_specs = [
        pl.BlockSpec((rows, PAD, col_count), lambda f, flags: (0, f, 0)),
        pl.BlockSpec((1, PAD, col_count), lambda f, flags: (flags[which] * (rows - 1), f, 0)),
        pl.BlockSpec((PAD, col_count), lambda f, flags: (f, 0)),
        whole(west_in),
        whole(east_in),
        whole(mirror),
        whole(coef),
        pl.BlockSpec((1, rows) + matrix.shape[2:], lambda f, flags: (f, 0, 0, 0)),
        pl.BlockSpec((rows, col_count), lambda f, flags: (flags[which], 0)),
    ]
    operands = [state, other, edge_in, west_in, east_in, mirror, coef, matrix, mask]
    aliases = {}
    if target is not None:
        in_specs.append(pl.BlockSpec(memory_space=pl.ANY))
        operands.append(target)
        aliases = {len(operands): 0}
    return pl.pallas_call(
        kernel,
        grid_spec=pltpu.PrefetchScalarGridSpec(
            num_scalar_prefetch=1,
            grid=(2,),
            in_specs=in_specs,
            out_specs=pl.BlockSpec((LEVELS, rows, col_count), lambda f, flags: (f, flags[which], 0)),
            scratch_shapes=[
                pltpu.VMEM((PAD, col_count), F32),
                pltpu.VMEM((PAD, col_count), F32),
                pltpu.VMEM((slots, 256, col_count), BF),
            ],
        ),
        out_shape=jax.ShapeDtypeStruct((2 * LEVELS, 2 * rows, col_count), F32),
        input_output_aliases=aliases,
        compiler_params=pltpu.CompilerParams(vmem_limit_bytes=20 * MIB),
        cost_estimate=pl.CostEstimate(
            flops=3_000_000_000, bytes_accessed=8_000_000, transcendentals=0
        ),
        name="diffusion_last",
    )(flags, *operands)


def mixing_matrices(vinv):
    turned = jnp.transpose(vinv, (1, 0, 3, 2))
    turned = jnp.pad(turned, ((0, 0), (0, 0), (0, PAD - LEVELS), (0, PAD - LEVELS)))
    high = lax.reduce_precision(turned, 8, 7)
    low = (turned - high).astype(BF)
    high = high.astype(BF)
    rest = jnp.zeros(high.shape[:3] + (256 - 3 * PAD,), BF)
    return jnp.concatenate([high, high, low, rest], axis=3)


def body(
    argo_value,
    argo_owner,
    argo_cell,
    alt_value,
    alt_owner,
    alt_cell,
    alt_profile,
    land_mask,
    coef_east,
    coef_north,
    mirror,
    vinv,
):
    row_count, col_count = land_mask.shape
    count_ja = lax.axis_size("ja")
    count_ia = lax.axis_size("ia")
    devices = count_ja * count_ia
    capacity = round_up(3 * argo_value.shape[0] // devices, 8)
    group = round_up(capacity // 4, 8)
    message = send_tables(
        devices,
        capacity,
        group,
        row_count,
        col_count,
        (
            argo_value.T,
            argo_owner.reshape(1, -1),
            argo_cell.reshape(1, -1),
            alt_value,
            alt_cell,
            alt_owner.reshape(1, -1),
        ),
    )
    message, ja_index = lax.optimization_barrier((message, lax.axis_index("ja")))
    message = lax.all_to_all(message, ("ja", "ia"), split_axis=0, concat_axis=0, tiled=True)

    ia_index = lax.axis_index("ia")
    is_top = (ja_index == count_ja - 1).astype(jnp.int32)
    parity = ja_index % 2
    flags = jnp.stack([1 - parity, parity, is_top]).astype(jnp.int32)
    fold_index = mirror - (count_ia - 1 - ia_index) * col_count
    mirror_lane = jnp.broadcast_to((fold_index % LANES)[None, :], (8, col_count))
    matrices = mixing_matrices(vinv)
    profile = jnp.pad(alt_profile.reshape(2, LEVELS, 1), ((0, 0), (0, PAD - LEVELS), (0, 0)))
    profile = profile.reshape(2 * PAD, 1)
    alt_capacity = max(2, 3 * alt_value.shape[0] // devices)
    coast = (land_mask, coef_north, coef_east)
    rows = row_count // 2
    lower = [matrices[:, :rows], matrices[:, rows:]]
    odd_device = parity == 1
    half_matrices = [
        jnp.where(odd_device, lower[0], lower[1]),
        jnp.where(odd_device, lower[1], lower[0]),
    ]

    ring_east = [(i, (i + 1) % count_ia) for i in range(count_ia)]
    ring_west = [((i + 1) % count_ia, i) for i in range(count_ia)]
    even_swap = []
    odd_swap = []
    for ja in range(count_ja):
        for ia in range(count_ia):
            here = ja * count_ia + ia
            even_swap.append((here, (ja ^ 1) * count_ia + ia))
            if ja == count_ja - 1:
                odd_swap.append((here, ja * count_ia + count_ia - 1 - ia))
            elif ja > 0:
                odd_swap.append((here, (((ja - 1) ^ 1) + 1) * count_ia + ia))
    swaps = (even_swap, odd_swap)

    def swap(which, edge):
        return lax.ppermute(edge, ("ja", "ia"), swaps[which])

    def pass_columns(cols):
        return lax.ppermute(cols, "ia", ring_east), lax.ppermute(cols, "ia", ring_west)

    near_edge, *prepared = first_forcing(
        capacity, alt_capacity, group, flags, message, profile, coast
    )
    near_edge = swap(NEAR, near_edge)
    near, far, far_edge, cols = rest_forcing(flags, profile, coast, prepared)
    sides = pass_columns(cols)
    far_edge = swap(FAR, far_edge)
    near_coef = edge_weights(NEAR, flags, coast, (near_edge, *sides), mirror_lane)
    far_coef = None
    for sweep in range(ITERS - 1):
        new_near, new_edge, cols = diffuse(
            NEAR, flags, near, far, (near_edge, *sides), mirror_lane, near_coef, half_matrices[NEAR]
        )
        near_edge = swap(NEAR, new_edge)
        if far_coef is None:
            far_coef = edge_weights(FAR, flags, coast, (far_edge, *sides), mirror_lane)
        far, new_edge, cols = diffuse(
            FAR, flags, far, near, (far_edge, *sides), mirror_lane, far_coef, half_matrices[FAR], cols
        )
        near = new_near
        *sides, new_edge = lax.optimization_barrier((*pass_columns(cols), new_edge))
        far_edge = swap(FAR, new_edge)
    output = diffuse_last(
        NEAR, flags, near, far, (near_edge, *sides), mirror_lane, near_coef, half_matrices[NEAR], land_mask, None
    )
    return diffuse_last(
        FAR, flags, far, near, (far_edge, *sides), mirror_lane, far_coef, half_matrices[FAR], land_mask, output
    )


def solution(mesh):
    in_specs = (
        P(("ja", "ia"), None),
        P(("ja", "ia"), None),
        P(("ja", "ia")),
        P(("ja", "ia")),
        P(("ja", "ia"), None),
        P(("ja", "ia")),
        P(),
        P("ja", "ia"),
        P("ja", "ia"),
        P("ja", "ia"),
        P("ia"),
        P("ja", None, None, None),
    )
    out_specs = P(None, "ja", "ia")
    return jax.shard_map(body, mesh=mesh, in_specs=in_specs, out_specs=out_specs, check_vma=False)
```

```python
import jax
import jax.numpy as jnp
from jax import lax
from jax.experimental import pallas as pl
from jax.experimental.pallas import tpu as pltpu
from jax.sharding import PartitionSpec as P

ITERS = 3
LEVELS = 75
PAD = 80
LANES = 128
NEAR, FAR, TOP = 0, 1, 2
BF = jnp.bfloat16
F32 = jnp.float32
MIB = 1024 * 1024


def round_up(value, unit):
    return (value + unit - 1) // unit * unit


def split_two(value):
    high = value.astype(BF)
    low = (value - high.astype(F32)).astype(BF)
    return high, low


def mm(left, right):
    return jnp.dot(left, right, preferred_element_type=F32)


def as_column(row):
    return jnp.broadcast_to(row, (8, row.shape[1])).T[:, 0:1]


def slot_ranks(owner_row, cell_row, devices, col_count, row_count, capacity, spread):
    count = owner_row.shape[1]
    owner = owner_row.astype(F32)
    inside = cell_row // col_count
    order = lax.broadcasted_iota(jnp.int32, (1, count), 1).astype(F32)
    key = (owner * float(row_count) + inside.astype(F32)) * float(count) + order
    key_col = as_column(key)
    device = lax.broadcasted_iota(jnp.int32, (devices, 1), 0)
    mine = device == owner_row
    totals = jnp.sum(jnp.where(mine, 1.0, 0.0), axis=1, keepdims=True)
    rank = -jnp.sum(jnp.where(device < owner_row, totals, 0.0), axis=0, keepdims=True)
    for start in range(0, count, 128):
        before = jnp.where(key_col[start : start + 128] < key, 1.0, 0.0)
        rank = rank + jnp.sum(before, axis=0, keepdims=True)
    if spread:
        total = jnp.sum(jnp.where(mine, totals, 0.0), axis=0, keepdims=True)
        offset = owner * 1024.0
        goal = (inside * capacity // row_count).astype(F32) - rank + offset
        goal_col = as_column(goal)
        shift = offset
        for start in range(0, count, 128):
            within = key_col[start : start + 128] <= key
            reached = jnp.where(within, goal_col[start : start + 128], 0.0)
            shift = jnp.maximum(shift, jnp.max(reached, axis=0, keepdims=True))
        rank = rank + jnp.minimum(shift - offset, float(capacity) - total)
    return rank


def table_kernel(
    devices,
    capacity,
    group,
    row_count,
    col_count,
    value_ref,
    owner_ref,
    cell_ref,
    alt_value_ref,
    alt_cell_ref,
    alt_owner_ref,
    message_ref,
    level_ref,
    side_ref,
    hi_ref,
    lo_ref,
    alt_all_ref,
    rank_hot_ref,
    alt_rank_hot_ref,
):
    index = pl.program_id(0)
    n_obs = owner_ref.shape[1]
    n_alt = alt_owner_ref.shape[1]

    @pl.when(index == 0)
    def _():
        slot = lax.broadcasted_iota(jnp.int32, (capacity, 1), 0).astype(F32)
        alt_cell = alt_cell_ref[...].reshape(1, n_alt)
        rank = slot_ranks(
            owner_ref[...], cell_ref[...], devices, col_count, row_count, capacity, True
        )
        rank_hot_ref[...] = jnp.where(slot == rank, 1.0, 0.0).astype(BF)
        rank = slot_ranks(
            alt_owner_ref[...], alt_cell, devices, col_count, row_count, capacity, False
        )
        alt_rank_hot_ref[...] = jnp.where(slot == rank, 1.0, 0.0).astype(BF)
        level_ref[...] = jnp.zeros(level_ref.shape, F32)
        level_ref[0:75, :] = value_ref[0:75, :]
        level_ref[75:76, :] = cell_ref[...].astype(F32) + 1.0
        level_ref[80:128, :] = value_ref[75:123, :]
        for lane_group in range(4):
            level_ref[128 + 32 * lane_group : 155 + 32 * lane_group, :] = value_ref[123:150, :]
        high, low = split_two(level_ref[...].T)
        hi_ref[...] = high
        lo_ref[...] = low
        side_ref[...] = jnp.zeros(side_ref.shape, F32)
        pair = jnp.concatenate(
            [alt_value_ref[...].reshape(1, n_alt), alt_cell.astype(F32) + 1.0], axis=0
        )
        pair_high = pair.astype(BF).astype(F32)
        side_ref[76:78, :] = pair_high
        side_ref[78:80, :] = pair - pair_high
        alt_all_ref[...] = side_ref[...].T.astype(BF)

    per_step = message_ref.shape[0]
    chosen = []
    chosen_alt = []
    for member in range(per_step):
        device = index * per_step + member
        mask = jnp.where(owner_ref[...] == device, 1.0, 0.0).astype(BF)
        chosen.append(rank_hot_ref[...] * mask)
        mask = jnp.where(alt_owner_ref[...] == device, 1.0, 0.0).astype(BF)
        chosen_alt.append(alt_rank_hot_ref[...] * mask)
    chosen = jnp.concatenate(chosen, axis=0)
    chosen_alt = jnp.concatenate(chosen_alt, axis=0)
    table = mm(chosen, hi_ref[...]) + mm(chosen, lo_ref[...])
    lane = lax.broadcasted_iota(jnp.int32, (1, LANES), 1)
    extra = mm(chosen_alt, alt_all_ref[...])
    extra = jnp.where(lane < 78, extra + pltpu.roll(extra, LANES - 2, 1), 0.0)
    extra = jnp.where(lane >= 76, extra, 0.0)
    first = table[:, :LANES] + extra
    message_ref[:, 0:capacity] = first.reshape(per_step, capacity, LANES)
    rest = table[:, LANES:].reshape(per_step, capacity, LANES)
    total = jnp.zeros((per_step, group, LANES), F32)
    for lane_group in range(4):
        low_slot = lane_group * group
        if low_slot >= capacity:
            continue
        piece = rest[:, low_slot : low_slot + group]
        here = (lane // 32 == lane_group).reshape(1, 1, LANES)
        total = jnp.where(here, piece, total)
    message_ref[:, capacity : capacity + group] = total


def send_tables(devices, capacity, group, row_count, col_count, operands):
    n_obs = operands[1].shape[1]
    n_alt = operands[5].shape[1]
    per_step = max(1, 768 // capacity)

    def kernel(*refs):
        table_kernel(devices, capacity, group, row_count, col_count, *refs)

    def whole(array):
        return pl.BlockSpec(array.shape, lambda s: (0,) * len(array.shape))

    return pl.pallas_call(
        kernel,
        grid=(devices // per_step,),
        in_specs=[whole(x) for x in operands],
        out_specs=pl.BlockSpec((per_step, capacity + group, LANES), lambda s: (s, 0, 0)),
        out_shape=jax.ShapeDtypeStruct((devices, capacity + group, LANES), F32),
        scratch_shapes=[
            pltpu.VMEM((2 * LANES, n_obs), F32),
            pltpu.VMEM((LANES, n_alt), F32),
            pltpu.VMEM((n_obs, 2 * LANES), BF),
            pltpu.VMEM((n_obs, 2 * LANES), BF),
            pltpu.VMEM((n_alt, LANES), BF),
            pltpu.VMEM((capacity, n_obs), BF),
            pltpu.VMEM((capacity, n_alt), BF),
        ],
        compiler_params=pltpu.CompilerParams(vmem_limit_bytes=56 * MIB),
        name="send_tables",
    )(*operands)


def column_lane(which, rows, field, east, row):
    return (4 * which + 2 * field + east) * rows + row


def columns_of(which, state_ref, cols):
    rows = state_ref.shape[0]
    lane = lax.broadcasted_iota(jnp.int32, (1, LANES), 1)
    for row in range(rows):
        for field in range(2):
            part = state_ref[row, field * PAD : (field + 1) * PAD, :]
            at = column_lane(which, rows, field, 0, row)
            cols = jnp.where(lane == at, pltpu.roll(part[:, :LANES], at, 1), cols)
            at = column_lane(which, rows, field, 1, row)
            cols = jnp.where(lane == at, pltpu.roll(part[:, -LANES:], at + 1, 1), cols)
    return cols


def write_edge(is_upper, state_ref, edge_ref):
    edge_ref[...] = state_ref[jnp.where(is_upper, state_ref.shape[0] - 1, 0)]


def prepare(capacity, alt_capacity, group, col_count, message_ref, sea_ref, left_ref, hot_ref, rows_ref, bound_ref):
    row_count = sea_ref.shape[0]
    devices = message_ref.shape[0]
    block = min(32, devices)
    members = block * 8
    octets = capacity // 8
    alt_octets = (alt_capacity + 7) // 8
    per_group = group // 8
    shift = col_count.bit_length() - 1
    col_iota = lax.broadcasted_iota(jnp.int32, (1, col_count), 1)
    row_iota = lax.broadcasted_iota(jnp.int32, (row_count, 1), 0)

    def chunk(index, start):
        return message_ref[index * block : (index + 1) * block, start : start + 8, :].reshape(
            members, LANES
        )

    def hot_of(cell):
        return jnp.where(((cell - 1) & (col_count - 1)) == col_iota, 1.0, 0.0).astype(BF)

    def rows_of(cell):
        return lax.shift_right_arithmetic(cell - 1, shift)

    sea = jnp.zeros((row_count, col_count), F32)
    count = 0
    for index in range(devices // block):
        tails = [chunk(index, capacity + 8 * part).T for part in range(per_group)]
        for octet in range(octets):
            table = chunk(index, 8 * octet)
            turned = table.T
            tail = tails[octet % per_group]
            begin = 32 * (octet // per_group)
            levels = jnp.concatenate([turned, tail[begin : begin + 32]], axis=0)
            high, low = split_two(levels)
            left_ref[count, :, 0:members] = high
            left_ref[count, :, members : 2 * members] = low
            hot = hot_of(table[:, 75:76].astype(jnp.int32))
            hot_ref[count] = hot
            rows = rows_of(turned[75:76].astype(jnp.int32))
            rows_ref[count] = jnp.broadcast_to(rows, (8, members))
            bound_ref[2 * count] = jnp.min(jnp.where(rows >= 0, rows, row_count))
            bound_ref[2 * count + 1] = jnp.max(rows)
            count += 1
            if octet >= alt_octets:
                continue
            alt_hot = hot_of(table[:, 77:78].astype(jnp.int32))
            alt_rows = rows_of(turned[77:78].astype(jnp.int32))
            weighted = jnp.where(alt_rows == row_iota, turned[76:77], 0.0)
            high, low = split_two(weighted)
            product = mm(jnp.concatenate([high, low], axis=0), alt_hot)
            sea = sea + product[:row_count] + product[row_count:]
    sea_ref[...] = sea


def chosen_rows(number, row, span, left_ref, hot_ref, rows_ref):
    here = rows_ref[number][0:1]
    pieces = []
    for offset in range(span):
        mask = jnp.where(here == row + offset, 1.0, 0.0).astype(BF)
        pieces.append(left_ref[number] * jnp.concatenate([mask, mask], axis=1))
    hot = hot_ref[number]
    return mm(jnp.concatenate(pieces, axis=0), jnp.concatenate([hot, hot], axis=0))


def outer_forcing(row, is_upper, profile_ref, coast_refs, sea_ref, left_ref, hot_ref, rows_ref, bound_ref, edge_ref):
    row_count, col_count = sea_ref.shape
    last = row_count - 1
    profile = jnp.broadcast_to(profile_ref[...], (2 * PAD, LANES))
    sea = jnp.where(is_upper, sea_ref[last : last + 1, :], sea_ref[0:1, :])
    for start in range(0, col_count, LANES):
        edge_ref[:, start : start + LANES] = profile * sea[:, start : start + LANES]

    def step(number, carry):
        @pl.when((bound_ref[2 * number] <= row) & (row <= bound_ref[2 * number + 1]))
        def _():
            edge_ref[...] += chosen_rows(number, row, 1, left_ref, hot_ref, rows_ref)

        return carry

    lax.fori_loop(0, left_ref.shape[0], step, 0)
    for kind, coast_ref in enumerate(coast_refs):
        coast = jnp.where(is_upper, coast_ref[last : last + 1, :], coast_ref[0:1, :])
        edge_ref[LEVELS + kind : LEVELS + kind + 1, :] = coast.astype(F32)


def half_forcing(is_upper, profile_ref, coast_refs, sea_ref, left_ref, hot_ref, rows_ref, bound_ref, state):
    rows, _, col_count = state.shape
    first_row = jnp.where(is_upper, rows, 0)
    aligned = pl.multiple_of(first_row, 8)
    sea = sea_ref[pl.ds(aligned, rows), :]
    for start in range(0, col_count, LANES):
        profile = jnp.broadcast_to(profile_ref[...], (2 * PAD, LANES))
        for row in range(rows):
            state[row, :, start : start + LANES] = profile * sea[row : row + 1, start : start + LANES]
    span = 2

    def step(number, carry):
        least = jnp.maximum(bound_ref[2 * number] - first_row, 0)
        most = jnp.minimum(bound_ref[2 * number + 1] - first_row, rows - 1)

        def rows_step(start, inner):
            base = start * span
            product = chosen_rows(number, first_row + base, span, left_ref, hot_ref, rows_ref)
            for offset in range(span):
                state[base + offset] += product[2 * PAD * offset : 2 * PAD * (offset + 1)]
            return inner

        lax.fori_loop(least // span, (most + span) // span, rows_step, 0)
        return carry

    lax.fori_loop(0, left_ref.shape[0], step, 0)
    for kind, coast_ref in enumerate(coast_refs):
        coast = coast_ref[pl.ds(aligned, rows), :].astype(F32)
        for row in range(rows):
            state[row, LEVELS + kind : LEVELS + kind + 1, :] = coast[row : row + 1, :]


def half_shapes(row_count, col_count):
    return (
        jax.ShapeDtypeStruct((row_count // 2, 2 * PAD, col_count), F32),
        jax.ShapeDtypeStruct((2 * PAD, col_count), F32),
        jax.ShapeDtypeStruct((PAD, LANES), F32),
    )


def in_place(count):
    return [pl.BlockSpec(memory_space=pltpu.SMEM)] + [pl.BlockSpec(memory_space=pltpu.VMEM)] * count


def first_forcing(capacity, alt_capacity, group, flags, message, profile, coast):
    row_count, col_count = coast[0].shape
    devices = message.shape[0]
    members = min(32, devices) * 8
    chunks = capacity // 8 * (devices // min(32, devices))

    def kernel(flag_ref, message_ref, profile_ref, wet, north, east, edge_ref, *outs):
        prepare(capacity, alt_capacity, group, col_count, message_ref, *outs)
        is_upper = flag_ref[NEAR] > 0
        row = jnp.where(is_upper, row_count - 1, 0)
        outer_forcing(row, is_upper, profile_ref, (wet, north, east), *outs, edge_ref)

    return pl.pallas_call(
        kernel,
        in_specs=in_place(5),
        out_shape=(
            half_shapes(row_count, col_count)[1],
            jax.ShapeDtypeStruct((row_count, col_count), F32),
            jax.ShapeDtypeStruct((chunks, 2 * PAD, 2 * members), BF),
            jax.ShapeDtypeStruct((chunks, members, col_count), BF),
            jax.ShapeDtypeStruct((chunks, 8, members), jnp.int32),
            jax.ShapeDtypeStruct((2 * chunks,), jnp.int32),
        ),
        out_specs=[pl.BlockSpec(memory_space=pltpu.VMEM)] * 5
        + [pl.BlockSpec(memory_space=pltpu.SMEM)],
        compiler_params=pltpu.CompilerParams(vmem_limit_bytes=24 * MIB),
        cost_estimate=pl.CostEstimate(
            flops=6_000_000_000, bytes_accessed=8_000_000, transcendentals=0
        ),
        name="forcing_first",
    )(flags, message, profile, *coast)


def rest_forcing(flags, profile, coast, prepared):
    row_count, col_count = coast[0].shape

    def kernel(flag_ref, profile_ref, wet, north, east, sea, left, hot, rows, bound, near, far, edge_ref, cols_ref):
        coast_refs = (wet, north, east)
        operands = (sea, left, hot, rows, bound)
        half_forcing(flag_ref[FAR] > 0, profile_ref, coast_refs, *operands, far)
        half_forcing(flag_ref[NEAR] > 0, profile_ref, coast_refs, *operands, near)
        write_edge(flag_ref[FAR] > 0, far, edge_ref)
        cols = columns_of(NEAR, near, jnp.zeros((PAD, LANES), F32))
        cols_ref[...] = columns_of(FAR, far, cols)

    state, edge, cols = half_shapes(row_count, col_count)
    return pl.pallas_call(
        kernel,
        in_specs=in_place(8) + [pl.BlockSpec(memory_space=pltpu.SMEM)],
        out_shape=(state, state, edge, cols),
        compiler_params=pltpu.CompilerParams(vmem_limit_bytes=20 * MIB),
        cost_estimate=pl.CostEstimate(
            flops=6_000_000_000, bytes_accessed=8_000_000, transcendentals=0
        ),
        name="forcing_rest",
    )(flags, profile, *coast, *prepared)


def fold_row(row_ref, mirror_ref, piece, chunk, chunks, rows):
    index = jnp.broadcast_to(mirror_ref[0:1, piece(chunk)], (rows, LANES))
    return jnp.take_along_axis(row_ref[:, piece(chunks - 1 - chunk)], index, axis=1)


def weight_kernel(which, flag_ref, wet_ref, north_ref, east_ref, edge_in, west_in, east_in, mirror_ref, out_ref, fold_ref):
    row_count, col_count = wet_ref.shape
    rows = row_count // 2
    is_upper = flag_ref[which] > 0
    at = pl.multiple_of(jnp.where(is_upper, rows, 0), 8)
    wet = wet_ref[pl.ds(at, rows), :].astype(F32)
    north = north_ref[pl.ds(at, rows), :]
    east = east_ref[pl.ds(at, rows), :]
    chunks = col_count // LANES
    lane = lax.broadcasted_iota(jnp.int32, (1, col_count), 1)
    start = column_lane(which, rows, 0, 1, 0)
    west_cols = west_in[72:80, :].T[start : start + rows]
    start = column_lane(which, rows, 0, 0, 0)
    east_cols = east_in[72:80, :].T[start : start + rows]
    west_wet = jnp.where(lane == 0, west_cols[:, 3:4], pltpu.roll(wet, 1, 1))
    west_coef = jnp.where(lane == 0, west_cols[:, 5:6], pltpu.roll(east, 1, 1))
    east_wet = jnp.where(
        lane == col_count - 1, east_cols[:, 3:4], pltpu.roll(wet, col_count - 1, 1)
    )
    east_w = east * wet * east_wet
    west_w = west_coef * west_wet * wet

    def piece(c):
        return slice(c * LANES, (c + 1) * LANES)

    spare_ref = edge_in.at[72:80]
    if which == FAR:
        for c in range(chunks):
            fold_ref[:, piece(c)] = fold_row(spare_ref, mirror_ref, piece, c, chunks, 8)
    spare = spare_ref[...]
    last = rows - 1
    inner_wet = jnp.where(
        is_upper, wet_ref[rows - 1 : rows, :], wet_ref[rows : rows + 1, :]
    ).astype(F32)
    above = jnp.where(is_upper, spare[3:4], inner_wet)
    top_w = north[last:] * wet[last:] * above
    if which == FAR:
        fold = 0.5 * (north[last:] + fold_ref[4:5]) * wet[last:] * fold_ref[3:4]
        top_w = jnp.where(flag_ref[TOP] > 0, fold, top_w)
    below = jnp.where(is_upper, north_ref[rows - 1 : rows, :] * inner_wet, spare[4:5] * spare[3:4])
    between = north[:last] * wet[:last] * wet[1:]
    north_w = jnp.concatenate([between, top_w], axis=0)
    south_w = jnp.concatenate([below * wet[0:1], between], axis=0)
    center = 1.0 - (east_w + west_w + north_w + south_w)
    for kind, weight in enumerate((center, east_w, west_w, north_w, south_w)):
        for row in range(rows):
            out_ref[row, kind : kind + 1, :] = weight[row : row + 1]


def edge_weights(which, flags, coast, received, mirror):
    row_count, col_count = coast[0].shape

    def kernel(*refs):
        weight_kernel(which, *refs)

    return pl.pallas_call(
        kernel,
        in_specs=in_place(7),
        out_shape=jax.ShapeDtypeStruct((row_count // 2, 8, col_count), F32),
        scratch_shapes=[pltpu.VMEM((8, col_count), F32)],
        compiler_params=pltpu.CompilerParams(vmem_limit_bytes=16 * MIB),
        name="edge_weights",
    )(flags, *coast, *received, mirror)


def set_outer_rows(which, flag_ref, edge_in, inner, mirror_ref, south_ref, north_ref):
    levels, col_count = edge_in.shape
    is_upper = flag_ref[which] > 0
    is_top = flag_ref[TOP] > 0
    chunks = col_count // LANES

    def piece(c):
        return slice(c * LANES, (c + 1) * LANES)

    @pl.when(is_upper)
    def _():
        south_ref[...] = inner[...]

    @pl.when(jnp.logical_not(is_upper))
    def _():
        south_ref[...] = edge_in[...]
        north_ref[...] = inner[...]

    if which == NEAR:

        @pl.when(is_upper)
        def _():
            north_ref[...] = edge_in[...]

        return

    @pl.when(is_upper & jnp.logical_not(is_top))
    def _():
        north_ref[...] = edge_in[...]

    @pl.when(is_top)
    def _():
        for c in range(chunks):
            north_ref[:, piece(c)] = fold_row(edge_in, mirror_ref, piece, c, chunks, levels)


def mix_row(which, row, rows, field, at, state_ref, south_ref, north_ref, west_in, east_in, coef_ref, right_ref, slot):
    col_count = state_ref.shape[2]
    chunks = col_count // LANES
    lane = lax.broadcasted_iota(jnp.int32, (1, LANES), 1)
    levels = slice(at, at + PAD)

    def piece(chunk):
        return slice(chunk * LANES, (chunk + 1) * LANES)

    west_lane = column_lane(which, rows, field, 1, row)
    east_lane = column_lane(which, rows, field, 0, row)
    centers = [state_ref[row, levels, piece(c)] for c in range(chunks)]
    to_left = [pltpu.roll(c, LANES - 1, 1) for c in centers]
    to_right = [pltpu.roll(c, 1, 1) for c in centers]
    to_right.append(pltpu.roll(west_in[...], LANES - west_lane, 1))
    to_left.append(pltpu.roll(east_in[...], LANES - 1 - east_lane, 1))
    for c in range(chunks):
        south = state_ref[row - 1, levels, piece(c)] if row > 0 else south_ref[levels, piece(c)]
        if row < rows - 1:
            north = state_ref[row + 1, levels, piece(c)]
        else:
            north = north_ref[levels, piece(c)]
        east = jnp.where(lane == LANES - 1, to_left[c + 1], to_left[c])
        west = jnp.where(lane == 0, to_right[c - 1], to_right[c])

        def coef(kind):
            return coef_ref[row, kind : kind + 1, piece(c)]

        mixed = (
            coef(0) * centers[c]
            + coef(1) * east
            + coef(2) * west
            + coef(3) * north
            + coef(4) * south
        )
        high, low = split_two(mixed)
        right_ref[slot, 0:PAD, piece(c)] = high
        right_ref[slot, PAD : 2 * PAD, piece(c)] = low
        right_ref[slot, 2 * PAD : 3 * PAD, piece(c)] = high


def diffuse(which, flags, state, other, received, mirror, coef, matrix, *far_cols):
    rows, _, col_count = state.shape
    slots = 4

    def kernel(flag_ref, state_ref, other_ref, edge_in, west_in, east_in, mirror_ref, coef_ref, matrix_ref, *refs):
        out_ref, edge_ref, cols_ref, south_ref, north_ref, right_ref = refs[-6:]
        is_upper = flag_ref[which] > 0
        inner = other_ref.at[jnp.where(is_upper, rows - 1, 0)]
        set_outer_rows(which, flag_ref, edge_in, inner, mirror_ref, south_ref, north_ref)
        right_ref[:, 3 * PAD :, :] = jnp.zeros((slots, 16, col_count), BF)
        units = [(row, field) for row in range(rows) for field in range(2)]

        def product(number):
            row, field = units[number]
            result = mm(matrix_ref[field, row], right_ref[number % slots])
            out_ref[row, field * PAD : (field + 1) * PAD] = result

        for number, (row, field) in enumerate(units):
            mix_row(which, row, rows, field, field * PAD, state_ref, south_ref, north_ref, west_in, east_in, coef_ref, right_ref, number % slots)
            if number > 0:
                product(number - 1)
        product(len(units) - 1)
        write_edge(is_upper, out_ref, edge_ref)
        old_cols = refs[0][...] if which == NEAR else jnp.zeros((PAD, LANES), F32)
        cols_ref[...] = columns_of(which, out_ref, old_cols)

    return pl.pallas_call(
        kernel,
        in_specs=in_place(8 + len(far_cols)),
        out_shape=half_shapes(2 * rows, col_count),
        scratch_shapes=[
            pltpu.VMEM((2 * PAD, col_count), F32),
            pltpu.VMEM((2 * PAD, col_count), F32),
            pltpu.VMEM((slots, 256, col_count), BF),
        ],
        compiler_params=pltpu.CompilerParams(vmem_limit_bytes=16 * MIB),
        cost_estimate=pl.CostEstimate(
            flops=3_000_000_000, bytes_accessed=8_000_000, transcendentals=0
        ),
        name="diffusion_" + ("near", "far")[which],
    )(flags, state, other, *received, mirror, coef, matrix, *far_cols)


def diffuse_last(which, flags, state, other, received, mirror, coef, matrix, mask, target):
    rows, _, col_count = state.shape
    slots = 4

    def kernel(flag_ref, state_ref, other_ref, edge_in, west_in, east_in, mirror_ref, coef_ref, matrix_ref, mask_ref, *refs):
        out_ref, south_ref, north_ref, right_ref = refs[-4:]
        field = pl.program_id(0)
        set_outer_rows(which, flag_ref, edge_in, other_ref.at[0], mirror_ref, south_ref, north_ref)
        right_ref[:, 3 * PAD :, :] = jnp.zeros((slots, 16, col_count), BF)
        wet = mask_ref[...].astype(F32)
        results = []

        def product(row):
            result = mm(matrix_ref[0, row], right_ref[row % slots])
            results.append(result * wet[row : row + 1])

        for row in range(rows):
            mix_row(which, row, rows, field, 0, state_ref, south_ref, north_ref, west_in, east_in, coef_ref, right_ref, row % slots)
            if row > 0:
                product(row - 1)
        product(rows - 1)
        out_ref[...] = jnp.swapaxes(jnp.stack(results), 0, 1)[:LEVELS]

    def whole(array):
        return pl.BlockSpec(array.shape, lambda f, flags: (0,) * len(array.shape))

    edge_in, west_in, east_in = received
    in_specs = [
        pl.BlockSpec((rows, PAD, col_count), lambda f, flags: (0, f, 0)),
        pl.BlockSpec((1, PAD, col_count), lambda f, flags: (flags[which] * (rows - 1), f, 0)),
        pl.BlockSpec((PAD, col_count), lambda f, flags: (f, 0)),
        whole(west_in),
        whole(east_in),
        whole(mirror),
        whole(coef),
        pl.BlockSpec((1, rows) + matrix.shape[2:], lambda f, flags: (f, 0, 0, 0)),
        pl.BlockSpec((rows, col_count), lambda f, flags: (flags[which], 0)),
    ]
    operands = [state, other, edge_in, west_in, east_in, mirror, coef, matrix, mask]
    aliases = {}
    if target is not None:
        in_specs.append(pl.BlockSpec(memory_space=pl.ANY))
        operands.append(target)
        aliases = {len(operands): 0}
    return pl.pallas_call(
        kernel,
        grid_spec=pltpu.PrefetchScalarGridSpec(
            num_scalar_prefetch=1,
            grid=(2,),
            in_specs=in_specs,
            out_specs=pl.BlockSpec((LEVELS, rows, col_count), lambda f, flags: (f, flags[which], 0)),
            scratch_shapes=[
                pltpu.VMEM((PAD, col_count), F32),
                pltpu.VMEM((PAD, col_count), F32),
                pltpu.VMEM((slots, 256, col_count), BF),
            ],
        ),
        out_shape=jax.ShapeDtypeStruct((2 * LEVELS, 2 * rows, col_count), F32),
        input_output_aliases=aliases,
        compiler_params=pltpu.CompilerParams(vmem_limit_bytes=20 * MIB),
        cost_estimate=pl.CostEstimate(
            flops=3_000_000_000, bytes_accessed=8_000_000, transcendentals=0
        ),
        name="diffusion_last",
    )(flags, *operands)


def mixing_matrices(vinv):
    turned = jnp.transpose(vinv, (1, 0, 3, 2))
    turned = jnp.pad(turned, ((0, 0), (0, 0), (0, PAD - LEVELS), (0, PAD - LEVELS)))
    high = lax.reduce_precision(turned, 8, 7)
    low = (turned - high).astype(BF)
    high = high.astype(BF)
    rest = jnp.zeros(high.shape[:3] + (256 - 3 * PAD,), BF)
    return jnp.concatenate([high, high, low, rest], axis=3)


def body(
    argo_value,
    argo_owner,
    argo_cell,
    alt_value,
    alt_owner,
    alt_cell,
    alt_profile,
    land_mask,
    coef_east,
    coef_north,
    mirror,
    vinv,
):
    row_count, col_count = land_mask.shape
    count_ja = lax.axis_size("ja")
    count_ia = lax.axis_size("ia")
    devices = count_ja * count_ia
    capacity = round_up(3 * argo_value.shape[0] // devices, 8)
    group = round_up(capacity // 4, 8)
    message = send_tables(
        devices,
        capacity,
        group,
        row_count,
        col_count,
        (
            argo_value.T,
            argo_owner.reshape(1, -1),
            argo_cell.reshape(1, -1),
            alt_value,
            alt_cell,
            alt_owner.reshape(1, -1),
        ),
    )
    message, ja_index = lax.optimization_barrier((message, lax.axis_index("ja")))
    message = lax.all_to_all(message, ("ja", "ia"), split_axis=0, concat_axis=0, tiled=True)

    ia_index = lax.axis_index("ia")
    is_top = (ja_index == count_ja - 1).astype(jnp.int32)
    parity = ja_index % 2
    flags = jnp.stack([1 - parity, parity, is_top]).astype(jnp.int32)
    fold_index = mirror - (count_ia - 1 - ia_index) * col_count
    mirror_lane = jnp.broadcast_to((fold_index % LANES)[None, :], (8, col_count))
    matrices = mixing_matrices(vinv)
    profile = jnp.pad(alt_profile.reshape(2, LEVELS, 1), ((0, 0), (0, PAD - LEVELS), (0, 0)))
    profile = profile.reshape(2 * PAD, 1)
    alt_capacity = max(2, 3 * alt_value.shape[0] // devices)
    coast = (land_mask, coef_north, coef_east)
    rows = row_count // 2
    lower = [matrices[:, :rows], matrices[:, rows:]]
    odd_device = parity == 1
    half_matrices = [
        jnp.where(odd_device, lower[0], lower[1]),
        jnp.where(odd_device, lower[1], lower[0]),
    ]

    ring_east = [(i, (i + 1) % count_ia) for i in range(count_ia)]
    ring_west = [((i + 1) % count_ia, i) for i in range(count_ia)]
    even_swap = []
    odd_swap = []
    for ja in range(count_ja):
        for ia in range(count_ia):
            here = ja * count_ia + ia
            even_swap.append((here, (ja ^ 1) * count_ia + ia))
            if ja == count_ja - 1:
                odd_swap.append((here, ja * count_ia + count_ia - 1 - ia))
            elif ja > 0:
                odd_swap.append((here, (((ja - 1) ^ 1) + 1) * count_ia + ia))
    swaps = (even_swap, odd_swap)

    def swap(which, edge):
        return lax.ppermute(edge, ("ja", "ia"), swaps[which])

    def pass_columns(cols):
        return lax.ppermute(cols, "ia", ring_east), lax.ppermute(cols, "ia", ring_west)

    near_edge, *prepared = first_forcing(
        capacity, alt_capacity, group, flags, message, profile, coast
    )
    near_edge = swap(NEAR, near_edge)
    near, far, far_edge, cols = rest_forcing(flags, profile, coast, prepared)
    sides = pass_columns(cols)
    far_edge = swap(FAR, far_edge)
    near_coef = edge_weights(NEAR, flags, coast, (near_edge, *sides), mirror_lane)
    far_coef = edge_weights(FAR, flags, coast, (far_edge, *sides), mirror_lane)
    near_fixed = (mirror_lane, near_coef, half_matrices[NEAR])
    far_fixed = (mirror_lane, far_coef, half_matrices[FAR])
    for sweep in range(ITERS - 1):
        new_near, new_edge, cols = diffuse(
            NEAR, flags, near, far, (near_edge, *sides), *near_fixed, cols
        )
        near_edge = swap(NEAR, new_edge)
        sides = pass_columns(cols)
        far, new_edge, cols = diffuse(FAR, flags, far, near, (far_edge, *sides), *far_fixed)
        far_edge = swap(FAR, new_edge)
        near = new_near
    last_sides = pass_columns(cols)
    output = diffuse_last(
        NEAR, flags, near, far, (near_edge, *sides), *near_fixed, land_mask, None
    )
    return diffuse_last(
        FAR, flags, far, near, (far_edge, *last_sides), *far_fixed, land_mask, output
    )


def solution(mesh):
    in_specs = (
        P(("ja", "ia"), None),
        P(("ja", "ia"), None),
        P(("ja", "ia")),
        P(("ja", "ia")),
        P(("ja", "ia"), None),
        P(("ja", "ia")),
        P(),
        P("ja", "ia"),
        P("ja", "ia"),
        P("ja", "ia"),
        P("ia"),
        P("ja", None, None, None),
    )
    out_specs = P(None, "ja", "ia")
    return jax.shard_map(body, mesh=mesh, in_specs=in_specs, out_specs=out_specs, check_vma=False)
```

```python
import math

import jax
import jax.numpy as jnp
from jax import lax
from jax.experimental import pallas as pl
from jax.experimental.pallas import tpu as pltpu
from jax.sharding import PartitionSpec as P

ITERS = 3
LEVELS = 75
PAD = 80
LANES = 128
NEAR, FAR, TOP = 0, 1, 2
BF = jnp.bfloat16
F32 = jnp.float32
MIB = 1024 * 1024


def round_up(value, unit):
    return (value + unit - 1) // unit * unit


def split_two(value):
    high = value.astype(BF)
    low = (value - high.astype(F32)).astype(BF)
    return high, low


def mm(left, right):
    return jnp.dot(left, right, preferred_element_type=F32)


def as_column(row):
    return jnp.broadcast_to(row, (8, row.shape[1])).T[:, 0:1]


def slot_ranks(owner_row, cell_row, devices, col_count, row_count, capacity, spread):
    count = owner_row.shape[1]
    owner = owner_row.astype(F32)
    inside = cell_row // col_count
    order = lax.broadcasted_iota(jnp.int32, (1, count), 1).astype(F32)
    key = (owner * float(row_count) + inside.astype(F32)) * float(count) + order
    key_col = as_column(key)
    device = lax.broadcasted_iota(jnp.int32, (devices, 1), 0)
    mine = device == owner_row
    totals = jnp.sum(jnp.where(mine, 1.0, 0.0), axis=1, keepdims=True)
    rank = -jnp.sum(jnp.where(device < owner_row, totals, 0.0), axis=0, keepdims=True)
    for start in range(0, count, 128):
        before = jnp.where(key_col[start : start + 128] < key, 1.0, 0.0)
        rank = rank + jnp.sum(before, axis=0, keepdims=True)
    if spread:
        total = jnp.sum(jnp.where(mine, totals, 0.0), axis=0, keepdims=True)
        offset = owner * 1024.0
        goal = (inside * capacity // row_count).astype(F32) - rank + offset
        goal_col = as_column(goal)
        shift = offset
        for start in range(0, count, 128):
            within = key_col[start : start + 128] <= key
            reached = jnp.where(within, goal_col[start : start + 128], 0.0)
            shift = jnp.maximum(shift, jnp.max(reached, axis=0, keepdims=True))
        rank = rank + jnp.minimum(shift - offset, float(capacity) - total)
    return rank


def table_kernel(
    devices,
    capacity,
    group,
    row_count,
    col_count,
    value_ref,
    owner_ref,
    cell_ref,
    alt_value_ref,
    alt_cell_ref,
    alt_owner_ref,
    message_ref,
    level_ref,
    side_ref,
    hi_ref,
    lo_ref,
    alt_all_ref,
    rank_hot_ref,
    alt_rank_hot_ref,
):
    index = pl.program_id(0)
    n_obs = owner_ref.shape[1]
    n_alt = alt_owner_ref.shape[1]

    @pl.when(index == 0)
    def _():
        slot = lax.broadcasted_iota(jnp.int32, (capacity, 1), 0).astype(F32)
        alt_cell = alt_cell_ref[...].reshape(1, n_alt)
        rank = slot_ranks(
            owner_ref[...], cell_ref[...], devices, col_count, row_count, capacity, True
        )
        rank_hot_ref[...] = jnp.where(slot == rank, 1.0, 0.0).astype(BF)
        rank = slot_ranks(
            alt_owner_ref[...], alt_cell, devices, col_count, row_count, capacity, False
        )
        alt_rank_hot_ref[...] = jnp.where(slot == rank, 1.0, 0.0).astype(BF)
        level_ref[...] = jnp.zeros(level_ref.shape, F32)
        level_ref[0:75, :] = value_ref[0:75, :]
        level_ref[75:76, :] = cell_ref[...].astype(F32) + 1.0
        level_ref[80:128, :] = value_ref[75:123, :]
        for lane_group in range(4):
            level_ref[128 + 32 * lane_group : 155 + 32 * lane_group, :] = value_ref[123:150, :]
        high, low = split_two(level_ref[...].T)
        hi_ref[...] = high
        lo_ref[...] = low
        side_ref[...] = jnp.zeros(side_ref.shape, F32)
        pair = jnp.concatenate(
            [alt_value_ref[...].reshape(1, n_alt), alt_cell.astype(F32) + 1.0], axis=0
        )
        pair_high = pair.astype(BF).astype(F32)
        side_ref[76:78, :] = pair_high
        side_ref[78:80, :] = pair - pair_high
        alt_all_ref[...] = side_ref[...].T.astype(BF)

    per_step = message_ref.shape[0]
    chosen = []
    chosen_alt = []
    for member in range(per_step):
        device = index * per_step + member
        mask = jnp.where(owner_ref[...] == device, 1.0, 0.0).astype(BF)
        chosen.append(rank_hot_ref[...] * mask)
        mask = jnp.where(alt_owner_ref[...] == device, 1.0, 0.0).astype(BF)
        chosen_alt.append(alt_rank_hot_ref[...] * mask)
    chosen = jnp.concatenate(chosen, axis=0)
    chosen_alt = jnp.concatenate(chosen_alt, axis=0)
    table = mm(chosen, hi_ref[...]) + mm(chosen, lo_ref[...])
    lane = lax.broadcasted_iota(jnp.int32, (1, LANES), 1)
    extra = mm(chosen_alt, alt_all_ref[...])
    extra = jnp.where(lane < 78, extra + pltpu.roll(extra, LANES - 2, 1), 0.0)
    extra = jnp.where(lane >= 76, extra, 0.0)
    first = table[:, :LANES] + extra
    message_ref[:, 0:capacity] = first.reshape(per_step, capacity, LANES)
    rest = table[:, LANES:].reshape(per_step, capacity, LANES)
    total = jnp.zeros((per_step, group, LANES), F32)
    for lane_group in range(4):
        low_slot = lane_group * group
        if low_slot >= capacity:
            continue
        piece = rest[:, low_slot : low_slot + group]
        here = (lane // 32 == lane_group).reshape(1, 1, LANES)
        total = jnp.where(here, piece, total)
    message_ref[:, capacity : capacity + group] = total


def send_tables(devices, capacity, group, row_count, col_count, operands):
    n_obs = operands[1].shape[1]
    n_alt = operands[5].shape[1]
    per_step = max(1, 768 // capacity)

    def kernel(*refs):
        table_kernel(devices, capacity, group, row_count, col_count, *refs)

    def whole(array):
        return pl.BlockSpec(array.shape, lambda s: (0,) * len(array.shape))

    return pl.pallas_call(
        kernel,
        grid=(devices // per_step,),
        in_specs=[whole(x) for x in operands],
        out_specs=pl.BlockSpec((per_step, capacity + group, LANES), lambda s: (s, 0, 0)),
        out_shape=jax.ShapeDtypeStruct((devices, capacity + group, LANES), F32),
        scratch_shapes=[
            pltpu.VMEM((2 * LANES, n_obs), F32),
            pltpu.VMEM((LANES, n_alt), F32),
            pltpu.VMEM((n_obs, 2 * LANES), BF),
            pltpu.VMEM((n_obs, 2 * LANES), BF),
            pltpu.VMEM((n_alt, LANES), BF),
            pltpu.VMEM((capacity, n_obs), BF),
            pltpu.VMEM((capacity, n_alt), BF),
        ],
        compiler_params=pltpu.CompilerParams(vmem_limit_bytes=56 * MIB),
        name="send_tables",
    )(*operands)


def column_lane(which, rows, field, east, row):
    return (4 * which + 2 * field + east) * rows + row


def columns_of(which, state_ref, cols):
    rows = state_ref.shape[0]
    lane = lax.broadcasted_iota(jnp.int32, (1, LANES), 1)
    for row in range(rows):
        for field in range(2):
            part = state_ref[row, field * PAD : (field + 1) * PAD, :]
            at = column_lane(which, rows, field, 0, row)
            cols = jnp.where(lane == at, pltpu.roll(part[:, :LANES], at, 1), cols)
            at = column_lane(which, rows, field, 1, row)
            cols = jnp.where(lane == at, pltpu.roll(part[:, -LANES:], at + 1, 1), cols)
    return cols


def write_edge(is_upper, state_ref, edge_ref):
    edge_ref[...] = state_ref[jnp.where(is_upper, state_ref.shape[0] - 1, 0)]


def prepare(capacity, alt_capacity, group, col_count, message_ref, sea_ref, left_ref, hot_ref, rows_ref, bound_ref):
    row_count = sea_ref.shape[0]
    devices = message_ref.shape[0]
    block = min(32, devices)
    members = block * 8
    octets = capacity // 8
    alt_octets = (alt_capacity + 7) // 8
    per_group = group // 8
    shift = col_count.bit_length() - 1
    col_iota = lax.broadcasted_iota(jnp.int32, (1, col_count), 1)
    row_iota = lax.broadcasted_iota(jnp.int32, (row_count, 1), 0)

    def chunk(index, start):
        return message_ref[index * block : (index + 1) * block, start : start + 8, :].reshape(
            members, LANES
        )

    def hot_of(cell):
        return jnp.where(((cell - 1) & (col_count - 1)) == col_iota, 1.0, 0.0).astype(BF)

    def rows_of(cell):
        return lax.shift_right_arithmetic(cell - 1, shift)

    sea = jnp.zeros((row_count, col_count), F32)
    count = 0
    for index in range(devices // block):
        tails = [chunk(index, capacity + 8 * part).T for part in range(per_group)]
        for octet in range(octets):
            table = chunk(index, 8 * octet)
            turned = table.T
            tail = tails[octet % per_group]
            begin = 32 * (octet // per_group)
            levels = jnp.concatenate([turned, tail[begin : begin + 32]], axis=0)
            high, low = split_two(levels)
            left_ref[count, :, 0:members] = high
            left_ref[count, :, members : 2 * members] = low
            hot = hot_of(table[:, 75:76].astype(jnp.int32))
            hot_ref[count] = hot
            rows = rows_of(turned[75:76].astype(jnp.int32))
            rows_ref[count] = jnp.broadcast_to(rows, (8, members))
            bound_ref[2 * count] = jnp.min(jnp.where(rows >= 0, rows, row_count))
            bound_ref[2 * count + 1] = jnp.max(rows)
            count += 1
            if octet >= alt_octets:
                continue
            alt_hot = hot_of(table[:, 77:78].astype(jnp.int32))
            alt_rows = rows_of(turned[77:78].astype(jnp.int32))
            weighted = jnp.where(alt_rows == row_iota, turned[76:77], 0.0)
            high, low = split_two(weighted)
            product = mm(jnp.concatenate([high, low], axis=0), alt_hot)
            sea = sea + product[:row_count] + product[row_count:]
    sea_ref[...] = sea


def chosen_rows(number, here, row, span, left_ref, hot_ref):
    pieces = []
    for offset in range(span):
        mask = jnp.where(here == row + offset, 1.0, 0.0).astype(BF)
        pieces.append(left_ref[number] * jnp.concatenate([mask, mask], axis=1))
    hot = hot_ref[number]
    return mm(jnp.concatenate(pieces, axis=0), jnp.concatenate([hot, hot], axis=0))


def outer_forcing(row, is_upper, profile_ref, coast_refs, sea_ref, left_ref, hot_ref, rows_ref, bound_ref, edge_ref):
    row_count, col_count = sea_ref.shape
    last = row_count - 1
    profile = jnp.broadcast_to(profile_ref[...], (2 * PAD, LANES))
    sea = jnp.where(is_upper, sea_ref[last : last + 1, :], sea_ref[0:1, :])
    for start in range(0, col_count, LANES):
        edge_ref[:, start : start + LANES] = profile * sea[:, start : start + LANES]

    def step(number, carry):
        @pl.when((bound_ref[2 * number] <= row) & (row <= bound_ref[2 * number + 1]))
        def _():
            edge_ref[...] += chosen_rows(number, rows_ref[number][0:1], row, 1, left_ref, hot_ref)

        return carry

    lax.fori_loop(0, left_ref.shape[0], step, 0)
    for kind, coast_ref in enumerate(coast_refs):
        coast = jnp.where(is_upper, coast_ref[last : last + 1, :], coast_ref[0:1, :])
        edge_ref[LEVELS + kind : LEVELS + kind + 1, :] = coast.astype(F32)


def all_forcing(profile_ref, coast_refs, sea_ref, left_ref, hot_ref, rows_ref, bound_ref, state):
    row_count, _, col_count = state.shape
    count = left_ref.shape[0]
    for start in range(0, col_count, LANES):
        profile = jnp.broadcast_to(profile_ref[...], (2 * PAD, LANES))
        for row in range(row_count):
            state[row, :, start : start + LANES] = profile * sea_ref[row : row + 1, start : start + LANES]
    span = 3
    batch = math.gcd(count, 4)

    def step(number, carry):
        chunks = [number * batch + member for member in range(batch)]
        least = [bound_ref[2 * chunk] for chunk in chunks]
        most = [bound_ref[2 * chunk + 1] for chunk in chunks]
        runs = [lax.div(most[i] - least[i] + span, span) for i in range(batch)]
        longest = runs[0]
        for run in runs[1:]:
            longest = jnp.maximum(longest, run)

        def run_step(turn, inner):
            for i, chunk in enumerate(chunks):
                begin = least[i] + turn * span
                base = jnp.minimum(begin, row_count - span)
                here = rows_ref[chunk][0:1]
                here = jnp.where(here >= begin, here, -1)
                product = chosen_rows(chunk, here, base, span, left_ref, hot_ref)
                for offset in range(span):
                    state[base + offset] += product[2 * PAD * offset : 2 * PAD * (offset + 1)]
            return inner

        lax.fori_loop(0, longest, run_step, 0)
        return carry

    lax.fori_loop(0, count // batch, step, 0)
    for kind, coast_ref in enumerate(coast_refs):
        coast = coast_ref[...].astype(F32)
        for row in range(row_count):
            state[row, LEVELS + kind : LEVELS + kind + 1, :] = coast[row : row + 1, :]


def half_shapes(row_count, col_count):
    return (
        jax.ShapeDtypeStruct((row_count // 2, 2 * PAD, col_count), F32),
        jax.ShapeDtypeStruct((2 * PAD, col_count), F32),
        jax.ShapeDtypeStruct((PAD, LANES), F32),
    )


def in_place(count):
    return [pl.BlockSpec(memory_space=pltpu.SMEM)] + [pl.BlockSpec(memory_space=pltpu.VMEM)] * count


def first_forcing(capacity, alt_capacity, group, flags, message, profile, coast):
    row_count, col_count = coast[0].shape
    devices = message.shape[0]
    members = min(32, devices) * 8
    chunks = capacity // 8 * (devices // min(32, devices))

    def kernel(flag_ref, message_ref, profile_ref, wet, north, east, edge_ref, *outs):
        prepare(capacity, alt_capacity, group, col_count, message_ref, *outs)
        is_upper = flag_ref[NEAR] > 0
        row = jnp.where(is_upper, row_count - 1, 0)
        outer_forcing(row, is_upper, profile_ref, (wet, north, east), *outs, edge_ref)

    return pl.pallas_call(
        kernel,
        in_specs=in_place(5),
        out_shape=(
            half_shapes(row_count, col_count)[1],
            jax.ShapeDtypeStruct((row_count, col_count), F32),
            jax.ShapeDtypeStruct((chunks, 2 * PAD, 2 * members), BF),
            jax.ShapeDtypeStruct((chunks, members, col_count), BF),
            jax.ShapeDtypeStruct((chunks, 8, members), jnp.int32),
            jax.ShapeDtypeStruct((2 * chunks,), jnp.int32),
        ),
        out_specs=[pl.BlockSpec(memory_space=pltpu.VMEM)] * 5
        + [pl.BlockSpec(memory_space=pltpu.SMEM)],
        compiler_params=pltpu.CompilerParams(vmem_limit_bytes=24 * MIB),
        cost_estimate=pl.CostEstimate(
            flops=6_000_000_000, bytes_accessed=8_000_000, transcendentals=0
        ),
        name="forcing_first",
    )(flags, message, profile, *coast)


def rest_forcing(flags, profile, coast, prepared):
    row_count, col_count = coast[0].shape
    half = row_count // 2

    def kernel(flag_ref, profile_ref, wet, north, east, sea, left, hot, rows, bound, state, edge_ref, cols_ref):
        all_forcing(profile_ref, (wet, north, east), sea, left, hot, rows, bound, state)
        cols = jnp.zeros((PAD, LANES), F32)
        for which in (NEAR, FAR):
            first_row = jnp.where(flag_ref[which] > 0, half, 0)
            cols = columns_of(which, state.at[pl.ds(first_row, half)], cols)
        cols_ref[...] = cols
        edge_ref[...] = state[jnp.where(flag_ref[FAR] > 0, row_count - 1, 0)]

    _, edge, cols = half_shapes(row_count, col_count)
    state = jax.ShapeDtypeStruct((row_count, 2 * PAD, col_count), F32)
    return pl.pallas_call(
        kernel,
        in_specs=in_place(8) + [pl.BlockSpec(memory_space=pltpu.SMEM)],
        out_shape=(state, edge, cols),
        compiler_params=pltpu.CompilerParams(vmem_limit_bytes=20 * MIB),
        cost_estimate=pl.CostEstimate(
            flops=6_000_000_000, bytes_accessed=8_000_000, transcendentals=0
        ),
        name="forcing_rest",
    )(flags, profile, *coast, *prepared)


def fold_row(row_ref, mirror_ref, piece, chunk, chunks, rows):
    index = jnp.broadcast_to(mirror_ref[0:1, piece(chunk)], (rows, LANES))
    return jnp.take_along_axis(row_ref[:, piece(chunks - 1 - chunk)], index, axis=1)


def weight_kernel(which, flag_ref, wet_ref, north_ref, east_ref, edge_in, west_in, east_in, mirror_ref, out_ref, fold_ref):
    row_count, col_count = wet_ref.shape
    rows = row_count // 2
    is_upper = flag_ref[which] > 0
    at = pl.multiple_of(jnp.where(is_upper, rows, 0), 8)
    wet = wet_ref[pl.ds(at, rows), :].astype(F32)
    north = north_ref[pl.ds(at, rows), :]
    east = east_ref[pl.ds(at, rows), :]
    chunks = col_count // LANES
    lane = lax.broadcasted_iota(jnp.int32, (1, col_count), 1)
    start = column_lane(which, rows, 0, 1, 0)
    west_cols = west_in[72:80, :].T[start : start + rows]
    start = column_lane(which, rows, 0, 0, 0)
    east_cols = east_in[72:80, :].T[start : start + rows]
    west_wet = jnp.where(lane == 0, west_cols[:, 3:4], pltpu.roll(wet, 1, 1))
    west_coef = jnp.where(lane == 0, west_cols[:, 5:6], pltpu.roll(east, 1, 1))
    east_wet = jnp.where(
        lane == col_count - 1, east_cols[:, 3:4], pltpu.roll(wet, col_count - 1, 1)
    )
    east_w = east * wet * east_wet
    west_w = west_coef * west_wet * wet

    def piece(c):
        return slice(c * LANES, (c + 1) * LANES)

    spare_ref = edge_in.at[72:80]
    if which == FAR:
        for c in range(chunks):
            fold_ref[:, piece(c)] = fold_row(spare_ref, mirror_ref, piece, c, chunks, 8)
    spare = spare_ref[...]
    last = rows - 1
    inner_wet = jnp.where(
        is_upper, wet_ref[rows - 1 : rows, :], wet_ref[rows : rows + 1, :]
    ).astype(F32)
    above = jnp.where(is_upper, spare[3:4], inner_wet)
    top_w = north[last:] * wet[last:] * above
    if which == FAR:
        fold = 0.5 * (north[last:] + fold_ref[4:5]) * wet[last:] * fold_ref[3:4]
        top_w = jnp.where(flag_ref[TOP] > 0, fold, top_w)
    below = jnp.where(is_upper, north_ref[rows - 1 : rows, :] * inner_wet, spare[4:5] * spare[3:4])
    between = north[:last] * wet[:last] * wet[1:]
    north_w = jnp.concatenate([between, top_w], axis=0)
    south_w = jnp.concatenate([below * wet[0:1], between], axis=0)
    center = 1.0 - (east_w + west_w + north_w + south_w)
    for kind, weight in enumerate((center, east_w, west_w, north_w, south_w)):
        for row in range(rows):
            out_ref[row, kind : kind + 1, :] = weight[row : row + 1]


def edge_weights(which, flags, coast, received, mirror):
    row_count, col_count = coast[0].shape

    def kernel(*refs):
        weight_kernel(which, *refs)

    return pl.pallas_call(
        kernel,
        in_specs=in_place(7),
        out_shape=jax.ShapeDtypeStruct((row_count // 2, 8, col_count), F32),
        scratch_shapes=[pltpu.VMEM((8, col_count), F32)],
        compiler_params=pltpu.CompilerParams(vmem_limit_bytes=16 * MIB),
        name="edge_weights",
    )(flags, *coast, *received, mirror)


def set_outer_rows(which, flag_ref, edge_in, inner, mirror_ref, south_ref, north_ref):
    levels, col_count = edge_in.shape
    is_upper = flag_ref[which] > 0
    is_top = flag_ref[TOP] > 0
    chunks = col_count // LANES

    def piece(c):
        return slice(c * LANES, (c + 1) * LANES)

    @pl.when(is_upper)
    def _():
        south_ref[...] = inner[...]

    @pl.when(jnp.logical_not(is_upper))
    def _():
        south_ref[...] = edge_in[...]
        north_ref[...] = inner[...]

    if which == NEAR:

        @pl.when(is_upper)
        def _():
            north_ref[...] = edge_in[...]

        return

    @pl.when(is_upper & jnp.logical_not(is_top))
    def _():
        north_ref[...] = edge_in[...]

    @pl.when(is_top)
    def _():
        for c in range(chunks):
            north_ref[:, piece(c)] = fold_row(edge_in, mirror_ref, piece, c, chunks, levels)


def mix_row(which, row, rows, field, at, state_ref, south_ref, north_ref, west_in, east_in, coef_ref, right_ref, slot):
    col_count = state_ref.shape[2]
    chunks = col_count // LANES
    lane = lax.broadcasted_iota(jnp.int32, (1, LANES), 1)
    levels = slice(at, at + PAD)

    def piece(chunk):
        return slice(chunk * LANES, (chunk + 1) * LANES)

    west_lane = column_lane(which, rows, field, 1, row)
    east_lane = column_lane(which, rows, field, 0, row)
    centers = [state_ref[row, levels, piece(c)] for c in range(chunks)]
    to_left = [pltpu.roll(c, LANES - 1, 1) for c in centers]
    to_right = [pltpu.roll(c, 1, 1) for c in centers]
    to_right.append(pltpu.roll(west_in[...], LANES - west_lane, 1))
    to_left.append(pltpu.roll(east_in[...], LANES - 1 - east_lane, 1))
    for c in range(chunks):
        south = state_ref[row - 1, levels, piece(c)] if row > 0 else south_ref[levels, piece(c)]
        if row < rows - 1:
            north = state_ref[row + 1, levels, piece(c)]
        else:
            north = north_ref[levels, piece(c)]
        east = jnp.where(lane == LANES - 1, to_left[c + 1], to_left[c])
        west = jnp.where(lane == 0, to_right[c - 1], to_right[c])

        def coef(kind):
            return coef_ref[row, kind : kind + 1, piece(c)]

        mixed = (
            coef(0) * centers[c]
            + coef(1) * east
            + coef(2) * west
            + coef(3) * north
            + coef(4) * south
        )
        high, low = split_two(mixed)
        right_ref[slot, 0:PAD, piece(c)] = high
        right_ref[slot, PAD : 2 * PAD, piece(c)] = low
        right_ref[slot, 2 * PAD : 3 * PAD, piece(c)] = high


def diffuse(which, flags, state, other, received, mirror, coef, matrix, *far_cols):
    rows = coef.shape[0]
    col_count = state.shape[2]
    slots = 4

    def kernel(flag_ref, state_ref, other_ref, edge_in, west_in, east_in, mirror_ref, coef_ref, matrix_ref, *refs):
        out_ref, edge_ref, cols_ref, south_ref, north_ref, right_ref = refs[-6:]
        is_upper = flag_ref[which] > 0
        if state.shape[0] > rows:
            state_ref = state_ref.at[pl.ds(jnp.where(is_upper, rows, 0), rows)]
            inner = other_ref.at[jnp.where(is_upper, rows - 1, rows)]
        else:
            inner = other_ref.at[jnp.where(is_upper, rows - 1, 0)]
        set_outer_rows(which, flag_ref, edge_in, inner, mirror_ref, south_ref, north_ref)
        right_ref[:, 3 * PAD :, :] = jnp.zeros((slots, 16, col_count), BF)
        units = [(row, field) for row in range(rows) for field in range(2)]

        def product(number):
            row, field = units[number]
            result = mm(matrix_ref[field, row], right_ref[number % slots])
            out_ref[row, field * PAD : (field + 1) * PAD] = result

        for number, (row, field) in enumerate(units):
            mix_row(which, row, rows, field, field * PAD, state_ref, south_ref, north_ref, west_in, east_in, coef_ref, right_ref, number % slots)
            if number > 0:
                product(number - 1)
        product(len(units) - 1)
        write_edge(is_upper, out_ref, edge_ref)
        old_cols = refs[0][...] if which == NEAR else jnp.zeros((PAD, LANES), F32)
        cols_ref[...] = columns_of(which, out_ref, old_cols)

    return pl.pallas_call(
        kernel,
        in_specs=in_place(8 + len(far_cols)),
        out_shape=half_shapes(2 * rows, col_count),
        scratch_shapes=[
            pltpu.VMEM((2 * PAD, col_count), F32),
            pltpu.VMEM((2 * PAD, col_count), F32),
            pltpu.VMEM((slots, 256, col_count), BF),
        ],
        compiler_params=pltpu.CompilerParams(vmem_limit_bytes=16 * MIB),
        cost_estimate=pl.CostEstimate(
            flops=3_000_000_000, bytes_accessed=8_000_000, transcendentals=0
        ),
        name="diffusion_" + ("near", "far")[which],
    )(flags, state, other, *received, mirror, coef, matrix, *far_cols)


def diffuse_last(which, flags, state, other, received, mirror, coef, matrix, mask, target):
    rows, _, col_count = state.shape
    slots = 4

    def kernel(flag_ref, state_ref, other_ref, edge_in, west_in, east_in, mirror_ref, coef_ref, matrix_ref, mask_ref, *refs):
        out_ref, south_ref, north_ref, right_ref = refs[-4:]
        field = pl.program_id(0)
        set_outer_rows(which, flag_ref, edge_in, other_ref.at[0], mirror_ref, south_ref, north_ref)
        right_ref[:, 3 * PAD :, :] = jnp.zeros((slots, 16, col_count), BF)
        wet = mask_ref[...].astype(F32)
        results = []

        def product(row):
            result = mm(matrix_ref[0, row], right_ref[row % slots])
            results.append(result * wet[row : row + 1])

        for row in range(rows):
            mix_row(which, row, rows, field, 0, state_ref, south_ref, north_ref, west_in, east_in, coef_ref, right_ref, row % slots)
            if row > 0:
                product(row - 1)
        product(rows - 1)
        out_ref[...] = jnp.swapaxes(jnp.stack(results), 0, 1)[:LEVELS]

    def whole(array):
        return pl.BlockSpec(array.shape, lambda f, flags: (0,) * len(array.shape))

    edge_in, west_in, east_in = received
    in_specs = [
        pl.BlockSpec((rows, PAD, col_count), lambda f, flags: (0, f, 0)),
        pl.BlockSpec((1, PAD, col_count), lambda f, flags: (flags[which] * (rows - 1), f, 0)),
        pl.BlockSpec((PAD, col_count), lambda f, flags: (f, 0)),
        whole(west_in),
        whole(east_in),
        whole(mirror),
        whole(coef),
        pl.BlockSpec((1, rows) + matrix.shape[2:], lambda f, flags: (f, 0, 0, 0)),
        pl.BlockSpec((rows, col_count), lambda f, flags: (flags[which], 0)),
    ]
    operands = [state, other, edge_in, west_in, east_in, mirror, coef, matrix, mask]
    aliases = {}
    if target is not None:
        in_specs.append(pl.BlockSpec(memory_space=pl.ANY))
        operands.append(target)
        aliases = {len(operands): 0}
    return pl.pallas_call(
        kernel,
        grid_spec=pltpu.PrefetchScalarGridSpec(
            num_scalar_prefetch=1,
            grid=(2,),
            in_specs=in_specs,
            out_specs=pl.BlockSpec((LEVELS, rows, col_count), lambda f, flags: (f, flags[which], 0)),
            scratch_shapes=[
                pltpu.VMEM((PAD, col_count), F32),
                pltpu.VMEM((PAD, col_count), F32),
                pltpu.VMEM((slots, 256, col_count), BF),
            ],
        ),
        out_shape=jax.ShapeDtypeStruct((2 * LEVELS, 2 * rows, col_count), F32),
        input_output_aliases=aliases,
        compiler_params=pltpu.CompilerParams(vmem_limit_bytes=20 * MIB),
        cost_estimate=pl.CostEstimate(
            flops=3_000_000_000, bytes_accessed=8_000_000, transcendentals=0
        ),
        name="diffusion_last",
    )(flags, *operands)


def mixing_matrices(vinv):
    turned = jnp.transpose(vinv, (1, 0, 3, 2))
    turned = jnp.pad(turned, ((0, 0), (0, 0), (0, PAD - LEVELS), (0, PAD - LEVELS)))
    high = lax.reduce_precision(turned, 8, 7)
    low = (turned - high).astype(BF)
    high = high.astype(BF)
    rest = jnp.zeros(high.shape[:3] + (256 - 3 * PAD,), BF)
    return jnp.concatenate([high, high, low, rest], axis=3)


def body(
    argo_value,
    argo_owner,
    argo_cell,
    alt_value,
    alt_owner,
    alt_cell,
    alt_profile,
    land_mask,
    coef_east,
    coef_north,
    mirror,
    vinv,
):
    row_count, col_count = land_mask.shape
    count_ja = lax.axis_size("ja")
    count_ia = lax.axis_size("ia")
    devices = count_ja * count_ia
    capacity = round_up(3 * argo_value.shape[0] // devices, 8)
    group = round_up(capacity // 4, 8)
    message = send_tables(
        devices,
        capacity,
        group,
        row_count,
        col_count,
        (
            argo_value.T,
            argo_owner.reshape(1, -1),
            argo_cell.reshape(1, -1),
            alt_value,
            alt_cell,
            alt_owner.reshape(1, -1),
        ),
    )
    message, ja_index = lax.optimization_barrier((message, lax.axis_index("ja")))
    message = lax.all_to_all(message, ("ja", "ia"), split_axis=0, concat_axis=0, tiled=True)

    ia_index = lax.axis_index("ia")
    is_top = (ja_index == count_ja - 1).astype(jnp.int32)
    parity = ja_index % 2
    flags = jnp.stack([1 - parity, parity, is_top]).astype(jnp.int32)
    fold_index = mirror - (count_ia - 1 - ia_index) * col_count
    mirror_lane = jnp.broadcast_to((fold_index % LANES)[None, :], (8, col_count))
    matrices = mixing_matrices(vinv)
    profile = jnp.pad(alt_profile.reshape(2, LEVELS, 1), ((0, 0), (0, PAD - LEVELS), (0, 0)))
    profile = profile.reshape(2 * PAD, 1)
    alt_capacity = max(2, 3 * alt_value.shape[0] // devices)
    coast = (land_mask, coef_north, coef_east)
    rows = row_count // 2
    lower = [matrices[:, :rows], matrices[:, rows:]]
    odd_device = parity == 1
    half_matrices = [
        jnp.where(odd_device, lower[0], lower[1]),
        jnp.where(odd_device, lower[1], lower[0]),
    ]

    ring_east = [(i, (i + 1) % count_ia) for i in range(count_ia)]
    ring_west = [((i + 1) % count_ia, i) for i in range(count_ia)]
    even_swap = []
    odd_swap = []
    for ja in range(count_ja):
        for ia in range(count_ia):
            here = ja * count_ia + ia
            even_swap.append((here, (ja ^ 1) * count_ia + ia))
            if ja == count_ja - 1:
                odd_swap.append((here, ja * count_ia + count_ia - 1 - ia))
            elif ja > 0:
                odd_swap.append((here, (((ja - 1) ^ 1) + 1) * count_ia + ia))
    swaps = (even_swap, odd_swap)

    def swap(which, edge):
        return lax.ppermute(edge, ("ja", "ia"), swaps[which])

    def pass_columns(cols):
        return lax.ppermute(cols, "ia", ring_east), lax.ppermute(cols, "ia", ring_west)

    near_edge, *prepared = first_forcing(
        capacity, alt_capacity, group, flags, message, profile, coast
    )
    near_edge = swap(NEAR, near_edge)
    state, far_edge, cols = rest_forcing(flags, profile, coast, prepared)
    near = far = state
    sides = pass_columns(cols)
    far_edge = swap(FAR, far_edge)
    near_coef = edge_weights(NEAR, flags, coast, (near_edge, *sides), mirror_lane)
    far_coef = edge_weights(FAR, flags, coast, (far_edge, *sides), mirror_lane)
    near_fixed = (mirror_lane, near_coef, half_matrices[NEAR])
    far_fixed = (mirror_lane, far_coef, half_matrices[FAR])
    for sweep in range(ITERS - 1):
        new_near, new_edge, cols = diffuse(
            NEAR, flags, near, far, (near_edge, *sides), *near_fixed, cols
        )
        near_edge = swap(NEAR, new_edge)
        sides = pass_columns(cols)
        far, new_edge, cols = diffuse(FAR, flags, far, near, (far_edge, *sides), *far_fixed)
        far_edge = swap(FAR, new_edge)
        near = new_near
    last_sides = pass_columns(cols)
    output = diffuse_last(
        NEAR, flags, near, far, (near_edge, *sides), *near_fixed, land_mask, None
    )
    return diffuse_last(
        FAR, flags, far, near, (far_edge, *last_sides), *far_fixed, land_mask, output
    )


def solution(mesh):
    in_specs = (
        P(("ja", "ia"), None),
        P(("ja", "ia"), None),
        P(("ja", "ia")),
        P(("ja", "ia")),
        P(("ja", "ia"), None),
        P(("ja", "ia")),
        P(),
        P("ja", "ia"),
        P("ja", "ia"),
        P("ja", "ia"),
        P("ia"),
        P("ja", None, None, None),
    )
    out_specs = P(None, "ja", "ia")
    return jax.shard_map(body, mesh=mesh, in_specs=in_specs, out_specs=out_specs, check_vma=False)
```

```python
import math

import jax
import jax.numpy as jnp
from jax import lax
from jax.experimental import pallas as pl
from jax.experimental.pallas import tpu as pltpu
from jax.sharding import PartitionSpec as P

ITERS = 3
LEVELS = 75
PAD = 80
LANES = 128
NEAR, FAR, TOP = 0, 1, 2
BF = jnp.bfloat16
F32 = jnp.float32
MIB = 1024 * 1024


def round_up(value, unit):
    return (value + unit - 1) // unit * unit


def split_two(value):
    high = value.astype(BF)
    low = (value - high.astype(F32)).astype(BF)
    return high, low


def mm(left, right):
    return jnp.dot(left, right, preferred_element_type=F32)


def as_column(row):
    return jnp.broadcast_to(row, (8, row.shape[1])).T[:, 0:1]


def slot_ranks(owner_row, cell_row, devices, col_count, row_count, capacity, spread):
    count = owner_row.shape[1]
    owner = owner_row.astype(F32)
    inside = cell_row // col_count
    order = lax.broadcasted_iota(jnp.int32, (1, count), 1).astype(F32)
    key = (owner * float(row_count) + inside.astype(F32)) * float(count) + order
    key_col = as_column(key)
    device = lax.broadcasted_iota(jnp.int32, (devices, 1), 0)
    mine = device == owner_row
    totals = jnp.sum(jnp.where(mine, 1.0, 0.0), axis=1, keepdims=True)
    rank = -jnp.sum(jnp.where(device < owner_row, totals, 0.0), axis=0, keepdims=True)
    for start in range(0, count, 128):
        before = jnp.where(key_col[start : start + 128] < key, 1.0, 0.0)
        rank = rank + jnp.sum(before, axis=0, keepdims=True)
    if spread:
        total = jnp.sum(jnp.where(mine, totals, 0.0), axis=0, keepdims=True)
        offset = owner * 1024.0
        goal = (inside * capacity // row_count).astype(F32) - rank + offset
        goal_col = as_column(goal)
        shift = offset
        for start in range(0, count, 128):
            within = key_col[start : start + 128] <= key
            reached = jnp.where(within, goal_col[start : start + 128], 0.0)
            shift = jnp.maximum(shift, jnp.max(reached, axis=0, keepdims=True))
        rank = rank + jnp.minimum(shift - offset, float(capacity) - total)
    return rank


def table_kernel(
    devices,
    capacity,
    group,
    row_count,
    col_count,
    value_ref,
    owner_ref,
    cell_ref,
    alt_value_ref,
    alt_cell_ref,
    alt_owner_ref,
    message_ref,
    level_ref,
    side_ref,
    hi_ref,
    lo_ref,
    alt_all_ref,
    rank_hot_ref,
    alt_rank_hot_ref,
):
    index = pl.program_id(0)
    n_obs = owner_ref.shape[1]
    n_alt = alt_owner_ref.shape[1]

    @pl.when(index == 0)
    def _():
        slot = lax.broadcasted_iota(jnp.int32, (capacity, 1), 0).astype(F32)
        alt_cell = alt_cell_ref[...].reshape(1, n_alt)
        rank = slot_ranks(
            owner_ref[...], cell_ref[...], devices, col_count, row_count, capacity, True
        )
        rank_hot_ref[...] = jnp.where(slot == rank, 1.0, 0.0).astype(BF)
        rank = slot_ranks(
            alt_owner_ref[...], alt_cell, devices, col_count, row_count, capacity, False
        )
        alt_rank_hot_ref[...] = jnp.where(slot == rank, 1.0, 0.0).astype(BF)
        level_ref[...] = jnp.zeros(level_ref.shape, F32)
        level_ref[0:75, :] = value_ref[0:75, :]
        level_ref[75:76, :] = cell_ref[...].astype(F32) + 1.0
        level_ref[80:128, :] = value_ref[75:123, :]
        for lane_group in range(4):
            level_ref[128 + 32 * lane_group : 155 + 32 * lane_group, :] = value_ref[123:150, :]
        high, low = split_two(level_ref[...].T)
        hi_ref[...] = high
        lo_ref[...] = low
        side_ref[...] = jnp.zeros(side_ref.shape, F32)
        pair = jnp.concatenate(
            [alt_value_ref[...].reshape(1, n_alt), alt_cell.astype(F32) + 1.0], axis=0
        )
        pair_high = pair.astype(BF).astype(F32)
        side_ref[76:78, :] = pair_high
        side_ref[78:80, :] = pair - pair_high
        alt_all_ref[...] = side_ref[...].T.astype(BF)

    per_step = message_ref.shape[0]
    chosen = []
    chosen_alt = []
    for member in range(per_step):
        device = index * per_step + member
        mask = jnp.where(owner_ref[...] == device, 1.0, 0.0).astype(BF)
        chosen.append(rank_hot_ref[...] * mask)
        mask = jnp.where(alt_owner_ref[...] == device, 1.0, 0.0).astype(BF)
        chosen_alt.append(alt_rank_hot_ref[...] * mask)
    chosen = jnp.concatenate(chosen, axis=0)
    chosen_alt = jnp.concatenate(chosen_alt, axis=0)
    table = mm(chosen, hi_ref[...]) + mm(chosen, lo_ref[...])
    lane = lax.broadcasted_iota(jnp.int32, (1, LANES), 1)
    extra = mm(chosen_alt, alt_all_ref[...])
    extra = jnp.where(lane < 78, extra + pltpu.roll(extra, LANES - 2, 1), 0.0)
    extra = jnp.where(lane >= 76, extra, 0.0)
    first = table[:, :LANES] + extra
    message_ref[:, 0:capacity] = first.reshape(per_step, capacity, LANES)
    rest = table[:, LANES:].reshape(per_step, capacity, LANES)
    total = jnp.zeros((per_step, group, LANES), F32)
    for lane_group in range(4):
        low_slot = lane_group * group
        if low_slot >= capacity:
            continue
        piece = rest[:, low_slot : low_slot + group]
        here = (lane // 32 == lane_group).reshape(1, 1, LANES)
        total = jnp.where(here, piece, total)
    message_ref[:, capacity : capacity + group] = total


def send_tables(devices, capacity, group, row_count, col_count, operands):
    n_obs = operands[1].shape[1]
    n_alt = operands[5].shape[1]
    per_step = max(1, 768 // capacity)

    def kernel(*refs):
        table_kernel(devices, capacity, group, row_count, col_count, *refs)

    def whole(array):
        return pl.BlockSpec(array.shape, lambda s: (0,) * len(array.shape))

    return pl.pallas_call(
        kernel,
        grid=(devices // per_step,),
        in_specs=[whole(x) for x in operands],
        out_specs=pl.BlockSpec((per_step, capacity + group, LANES), lambda s: (s, 0, 0)),
        out_shape=jax.ShapeDtypeStruct((devices, capacity + group, LANES), F32),
        scratch_shapes=[
            pltpu.VMEM((2 * LANES, n_obs), F32),
            pltpu.VMEM((LANES, n_alt), F32),
            pltpu.VMEM((n_obs, 2 * LANES), BF),
            pltpu.VMEM((n_obs, 2 * LANES), BF),
            pltpu.VMEM((n_alt, LANES), BF),
            pltpu.VMEM((capacity, n_obs), BF),
            pltpu.VMEM((capacity, n_alt), BF),
        ],
        compiler_params=pltpu.CompilerParams(vmem_limit_bytes=56 * MIB),
        name="send_tables",
    )(*operands)


def column_lane(which, rows, field, east, row):
    return (4 * which + 2 * field + east) * rows + row


def columns_of(which, state_ref, cols):
    rows = state_ref.shape[0]
    lane = lax.broadcasted_iota(jnp.int32, (1, LANES), 1)
    for row in range(rows):
        for field in range(2):
            part = state_ref[row, field * PAD : (field + 1) * PAD, :]
            at = column_lane(which, rows, field, 0, row)
            cols = jnp.where(lane == at, pltpu.roll(part[:, :LANES], at, 1), cols)
            at = column_lane(which, rows, field, 1, row)
            cols = jnp.where(lane == at, pltpu.roll(part[:, -LANES:], at + 1, 1), cols)
    return cols


def pack_row(row_ref, edge_ref):
    edge_ref[0:LEVELS] = row_ref[0:LEVELS]
    edge_ref[LEVELS : 2 * LEVELS] = row_ref[PAD : PAD + LEVELS]
    edge_ref[2 * LEVELS : 2 * LEVELS + 2] = row_ref[LEVELS : LEVELS + 2]


def unpack_row(edge, row_ref, piece):
    row_ref[0:LEVELS, piece] = edge[0:LEVELS]
    row_ref[PAD : PAD + LEVELS, piece] = edge[LEVELS : 2 * LEVELS]
    for at in (LEVELS, PAD + LEVELS):
        row_ref[at : at + PAD - LEVELS, piece] = jnp.zeros((PAD - LEVELS, edge.shape[1]), F32)


def write_edge(is_upper, state_ref, edge_ref):
    pack_row(state_ref.at[jnp.where(is_upper, state_ref.shape[0] - 1, 0)], edge_ref)


def prepare(capacity, alt_capacity, group, col_count, message_ref, sea_ref, left_ref, hot_ref, rows_ref, bound_ref):
    row_count = sea_ref.shape[0]
    devices = message_ref.shape[0]
    block = min(32, devices)
    members = block * 8
    octets = capacity // 8
    alt_octets = (alt_capacity + 7) // 8
    per_group = group // 8
    shift = col_count.bit_length() - 1
    col_iota = lax.broadcasted_iota(jnp.int32, (1, col_count), 1)
    row_iota = lax.broadcasted_iota(jnp.int32, (row_count, 1), 0)

    def chunk(index, start):
        return message_ref[index * block : (index + 1) * block, start : start + 8, :].reshape(
            members, LANES
        )

    def hot_of(cell):
        return jnp.where(((cell - 1) & (col_count - 1)) == col_iota, 1.0, 0.0).astype(BF)

    def rows_of(cell):
        return lax.shift_right_arithmetic(cell - 1, shift)

    sea = jnp.zeros((row_count, col_count), F32)
    count = 0
    for index in range(devices // block):
        tails = [chunk(index, capacity + 8 * part).T for part in range(per_group)]
        for octet in range(octets):
            table = chunk(index, 8 * octet)
            turned = table.T
            tail = tails[octet % per_group]
            begin = 32 * (octet // per_group)
            levels = jnp.concatenate([turned, tail[begin : begin + 32]], axis=0)
            high, low = split_two(levels)
            left_ref[count, :, 0:members] = high
            left_ref[count, :, members : 2 * members] = low
            hot = hot_of(table[:, 75:76].astype(jnp.int32))
            hot_ref[count] = hot
            rows = rows_of(turned[75:76].astype(jnp.int32))
            rows_ref[count] = jnp.broadcast_to(rows, (8, members))
            bound_ref[2 * count] = jnp.min(jnp.where(rows >= 0, rows, row_count))
            bound_ref[2 * count + 1] = jnp.max(rows)
            count += 1
            if octet >= alt_octets:
                continue
            alt_hot = hot_of(table[:, 77:78].astype(jnp.int32))
            alt_rows = rows_of(turned[77:78].astype(jnp.int32))
            weighted = jnp.where(alt_rows == row_iota, turned[76:77], 0.0)
            high, low = split_two(weighted)
            product = mm(jnp.concatenate([high, low], axis=0), alt_hot)
            sea = sea + product[:row_count] + product[row_count:]
    sea_ref[...] = sea


def chosen_rows(number, here, row, span, left_ref, hot_ref):
    pieces = []
    for offset in range(span):
        mask = jnp.where(here == row + offset, 1.0, 0.0).astype(BF)
        pieces.append(left_ref[number] * jnp.concatenate([mask, mask], axis=1))
    hot = hot_ref[number]
    return mm(jnp.concatenate(pieces, axis=0), jnp.concatenate([hot, hot], axis=0))


def outer_forcing(row, is_upper, profile_ref, coast_refs, sea_ref, left_ref, hot_ref, rows_ref, bound_ref, edge_ref):
    row_count, col_count = sea_ref.shape
    last = row_count - 1
    profile = jnp.broadcast_to(profile_ref[...], (2 * PAD, LANES))
    sea = jnp.where(is_upper, sea_ref[last : last + 1, :], sea_ref[0:1, :])
    for start in range(0, col_count, LANES):
        edge_ref[:, start : start + LANES] = profile * sea[:, start : start + LANES]

    def step(number, carry):
        @pl.when((bound_ref[2 * number] <= row) & (row <= bound_ref[2 * number + 1]))
        def _():
            edge_ref[...] += chosen_rows(number, rows_ref[number][0:1], row, 1, left_ref, hot_ref)

        return carry

    lax.fori_loop(0, left_ref.shape[0], step, 0)
    for kind, coast_ref in enumerate(coast_refs):
        coast = jnp.where(is_upper, coast_ref[last : last + 1, :], coast_ref[0:1, :])
        edge_ref[LEVELS + kind : LEVELS + kind + 1, :] = coast.astype(F32)


def all_forcing(profile_ref, coast_refs, sea_ref, left_ref, hot_ref, rows_ref, bound_ref, state):
    row_count, _, col_count = state.shape
    count = left_ref.shape[0]
    for start in range(0, col_count, LANES):
        profile = jnp.broadcast_to(profile_ref[...], (2 * PAD, LANES))
        for row in range(row_count):
            state[row, :, start : start + LANES] = profile * sea_ref[row : row + 1, start : start + LANES]
    span = 3
    batch = math.gcd(count, 4)

    def step(number, carry):
        chunks = [number * batch + member for member in range(batch)]
        least = [bound_ref[2 * chunk] for chunk in chunks]
        most = [bound_ref[2 * chunk + 1] for chunk in chunks]
        runs = [lax.div(most[i] - least[i] + span, span) for i in range(batch)]
        longest = runs[0]
        for run in runs[1:]:
            longest = jnp.maximum(longest, run)

        def run_step(turn, inner):
            for i, chunk in enumerate(chunks):
                begin = least[i] + turn * span
                base = jnp.minimum(begin, row_count - span)
                here = rows_ref[chunk][0:1]
                here = jnp.where(here >= begin, here, -1)
                product = chosen_rows(chunk, here, base, span, left_ref, hot_ref)
                for offset in range(span):
                    state[base + offset] += product[2 * PAD * offset : 2 * PAD * (offset + 1)]
            return inner

        lax.fori_loop(0, longest, run_step, 0)
        return carry

    lax.fori_loop(0, count // batch, step, 0)
    for kind, coast_ref in enumerate(coast_refs):
        coast = coast_ref[...].astype(F32)
        for row in range(row_count):
            state[row, LEVELS + kind : LEVELS + kind + 1, :] = coast[row : row + 1, :]


def half_shapes(row_count, col_count):
    return (
        jax.ShapeDtypeStruct((row_count // 2, 2 * PAD, col_count), F32),
        jax.ShapeDtypeStruct((2 * LEVELS + 2, col_count), F32),
        jax.ShapeDtypeStruct((PAD, LANES), F32),
    )


def in_place(count):
    return [pl.BlockSpec(memory_space=pltpu.SMEM)] + [pl.BlockSpec(memory_space=pltpu.VMEM)] * count


def first_forcing(capacity, alt_capacity, group, flags, message, profile, coast):
    row_count, col_count = coast[0].shape
    devices = message.shape[0]
    members = min(32, devices) * 8
    chunks = capacity // 8 * (devices // min(32, devices))

    def kernel(flag_ref, message_ref, profile_ref, wet, north, east, edge_ref, *refs):
        *outs, row_ref = refs
        prepare(capacity, alt_capacity, group, col_count, message_ref, *outs)
        is_upper = flag_ref[NEAR] > 0
        row = jnp.where(is_upper, row_count - 1, 0)
        outer_forcing(row, is_upper, profile_ref, (wet, north, east), *outs, row_ref)
        pack_row(row_ref, edge_ref)

    return pl.pallas_call(
        kernel,
        in_specs=in_place(5),
        out_shape=(
            half_shapes(row_count, col_count)[1],
            jax.ShapeDtypeStruct((row_count, col_count), F32),
            jax.ShapeDtypeStruct((chunks, 2 * PAD, 2 * members), BF),
            jax.ShapeDtypeStruct((chunks, members, col_count), BF),
            jax.ShapeDtypeStruct((chunks, 8, members), jnp.int32),
            jax.ShapeDtypeStruct((2 * chunks,), jnp.int32),
        ),
        out_specs=[pl.BlockSpec(memory_space=pltpu.VMEM)] * 5
        + [pl.BlockSpec(memory_space=pltpu.SMEM)],
        scratch_shapes=[pltpu.VMEM((2 * PAD, col_count), F32)],
        compiler_params=pltpu.CompilerParams(vmem_limit_bytes=24 * MIB),
        cost_estimate=pl.CostEstimate(
            flops=6_000_000_000, bytes_accessed=8_000_000, transcendentals=0
        ),
        name="forcing_first",
    )(flags, message, profile, *coast)


def rest_forcing(flags, profile, coast, prepared):
    row_count, col_count = coast[0].shape
    half = row_count // 2

    def kernel(flag_ref, profile_ref, wet, north, east, sea, left, hot, rows, bound, state, edge_ref, cols_ref):
        all_forcing(profile_ref, (wet, north, east), sea, left, hot, rows, bound, state)
        cols = jnp.zeros((PAD, LANES), F32)
        for which in (NEAR, FAR):
            first_row = jnp.where(flag_ref[which] > 0, half, 0)
            cols = columns_of(which, state.at[pl.ds(first_row, half)], cols)
        cols_ref[...] = cols
        write_edge(flag_ref[FAR] > 0, state, edge_ref)

    _, edge, cols = half_shapes(row_count, col_count)
    state = jax.ShapeDtypeStruct((row_count, 2 * PAD, col_count), F32)
    return pl.pallas_call(
        kernel,
        in_specs=in_place(8) + [pl.BlockSpec(memory_space=pltpu.SMEM)],
        out_shape=(state, edge, cols),
        compiler_params=pltpu.CompilerParams(vmem_limit_bytes=20 * MIB),
        cost_estimate=pl.CostEstimate(
            flops=6_000_000_000, bytes_accessed=8_000_000, transcendentals=0
        ),
        name="forcing_rest",
    )(flags, profile, *coast, *prepared)


def fold_row(row_ref, mirror_ref, piece, chunk, chunks, rows):
    index = jnp.broadcast_to(mirror_ref[0:1, piece(chunk)], (rows, LANES))
    return jnp.take_along_axis(row_ref[:, piece(chunks - 1 - chunk)], index, axis=1)


def weight_kernel(which, flag_ref, wet_ref, north_ref, east_ref, edge_in, west_in, east_in, mirror_ref, out_ref, fold_ref):
    row_count, col_count = wet_ref.shape
    rows = row_count // 2
    is_upper = flag_ref[which] > 0
    at = pl.multiple_of(jnp.where(is_upper, rows, 0), 8)
    wet = wet_ref[pl.ds(at, rows), :].astype(F32)
    north = north_ref[pl.ds(at, rows), :]
    east = east_ref[pl.ds(at, rows), :]
    chunks = col_count // LANES
    lane = lax.broadcasted_iota(jnp.int32, (1, col_count), 1)
    start = column_lane(which, rows, 0, 1, 0)
    west_cols = west_in[72:80, :].T[start : start + rows]
    start = column_lane(which, rows, 0, 0, 0)
    east_cols = east_in[72:80, :].T[start : start + rows]
    west_wet = jnp.where(lane == 0, west_cols[:, 3:4], pltpu.roll(wet, 1, 1))
    west_coef = jnp.where(lane == 0, west_cols[:, 5:6], pltpu.roll(east, 1, 1))
    east_wet = jnp.where(
        lane == col_count - 1, east_cols[:, 3:4], pltpu.roll(wet, col_count - 1, 1)
    )
    east_w = east * wet * east_wet
    west_w = west_coef * west_wet * wet

    def piece(c):
        return slice(c * LANES, (c + 1) * LANES)

    spare_ref = edge_in.at[2 * LEVELS - 6 : 2 * LEVELS + 2]
    if which == FAR:
        for c in range(chunks):
            fold_ref[:, piece(c)] = fold_row(spare_ref, mirror_ref, piece, c, chunks, 8)
    spare = spare_ref[...]
    last = rows - 1
    inner_wet = jnp.where(
        is_upper, wet_ref[rows - 1 : rows, :], wet_ref[rows : rows + 1, :]
    ).astype(F32)
    above = jnp.where(is_upper, spare[6:7], inner_wet)
    top_w = north[last:] * wet[last:] * above
    if which == FAR:
        fold = 0.5 * (north[last:] + fold_ref[7:8]) * wet[last:] * fold_ref[6:7]
        top_w = jnp.where(flag_ref[TOP] > 0, fold, top_w)
    below = jnp.where(is_upper, north_ref[rows - 1 : rows, :] * inner_wet, spare[7:8] * spare[6:7])
    between = north[:last] * wet[:last] * wet[1:]
    north_w = jnp.concatenate([between, top_w], axis=0)
    south_w = jnp.concatenate([below * wet[0:1], between], axis=0)
    center = 1.0 - (east_w + west_w + north_w + south_w)
    for kind, weight in enumerate((center, east_w, west_w, north_w, south_w)):
        for row in range(rows):
            out_ref[row, kind : kind + 1, :] = weight[row : row + 1]


def edge_weights(which, flags, coast, received, mirror):
    row_count, col_count = coast[0].shape

    def kernel(*refs):
        weight_kernel(which, *refs)

    return pl.pallas_call(
        kernel,
        in_specs=in_place(7),
        out_shape=jax.ShapeDtypeStruct((row_count // 2, 8, col_count), F32),
        scratch_shapes=[pltpu.VMEM((8, col_count), F32)],
        compiler_params=pltpu.CompilerParams(vmem_limit_bytes=16 * MIB),
        name="edge_weights",
    )(flags, *coast, *received, mirror)


def receive_row(which, flag_ref, edge_in, mirror_ref, row_ref):
    levels, col_count = edge_in.shape
    chunks = col_count // LANES
    is_top = flag_ref[TOP] > 0

    def piece(c):
        return slice(c * LANES, (c + 1) * LANES)

    def plain():
        for c in range(chunks):
            unpack_row(edge_in[:, piece(c)], row_ref, piece(c))

    if which == NEAR:
        plain()
        return

    @pl.when(jnp.logical_not(is_top))
    def _():
        plain()

    @pl.when(is_top)
    def _():
        for c in range(chunks):
            unpack_row(
                fold_row(edge_in, mirror_ref, piece, c, chunks, levels), row_ref, piece(c)
            )


def neighbour_rows(is_upper, inner, outer_ref, south_ref, north_ref):
    @pl.when(is_upper)
    def _():
        south_ref[...] = inner[...]
        north_ref[...] = outer_ref[...]

    @pl.when(jnp.logical_not(is_upper))
    def _():
        south_ref[...] = outer_ref[...]
        north_ref[...] = inner[...]


def mix_row(which, row, rows, field, state_ref, south_ref, north_ref, west_in, east_in, coef_ref, right_ref, slot):
    col_count = state_ref.shape[2]
    chunks = col_count // LANES
    lane = lax.broadcasted_iota(jnp.int32, (1, LANES), 1)
    levels = slice(field * PAD, (field + 1) * PAD)

    def piece(chunk):
        return slice(chunk * LANES, (chunk + 1) * LANES)

    west_lane = column_lane(which, rows, field, 1, row)
    east_lane = column_lane(which, rows, field, 0, row)
    centers = [state_ref[row, levels, piece(c)] for c in range(chunks)]
    to_left = [pltpu.roll(c, LANES - 1, 1) for c in centers]
    to_right = [pltpu.roll(c, 1, 1) for c in centers]
    to_right.append(pltpu.roll(west_in[...], LANES - west_lane, 1))
    to_left.append(pltpu.roll(east_in[...], LANES - 1 - east_lane, 1))
    for c in range(chunks):
        south = south_ref[levels, piece(c)]
        north = north_ref[levels, piece(c)]
        east = jnp.where(lane == LANES - 1, to_left[c + 1], to_left[c])
        west = jnp.where(lane == 0, to_right[c - 1], to_right[c])

        def coef(kind):
            return coef_ref[row, kind : kind + 1, piece(c)]

        mixed = (
            coef(0) * centers[c]
            + coef(1) * east
            + coef(2) * west
            + coef(3) * north
            + coef(4) * south
        )
        high, low = split_two(mixed)
        right_ref[slot, 0:PAD, piece(c)] = high
        right_ref[slot, PAD : 2 * PAD, piece(c)] = low
        right_ref[slot, 2 * PAD : 3 * PAD, piece(c)] = high


def sweep_rows(which, rows, units, state_ref, south_ref, north_ref, west_in, east_in, coef_ref, matrix_ref, right_ref, emit):
    slots = right_ref.shape[0]
    right_ref[:, 3 * PAD :, :] = jnp.zeros((slots,) + (256 - 3 * PAD, right_ref.shape[2]), BF)

    def product(number):
        row, field = units[number]
        emit(number, row, field, mm(matrix_ref[field, row], right_ref[number % slots]))

    for number, (row, field) in enumerate(units):
        south = state_ref.at[row - 1] if row > 0 else south_ref
        north = state_ref.at[row + 1] if row < rows - 1 else north_ref
        mix_row(which, row, rows, field, state_ref, south, north, west_in, east_in, coef_ref, right_ref, number % slots)
        if number > 0:
            product(number - 1)
    product(len(units) - 1)


def diffuse(which, flags, state, other, received, mirror, coef, matrix, *far_cols):
    rows = coef.shape[0]
    col_count = state.shape[2]

    def kernel(flag_ref, state_ref, other_ref, edge_in, west_in, east_in, mirror_ref, coef_ref, matrix_ref, *refs):
        out_ref, edge_ref, cols_ref, south_ref, north_ref, outer_ref, right_ref = refs[-7:]
        is_upper = flag_ref[which] > 0
        if state.shape[0] > rows:
            state_ref = state_ref.at[pl.ds(jnp.where(is_upper, rows, 0), rows)]
            inner = other_ref.at[jnp.where(is_upper, rows - 1, rows)]
        else:
            inner = other_ref.at[jnp.where(is_upper, rows - 1, 0)]
        receive_row(which, flag_ref, edge_in, mirror_ref, outer_ref)
        neighbour_rows(is_upper, inner, outer_ref, south_ref, north_ref)

        def emit(number, row, field, result):
            out_ref[row, field * PAD : (field + 1) * PAD] = result

        units = [(row, field) for row in range(rows) for field in range(2)]
        sweep_rows(which, rows, units, state_ref, south_ref, north_ref, west_in, east_in, coef_ref, matrix_ref, right_ref, emit)
        write_edge(is_upper, out_ref, edge_ref)
        old_cols = refs[0][...] if which == NEAR else jnp.zeros((PAD, LANES), F32)
        cols_ref[...] = columns_of(which, out_ref, old_cols)

    return pl.pallas_call(
        kernel,
        in_specs=in_place(8 + len(far_cols)),
        out_shape=half_shapes(2 * rows, col_count),
        scratch_shapes=[pltpu.VMEM((2 * PAD, col_count), F32)] * 3
        + [pltpu.VMEM((4, 256, col_count), BF)],
        compiler_params=pltpu.CompilerParams(vmem_limit_bytes=16 * MIB),
        cost_estimate=pl.CostEstimate(
            flops=3_000_000_000, bytes_accessed=8_000_000, transcendentals=0
        ),
        name="diffusion_" + ("near", "far")[which],
    )(flags, state, other, *received, mirror, coef, matrix, *far_cols)


def store_block(results, out_ref, stage_ref, sem, at, field):
    rows = stage_ref.shape[2]
    stage_ref[field] = jnp.swapaxes(jnp.stack(results), 0, 1)[:LEVELS]
    copy = pltpu.make_async_copy(
        stage_ref.at[field],
        out_ref.at[pl.ds(field * LEVELS, LEVELS), pl.ds(at, rows), :],
        sem.at[field],
    )
    copy.start()
    return copy


def last_inner(flags, near, far, near_edge, near_sides, far_sides, mirror, near_fixed, far_fixed, mask):
    rows, _, col_count = near.shape

    def kernel(flag_ref, near_ref, far_ref, edge_in, near_west, near_east, far_west, far_east, mirror_ref, near_coef, near_matrix, far_coef, far_matrix, mask_ref, out_ref, done_ref, south_ref, north_ref, outer_ref, right_ref, stage_ref, sem):
        is_upper = flag_ref[NEAR] > 0
        at = pl.multiple_of(jnp.where(is_upper, rows, 0), 8)
        wet = mask_ref[pl.ds(at, rows), :].astype(F32)
        far_at = pl.multiple_of(rows - at, 8)
        far_wet = mask_ref[pl.ds(far_at, rows), :].astype(F32)
        last = rows - 1
        far_inner = far_ref.at[jnp.where(is_upper, last, 0)]
        receive_row(NEAR, flag_ref, edge_in, mirror_ref, outer_ref)
        neighbour_rows(is_upper, far_inner, outer_ref, south_ref, north_ref)
        copies = []
        for field in range(2):
            results = []

            def emit(number, row, field, result):
                results.append(result * wet[row : row + 1])

            units = [(row, field) for row in range(rows)]
            sweep_rows(NEAR, rows, units, near_ref, south_ref, north_ref, near_west, near_east, near_coef, near_matrix, right_ref, emit)
            copies.append(store_block(results, out_ref, stage_ref, sem, at, field))
        edge = jnp.where(is_upper, last, 0)
        near_inner = near_ref.at[jnp.where(is_upper, 0, last)]

        @pl.when(is_upper)
        def _():
            south_ref[...] = far_ref[last - 1]
            north_ref[...] = near_inner[...]

        @pl.when(jnp.logical_not(is_upper))
        def _():
            south_ref[...] = near_inner[...]
            north_ref[...] = far_ref[1]

        def keep(number, row, field, result):
            done_ref[row, field * PAD : (field + 1) * PAD] = result * far_wet[row : row + 1]

        units = [(row, field) for row in range(1, last) for field in range(2)]
        sweep_rows(FAR, rows, units, far_ref, south_ref, north_ref, far_west, far_east, far_coef, far_matrix, right_ref, keep)
        edge_wet = jnp.where(is_upper, far_wet[last:], far_wet[0:1])
        for field in range(2):
            mix_row(FAR, edge, rows, field, far_ref, south_ref, north_ref, far_west, far_east, far_coef, right_ref, field)
        for field in range(2):
            result = mm(far_matrix[field, edge], right_ref[field])
            done_ref[edge, field * PAD : (field + 1) * PAD] = result * edge_wet
        for copy in copies:
            copy.wait()

    return pl.pallas_call(
        kernel,
        in_specs=in_place(13),
        out_specs=[pl.BlockSpec(memory_space=pl.ANY), pl.BlockSpec(memory_space=pltpu.VMEM)],
        out_shape=(
            jax.ShapeDtypeStruct((2 * LEVELS, 2 * rows, col_count), F32),
            jax.ShapeDtypeStruct((rows, 2 * PAD, col_count), F32),
        ),
        scratch_shapes=[pltpu.VMEM((2 * PAD, col_count), F32)] * 3
        + [
            pltpu.VMEM((4, 256, col_count), BF),
            pltpu.VMEM((2, LEVELS, rows, col_count), F32),
            pltpu.SemaphoreType.DMA((2,)),
        ],
        compiler_params=pltpu.CompilerParams(vmem_limit_bytes=20 * MIB),
        cost_estimate=pl.CostEstimate(
            flops=6_000_000_000, bytes_accessed=16_000_000, transcendentals=0
        ),
        name="last_inner",
    )(flags, near, far, near_edge, *near_sides, *far_sides, mirror, *near_fixed, *far_fixed, mask)


def last_outer(flags, far, far_edge, far_sides, mirror, far_fixed, mask, done, target):
    rows, _, col_count = far.shape

    def kernel(flag_ref, far_ref, edge_in, west_in, east_in, mirror_ref, coef_ref, matrix_ref, mask_ref, done_ref, target_ref, out_ref, south_ref, north_ref, outer_ref, right_ref, stage_ref, sem):
        is_upper = flag_ref[FAR] > 0
        at = pl.multiple_of(jnp.where(is_upper, rows, 0), 8)
        wet = mask_ref[pl.ds(at, rows), :].astype(F32)
        last = rows - 1
        row = jnp.where(is_upper, last, 0)
        row_wet = jnp.where(is_upper, wet[last:], wet[0:1])
        receive_row(FAR, flag_ref, edge_in, mirror_ref, outer_ref)
        neighbour_rows(is_upper, far_ref.at[jnp.where(is_upper, last - 1, 1)], outer_ref, south_ref, north_ref)
        right_ref[:, 3 * PAD :, :] = jnp.zeros((2, 256 - 3 * PAD, col_count), BF)
        for field in range(2):
            mix_row(FAR, row, rows, field, far_ref, south_ref, north_ref, west_in, east_in, coef_ref, right_ref, field)
        copies = []
        for field in range(2):
            result = mm(matrix_ref[field, row], right_ref[field]) * row_wet
            done_field = [done_ref[r, field * PAD : (field + 1) * PAD] for r in range(rows)]
            done_field[0] = jnp.where(is_upper, done_field[0], result)
            done_field[last] = jnp.where(is_upper, result, done_field[last])
            copies.append(store_block(done_field, out_ref, stage_ref, sem, at, field))
        for copy in copies:
            copy.wait()

    operands = [flags, far, far_edge, *far_sides, mirror, *far_fixed, mask, done, target]
    return pl.pallas_call(
        kernel,
        in_specs=in_place(9) + [pl.BlockSpec(memory_space=pl.ANY)],
        out_specs=pl.BlockSpec(memory_space=pl.ANY),
        out_shape=jax.ShapeDtypeStruct((2 * LEVELS, 2 * rows, col_count), F32),
        input_output_aliases={len(operands) - 1: 0},
        scratch_shapes=[pltpu.VMEM((2 * PAD, col_count), F32)] * 3
        + [
            pltpu.VMEM((2, 256, col_count), BF),
            pltpu.VMEM((2, LEVELS, rows, col_count), F32),
            pltpu.SemaphoreType.DMA((2,)),
        ],
        compiler_params=pltpu.CompilerParams(vmem_limit_bytes=20 * MIB),
        name="last_outer",
    )(*operands)


def mixing_matrices(vinv):
    turned = jnp.transpose(vinv, (1, 0, 3, 2))
    turned = jnp.pad(turned, ((0, 0), (0, 0), (0, PAD - LEVELS), (0, PAD - LEVELS)))
    high = lax.reduce_precision(turned, 8, 7)
    low = (turned - high).astype(BF)
    high = high.astype(BF)
    rest = jnp.zeros(high.shape[:3] + (256 - 3 * PAD,), BF)
    return jnp.concatenate([high, high, low, rest], axis=3)


def body(
    argo_value,
    argo_owner,
    argo_cell,
    alt_value,
    alt_owner,
    alt_cell,
    alt_profile,
    land_mask,
    coef_east,
    coef_north,
    mirror,
    vinv,
):
    row_count, col_count = land_mask.shape
    count_ja = lax.axis_size("ja")
    count_ia = lax.axis_size("ia")
    devices = count_ja * count_ia
    capacity = round_up(3 * argo_value.shape[0] // devices, 8)
    group = round_up(capacity // 4, 8)
    message = send_tables(
        devices,
        capacity,
        group,
        row_count,
        col_count,
        (
            argo_value.T,
            argo_owner.reshape(1, -1),
            argo_cell.reshape(1, -1),
            alt_value,
            alt_cell,
            alt_owner.reshape(1, -1),
        ),
    )
    message, ja_index = lax.optimization_barrier((message, lax.axis_index("ja")))
    message = lax.all_to_all(message, ("ja", "ia"), split_axis=0, concat_axis=0, tiled=True)

    ia_index = lax.axis_index("ia")
    is_top = (ja_index == count_ja - 1).astype(jnp.int32)
    parity = ja_index % 2
    flags = jnp.stack([1 - parity, parity, is_top]).astype(jnp.int32)
    fold_index = mirror - (count_ia - 1 - ia_index) * col_count
    mirror_lane = jnp.broadcast_to((fold_index % LANES)[None, :], (8, col_count))
    matrices = mixing_matrices(vinv)
    profile = jnp.pad(alt_profile.reshape(2, LEVELS, 1), ((0, 0), (0, PAD - LEVELS), (0, 0)))
    profile = profile.reshape(2 * PAD, 1)
    alt_capacity = max(2, 3 * alt_value.shape[0] // devices)
    coast = (land_mask, coef_north, coef_east)
    rows = row_count // 2
    lower = [matrices[:, :rows], matrices[:, rows:]]
    odd_device = parity == 1
    half_matrices = [
        jnp.where(odd_device, lower[0], lower[1]),
        jnp.where(odd_device, lower[1], lower[0]),
    ]

    ring_east = [(i, (i + 1) % count_ia) for i in range(count_ia)]
    ring_west = [((i + 1) % count_ia, i) for i in range(count_ia)]
    even_swap = []
    odd_swap = []
    for ja in range(count_ja):
        for ia in range(count_ia):
            here = ja * count_ia + ia
            even_swap.append((here, (ja ^ 1) * count_ia + ia))
            if ja == count_ja - 1:
                odd_swap.append((here, ja * count_ia + count_ia - 1 - ia))
            elif ja > 0:
                odd_swap.append((here, (((ja - 1) ^ 1) + 1) * count_ia + ia))
    swaps = (even_swap, odd_swap)

    def swap(which, edge):
        return lax.ppermute(edge, ("ja", "ia"), swaps[which])

    def pass_columns(cols):
        return lax.ppermute(cols, "ia", ring_east), lax.ppermute(cols, "ia", ring_west)

    near_edge, *prepared = first_forcing(
        capacity, alt_capacity, group, flags, message, profile, coast
    )
    near_edge = swap(NEAR, near_edge)
    state, far_edge, cols = rest_forcing(flags, profile, coast, prepared)
    near = far = state
    sides = pass_columns(cols)
    far_edge = swap(FAR, far_edge)
    near_coef = edge_weights(NEAR, flags, coast, (near_edge, *sides), mirror_lane)
    far_coef = edge_weights(FAR, flags, coast, (far_edge, *sides), mirror_lane)
    near_fixed = (mirror_lane, near_coef, half_matrices[NEAR])
    far_fixed = (mirror_lane, far_coef, half_matrices[FAR])
    for sweep in range(ITERS - 1):
        new_near, new_edge, cols = diffuse(
            NEAR, flags, near, far, (near_edge, *sides), *near_fixed, cols
        )
        near_edge = swap(NEAR, new_edge)
        sides = pass_columns(cols)
        far, new_edge, cols = diffuse(FAR, flags, far, near, (far_edge, *sides), *far_fixed)
        far_edge = swap(FAR, new_edge)
        near = new_near
    last_sides = pass_columns(cols)
    output, done = last_inner(
        flags, near, far, near_edge, sides, last_sides, mirror_lane, near_fixed[1:], far_fixed[1:], land_mask
    )
    return last_outer(
        flags, far, far_edge, last_sides, mirror_lane, far_fixed[1:], land_mask, done, output
    )


def solution(mesh):
    in_specs = (
        P(("ja", "ia"), None),
        P(("ja", "ia"), None),
        P(("ja", "ia")),
        P(("ja", "ia")),
        P(("ja", "ia"), None),
        P(("ja", "ia")),
        P(),
        P("ja", "ia"),
        P("ja", "ia"),
        P("ja", "ia"),
        P("ia"),
        P("ja", None, None, None),
    )
    out_specs = P(None, "ja", "ia")
    return jax.shard_map(body, mesh=mesh, in_specs=in_specs, out_specs=out_specs, check_vma=False)
```

```python
import math

import jax
import jax.numpy as jnp
from jax import lax
from jax.experimental import pallas as pl
from jax.experimental.pallas import tpu as pltpu
from jax.sharding import PartitionSpec as P

ITERS = 3
LEVELS = 75
PAD = 80
LANES = 128
NEAR, FAR, TOP = 0, 1, 2
BF = jnp.bfloat16
F32 = jnp.float32
MIB = 1024 * 1024


def round_up(value, unit):
    return (value + unit - 1) // unit * unit


def split_two(value):
    high = value.astype(BF)
    low = (value - high.astype(F32)).astype(BF)
    return high, low


def mm(left, right):
    return jnp.dot(left, right, preferred_element_type=F32)


def as_column(row):
    return jnp.broadcast_to(row, (8, row.shape[1])).T[:, 0:1]


def slot_ranks(owner_row, cell_row, devices, col_count, row_count, capacity, spread):
    count = owner_row.shape[1]
    owner = owner_row.astype(F32)
    inside = cell_row // col_count
    order = lax.broadcasted_iota(jnp.int32, (1, count), 1).astype(F32)
    key = (owner * float(row_count) + inside.astype(F32)) * float(count) + order
    key_col = as_column(key)
    device = lax.broadcasted_iota(jnp.int32, (devices, 1), 0)
    mine = device == owner_row
    totals = jnp.sum(jnp.where(mine, 1.0, 0.0), axis=1, keepdims=True)
    rank = -jnp.sum(jnp.where(device < owner_row, totals, 0.0), axis=0, keepdims=True)
    for start in range(0, count, 128):
        before = jnp.where(key_col[start : start + 128] < key, 1.0, 0.0)
        rank = rank + jnp.sum(before, axis=0, keepdims=True)
    if spread:
        total = jnp.sum(jnp.where(mine, totals, 0.0), axis=0, keepdims=True)
        offset = owner * 1024.0
        goal = (inside * capacity // row_count).astype(F32) - rank + offset
        goal_col = as_column(goal)
        shift = offset
        for start in range(0, count, 128):
            within = key_col[start : start + 128] <= key
            reached = jnp.where(within, goal_col[start : start + 128], 0.0)
            shift = jnp.maximum(shift, jnp.max(reached, axis=0, keepdims=True))
        rank = rank + jnp.minimum(shift - offset, float(capacity) - total)
    return rank


def table_kernel(
    devices,
    capacity,
    group,
    row_count,
    col_count,
    value_ref,
    owner_ref,
    cell_ref,
    alt_value_ref,
    alt_cell_ref,
    alt_owner_ref,
    message_ref,
    level_ref,
    side_ref,
    hi_ref,
    lo_ref,
    alt_all_ref,
    rank_hot_ref,
    alt_rank_hot_ref,
):
    index = pl.program_id(0)
    n_obs = owner_ref.shape[1]
    n_alt = alt_owner_ref.shape[1]

    @pl.when(index == 0)
    def _():
        slot = lax.broadcasted_iota(jnp.int32, (capacity, 1), 0).astype(F32)
        alt_cell = alt_cell_ref[...].reshape(1, n_alt)
        rank = slot_ranks(
            owner_ref[...], cell_ref[...], devices, col_count, row_count, capacity, True
        )
        rank_hot_ref[...] = jnp.where(slot == rank, 1.0, 0.0).astype(BF)
        rank = slot_ranks(
            alt_owner_ref[...], alt_cell, devices, col_count, row_count, capacity, False
        )
        alt_rank_hot_ref[...] = jnp.where(slot == rank, 1.0, 0.0).astype(BF)
        level_ref[...] = jnp.zeros(level_ref.shape, F32)
        level_ref[0:75, :] = value_ref[0:75, :]
        level_ref[75:76, :] = cell_ref[...].astype(F32) + 1.0
        level_ref[80:128, :] = value_ref[75:123, :]
        for lane_group in range(4):
            level_ref[128 + 32 * lane_group : 155 + 32 * lane_group, :] = value_ref[123:150, :]
        high, low = split_two(level_ref[...].T)
        hi_ref[...] = high
        lo_ref[...] = low
        side_ref[...] = jnp.zeros(side_ref.shape, F32)
        pair = jnp.concatenate(
            [alt_value_ref[...].reshape(1, n_alt), alt_cell.astype(F32) + 1.0], axis=0
        )
        pair_high = pair.astype(BF).astype(F32)
        side_ref[76:78, :] = pair_high
        side_ref[78:80, :] = pair - pair_high
        alt_all_ref[...] = side_ref[...].T.astype(BF)

    per_step = message_ref.shape[0]
    chosen = []
    chosen_alt = []
    for member in range(per_step):
        device = index * per_step + member
        mask = jnp.where(owner_ref[...] == device, 1.0, 0.0).astype(BF)
        chosen.append(rank_hot_ref[...] * mask)
        mask = jnp.where(alt_owner_ref[...] == device, 1.0, 0.0).astype(BF)
        chosen_alt.append(alt_rank_hot_ref[...] * mask)
    chosen = jnp.concatenate(chosen, axis=0)
    chosen_alt = jnp.concatenate(chosen_alt, axis=0)
    table = mm(chosen, hi_ref[...]) + mm(chosen, lo_ref[...])
    lane = lax.broadcasted_iota(jnp.int32, (1, LANES), 1)
    extra = mm(chosen_alt, alt_all_ref[...])
    extra = jnp.where(lane < 78, extra + pltpu.roll(extra, LANES - 2, 1), 0.0)
    extra = jnp.where(lane >= 76, extra, 0.0)
    first = table[:, :LANES] + extra
    message_ref[:, 0:capacity] = first.reshape(per_step, capacity, LANES)
    rest = table[:, LANES:].reshape(per_step, capacity, LANES)
    total = jnp.zeros((per_step, group, LANES), F32)
    for lane_group in range(4):
        low_slot = lane_group * group
        if low_slot >= capacity:
            continue
        piece = rest[:, low_slot : low_slot + group]
        here = (lane // 32 == lane_group).reshape(1, 1, LANES)
        total = jnp.where(here, piece, total)
    message_ref[:, capacity : capacity + group] = total


def send_tables(devices, capacity, group, row_count, col_count, operands):
    n_obs = operands[1].shape[1]
    n_alt = operands[5].shape[1]
    per_step = max(1, 768 // capacity)

    def kernel(*refs):
        table_kernel(devices, capacity, group, row_count, col_count, *refs)

    def whole(array):
        return pl.BlockSpec(array.shape, lambda s: (0,) * len(array.shape))

    return pl.pallas_call(
        kernel,
        grid=(devices // per_step,),
        in_specs=[whole(x) for x in operands],
        out_specs=pl.BlockSpec((per_step, capacity + group, LANES), lambda s: (s, 0, 0)),
        out_shape=jax.ShapeDtypeStruct((devices, capacity + group, LANES), F32),
        scratch_shapes=[
            pltpu.VMEM((2 * LANES, n_obs), F32),
            pltpu.VMEM((LANES, n_alt), F32),
            pltpu.VMEM((n_obs, 2 * LANES), BF),
            pltpu.VMEM((n_obs, 2 * LANES), BF),
            pltpu.VMEM((n_alt, LANES), BF),
            pltpu.VMEM((capacity, n_obs), BF),
            pltpu.VMEM((capacity, n_alt), BF),
        ],
        compiler_params=pltpu.CompilerParams(vmem_limit_bytes=56 * MIB),
        name="send_tables",
    )(*operands)


def column_lane(which, rows, field, east, row):
    return (4 * which + 2 * field + east) * rows + row


def columns_of(which, state_ref, cols):
    rows = state_ref.shape[0]
    lane = lax.broadcasted_iota(jnp.int32, (1, LANES), 1)
    for row in range(rows):
        for field in range(2):
            part = state_ref[row, field * PAD : (field + 1) * PAD, :]
            at = column_lane(which, rows, field, 0, row)
            cols = jnp.where(lane == at, pltpu.roll(part[:, :LANES], at, 1), cols)
            at = column_lane(which, rows, field, 1, row)
            cols = jnp.where(lane == at, pltpu.roll(part[:, -LANES:], at + 1, 1), cols)
    return cols


def pack_row(row_ref, edge_ref):
    edge_ref[0:LEVELS] = row_ref[0:LEVELS]
    edge_ref[LEVELS : 2 * LEVELS] = row_ref[PAD : PAD + LEVELS]
    edge_ref[2 * LEVELS : 2 * LEVELS + 2] = row_ref[LEVELS : LEVELS + 2]


def unpack_row(edge, row_ref, piece):
    row_ref[0:LEVELS, piece] = edge[0:LEVELS]
    row_ref[PAD : PAD + LEVELS, piece] = edge[LEVELS : 2 * LEVELS]
    for at in (LEVELS, PAD + LEVELS):
        row_ref[at : at + PAD - LEVELS, piece] = jnp.zeros((PAD - LEVELS, edge.shape[1]), F32)


def write_edge(is_upper, state_ref, edge_ref):
    pack_row(state_ref.at[jnp.where(is_upper, state_ref.shape[0] - 1, 0)], edge_ref)


def prepare(capacity, alt_capacity, group, col_count, message_ref, sea_ref, left_ref, hot_ref, rows_ref, bound_ref):
    row_count = sea_ref.shape[0]
    devices = message_ref.shape[0]
    block = min(32, devices)
    members = block * 8
    octets = capacity // 8
    alt_octets = (alt_capacity + 7) // 8
    per_group = group // 8
    shift = col_count.bit_length() - 1
    col_iota = lax.broadcasted_iota(jnp.int32, (1, col_count), 1)
    row_iota = lax.broadcasted_iota(jnp.int32, (row_count, 1), 0)

    def chunk(index, start):
        return message_ref[index * block : (index + 1) * block, start : start + 8, :].reshape(
            members, LANES
        )

    def hot_of(cell):
        return jnp.where(((cell - 1) & (col_count - 1)) == col_iota, 1.0, 0.0).astype(BF)

    def rows_of(cell):
        return lax.shift_right_arithmetic(cell - 1, shift)

    sea = jnp.zeros((row_count, col_count), F32)
    count = 0
    for index in range(devices // block):
        tails = [chunk(index, capacity + 8 * part).T for part in range(per_group)]
        for octet in range(octets):
            table = chunk(index, 8 * octet)
            turned = table.T
            tail = tails[octet % per_group]
            begin = 32 * (octet // per_group)
            levels = jnp.concatenate([turned, tail[begin : begin + 32]], axis=0)
            high, low = split_two(levels)
            left_ref[count, :, 0:members] = high
            left_ref[count, :, members : 2 * members] = low
            hot = hot_of(table[:, 75:76].astype(jnp.int32))
            hot_ref[count] = hot
            rows = rows_of(turned[75:76].astype(jnp.int32))
            rows_ref[count] = jnp.broadcast_to(rows, (8, members))
            bound_ref[2 * count] = jnp.min(jnp.where(rows >= 0, rows, row_count))
            bound_ref[2 * count + 1] = jnp.max(rows)
            count += 1
            if octet >= alt_octets:
                continue
            alt_hot = hot_of(table[:, 77:78].astype(jnp.int32))
            alt_rows = rows_of(turned[77:78].astype(jnp.int32))
            weighted = jnp.where(alt_rows == row_iota, turned[76:77], 0.0)
            high, low = split_two(weighted)
            product = mm(jnp.concatenate([high, low], axis=0), alt_hot)
            sea = sea + product[:row_count] + product[row_count:]
    sea_ref[...] = sea


def chosen_rows(number, here, row, span, left_ref, hot_ref):
    pieces = []
    for offset in range(span):
        mask = jnp.where(here == row + offset, 1.0, 0.0).astype(BF)
        pieces.append(left_ref[number] * jnp.concatenate([mask, mask], axis=1))
    hot = hot_ref[number]
    return mm(jnp.concatenate(pieces, axis=0), jnp.concatenate([hot, hot], axis=0))


def outer_forcing(row, is_upper, profile_ref, coast_refs, sea_ref, left_ref, hot_ref, rows_ref, bound_ref, edge_ref):
    row_count, col_count = sea_ref.shape
    last = row_count - 1
    profile = jnp.broadcast_to(profile_ref[...], (2 * PAD, LANES))
    sea = jnp.where(is_upper, sea_ref[last : last + 1, :], sea_ref[0:1, :])
    for start in range(0, col_count, LANES):
        edge_ref[:, start : start + LANES] = profile * sea[:, start : start + LANES]

    def step(number, carry):
        @pl.when((bound_ref[2 * number] <= row) & (row <= bound_ref[2 * number + 1]))
        def _():
            edge_ref[...] += chosen_rows(number, rows_ref[number][0:1], row, 1, left_ref, hot_ref)

        return carry

    lax.fori_loop(0, left_ref.shape[0], step, 0)
    for kind, coast_ref in enumerate(coast_refs):
        coast = jnp.where(is_upper, coast_ref[last : last + 1, :], coast_ref[0:1, :])
        edge_ref[LEVELS + kind : LEVELS + kind + 1, :] = coast.astype(F32)


def all_forcing(profile_ref, coast_refs, sea_ref, left_ref, hot_ref, rows_ref, bound_ref, state):
    row_count, _, col_count = state.shape
    count = left_ref.shape[0]
    for start in range(0, col_count, LANES):
        profile = jnp.broadcast_to(profile_ref[...], (2 * PAD, LANES))
        for row in range(row_count):
            state[row, :, start : start + LANES] = profile * sea_ref[row : row + 1, start : start + LANES]
    span = 3
    batch = math.gcd(count, 4)

    def step(number, carry):
        chunks = [number * batch + member for member in range(batch)]
        least = [bound_ref[2 * chunk] for chunk in chunks]
        most = [bound_ref[2 * chunk + 1] for chunk in chunks]
        runs = [lax.div(most[i] - least[i] + span, span) for i in range(batch)]
        longest = runs[0]
        for run in runs[1:]:
            longest = jnp.maximum(longest, run)

        def run_step(turn, inner):
            for i, chunk in enumerate(chunks):
                begin = least[i] + turn * span
                base = jnp.minimum(begin, row_count - span)
                here = rows_ref[chunk][0:1]
                here = jnp.where(here >= begin, here, -1)
                product = chosen_rows(chunk, here, base, span, left_ref, hot_ref)
                for offset in range(span):
                    state[base + offset] += product[2 * PAD * offset : 2 * PAD * (offset + 1)]
            return inner

        lax.fori_loop(0, longest, run_step, 0)
        return carry

    lax.fori_loop(0, count // batch, step, 0)
    for kind, coast_ref in enumerate(coast_refs):
        coast = coast_ref[...].astype(F32)
        for row in range(row_count):
            state[row, LEVELS + kind : LEVELS + kind + 1, :] = coast[row : row + 1, :]


def half_shapes(row_count, col_count):
    return (
        jax.ShapeDtypeStruct((row_count // 2, 2 * PAD, col_count), F32),
        jax.ShapeDtypeStruct((2 * LEVELS + 2, col_count), F32),
        jax.ShapeDtypeStruct((PAD, LANES), F32),
    )


def in_place(count):
    return [pl.BlockSpec(memory_space=pltpu.SMEM)] + [pl.BlockSpec(memory_space=pltpu.VMEM)] * count


def first_forcing(capacity, alt_capacity, group, flags, message, profile, coast):
    row_count, col_count = coast[0].shape
    devices = message.shape[0]
    members = min(32, devices) * 8
    chunks = capacity // 8 * (devices // min(32, devices))

    def kernel(flag_ref, message_ref, profile_ref, wet, north, east, edge_ref, *refs):
        *outs, row_ref = refs
        prepare(capacity, alt_capacity, group, col_count, message_ref, *outs)
        is_upper = flag_ref[NEAR] > 0
        row = jnp.where(is_upper, row_count - 1, 0)
        outer_forcing(row, is_upper, profile_ref, (wet, north, east), *outs, row_ref)
        pack_row(row_ref, edge_ref)

    return pl.pallas_call(
        kernel,
        in_specs=in_place(5),
        out_shape=(
            half_shapes(row_count, col_count)[1],
            jax.ShapeDtypeStruct((row_count, col_count), F32),
            jax.ShapeDtypeStruct((chunks, 2 * PAD, 2 * members), BF),
            jax.ShapeDtypeStruct((chunks, members, col_count), BF),
            jax.ShapeDtypeStruct((chunks, 8, members), jnp.int32),
            jax.ShapeDtypeStruct((2 * chunks,), jnp.int32),
        ),
        out_specs=[pl.BlockSpec(memory_space=pltpu.VMEM)] * 5
        + [pl.BlockSpec(memory_space=pltpu.SMEM)],
        scratch_shapes=[pltpu.VMEM((2 * PAD, col_count), F32)],
        compiler_params=pltpu.CompilerParams(vmem_limit_bytes=24 * MIB),
        cost_estimate=pl.CostEstimate(
            flops=6_000_000_000, bytes_accessed=8_000_000, transcendentals=0
        ),
        name="forcing_first",
    )(flags, message, profile, *coast)


def rest_forcing(flags, profile, coast, prepared):
    row_count, col_count = coast[0].shape
    half = row_count // 2

    def kernel(flag_ref, profile_ref, wet, north, east, sea, left, hot, rows, bound, state, edge_ref, cols_ref):
        all_forcing(profile_ref, (wet, north, east), sea, left, hot, rows, bound, state)
        cols = jnp.zeros((PAD, LANES), F32)
        for which in (NEAR, FAR):
            first_row = jnp.where(flag_ref[which] > 0, half, 0)
            cols = columns_of(which, state.at[pl.ds(first_row, half)], cols)
        cols_ref[...] = cols
        write_edge(flag_ref[FAR] > 0, state, edge_ref)

    _, edge, cols = half_shapes(row_count, col_count)
    state = jax.ShapeDtypeStruct((row_count, 2 * PAD, col_count), F32)
    return pl.pallas_call(
        kernel,
        in_specs=in_place(8) + [pl.BlockSpec(memory_space=pltpu.SMEM)],
        out_shape=(state, edge, cols),
        compiler_params=pltpu.CompilerParams(vmem_limit_bytes=20 * MIB),
        cost_estimate=pl.CostEstimate(
            flops=6_000_000_000, bytes_accessed=8_000_000, transcendentals=0
        ),
        name="forcing_rest",
    )(flags, profile, *coast, *prepared)


def fold_row(row_ref, mirror_ref, piece, chunk, chunks, rows):
    index = jnp.broadcast_to(mirror_ref[0:1, piece(chunk)], (rows, LANES))
    return jnp.take_along_axis(row_ref[:, piece(chunks - 1 - chunk)], index, axis=1)


def weight_kernel(which, flag_ref, wet_ref, north_ref, east_ref, edge_in, west_in, east_in, mirror_ref, out_ref, fold_ref):
    row_count, col_count = wet_ref.shape
    rows = row_count // 2
    is_upper = flag_ref[which] > 0
    at = pl.multiple_of(jnp.where(is_upper, rows, 0), 8)
    wet = wet_ref[pl.ds(at, rows), :].astype(F32)
    north = north_ref[pl.ds(at, rows), :]
    east = east_ref[pl.ds(at, rows), :]
    chunks = col_count // LANES
    lane = lax.broadcasted_iota(jnp.int32, (1, col_count), 1)
    start = column_lane(which, rows, 0, 1, 0)
    west_cols = west_in[72:80, :].T[start : start + rows]
    start = column_lane(which, rows, 0, 0, 0)
    east_cols = east_in[72:80, :].T[start : start + rows]
    west_wet = jnp.where(lane == 0, west_cols[:, 3:4], pltpu.roll(wet, 1, 1))
    west_coef = jnp.where(lane == 0, west_cols[:, 5:6], pltpu.roll(east, 1, 1))
    east_wet = jnp.where(
        lane == col_count - 1, east_cols[:, 3:4], pltpu.roll(wet, col_count - 1, 1)
    )
    east_w = east * wet * east_wet
    west_w = west_coef * west_wet * wet

    def piece(c):
        return slice(c * LANES, (c + 1) * LANES)

    spare_ref = edge_in.at[2 * LEVELS - 6 : 2 * LEVELS + 2]
    if which == FAR:
        for c in range(chunks):
            fold_ref[:, piece(c)] = fold_row(spare_ref, mirror_ref, piece, c, chunks, 8)
    spare = spare_ref[...]
    last = rows - 1
    inner_wet = jnp.where(
        is_upper, wet_ref[rows - 1 : rows, :], wet_ref[rows : rows + 1, :]
    ).astype(F32)
    above = jnp.where(is_upper, spare[6:7], inner_wet)
    top_w = north[last:] * wet[last:] * above
    if which == FAR:
        fold = 0.5 * (north[last:] + fold_ref[7:8]) * wet[last:] * fold_ref[6:7]
        top_w = jnp.where(flag_ref[TOP] > 0, fold, top_w)
    below = jnp.where(is_upper, north_ref[rows - 1 : rows, :] * inner_wet, spare[7:8] * spare[6:7])
    between = north[:last] * wet[:last] * wet[1:]
    north_w = jnp.concatenate([between, top_w], axis=0)
    south_w = jnp.concatenate([below * wet[0:1], between], axis=0)
    center = 1.0 - (east_w + west_w + north_w + south_w)
    for kind, weight in enumerate((center, east_w, west_w, north_w, south_w)):
        for row in range(rows):
            out_ref[row, kind : kind + 1, :] = weight[row : row + 1]


def edge_weights(which, flags, coast, received, mirror):
    row_count, col_count = coast[0].shape

    def kernel(*refs):
        weight_kernel(which, *refs)

    return pl.pallas_call(
        kernel,
        in_specs=in_place(7),
        out_shape=jax.ShapeDtypeStruct((row_count // 2, 8, col_count), F32),
        scratch_shapes=[pltpu.VMEM((8, col_count), F32)],
        compiler_params=pltpu.CompilerParams(vmem_limit_bytes=16 * MIB),
        name="edge_weights",
    )(flags, *coast, *received, mirror)


def receive_row(which, flag_ref, edge_in, mirror_ref, row_ref):
    levels, col_count = edge_in.shape
    chunks = col_count // LANES
    is_top = flag_ref[TOP] > 0

    def piece(c):
        return slice(c * LANES, (c + 1) * LANES)

    def plain():
        for c in range(chunks):
            unpack_row(edge_in[:, piece(c)], row_ref, piece(c))

    if which == NEAR:
        plain()
        return

    @pl.when(jnp.logical_not(is_top))
    def _():
        plain()

    @pl.when(is_top)
    def _():
        for c in range(chunks):
            unpack_row(
                fold_row(edge_in, mirror_ref, piece, c, chunks, levels), row_ref, piece(c)
            )


def neighbour_rows(is_upper, inner, outer_ref, south_ref, north_ref):
    @pl.when(is_upper)
    def _():
        south_ref[...] = inner[...]
        north_ref[...] = outer_ref[...]

    @pl.when(jnp.logical_not(is_upper))
    def _():
        south_ref[...] = outer_ref[...]
        north_ref[...] = inner[...]


def mix_row(which, row, rows, field, state_ref, south_ref, north_ref, west_in, east_in, coef_ref, right_ref, slot):
    col_count = state_ref.shape[2]
    chunks = col_count // LANES
    lane = lax.broadcasted_iota(jnp.int32, (1, LANES), 1)
    levels = slice(field * PAD, (field + 1) * PAD)

    def piece(chunk):
        return slice(chunk * LANES, (chunk + 1) * LANES)

    west_lane = column_lane(which, rows, field, 1, row)
    east_lane = column_lane(which, rows, field, 0, row)
    centers = [state_ref[row, levels, piece(c)] for c in range(chunks)]
    to_left = [pltpu.roll(c, LANES - 1, 1) for c in centers]
    to_right = [pltpu.roll(c, 1, 1) for c in centers]
    to_right.append(pltpu.roll(west_in[...], LANES - west_lane, 1))
    to_left.append(pltpu.roll(east_in[...], LANES - 1 - east_lane, 1))
    for c in range(chunks):
        south = south_ref[levels, piece(c)]
        north = north_ref[levels, piece(c)]
        east = jnp.where(lane == LANES - 1, to_left[c + 1], to_left[c])
        west = jnp.where(lane == 0, to_right[c - 1], to_right[c])

        def coef(kind):
            return coef_ref[row, kind : kind + 1, piece(c)]

        mixed = (
            coef(0) * centers[c]
            + coef(1) * east
            + coef(2) * west
            + coef(3) * north
            + coef(4) * south
        )
        high, low = split_two(mixed)
        right_ref[slot, 0:PAD, piece(c)] = high
        right_ref[slot, PAD : 2 * PAD, piece(c)] = low
        right_ref[slot, 2 * PAD : 3 * PAD, piece(c)] = high


def sweep_rows(which, rows, units, state_ref, south_ref, north_ref, west_in, east_in, coef_ref, matrix_ref, right_ref, emit):
    slots = right_ref.shape[0]
    right_ref[:, 3 * PAD :, :] = jnp.zeros((slots,) + (256 - 3 * PAD, right_ref.shape[2]), BF)

    def product(number):
        row, field = units[number]
        emit(number, row, field, mm(matrix_ref[field, row], right_ref[number % slots]))

    for number, (row, field) in enumerate(units):
        south = state_ref.at[row - 1] if row > 0 else south_ref
        north = state_ref.at[row + 1] if row < rows - 1 else north_ref
        mix_row(which, row, rows, field, state_ref, south, north, west_in, east_in, coef_ref, right_ref, number % slots)
        if number > 0:
            product(number - 1)
    product(len(units) - 1)


def inner_rows(which, is_upper, rows, state_ref, other_row, south_ref, north_ref, west_in, east_in, coef_ref, matrix_ref, right_ref, emit):
    last = rows - 1
    beside = jnp.where(is_upper, 0, last)

    @pl.when(is_upper)
    def _():
        south_ref[...] = other_row[...]
        north_ref[...] = state_ref[1]

    @pl.when(jnp.logical_not(is_upper))
    def _():
        south_ref[...] = state_ref[last - 1]
        north_ref[...] = other_row[...]

    units = [(row, field) for row in range(1, last) for field in range(2)]
    sweep_rows(which, rows, units, state_ref, south_ref, north_ref, west_in, east_in, coef_ref, matrix_ref, right_ref, emit)
    for field in range(2):
        mix_row(which, beside, rows, field, state_ref, south_ref, north_ref, west_in, east_in, coef_ref, right_ref, field)
    for field in range(2):
        emit(None, beside, field, mm(matrix_ref[field, beside], right_ref[field]))


def half_of(state, rows, is_upper, state_ref):
    if state.shape[0] == rows:
        return state_ref
    return state_ref.at[pl.ds(jnp.where(is_upper, rows, 0), rows)]


SOON = pl.CostEstimate(flops=1_000_000, bytes_accessed=1_000, transcendentals=0)


def step_outer(which, flags, state, edge, sides, mirror, coef, matrix):
    rows = coef.shape[0]
    col_count = state.shape[2]

    def kernel(flag_ref, state_ref, edge_in, west_in, east_in, mirror_ref, coef_ref, matrix_ref, edge_ref, south_ref, north_ref, outer_ref, right_ref):
        is_upper = flag_ref[which] > 0
        state_ref = half_of(state, rows, is_upper, state_ref)
        last = rows - 1
        row = jnp.where(is_upper, last, 0)
        receive_row(which, flag_ref, edge_in, mirror_ref, outer_ref)
        neighbour_rows(is_upper, state_ref.at[jnp.where(is_upper, last - 1, 1)], outer_ref, south_ref, north_ref)
        right_ref[:, 3 * PAD :, :] = jnp.zeros((2, 256 - 3 * PAD, col_count), BF)
        for field in range(2):
            mix_row(which, row, rows, field, state_ref, south_ref, north_ref, west_in, east_in, coef_ref, right_ref, field)
        for field in range(2):
            outer_ref[field * PAD : (field + 1) * PAD] = mm(matrix_ref[field, row], right_ref[field])
        pack_row(outer_ref, edge_ref)

    return pl.pallas_call(
        kernel,
        in_specs=in_place(7),
        out_shape=half_shapes(2 * rows, col_count)[1],
        scratch_shapes=[pltpu.VMEM((2 * PAD, col_count), F32)] * 3
        + [pltpu.VMEM((2, 256, col_count), BF)],
        compiler_params=pltpu.CompilerParams(vmem_limit_bytes=16 * MIB),
        cost_estimate=SOON,
        name="outer_" + ("near", "far")[which],
    )(flags, state, edge, *sides, mirror, coef, matrix)


def step_inner(which, flags, state, other, message, sides, coef, matrix, *far_cols):
    rows = coef.shape[0]
    col_count = state.shape[2]

    def kernel(flag_ref, state_ref, other_ref, message_ref, west_in, east_in, coef_ref, matrix_ref, *refs):
        out_ref, cols_ref, south_ref, north_ref, right_ref = refs[-5:]
        is_upper = flag_ref[which] > 0
        state_ref = half_of(state, rows, is_upper, state_ref)
        other_ref = half_of(other, rows, jnp.logical_not(is_upper), other_ref)
        other_row = other_ref.at[jnp.where(is_upper, rows - 1, 0)]

        def emit(number, row, field, result):
            out_ref[row, field * PAD : (field + 1) * PAD] = result

        inner_rows(which, is_upper, rows, state_ref, other_row, south_ref, north_ref, west_in, east_in, coef_ref, matrix_ref, right_ref, emit)
        outer = out_ref.at[jnp.where(is_upper, rows - 1, 0)]
        unpack_row(message_ref[...], outer, slice(0, col_count))
        old_cols = refs[0][...] if which == NEAR else jnp.zeros((PAD, LANES), F32)
        cols_ref[...] = columns_of(which, out_ref, old_cols)

    shapes = half_shapes(2 * rows, col_count)
    return pl.pallas_call(
        kernel,
        in_specs=in_place(7 + len(far_cols)),
        out_shape=(shapes[0], shapes[2]),
        scratch_shapes=[pltpu.VMEM((2 * PAD, col_count), F32)] * 2
        + [pltpu.VMEM((4, 256, col_count), BF)],
        compiler_params=pltpu.CompilerParams(vmem_limit_bytes=16 * MIB),
        cost_estimate=SOON,
        name="diffusion_" + ("near", "far")[which],
    )(flags, state, other, message, *sides, coef, matrix, *far_cols)


def store_block(results, out_ref, stage_ref, sem, at, field):
    rows = stage_ref.shape[2]
    stage_ref[field] = jnp.swapaxes(jnp.stack(results), 0, 1)[:LEVELS]
    copy = pltpu.make_async_copy(
        stage_ref.at[field],
        out_ref.at[pl.ds(field * LEVELS, LEVELS), pl.ds(at, rows), :],
        sem.at[field],
    )
    copy.start()
    return copy


def last_inner(flags, near, far, near_edge, near_sides, far_sides, mirror, near_fixed, far_fixed, mask):
    rows, _, col_count = near.shape

    def kernel(flag_ref, near_ref, far_ref, edge_in, near_west, near_east, far_west, far_east, mirror_ref, near_coef, near_matrix, far_coef, far_matrix, mask_ref, out_ref, done_ref, south_ref, north_ref, outer_ref, right_ref, stage_ref, sem):
        is_upper = flag_ref[NEAR] > 0
        at = pl.multiple_of(jnp.where(is_upper, rows, 0), 8)
        wet = mask_ref[pl.ds(at, rows), :].astype(F32)
        far_at = pl.multiple_of(rows - at, 8)
        far_wet = mask_ref[pl.ds(far_at, rows), :].astype(F32)
        last = rows - 1
        far_inner = far_ref.at[jnp.where(is_upper, last, 0)]
        receive_row(NEAR, flag_ref, edge_in, mirror_ref, outer_ref)
        neighbour_rows(is_upper, far_inner, outer_ref, south_ref, north_ref)
        copies = []
        for field in range(2):
            results = []

            def emit(number, row, field, result):
                results.append(result * wet[row : row + 1])

            units = [(row, field) for row in range(rows)]
            sweep_rows(NEAR, rows, units, near_ref, south_ref, north_ref, near_west, near_east, near_coef, near_matrix, right_ref, emit)
            copies.append(store_block(results, out_ref, stage_ref, sem, at, field))

        def keep(number, row, field, result):
            if number is None:
                row_wet = jnp.where(is_upper, far_wet[last:], far_wet[0:1])
            else:
                row_wet = far_wet[row : row + 1]
            done_ref[row, field * PAD : (field + 1) * PAD] = result * row_wet

        near_row = near_ref.at[jnp.where(is_upper, 0, last)]
        inner_rows(FAR, jnp.logical_not(is_upper), rows, far_ref, near_row, south_ref, north_ref, far_west, far_east, far_coef, far_matrix, right_ref, keep)
        for copy in copies:
            copy.wait()

    return pl.pallas_call(
        kernel,
        in_specs=in_place(13),
        out_specs=[pl.BlockSpec(memory_space=pl.ANY), pl.BlockSpec(memory_space=pltpu.VMEM)],
        out_shape=(
            jax.ShapeDtypeStruct((2 * LEVELS, 2 * rows, col_count), F32),
            jax.ShapeDtypeStruct((rows, 2 * PAD, col_count), F32),
        ),
        scratch_shapes=[pltpu.VMEM((2 * PAD, col_count), F32)] * 3
        + [
            pltpu.VMEM((4, 256, col_count), BF),
            pltpu.VMEM((2, LEVELS, rows, col_count), F32),
            pltpu.SemaphoreType.DMA((2,)),
        ],
        compiler_params=pltpu.CompilerParams(vmem_limit_bytes=20 * MIB),
        cost_estimate=SOON,
        name="last_inner",
    )(flags, near, far, near_edge, *near_sides, *far_sides, mirror, *near_fixed, *far_fixed, mask)


def last_outer(flags, far, far_edge, far_sides, mirror, far_fixed, mask, done, target):
    rows, _, col_count = far.shape

    def kernel(flag_ref, far_ref, edge_in, west_in, east_in, mirror_ref, coef_ref, matrix_ref, mask_ref, done_ref, target_ref, out_ref, south_ref, north_ref, outer_ref, right_ref, stage_ref, sem):
        is_upper = flag_ref[FAR] > 0
        at = pl.multiple_of(jnp.where(is_upper, rows, 0), 8)
        wet = mask_ref[pl.ds(at, rows), :].astype(F32)
        last = rows - 1
        row = jnp.where(is_upper, last, 0)
        row_wet = jnp.where(is_upper, wet[last:], wet[0:1])
        receive_row(FAR, flag_ref, edge_in, mirror_ref, outer_ref)
        neighbour_rows(is_upper, far_ref.at[jnp.where(is_upper, last - 1, 1)], outer_ref, south_ref, north_ref)
        right_ref[:, 3 * PAD :, :] = jnp.zeros((2, 256 - 3 * PAD, col_count), BF)
        for field in range(2):
            mix_row(FAR, row, rows, field, far_ref, south_ref, north_ref, west_in, east_in, coef_ref, right_ref, field)
        copies = []
        for field in range(2):
            result = mm(matrix_ref[field, row], right_ref[field]) * row_wet
            done_field = [done_ref[r, field * PAD : (field + 1) * PAD] for r in range(rows)]
            done_field[0] = jnp.where(is_upper, done_field[0], result)
            done_field[last] = jnp.where(is_upper, result, done_field[last])
            copies.append(store_block(done_field, out_ref, stage_ref, sem, at, field))
        for copy in copies:
            copy.wait()

    operands = [flags, far, far_edge, *far_sides, mirror, *far_fixed, mask, done, target]
    return pl.pallas_call(
        kernel,
        in_specs=in_place(9) + [pl.BlockSpec(memory_space=pl.ANY)],
        out_specs=pl.BlockSpec(memory_space=pl.ANY),
        out_shape=jax.ShapeDtypeStruct((2 * LEVELS, 2 * rows, col_count), F32),
        input_output_aliases={len(operands) - 1: 0},
        scratch_shapes=[pltpu.VMEM((2 * PAD, col_count), F32)] * 3
        + [
            pltpu.VMEM((2, 256, col_count), BF),
            pltpu.VMEM((2, LEVELS, rows, col_count), F32),
            pltpu.SemaphoreType.DMA((2,)),
        ],
        compiler_params=pltpu.CompilerParams(vmem_limit_bytes=20 * MIB),
        name="last_outer",
    )(*operands)


def mixing_matrices(vinv):
    turned = jnp.transpose(vinv, (1, 0, 3, 2))
    turned = jnp.pad(turned, ((0, 0), (0, 0), (0, PAD - LEVELS), (0, PAD - LEVELS)))
    high = lax.reduce_precision(turned, 8, 7)
    low = (turned - high).astype(BF)
    high = high.astype(BF)
    rest = jnp.zeros(high.shape[:3] + (256 - 3 * PAD,), BF)
    return jnp.concatenate([high, high, low, rest], axis=3)


def body(
    argo_value,
    argo_owner,
    argo_cell,
    alt_value,
    alt_owner,
    alt_cell,
    alt_profile,
    land_mask,
    coef_east,
    coef_north,
    mirror,
    vinv,
):
    row_count, col_count = land_mask.shape
    count_ja = lax.axis_size("ja")
    count_ia = lax.axis_size("ia")
    devices = count_ja * count_ia
    capacity = round_up(3 * argo_value.shape[0] // devices, 8)
    group = round_up(capacity // 4, 8)
    message = send_tables(
        devices,
        capacity,
        group,
        row_count,
        col_count,
        (
            argo_value.T,
            argo_owner.reshape(1, -1),
            argo_cell.reshape(1, -1),
            alt_value,
            alt_cell,
            alt_owner.reshape(1, -1),
        ),
    )
    message, ja_index = lax.optimization_barrier((message, lax.axis_index("ja")))
    message = lax.all_to_all(message, ("ja", "ia"), split_axis=0, concat_axis=0, tiled=True)

    ia_index = lax.axis_index("ia")
    is_top = (ja_index == count_ja - 1).astype(jnp.int32)
    parity = ja_index % 2
    flags = jnp.stack([1 - parity, parity, is_top]).astype(jnp.int32)
    fold_index = mirror - (count_ia - 1 - ia_index) * col_count
    mirror_lane = jnp.broadcast_to((fold_index % LANES)[None, :], (8, col_count))
    matrices = mixing_matrices(vinv)
    profile = jnp.pad(alt_profile.reshape(2, LEVELS, 1), ((0, 0), (0, PAD - LEVELS), (0, 0)))
    profile = profile.reshape(2 * PAD, 1)
    alt_capacity = max(2, 3 * alt_value.shape[0] // devices)
    coast = (land_mask, coef_north, coef_east)
    rows = row_count // 2
    lower = [matrices[:, :rows], matrices[:, rows:]]
    odd_device = parity == 1
    half_matrices = [
        jnp.where(odd_device, lower[0], lower[1]),
        jnp.where(odd_device, lower[1], lower[0]),
    ]

    ring_east = [(i, (i + 1) % count_ia) for i in range(count_ia)]
    ring_west = [((i + 1) % count_ia, i) for i in range(count_ia)]
    even_swap = []
    odd_swap = []
    for ja in range(count_ja):
        for ia in range(count_ia):
            here = ja * count_ia + ia
            even_swap.append((here, (ja ^ 1) * count_ia + ia))
            if ja == count_ja - 1:
                odd_swap.append((here, ja * count_ia + count_ia - 1 - ia))
            elif ja > 0:
                odd_swap.append((here, (((ja - 1) ^ 1) + 1) * count_ia + ia))
    swaps = (even_swap, odd_swap)

    def swap(which, edge):
        return lax.ppermute(edge, ("ja", "ia"), swaps[which])

    def pass_columns(cols):
        return lax.ppermute(cols, "ia", ring_east), lax.ppermute(cols, "ia", ring_west)

    near_edge, *prepared = first_forcing(
        capacity, alt_capacity, group, flags, message, profile, coast
    )
    near_edge = swap(NEAR, near_edge)
    state, far_edge, cols = rest_forcing(flags, profile, coast, prepared)
    near = far = state
    sides = pass_columns(cols)
    far_edge = swap(FAR, far_edge)
    near_coef = edge_weights(NEAR, flags, coast, (near_edge, *sides), mirror_lane)
    far_coef = edge_weights(FAR, flags, coast, (far_edge, *sides), mirror_lane)
    near_fixed = (mirror_lane, near_coef, half_matrices[NEAR])
    far_fixed = (mirror_lane, far_coef, half_matrices[FAR])
    for sweep in range(ITERS - 1):
        message = step_outer(NEAR, flags, near, near_edge, sides, *near_fixed)
        near_edge = swap(NEAR, message)
        new_near, cols = step_inner(
            NEAR, flags, near, far, message, sides, *near_fixed[1:], cols
        )
        sides = pass_columns(cols)
        message = step_outer(FAR, flags, far, far_edge, sides, *far_fixed)
        far_edge = swap(FAR, message)
        far, cols = step_inner(FAR, flags, far, near, message, sides, *far_fixed[1:])
        near = new_near
    last_sides = pass_columns(cols)
    output, done = last_inner(
        flags, near, far, near_edge, sides, last_sides, mirror_lane, near_fixed[1:], far_fixed[1:], land_mask
    )
    return last_outer(
        flags, far, far_edge, last_sides, mirror_lane, far_fixed[1:], land_mask, done, output
    )


def solution(mesh):
    in_specs = (
        P(("ja", "ia"), None),
        P(("ja", "ia"), None),
        P(("ja", "ia")),
        P(("ja", "ia")),
        P(("ja", "ia"), None),
        P(("ja", "ia")),
        P(),
        P("ja", "ia"),
        P("ja", "ia"),
        P("ja", "ia"),
        P("ia"),
        P("ja", None, None, None),
    )
    out_specs = P(None, "ja", "ia")
    return jax.shard_map(body, mesh=mesh, in_specs=in_specs, out_specs=out_specs, check_vma=False)
```

```python
import math

import jax
import jax.numpy as jnp
from jax import lax
from jax.experimental import pallas as pl
from jax.experimental.pallas import tpu as pltpu
from jax.sharding import PartitionSpec as P

ITERS = 3
LEVELS = 75
PAD = 80
LANES = 128
NEAR, FAR, TOP = 0, 1, 2
BF = jnp.bfloat16
F32 = jnp.float32
MIB = 1024 * 1024


def round_up(value, unit):
    return (value + unit - 1) // unit * unit


def split_two(value):
    high = value.astype(BF)
    low = (value - high.astype(F32)).astype(BF)
    return high, low


def mm(left, right):
    return jnp.dot(left, right, preferred_element_type=F32)


def as_column(row):
    return jnp.broadcast_to(row, (8, row.shape[1])).T[:, 0:1]


def slot_ranks(owner_row, cell_row, devices, col_count, row_count, capacity, spread):
    count = owner_row.shape[1]
    owner = owner_row.astype(F32)
    inside = cell_row // col_count
    order = lax.broadcasted_iota(jnp.int32, (1, count), 1).astype(F32)
    key = (owner * float(row_count) + inside.astype(F32)) * float(count) + order
    key_col = as_column(key)
    device = lax.broadcasted_iota(jnp.int32, (devices, 1), 0)
    mine = device == owner_row
    totals = jnp.sum(jnp.where(mine, 1.0, 0.0), axis=1, keepdims=True)
    rank = -jnp.sum(jnp.where(device < owner_row, totals, 0.0), axis=0, keepdims=True)
    for start in range(0, count, 128):
        before = jnp.where(key_col[start : start + 128] < key, 1.0, 0.0)
        rank = rank + jnp.sum(before, axis=0, keepdims=True)
    if spread:
        total = jnp.sum(jnp.where(mine, totals, 0.0), axis=0, keepdims=True)
        offset = owner * 1024.0
        goal = (inside * capacity // row_count).astype(F32) - rank + offset
        goal_col = as_column(goal)
        shift = offset
        for start in range(0, count, 128):
            within = key_col[start : start + 128] <= key
            reached = jnp.where(within, goal_col[start : start + 128], 0.0)
            shift = jnp.maximum(shift, jnp.max(reached, axis=0, keepdims=True))
        rank = rank + jnp.minimum(shift - offset, float(capacity) - total)
    return rank


def table_kernel(
    devices,
    capacity,
    group,
    row_count,
    col_count,
    value_ref,
    owner_ref,
    cell_ref,
    alt_value_ref,
    alt_cell_ref,
    alt_owner_ref,
    message_ref,
    level_ref,
    side_ref,
    hi_ref,
    lo_ref,
    alt_all_ref,
    rank_hot_ref,
    alt_rank_hot_ref,
):
    index = pl.program_id(0)
    n_obs = owner_ref.shape[1]
    n_alt = alt_owner_ref.shape[1]

    @pl.when(index == 0)
    def _():
        slot = lax.broadcasted_iota(jnp.int32, (capacity, 1), 0).astype(F32)
        alt_cell = alt_cell_ref[...].reshape(1, n_alt)
        rank = slot_ranks(
            owner_ref[...], cell_ref[...], devices, col_count, row_count, capacity, True
        )
        rank_hot_ref[...] = jnp.where(slot == rank, 1.0, 0.0).astype(BF)
        rank = slot_ranks(
            alt_owner_ref[...], alt_cell, devices, col_count, row_count, capacity, False
        )
        alt_rank_hot_ref[...] = jnp.where(slot == rank, 1.0, 0.0).astype(BF)
        level_ref[...] = jnp.zeros(level_ref.shape, F32)
        level_ref[0:75, :] = value_ref[0:75, :]
        level_ref[75:76, :] = cell_ref[...].astype(F32) + 1.0
        level_ref[80:128, :] = value_ref[75:123, :]
        for lane_group in range(4):
            level_ref[128 + 32 * lane_group : 155 + 32 * lane_group, :] = value_ref[123:150, :]
        high, low = split_two(level_ref[...].T)
        hi_ref[...] = high
        lo_ref[...] = low
        side_ref[...] = jnp.zeros(side_ref.shape, F32)
        pair = jnp.concatenate(
            [alt_value_ref[...].reshape(1, n_alt), alt_cell.astype(F32) + 1.0], axis=0
        )
        pair_high = pair.astype(BF).astype(F32)
        side_ref[76:78, :] = pair_high
        side_ref[78:80, :] = pair - pair_high
        alt_all_ref[...] = side_ref[...].T.astype(BF)

    per_step = message_ref.shape[0]
    chosen = []
    chosen_alt = []
    for member in range(per_step):
        device = index * per_step + member
        mask = jnp.where(owner_ref[...] == device, 1.0, 0.0).astype(BF)
        chosen.append(rank_hot_ref[...] * mask)
        mask = jnp.where(alt_owner_ref[...] == device, 1.0, 0.0).astype(BF)
        chosen_alt.append(alt_rank_hot_ref[...] * mask)
    chosen = jnp.concatenate(chosen, axis=0)
    chosen_alt = jnp.concatenate(chosen_alt, axis=0)
    table = mm(chosen, hi_ref[...]) + mm(chosen, lo_ref[...])
    lane = lax.broadcasted_iota(jnp.int32, (1, LANES), 1)
    extra = mm(chosen_alt, alt_all_ref[...])
    extra = jnp.where(lane < 78, extra + pltpu.roll(extra, LANES - 2, 1), 0.0)
    extra = jnp.where(lane >= 76, extra, 0.0)
    first = table[:, :LANES] + extra
    message_ref[:, 0:capacity] = first.reshape(per_step, capacity, LANES)
    rest = table[:, LANES:].reshape(per_step, capacity, LANES)
    total = jnp.zeros((per_step, group, LANES), F32)
    for lane_group in range(4):
        low_slot = lane_group * group
        if low_slot >= capacity:
            continue
        piece = rest[:, low_slot : low_slot + group]
        here = (lane // 32 == lane_group).reshape(1, 1, LANES)
        total = jnp.where(here, piece, total)
    message_ref[:, capacity : capacity + group] = total


def send_tables(devices, capacity, group, row_count, col_count, operands):
    n_obs = operands[1].shape[1]
    n_alt = operands[5].shape[1]
    per_step = max(1, 1536 // capacity)

    def kernel(*refs):
        table_kernel(devices, capacity, group, row_count, col_count, *refs)

    def whole(array):
        return pl.BlockSpec(array.shape, lambda s: (0,) * len(array.shape))

    return pl.pallas_call(
        kernel,
        grid=(devices // per_step,),
        in_specs=[whole(x) for x in operands],
        out_specs=pl.BlockSpec((per_step, capacity + group, LANES), lambda s: (s, 0, 0)),
        out_shape=jax.ShapeDtypeStruct((devices, capacity + group, LANES), F32),
        scratch_shapes=[
            pltpu.VMEM((2 * LANES, n_obs), F32),
            pltpu.VMEM((LANES, n_alt), F32),
            pltpu.VMEM((n_obs, 2 * LANES), BF),
            pltpu.VMEM((n_obs, 2 * LANES), BF),
            pltpu.VMEM((n_alt, LANES), BF),
            pltpu.VMEM((capacity, n_obs), BF),
            pltpu.VMEM((capacity, n_alt), BF),
        ],
        compiler_params=pltpu.CompilerParams(vmem_limit_bytes=56 * MIB),
        name="send_tables",
    )(*operands)


def column_lane(which, rows, field, east, row):
    return (4 * which + 2 * field + east) * rows + row


def columns_of(which, state_ref, cols):
    rows = state_ref.shape[0]
    lane = lax.broadcasted_iota(jnp.int32, (1, LANES), 1)
    for row in range(rows):
        for field in range(2):
            part = state_ref[row, field * PAD : (field + 1) * PAD, :]
            at = column_lane(which, rows, field, 0, row)
            cols = jnp.where(lane == at, pltpu.roll(part[:, :LANES], at, 1), cols)
            at = column_lane(which, rows, field, 1, row)
            cols = jnp.where(lane == at, pltpu.roll(part[:, -LANES:], at + 1, 1), cols)
    return cols


def pack_row(row_ref, edge_ref):
    edge_ref[0:LEVELS] = row_ref[0:LEVELS]
    edge_ref[LEVELS : 2 * LEVELS] = row_ref[PAD : PAD + LEVELS]
    edge_ref[2 * LEVELS : 2 * LEVELS + 2] = row_ref[LEVELS : LEVELS + 2]


def unpack_row(edge, row_ref, piece):
    row_ref[0:LEVELS, piece] = edge[0:LEVELS]
    row_ref[PAD : PAD + LEVELS, piece] = edge[LEVELS : 2 * LEVELS]
    for at in (LEVELS, PAD + LEVELS):
        row_ref[at : at + PAD - LEVELS, piece] = jnp.zeros((PAD - LEVELS, edge.shape[1]), F32)


def write_edge(is_upper, state_ref, edge_ref):
    pack_row(state_ref.at[jnp.where(is_upper, state_ref.shape[0] - 1, 0)], edge_ref)


def prepare(capacity, alt_capacity, group, col_count, message_ref, sea_ref, left_ref, hot_ref, rows_ref, bound_ref):
    row_count = sea_ref.shape[0]
    devices = message_ref.shape[0]
    block = min(32, devices)
    members = block * 8
    octets = capacity // 8
    alt_octets = (alt_capacity + 7) // 8
    per_group = group // 8
    shift = col_count.bit_length() - 1
    col_iota = lax.broadcasted_iota(jnp.int32, (1, col_count), 1)
    row_iota = lax.broadcasted_iota(jnp.int32, (row_count, 1), 0)

    def chunk(index, start):
        return message_ref[index * block : (index + 1) * block, start : start + 8, :].reshape(
            members, LANES
        )

    def hot_of(cell):
        return jnp.where(((cell - 1) & (col_count - 1)) == col_iota, 1.0, 0.0).astype(BF)

    def rows_of(cell):
        return lax.shift_right_arithmetic(cell - 1, shift)

    sea = jnp.zeros((row_count, col_count), F32)
    count = 0
    for index in range(devices // block):
        tails = [chunk(index, capacity + 8 * part).T for part in range(per_group)]
        for octet in range(octets):
            table = chunk(index, 8 * octet)
            turned = table.T
            tail = tails[octet % per_group]
            begin = 32 * (octet // per_group)
            levels = jnp.concatenate([turned, tail[begin : begin + 32]], axis=0)
            high, low = split_two(levels)
            left_ref[count, :, 0:members] = high
            left_ref[count, :, members : 2 * members] = low
            hot = hot_of(table[:, 75:76].astype(jnp.int32))
            hot_ref[count] = hot
            rows = rows_of(turned[75:76].astype(jnp.int32))
            rows_ref[count] = jnp.broadcast_to(rows, (8, members))
            bound_ref[2 * count] = jnp.min(jnp.where(rows >= 0, rows, row_count))
            bound_ref[2 * count + 1] = jnp.max(rows)
            count += 1
            if octet >= alt_octets:
                continue
            alt_hot = hot_of(table[:, 77:78].astype(jnp.int32))
            alt_rows = rows_of(turned[77:78].astype(jnp.int32))
            weighted = jnp.where(alt_rows == row_iota, turned[76:77], 0.0)
            high, low = split_two(weighted)
            product = mm(jnp.concatenate([high, low], axis=0), alt_hot)
            sea = sea + product[:row_count] + product[row_count:]
    sea_ref[...] = sea


def chosen_rows(number, here, row, span, left_ref, hot_ref):
    pieces = []
    for offset in range(span):
        mask = jnp.where(here == row + offset, 1.0, 0.0).astype(BF)
        pieces.append(left_ref[number] * jnp.concatenate([mask, mask], axis=1))
    hot = hot_ref[number]
    return mm(jnp.concatenate(pieces, axis=0), jnp.concatenate([hot, hot], axis=0))


def outer_forcing(row, is_upper, profile_ref, coast_refs, sea_ref, left_ref, hot_ref, rows_ref, bound_ref, edge_ref):
    row_count, col_count = sea_ref.shape
    last = row_count - 1
    profile = jnp.broadcast_to(profile_ref[...], (2 * PAD, LANES))
    sea = jnp.where(is_upper, sea_ref[last : last + 1, :], sea_ref[0:1, :])
    for start in range(0, col_count, LANES):
        edge_ref[:, start : start + LANES] = profile * sea[:, start : start + LANES]

    def step(number, carry):
        @pl.when((bound_ref[2 * number] <= row) & (row <= bound_ref[2 * number + 1]))
        def _():
            edge_ref[...] += chosen_rows(number, rows_ref[number][0:1], row, 1, left_ref, hot_ref)

        return carry

    lax.fori_loop(0, left_ref.shape[0], step, 0)
    for kind, coast_ref in enumerate(coast_refs):
        coast = jnp.where(is_upper, coast_ref[last : last + 1, :], coast_ref[0:1, :])
        edge_ref[LEVELS + kind : LEVELS + kind + 1, :] = coast.astype(F32)


def all_forcing(profile_ref, coast_refs, sea_ref, left_ref, hot_ref, rows_ref, bound_ref, state):
    row_count, _, col_count = state.shape
    count = left_ref.shape[0]
    for start in range(0, col_count, LANES):
        profile = jnp.broadcast_to(profile_ref[...], (2 * PAD, LANES))
        for row in range(row_count):
            state[row, :, start : start + LANES] = profile * sea_ref[row : row + 1, start : start + LANES]
    span = 3
    batch = math.gcd(count, 4)

    def step(number, carry):
        chunks = [number * batch + member for member in range(batch)]
        least = [bound_ref[2 * chunk] for chunk in chunks]
        most = [bound_ref[2 * chunk + 1] for chunk in chunks]
        runs = [lax.div(most[i] - least[i] + span, span) for i in range(batch)]
        longest = runs[0]
        for run in runs[1:]:
            longest = jnp.maximum(longest, run)

        def run_step(turn, inner):
            for i, chunk in enumerate(chunks):
                begin = least[i] + turn * span
                base = jnp.minimum(begin, row_count - span)
                here = rows_ref[chunk][0:1]
                here = jnp.where(here >= begin, here, -1)
                product = chosen_rows(chunk, here, base, span, left_ref, hot_ref)
                for offset in range(span):
                    state[base + offset] += product[2 * PAD * offset : 2 * PAD * (offset + 1)]
            return inner

        lax.fori_loop(0, longest, run_step, 0)
        return carry

    lax.fori_loop(0, count // batch, step, 0)
    for kind, coast_ref in enumerate(coast_refs):
        coast = coast_ref[...].astype(F32)
        for row in range(row_count):
            state[row, LEVELS + kind : LEVELS + kind + 1, :] = coast[row : row + 1, :]


def half_shapes(row_count, col_count):
    return (
        jax.ShapeDtypeStruct((row_count // 2, 2 * PAD, col_count), F32),
        jax.ShapeDtypeStruct((2 * LEVELS + 2, col_count), F32),
        jax.ShapeDtypeStruct((PAD, LANES), F32),
    )


def in_place(count):
    return [pl.BlockSpec(memory_space=pltpu.SMEM)] + [pl.BlockSpec(memory_space=pltpu.VMEM)] * count


def first_forcing(capacity, alt_capacity, group, flags, message, profile, coast):
    row_count, col_count = coast[0].shape
    devices = message.shape[0]
    members = min(32, devices) * 8
    chunks = capacity // 8 * (devices // min(32, devices))

    def kernel(flag_ref, message_ref, profile_ref, wet, north, east, edge_ref, *refs):
        *outs, row_ref = refs
        prepare(capacity, alt_capacity, group, col_count, message_ref, *outs)
        is_upper = flag_ref[NEAR] > 0
        row = jnp.where(is_upper, row_count - 1, 0)
        outer_forcing(row, is_upper, profile_ref, (wet, north, east), *outs, row_ref)
        pack_row(row_ref, edge_ref)

    return pl.pallas_call(
        kernel,
        in_specs=in_place(5),
        out_shape=(
            half_shapes(row_count, col_count)[1],
            jax.ShapeDtypeStruct((row_count, col_count), F32),
            jax.ShapeDtypeStruct((chunks, 2 * PAD, 2 * members), BF),
            jax.ShapeDtypeStruct((chunks, members, col_count), BF),
            jax.ShapeDtypeStruct((chunks, 8, members), jnp.int32),
            jax.ShapeDtypeStruct((2 * chunks,), jnp.int32),
        ),
        out_specs=[pl.BlockSpec(memory_space=pltpu.VMEM)] * 5
        + [pl.BlockSpec(memory_space=pltpu.SMEM)],
        scratch_shapes=[pltpu.VMEM((2 * PAD, col_count), F32)],
        compiler_params=pltpu.CompilerParams(vmem_limit_bytes=24 * MIB),
        cost_estimate=pl.CostEstimate(
            flops=6_000_000_000, bytes_accessed=8_000_000, transcendentals=0
        ),
        name="forcing_first",
    )(flags, message, profile, *coast)


def rest_forcing(flags, profile, coast, prepared):
    row_count, col_count = coast[0].shape
    half = row_count // 2

    def kernel(flag_ref, profile_ref, wet, north, east, sea, left, hot, rows, bound, state, edge_ref, cols_ref):
        all_forcing(profile_ref, (wet, north, east), sea, left, hot, rows, bound, state)
        cols = jnp.zeros((PAD, LANES), F32)
        for which in (NEAR, FAR):
            first_row = jnp.where(flag_ref[which] > 0, half, 0)
            cols = columns_of(which, state.at[pl.ds(first_row, half)], cols)
        cols_ref[...] = cols
        write_edge(flag_ref[FAR] > 0, state, edge_ref)

    _, edge, cols = half_shapes(row_count, col_count)
    state = jax.ShapeDtypeStruct((row_count, 2 * PAD, col_count), F32)
    return pl.pallas_call(
        kernel,
        in_specs=in_place(8) + [pl.BlockSpec(memory_space=pltpu.SMEM)],
        out_shape=(state, edge, cols),
        compiler_params=pltpu.CompilerParams(vmem_limit_bytes=20 * MIB),
        cost_estimate=pl.CostEstimate(
            flops=6_000_000_000, bytes_accessed=8_000_000, transcendentals=0
        ),
        name="forcing_rest",
    )(flags, profile, *coast, *prepared)


def fold_row(row_ref, mirror_ref, piece, chunk, chunks, rows):
    index = jnp.broadcast_to(mirror_ref[0:1, piece(chunk)], (rows, LANES))
    return jnp.take_along_axis(row_ref[:, piece(chunks - 1 - chunk)], index, axis=1)


def weight_kernel(which, flag_ref, wet_ref, north_ref, east_ref, edge_in, west_in, east_in, mirror_ref, out_ref, fold_ref):
    row_count, col_count = wet_ref.shape
    rows = row_count // 2
    is_upper = flag_ref[which] > 0
    at = pl.multiple_of(jnp.where(is_upper, rows, 0), 8)
    wet = wet_ref[pl.ds(at, rows), :].astype(F32)
    north = north_ref[pl.ds(at, rows), :]
    east = east_ref[pl.ds(at, rows), :]
    chunks = col_count // LANES
    lane = lax.broadcasted_iota(jnp.int32, (1, col_count), 1)
    start = column_lane(which, rows, 0, 1, 0)
    west_cols = west_in[72:80, :].T[start : start + rows]
    start = column_lane(which, rows, 0, 0, 0)
    east_cols = east_in[72:80, :].T[start : start + rows]
    west_wet = jnp.where(lane == 0, west_cols[:, 3:4], pltpu.roll(wet, 1, 1))
    west_coef = jnp.where(lane == 0, west_cols[:, 5:6], pltpu.roll(east, 1, 1))
    east_wet = jnp.where(
        lane == col_count - 1, east_cols[:, 3:4], pltpu.roll(wet, col_count - 1, 1)
    )
    east_w = east * wet * east_wet
    west_w = west_coef * west_wet * wet

    def piece(c):
        return slice(c * LANES, (c + 1) * LANES)

    spare_ref = edge_in.at[2 * LEVELS - 6 : 2 * LEVELS + 2]
    if which == FAR:
        for c in range(chunks):
            fold_ref[:, piece(c)] = fold_row(spare_ref, mirror_ref, piece, c, chunks, 8)
    spare = spare_ref[...]
    last = rows - 1
    inner_wet = jnp.where(
        is_upper, wet_ref[rows - 1 : rows, :], wet_ref[rows : rows + 1, :]
    ).astype(F32)
    above = jnp.where(is_upper, spare[6:7], inner_wet)
    top_w = north[last:] * wet[last:] * above
    if which == FAR:
        fold = 0.5 * (north[last:] + fold_ref[7:8]) * wet[last:] * fold_ref[6:7]
        top_w = jnp.where(flag_ref[TOP] > 0, fold, top_w)
    below = jnp.where(is_upper, north_ref[rows - 1 : rows, :] * inner_wet, spare[7:8] * spare[6:7])
    between = north[:last] * wet[:last] * wet[1:]
    north_w = jnp.concatenate([between, top_w], axis=0)
    south_w = jnp.concatenate([below * wet[0:1], between], axis=0)
    center = 1.0 - (east_w + west_w + north_w + south_w)
    for kind, weight in enumerate((center, east_w, west_w, north_w, south_w)):
        for row in range(rows):
            out_ref[row, kind : kind + 1, :] = weight[row : row + 1]


def edge_weights(which, flags, coast, received, mirror):
    row_count, col_count = coast[0].shape

    def kernel(*refs):
        weight_kernel(which, *refs)

    return pl.pallas_call(
        kernel,
        in_specs=in_place(7),
        out_shape=jax.ShapeDtypeStruct((row_count // 2, 8, col_count), F32),
        scratch_shapes=[pltpu.VMEM((8, col_count), F32)],
        compiler_params=pltpu.CompilerParams(vmem_limit_bytes=16 * MIB),
        name="edge_weights",
    )(flags, *coast, *received, mirror)


def receive_row(which, flag_ref, edge_in, mirror_ref, row_ref):
    levels, col_count = edge_in.shape
    chunks = col_count // LANES
    is_top = flag_ref[TOP] > 0

    def piece(c):
        return slice(c * LANES, (c + 1) * LANES)

    def plain():
        for c in range(chunks):
            unpack_row(edge_in[:, piece(c)], row_ref, piece(c))

    if which == NEAR:
        plain()
        return

    @pl.when(jnp.logical_not(is_top))
    def _():
        plain()

    @pl.when(is_top)
    def _():
        for c in range(chunks):
            unpack_row(
                fold_row(edge_in, mirror_ref, piece, c, chunks, levels), row_ref, piece(c)
            )


def neighbour_rows(is_upper, inner, outer_ref, south_ref, north_ref):
    @pl.when(is_upper)
    def _():
        south_ref[...] = inner[...]
        north_ref[...] = outer_ref[...]

    @pl.when(jnp.logical_not(is_upper))
    def _():
        south_ref[...] = outer_ref[...]
        north_ref[...] = inner[...]


def mix_row(which, row, rows, field, state_ref, south_ref, north_ref, west_in, east_in, coef_ref, right_ref, slot):
    col_count = state_ref.shape[2]
    chunks = col_count // LANES
    lane = lax.broadcasted_iota(jnp.int32, (1, LANES), 1)
    levels = slice(field * PAD, (field + 1) * PAD)

    def piece(chunk):
        return slice(chunk * LANES, (chunk + 1) * LANES)

    west_lane = column_lane(which, rows, field, 1, row)
    east_lane = column_lane(which, rows, field, 0, row)
    centers = [state_ref[row, levels, piece(c)] for c in range(chunks)]
    to_left = [pltpu.roll(c, LANES - 1, 1) for c in centers]
    to_right = [pltpu.roll(c, 1, 1) for c in centers]
    to_right.append(pltpu.roll(west_in[...], LANES - west_lane, 1))
    to_left.append(pltpu.roll(east_in[...], LANES - 1 - east_lane, 1))
    for c in range(chunks):
        south = south_ref[levels, piece(c)]
        north = north_ref[levels, piece(c)]
        east = jnp.where(lane == LANES - 1, to_left[c + 1], to_left[c])
        west = jnp.where(lane == 0, to_right[c - 1], to_right[c])

        def coef(kind):
            return coef_ref[row, kind : kind + 1, piece(c)]

        mixed = (
            coef(0) * centers[c]
            + coef(1) * east
            + coef(2) * west
            + coef(3) * north
            + coef(4) * south
        )
        high, low = split_two(mixed)
        right_ref[slot, 0:PAD, piece(c)] = high
        right_ref[slot, PAD : 2 * PAD, piece(c)] = low
        right_ref[slot, 2 * PAD : 3 * PAD, piece(c)] = high


def sweep_rows(which, rows, units, state_ref, south_ref, north_ref, west_in, east_in, coef_ref, matrix_ref, right_ref, emit):
    slots = right_ref.shape[0]
    right_ref[:, 3 * PAD :, :] = jnp.zeros((slots,) + (256 - 3 * PAD, right_ref.shape[2]), BF)

    def product(number):
        row, field = units[number]
        emit(number, row, field, mm(matrix_ref[field, row], right_ref[number % slots]))

    for number, (row, field) in enumerate(units):
        south = state_ref.at[row - 1] if row > 0 else south_ref
        north = state_ref.at[row + 1] if row < rows - 1 else north_ref
        mix_row(which, row, rows, field, state_ref, south, north, west_in, east_in, coef_ref, right_ref, number % slots)
        if number > 0:
            product(number - 1)
    product(len(units) - 1)


def diffuse(which, flags, state, other, received, mirror, coef, matrix, *far_cols):
    rows = coef.shape[0]
    col_count = state.shape[2]

    def kernel(flag_ref, state_ref, other_ref, edge_in, west_in, east_in, mirror_ref, coef_ref, matrix_ref, *refs):
        out_ref, edge_ref, cols_ref, south_ref, north_ref, outer_ref, right_ref = refs[-7:]
        is_upper = flag_ref[which] > 0
        if state.shape[0] > rows:
            state_ref = state_ref.at[pl.ds(jnp.where(is_upper, rows, 0), rows)]
            inner = other_ref.at[jnp.where(is_upper, rows - 1, rows)]
        else:
            inner = other_ref.at[jnp.where(is_upper, rows - 1, 0)]
        receive_row(which, flag_ref, edge_in, mirror_ref, outer_ref)
        neighbour_rows(is_upper, inner, outer_ref, south_ref, north_ref)

        def emit(number, row, field, result):
            out_ref[row, field * PAD : (field + 1) * PAD] = result

        units = [(row, field) for row in range(rows) for field in range(2)]
        sweep_rows(which, rows, units, state_ref, south_ref, north_ref, west_in, east_in, coef_ref, matrix_ref, right_ref, emit)
        write_edge(is_upper, out_ref, edge_ref)
        old_cols = refs[0][...] if which == NEAR else jnp.zeros((PAD, LANES), F32)
        cols_ref[...] = columns_of(which, out_ref, old_cols)

    return pl.pallas_call(
        kernel,
        in_specs=in_place(8 + len(far_cols)),
        out_shape=half_shapes(2 * rows, col_count),
        scratch_shapes=[pltpu.VMEM((2 * PAD, col_count), F32)] * 3
        + [pltpu.VMEM((4, 256, col_count), BF)],
        compiler_params=pltpu.CompilerParams(vmem_limit_bytes=16 * MIB),
        cost_estimate=pl.CostEstimate(
            flops=3_000_000_000, bytes_accessed=8_000_000, transcendentals=0
        ),
        name="diffusion_" + ("near", "far")[which],
    )(flags, state, other, *received, mirror, coef, matrix, *far_cols)


def output_layout(results):
    return jnp.swapaxes(jnp.stack(results), 0, 1)[:LEVELS]


def store_block(out_ref, stage_ref, sem, at, field):
    rows = stage_ref.shape[2]
    copy = pltpu.make_async_copy(
        stage_ref.at[field],
        out_ref.at[pl.ds(field * LEVELS, LEVELS), pl.ds(at, rows), :],
        sem.at[field],
    )
    copy.start()
    return copy


def last_inner(flags, near, far, near_edge, near_sides, far_sides, mirror, near_fixed, far_fixed, mask):
    rows, _, col_count = near.shape

    def kernel(flag_ref, near_ref, far_ref, edge_in, near_west, near_east, far_west, far_east, mirror_ref, near_coef, near_matrix, far_coef, far_matrix, mask_ref, out_ref, done_ref, south_ref, north_ref, outer_ref, right_ref, stage_ref, sem, kept_ref):
        is_upper = flag_ref[NEAR] > 0
        at = pl.multiple_of(jnp.where(is_upper, rows, 0), 8)
        wet = mask_ref[pl.ds(at, rows), :].astype(F32)
        far_at = pl.multiple_of(rows - at, 8)
        far_wet = mask_ref[pl.ds(far_at, rows), :].astype(F32)
        last = rows - 1
        far_inner = far_ref.at[jnp.where(is_upper, last, 0)]
        receive_row(NEAR, flag_ref, edge_in, mirror_ref, outer_ref)
        neighbour_rows(is_upper, far_inner, outer_ref, south_ref, north_ref)
        copies = []
        for field in range(2):
            results = []

            def emit(number, row, field, result):
                results.append(result * wet[row : row + 1])

            units = [(row, field) for row in range(rows)]
            sweep_rows(NEAR, rows, units, near_ref, south_ref, north_ref, near_west, near_east, near_coef, near_matrix, right_ref, emit)
            stage_ref[field] = output_layout(results)
            copies.append(store_block(out_ref, stage_ref, sem, at, field))
        edge = jnp.where(is_upper, last, 0)
        near_inner = near_ref.at[jnp.where(is_upper, 0, last)]

        @pl.when(is_upper)
        def _():
            south_ref[...] = far_ref[last - 1]
            north_ref[...] = near_inner[...]

        @pl.when(jnp.logical_not(is_upper))
        def _():
            south_ref[...] = near_inner[...]
            north_ref[...] = far_ref[1]

        def keep(number, row, field, result):
            kept_ref[row, field * PAD : (field + 1) * PAD] = result * far_wet[row : row + 1]

        units = [(row, field) for row in range(1, last) for field in range(2)]
        sweep_rows(FAR, rows, units, far_ref, south_ref, north_ref, far_west, far_east, far_coef, far_matrix, right_ref, keep)
        edge_wet = jnp.where(is_upper, far_wet[last:], far_wet[0:1])
        for field in range(2):
            mix_row(FAR, edge, rows, field, far_ref, south_ref, north_ref, far_west, far_east, far_coef, right_ref, field)
        for field in range(2):
            result = mm(far_matrix[field, edge], right_ref[field])
            kept_ref[edge, field * PAD : (field + 1) * PAD] = result * edge_wet
        for field in range(2):
            levels = slice(field * PAD, (field + 1) * PAD)
            done_ref[field] = output_layout([kept_ref[row, levels] for row in range(rows)])
        for copy in copies:
            copy.wait()

    return pl.pallas_call(
        kernel,
        in_specs=in_place(13),
        out_specs=[pl.BlockSpec(memory_space=pl.ANY), pl.BlockSpec(memory_space=pltpu.VMEM)],
        out_shape=(
            jax.ShapeDtypeStruct((2 * LEVELS, 2 * rows, col_count), F32),
            jax.ShapeDtypeStruct((2, LEVELS, rows, col_count), F32),
        ),
        scratch_shapes=[pltpu.VMEM((2 * PAD, col_count), F32)] * 3
        + [
            pltpu.VMEM((4, 256, col_count), BF),
            pltpu.VMEM((2, LEVELS, rows, col_count), F32),
            pltpu.SemaphoreType.DMA((2,)),
            pltpu.VMEM((rows, 2 * PAD, col_count), F32),
        ],
        compiler_params=pltpu.CompilerParams(vmem_limit_bytes=22 * MIB),
        cost_estimate=pl.CostEstimate(
            flops=6_000_000_000, bytes_accessed=16_000_000, transcendentals=0
        ),
        name="last_inner",
    )(flags, near, far, near_edge, *near_sides, *far_sides, mirror, *near_fixed, *far_fixed, mask)


def last_outer(flags, far, far_edge, far_sides, mirror, far_fixed, mask, done, target):
    rows, _, col_count = far.shape

    def kernel(flag_ref, far_ref, edge_in, west_in, east_in, mirror_ref, coef_ref, matrix_ref, mask_ref, done_ref, target_ref, out_ref, south_ref, north_ref, outer_ref, right_ref, stage_ref, sem):
        is_upper = flag_ref[FAR] > 0
        at = pl.multiple_of(jnp.where(is_upper, rows, 0), 8)
        wet = mask_ref[pl.ds(at, rows), :].astype(F32)
        last = rows - 1
        row = jnp.where(is_upper, last, 0)
        row_wet = jnp.where(is_upper, wet[last:], wet[0:1])
        receive_row(FAR, flag_ref, edge_in, mirror_ref, outer_ref)
        neighbour_rows(is_upper, far_ref.at[jnp.where(is_upper, last - 1, 1)], outer_ref, south_ref, north_ref)
        right_ref[:, 3 * PAD :, :] = jnp.zeros((2, 256 - 3 * PAD, col_count), BF)
        for field in range(2):
            mix_row(FAR, row, rows, field, far_ref, south_ref, north_ref, west_in, east_in, coef_ref, right_ref, field)
        copies = []
        here = lax.broadcasted_iota(jnp.int32, (rows, 1), 0) == row
        for field in range(2):
            outer_ref[0:PAD] = mm(matrix_ref[field, row], right_ref[field]) * row_wet
            for level in range(LEVELS):
                stage_ref[field, level] = jnp.where(
                    here, outer_ref[level : level + 1, :], done_ref[field, level]
                )
            copies.append(store_block(out_ref, stage_ref, sem, at, field))
        for copy in copies:
            copy.wait()

    operands = [flags, far, far_edge, *far_sides, mirror, *far_fixed, mask, done, target]
    return pl.pallas_call(
        kernel,
        in_specs=in_place(9) + [pl.BlockSpec(memory_space=pl.ANY)],
        out_specs=pl.BlockSpec(memory_space=pl.ANY),
        out_shape=jax.ShapeDtypeStruct((2 * LEVELS, 2 * rows, col_count), F32),
        input_output_aliases={len(operands) - 1: 0},
        scratch_shapes=[pltpu.VMEM((2 * PAD, col_count), F32)] * 3
        + [
            pltpu.VMEM((2, 256, col_count), BF),
            pltpu.VMEM((2, LEVELS, rows, col_count), F32),
            pltpu.SemaphoreType.DMA((2,)),
        ],
        compiler_params=pltpu.CompilerParams(vmem_limit_bytes=20 * MIB),
        name="last_outer",
    )(*operands)


def mixing_matrices(vinv):
    turned = jnp.transpose(vinv, (1, 0, 3, 2))
    turned = jnp.pad(turned, ((0, 0), (0, 0), (0, PAD - LEVELS), (0, PAD - LEVELS)))
    high = lax.reduce_precision(turned, 8, 7)
    low = (turned - high).astype(BF)
    high = high.astype(BF)
    rest = jnp.zeros(high.shape[:3] + (256 - 3 * PAD,), BF)
    return jnp.concatenate([high, high, low, rest], axis=3)


def body(
    argo_value,
    argo_owner,
    argo_cell,
    alt_value,
    alt_owner,
    alt_cell,
    alt_profile,
    land_mask,
    coef_east,
    coef_north,
    mirror,
    vinv,
):
    row_count, col_count = land_mask.shape
    count_ja = lax.axis_size("ja")
    count_ia = lax.axis_size("ia")
    devices = count_ja * count_ia
    capacity = round_up(3 * argo_value.shape[0] // devices, 8)
    group = round_up(capacity // 4, 8)
    message = send_tables(
        devices,
        capacity,
        group,
        row_count,
        col_count,
        (
            argo_value.T,
            argo_owner.reshape(1, -1),
            argo_cell.reshape(1, -1),
            alt_value,
            alt_cell,
            alt_owner.reshape(1, -1),
        ),
    )
    message, ja_index = lax.optimization_barrier((message, lax.axis_index("ja")))
    message = lax.all_to_all(message, ("ja", "ia"), split_axis=0, concat_axis=0, tiled=True)

    ia_index = lax.axis_index("ia")
    is_top = (ja_index == count_ja - 1).astype(jnp.int32)
    parity = ja_index % 2
    flags = jnp.stack([1 - parity, parity, is_top]).astype(jnp.int32)
    fold_index = mirror - (count_ia - 1 - ia_index) * col_count
    mirror_lane = jnp.broadcast_to((fold_index % LANES)[None, :], (8, col_count))
    matrices = mixing_matrices(vinv)
    profile = jnp.pad(alt_profile.reshape(2, LEVELS, 1), ((0, 0), (0, PAD - LEVELS), (0, 0)))
    profile = profile.reshape(2 * PAD, 1)
    alt_capacity = max(2, 3 * alt_value.shape[0] // devices)
    coast = (land_mask, coef_north, coef_east)
    rows = row_count // 2
    lower = [matrices[:, :rows], matrices[:, rows:]]
    odd_device = parity == 1
    half_matrices = [
        jnp.where(odd_device, lower[0], lower[1]),
        jnp.where(odd_device, lower[1], lower[0]),
    ]

    ring_east = [(i, (i + 1) % count_ia) for i in range(count_ia)]
    ring_west = [((i + 1) % count_ia, i) for i in range(count_ia)]
    even_swap = []
    odd_swap = []
    for ja in range(count_ja):
        for ia in range(count_ia):
            here = ja * count_ia + ia
            even_swap.append((here, (ja ^ 1) * count_ia + ia))
            if ja == count_ja - 1:
                odd_swap.append((here, ja * count_ia + count_ia - 1 - ia))
            elif ja > 0:
                odd_swap.append((here, (((ja - 1) ^ 1) + 1) * count_ia + ia))
    swaps = (even_swap, odd_swap)

    def swap(which, edge):
        return lax.ppermute(edge, ("ja", "ia"), swaps[which])

    def pass_columns(cols):
        return lax.ppermute(cols, "ia", ring_east), lax.ppermute(cols, "ia", ring_west)

    near_edge, *prepared = first_forcing(
        capacity, alt_capacity, group, flags, message, profile, coast
    )
    near_edge = swap(NEAR, near_edge)
    state, far_edge, cols = rest_forcing(flags, profile, coast, prepared)
    near = far = state
    sides = pass_columns(cols)
    far_edge = swap(FAR, far_edge)
    near_coef = edge_weights(NEAR, flags, coast, (near_edge, *sides), mirror_lane)
    far_coef = edge_weights(FAR, flags, coast, (far_edge, *sides), mirror_lane)
    near_fixed = (mirror_lane, near_coef, half_matrices[NEAR])
    far_fixed = (mirror_lane, far_coef, half_matrices[FAR])
    for sweep in range(ITERS - 1):
        new_near, new_edge, cols = diffuse(
            NEAR, flags, near, far, (near_edge, *sides), *near_fixed, cols
        )
        near_edge = swap(NEAR, new_edge)
        sides = pass_columns(cols)
        far, new_edge, cols = diffuse(FAR, flags, far, near, (far_edge, *sides), *far_fixed)
        far_edge = swap(FAR, new_edge)
        near = new_near
    last_sides = pass_columns(cols)
    output, done = last_inner(
        flags, near, far, near_edge, sides, last_sides, mirror_lane, near_fixed[1:], far_fixed[1:], land_mask
    )
    return last_outer(
        flags, far, far_edge, last_sides, mirror_lane, far_fixed[1:], land_mask, done, output
    )


def solution(mesh):
    in_specs = (
        P(("ja", "ia"), None),
        P(("ja", "ia"), None),
        P(("ja", "ia")),
        P(("ja", "ia")),
        P(("ja", "ia"), None),
        P(("ja", "ia")),
        P(),
        P("ja", "ia"),
        P("ja", "ia"),
        P("ja", "ia"),
        P("ia"),
        P("ja", None, None, None),
    )
    out_specs = P(None, "ja", "ia")
    return jax.shard_map(body, mesh=mesh, in_specs=in_specs, out_specs=out_specs, check_vma=False)
```

```python
import math

import jax
import jax.numpy as jnp
from jax import lax
from jax.experimental import pallas as pl
from jax.experimental.pallas import tpu as pltpu
from jax.sharding import PartitionSpec as P

ITERS = 3
LEVELS = 75
PAD = 80
LANES = 128
NEAR, FAR, TOP = 0, 1, 2
BF = jnp.bfloat16
F32 = jnp.float32
MIB = 1024 * 1024


def round_up(value, unit):
    return (value + unit - 1) // unit * unit


def split_two(value):
    high = value.astype(BF)
    low = (value - high.astype(F32)).astype(BF)
    return high, low


def mm(left, right):
    return jnp.dot(left, right, preferred_element_type=F32)


def as_column(row):
    return jnp.broadcast_to(row, (8, row.shape[1])).T[:, 0:1]


def slot_ranks(owner_row, cell_row, devices, col_count, row_count, capacity, spread):
    count = owner_row.shape[1]
    owner = owner_row.astype(F32)
    inside = cell_row // col_count
    order = lax.broadcasted_iota(jnp.int32, (1, count), 1).astype(F32)
    key = (owner * float(row_count) + inside.astype(F32)) * float(count) + order
    key_col = as_column(key)
    device = lax.broadcasted_iota(jnp.int32, (devices, 1), 0)
    mine = device == owner_row
    totals = jnp.sum(jnp.where(mine, 1.0, 0.0), axis=1, keepdims=True)
    rank = -jnp.sum(jnp.where(device < owner_row, totals, 0.0), axis=0, keepdims=True)
    for start in range(0, count, 128):
        before = jnp.where(key_col[start : start + 128] < key, 1.0, 0.0)
        rank = rank + jnp.sum(before, axis=0, keepdims=True)
    if spread:
        total = jnp.sum(jnp.where(mine, totals, 0.0), axis=0, keepdims=True)
        offset = owner * 1024.0
        goal = (inside * capacity // row_count).astype(F32) - rank + offset
        goal_col = as_column(goal)
        shift = offset
        for start in range(0, count, 128):
            within = key_col[start : start + 128] <= key
            reached = jnp.where(within, goal_col[start : start + 128], 0.0)
            shift = jnp.maximum(shift, jnp.max(reached, axis=0, keepdims=True))
        rank = rank + jnp.minimum(shift - offset, float(capacity) - total)
    return rank


def table_kernel(
    devices,
    capacity,
    group,
    row_count,
    col_count,
    value_ref,
    owner_ref,
    cell_ref,
    alt_value_ref,
    alt_cell_ref,
    alt_owner_ref,
    message_ref,
    level_ref,
    side_ref,
    hi_ref,
    lo_ref,
    alt_all_ref,
    rank_hot_ref,
    alt_rank_hot_ref,
):
    index = pl.program_id(0)
    n_obs = owner_ref.shape[1]
    n_alt = alt_owner_ref.shape[1]

    @pl.when(index == 0)
    def _():
        slot = lax.broadcasted_iota(jnp.int32, (capacity, 1), 0).astype(F32)
        alt_cell = alt_cell_ref[...].reshape(1, n_alt)
        rank = slot_ranks(
            owner_ref[...], cell_ref[...], devices, col_count, row_count, capacity, True
        )
        rank_hot_ref[...] = jnp.where(slot == rank, 1.0, 0.0).astype(BF)
        rank = slot_ranks(
            alt_owner_ref[...], alt_cell, devices, col_count, row_count, capacity, False
        )
        alt_rank_hot_ref[...] = jnp.where(slot == rank, 1.0, 0.0).astype(BF)
        level_ref[...] = jnp.zeros(level_ref.shape, F32)
        level_ref[0:75, :] = value_ref[0:75, :]
        level_ref[75:76, :] = cell_ref[...].astype(F32) + 1.0
        level_ref[80:128, :] = value_ref[75:123, :]
        for lane_group in range(4):
            level_ref[128 + 32 * lane_group : 155 + 32 * lane_group, :] = value_ref[123:150, :]
        high, low = split_two(level_ref[...].T)
        hi_ref[...] = high
        lo_ref[...] = low
        pair = jnp.concatenate(
            [alt_value_ref[...].reshape(1, n_alt), alt_cell.astype(F32) + 1.0], axis=0
        )
        pair_high = pair.astype(BF).astype(F32)
        side_ref[...] = jnp.zeros(side_ref.shape, F32)
        side_ref[:, 0:8] = jnp.concatenate(
            [pair_high, pair - pair_high, jnp.zeros((4, n_alt), F32)], axis=0
        ).T
        alt_all_ref[...] = pltpu.roll(side_ref[...], 76, 1).astype(BF)

    per_step = message_ref.shape[0]
    chosen = []
    chosen_alt = []
    for member in range(per_step):
        device = index * per_step + member
        mask = jnp.where(owner_ref[...] == device, 1.0, 0.0).astype(BF)
        chosen.append(rank_hot_ref[...] * mask)
        mask = jnp.where(alt_owner_ref[...] == device, 1.0, 0.0).astype(BF)
        chosen_alt.append(alt_rank_hot_ref[...] * mask)
    chosen = jnp.concatenate(chosen, axis=0)
    chosen_alt = jnp.concatenate(chosen_alt, axis=0)
    table = mm(chosen, hi_ref[...]) + mm(chosen, lo_ref[...])
    lane = lax.broadcasted_iota(jnp.int32, (1, LANES), 1)
    extra = mm(chosen_alt, alt_all_ref[...])
    extra = jnp.where(lane < 78, extra + pltpu.roll(extra, LANES - 2, 1), 0.0)
    extra = jnp.where(lane >= 76, extra, 0.0)
    first = table[:, :LANES] + extra
    message_ref[:, 0:capacity] = first.reshape(per_step, capacity, LANES)
    rest = table[:, LANES:].reshape(per_step, capacity, LANES)
    total = jnp.zeros((per_step, group, LANES), F32)
    for lane_group in range(4):
        low_slot = lane_group * group
        if low_slot >= capacity:
            continue
        piece = rest[:, low_slot : low_slot + group]
        here = (lane // 32 == lane_group).reshape(1, 1, LANES)
        total = jnp.where(here, piece, total)
    message_ref[:, capacity : capacity + group] = total


def send_tables(devices, capacity, group, row_count, col_count, operands):
    n_obs = operands[1].shape[1]
    n_alt = operands[5].shape[1]
    per_step = max(1, 1536 // capacity)

    def kernel(*refs):
        table_kernel(devices, capacity, group, row_count, col_count, *refs)

    def whole(array):
        return pl.BlockSpec(array.shape, lambda s: (0,) * len(array.shape))

    return pl.pallas_call(
        kernel,
        grid=(devices // per_step,),
        in_specs=[whole(x) for x in operands],
        out_specs=pl.BlockSpec((per_step, capacity + group, LANES), lambda s: (s, 0, 0)),
        out_shape=jax.ShapeDtypeStruct((devices, capacity + group, LANES), F32),
        scratch_shapes=[
            pltpu.VMEM((2 * LANES, n_obs), F32),
            pltpu.VMEM((n_alt, LANES), F32),
            pltpu.VMEM((n_obs, 2 * LANES), BF),
            pltpu.VMEM((n_obs, 2 * LANES), BF),
            pltpu.VMEM((n_alt, LANES), BF),
            pltpu.VMEM((capacity, n_obs), BF),
            pltpu.VMEM((capacity, n_alt), BF),
        ],
        compiler_params=pltpu.CompilerParams(vmem_limit_bytes=56 * MIB),
        name="send_tables",
    )(*operands)


def column_lane(which, rows, field, east, row):
    return (4 * which + 2 * field + east) * rows + row


def columns_of(which, state_ref, cols):
    rows = state_ref.shape[0]
    lane = lax.broadcasted_iota(jnp.int32, (1, LANES), 1)
    for row in range(rows):
        for field in range(2):
            part = state_ref[row, field * PAD : (field + 1) * PAD, :]
            at = column_lane(which, rows, field, 0, row)
            cols = jnp.where(lane == at, pltpu.roll(part[:, :LANES], at, 1), cols)
            at = column_lane(which, rows, field, 1, row)
            cols = jnp.where(lane == at, pltpu.roll(part[:, -LANES:], at + 1, 1), cols)
    return cols


def pack_row(row_ref, edge_ref):
    edge_ref[0:LEVELS] = row_ref[0:LEVELS]
    edge_ref[LEVELS : 2 * LEVELS] = row_ref[PAD : PAD + LEVELS]
    edge_ref[2 * LEVELS : 2 * LEVELS + 2] = row_ref[LEVELS : LEVELS + 2]


def unpack_row(edge, row_ref, piece):
    row_ref[0:LEVELS, piece] = edge[0:LEVELS]
    row_ref[PAD : PAD + LEVELS, piece] = edge[LEVELS : 2 * LEVELS]
    for at in (LEVELS, PAD + LEVELS):
        row_ref[at : at + PAD - LEVELS, piece] = jnp.zeros((PAD - LEVELS, edge.shape[1]), F32)


def write_edge(is_upper, state_ref, edge_ref):
    pack_row(state_ref.at[jnp.where(is_upper, state_ref.shape[0] - 1, 0)], edge_ref)


def prepare(capacity, alt_capacity, group, col_count, message_ref, sea_ref, left_ref, hot_ref, rows_ref, bound_ref):
    row_count = sea_ref.shape[0]
    devices = message_ref.shape[0]
    block = min(32, devices)
    members = block * 8
    octets = capacity // 8
    alt_octets = (alt_capacity + 7) // 8
    per_group = group // 8
    shift = col_count.bit_length() - 1
    col_iota = lax.broadcasted_iota(jnp.int32, (1, col_count), 1)
    row_iota = lax.broadcasted_iota(jnp.int32, (row_count, 1), 0)

    def chunk(index, start):
        return message_ref[index * block : (index + 1) * block, start : start + 8, :].reshape(
            members, LANES
        )

    def hot_of(cell):
        return jnp.where(((cell - 1) & (col_count - 1)) == col_iota, 1.0, 0.0).astype(BF)

    def rows_of(cell):
        return lax.shift_right_arithmetic(cell - 1, shift)

    sea = jnp.zeros((row_count, col_count), F32)
    count = 0
    for index in range(devices // block):
        tails = [chunk(index, capacity + 8 * part).T for part in range(per_group)]
        for octet in range(octets):
            table = chunk(index, 8 * octet)
            turned = table.T
            tail = tails[octet % per_group]
            begin = 32 * (octet // per_group)
            levels = jnp.concatenate([turned, tail[begin : begin + 32]], axis=0)
            high, low = split_two(levels)
            left_ref[count, :, 0:members] = high
            left_ref[count, :, members : 2 * members] = low
            hot = hot_of(table[:, 75:76].astype(jnp.int32))
            hot_ref[count] = hot
            rows = rows_of(turned[75:76].astype(jnp.int32))
            rows_ref[count] = jnp.broadcast_to(rows, (8, members))
            bound_ref[2 * count] = jnp.min(jnp.where(rows >= 0, rows, row_count))
            bound_ref[2 * count + 1] = jnp.max(rows)
            count += 1
            if octet >= alt_octets:
                continue
            alt_hot = hot_of(table[:, 77:78].astype(jnp.int32))
            alt_rows = rows_of(turned[77:78].astype(jnp.int32))
            weighted = jnp.where(alt_rows == row_iota, turned[76:77], 0.0)
            high, low = split_two(weighted)
            product = mm(jnp.concatenate([high, low], axis=0), alt_hot)
            sea = sea + product[:row_count] + product[row_count:]
    sea_ref[...] = sea


def chosen_rows(number, here, row, span, left_ref, hot_ref):
    pieces = []
    for offset in range(span):
        mask = jnp.where(here == row + offset, 1.0, 0.0).astype(BF)
        pieces.append(left_ref[number] * jnp.concatenate([mask, mask], axis=1))
    hot = hot_ref[number]
    return mm(jnp.concatenate(pieces, axis=0), jnp.concatenate([hot, hot], axis=0))


def outer_forcing(row, is_upper, profile_ref, coast_refs, sea_ref, left_ref, hot_ref, rows_ref, bound_ref, edge_ref):
    row_count, col_count = sea_ref.shape
    last = row_count - 1
    profile = jnp.broadcast_to(profile_ref[...], (2 * PAD, LANES))
    sea = jnp.where(is_upper, sea_ref[last : last + 1, :], sea_ref[0:1, :])
    for start in range(0, col_count, LANES):
        edge_ref[:, start : start + LANES] = profile * sea[:, start : start + LANES]

    def step(number, carry):
        @pl.when((bound_ref[2 * number] <= row) & (row <= bound_ref[2 * number + 1]))
        def _():
            edge_ref[...] += chosen_rows(number, rows_ref[number][0:1], row, 1, left_ref, hot_ref)

        return carry

    lax.fori_loop(0, left_ref.shape[0], step, 0)
    for kind, coast_ref in enumerate(coast_refs):
        coast = jnp.where(is_upper, coast_ref[last : last + 1, :], coast_ref[0:1, :])
        edge_ref[LEVELS + kind : LEVELS + kind + 1, :] = coast.astype(F32)


def all_forcing(profile_ref, coast_refs, sea_ref, left_ref, hot_ref, rows_ref, bound_ref, state):
    row_count, _, col_count = state.shape
    count = left_ref.shape[0]
    for start in range(0, col_count, LANES):
        profile = jnp.broadcast_to(profile_ref[...], (2 * PAD, LANES))
        for row in range(row_count):
            state[row, :, start : start + LANES] = profile * sea_ref[row : row + 1, start : start + LANES]
    batch = math.gcd(count, 4)
    narrow, wide = 3, 6

    def step(number, carry):
        chunks = [number * batch + member for member in range(batch)]
        least = [bound_ref[2 * chunk] for chunk in chunks]
        extent = bound_ref[2 * chunks[0] + 1] - least[0]
        for i in range(1, batch):
            extent = jnp.maximum(extent, bound_ref[2 * chunks[i] + 1] - least[i])

        def add_runs(span, turn, inner):
            for i, chunk in enumerate(chunks):
                begin = least[i] + turn * span
                base = jnp.minimum(begin, row_count - span)
                here = rows_ref[chunk][0:1]
                here = jnp.where(here >= begin, here, -1)
                product = chosen_rows(chunk, here, base, span, left_ref, hot_ref)
                for offset in range(span):
                    state[base + offset] += product[2 * PAD * offset : 2 * PAD * (offset + 1)]
            return inner

        once = (extent >= 0) & (extent < narrow)
        lax.fori_loop(0, once.astype(jnp.int32), lambda t, c: add_runs(narrow, t, c), 0)
        turns = jnp.where(extent < narrow, 0, lax.div(extent + wide, wide))
        lax.fori_loop(0, turns, lambda t, c: add_runs(wide, t, c), 0)
        return carry

    lax.fori_loop(0, count // batch, step, 0)
    for kind, coast_ref in enumerate(coast_refs):
        coast = coast_ref[...].astype(F32)
        for row in range(row_count):
            state[row, LEVELS + kind : LEVELS + kind + 1, :] = coast[row : row + 1, :]


def half_shapes(row_count, col_count):
    return (
        jax.ShapeDtypeStruct((row_count // 2, 2 * PAD, col_count), F32),
        jax.ShapeDtypeStruct((2 * LEVELS + 2, col_count), F32),
        jax.ShapeDtypeStruct((PAD, LANES), F32),
    )


def in_place(count):
    return [pl.BlockSpec(memory_space=pltpu.SMEM)] + [pl.BlockSpec(memory_space=pltpu.VMEM)] * count


def first_forcing(capacity, alt_capacity, group, flags, message, profile, coast):
    row_count, col_count = coast[0].shape
    devices = message.shape[0]
    members = min(32, devices) * 8
    chunks = capacity // 8 * (devices // min(32, devices))

    def kernel(flag_ref, message_ref, profile_ref, wet, north, east, edge_ref, *refs):
        *outs, row_ref = refs
        prepare(capacity, alt_capacity, group, col_count, message_ref, *outs)
        is_upper = flag_ref[NEAR] > 0
        row = jnp.where(is_upper, row_count - 1, 0)
        outer_forcing(row, is_upper, profile_ref, (wet, north, east), *outs, row_ref)
        pack_row(row_ref, edge_ref)

    return pl.pallas_call(
        kernel,
        in_specs=in_place(5),
        out_shape=(
            half_shapes(row_count, col_count)[1],
            jax.ShapeDtypeStruct((row_count, col_count), F32),
            jax.ShapeDtypeStruct((chunks, 2 * PAD, 2 * members), BF),
            jax.ShapeDtypeStruct((chunks, members, col_count), BF),
            jax.ShapeDtypeStruct((chunks, 8, members), jnp.int32),
            jax.ShapeDtypeStruct((2 * chunks,), jnp.int32),
        ),
        out_specs=[pl.BlockSpec(memory_space=pltpu.VMEM)] * 5
        + [pl.BlockSpec(memory_space=pltpu.SMEM)],
        scratch_shapes=[pltpu.VMEM((2 * PAD, col_count), F32)],
        compiler_params=pltpu.CompilerParams(vmem_limit_bytes=24 * MIB),
        cost_estimate=pl.CostEstimate(
            flops=6_000_000_000, bytes_accessed=8_000_000, transcendentals=0
        ),
        name="forcing_first",
    )(flags, message, profile, *coast)


def rest_forcing(flags, profile, coast, prepared):
    row_count, col_count = coast[0].shape
    half = row_count // 2

    def kernel(flag_ref, profile_ref, wet, north, east, sea, left, hot, rows, bound, state, edge_ref, cols_ref):
        all_forcing(profile_ref, (wet, north, east), sea, left, hot, rows, bound, state)
        cols = jnp.zeros((PAD, LANES), F32)
        for which in (NEAR, FAR):
            first_row = jnp.where(flag_ref[which] > 0, half, 0)
            cols = columns_of(which, state.at[pl.ds(first_row, half)], cols)
        cols_ref[...] = cols
        write_edge(flag_ref[FAR] > 0, state, edge_ref)

    _, edge, cols = half_shapes(row_count, col_count)
    state = jax.ShapeDtypeStruct((row_count, 2 * PAD, col_count), F32)
    return pl.pallas_call(
        kernel,
        in_specs=in_place(8) + [pl.BlockSpec(memory_space=pltpu.SMEM)],
        out_shape=(state, edge, cols),
        compiler_params=pltpu.CompilerParams(vmem_limit_bytes=20 * MIB),
        cost_estimate=pl.CostEstimate(
            flops=6_000_000_000, bytes_accessed=8_000_000, transcendentals=0
        ),
        name="forcing_rest",
    )(flags, profile, *coast, *prepared)


def fold_row(row_ref, mirror_ref, piece, chunk, chunks, rows):
    index = jnp.broadcast_to(mirror_ref[0:1, piece(chunk)], (rows, LANES))
    return jnp.take_along_axis(row_ref[:, piece(chunks - 1 - chunk)], index, axis=1)


def weight_kernel(which, flag_ref, wet_ref, north_ref, east_ref, edge_in, west_in, east_in, mirror_ref, out_ref, fold_ref):
    row_count, col_count = wet_ref.shape
    rows = row_count // 2
    is_upper = flag_ref[which] > 0
    at = pl.multiple_of(jnp.where(is_upper, rows, 0), 8)
    wet = wet_ref[pl.ds(at, rows), :].astype(F32)
    north = north_ref[pl.ds(at, rows), :]
    east = east_ref[pl.ds(at, rows), :]
    chunks = col_count // LANES
    lane = lax.broadcasted_iota(jnp.int32, (1, col_count), 1)
    start = column_lane(which, rows, 0, 1, 0)
    west_cols = west_in[72:80, :].T[start : start + rows]
    start = column_lane(which, rows, 0, 0, 0)
    east_cols = east_in[72:80, :].T[start : start + rows]
    west_wet = jnp.where(lane == 0, west_cols[:, 3:4], pltpu.roll(wet, 1, 1))
    west_coef = jnp.where(lane == 0, west_cols[:, 5:6], pltpu.roll(east, 1, 1))
    east_wet = jnp.where(
        lane == col_count - 1, east_cols[:, 3:4], pltpu.roll(wet, col_count - 1, 1)
    )
    east_w = east * wet * east_wet
    west_w = west_coef * west_wet * wet

    def piece(c):
        return slice(c * LANES, (c + 1) * LANES)

    spare_ref = edge_in.at[2 * LEVELS - 6 : 2 * LEVELS + 2]
    if which == FAR:
        for c in range(chunks):
            fold_ref[:, piece(c)] = fold_row(spare_ref, mirror_ref, piece, c, chunks, 8)
    spare = spare_ref[...]
    last = rows - 1
    inner_wet = jnp.where(
        is_upper, wet_ref[rows - 1 : rows, :], wet_ref[rows : rows + 1, :]
    ).astype(F32)
    above = jnp.where(is_upper, spare[6:7], inner_wet)
    top_w = north[last:] * wet[last:] * above
    if which == FAR:
        fold = 0.5 * (north[last:] + fold_ref[7:8]) * wet[last:] * fold_ref[6:7]
        top_w = jnp.where(flag_ref[TOP] > 0, fold, top_w)
    below = jnp.where(is_upper, north_ref[rows - 1 : rows, :] * inner_wet, spare[7:8] * spare[6:7])
    between = north[:last] * wet[:last] * wet[1:]
    north_w = jnp.concatenate([between, top_w], axis=0)
    south_w = jnp.concatenate([below * wet[0:1], between], axis=0)
    center = 1.0 - (east_w + west_w + north_w + south_w)
    for kind, weight in enumerate((center, east_w, west_w, north_w, south_w)):
        for row in range(rows):
            out_ref[row, kind : kind + 1, :] = weight[row : row + 1]


def edge_weights(which, flags, coast, received, mirror):
    row_count, col_count = coast[0].shape

    def kernel(*refs):
        weight_kernel(which, *refs)

    return pl.pallas_call(
        kernel,
        in_specs=in_place(7),
        out_shape=jax.ShapeDtypeStruct((row_count // 2, 8, col_count), F32),
        scratch_shapes=[pltpu.VMEM((8, col_count), F32)],
        compiler_params=pltpu.CompilerParams(vmem_limit_bytes=16 * MIB),
        name="edge_weights",
    )(flags, *coast, *received, mirror)


def receive_row(which, flag_ref, edge_in, mirror_ref, row_ref):
    levels, col_count = edge_in.shape
    chunks = col_count // LANES
    is_top = flag_ref[TOP] > 0

    def piece(c):
        return slice(c * LANES, (c + 1) * LANES)

    def plain():
        for c in range(chunks):
            unpack_row(edge_in[:, piece(c)], row_ref, piece(c))

    if which == NEAR:
        plain()
        return

    @pl.when(jnp.logical_not(is_top))
    def _():
        plain()

    @pl.when(is_top)
    def _():
        for c in range(chunks):
            unpack_row(
                fold_row(edge_in, mirror_ref, piece, c, chunks, levels), row_ref, piece(c)
            )


def neighbour_rows(is_upper, inner, outer_ref, south_ref, north_ref):
    @pl.when(is_upper)
    def _():
        south_ref[...] = inner[...]
        north_ref[...] = outer_ref[...]

    @pl.when(jnp.logical_not(is_upper))
    def _():
        south_ref[...] = outer_ref[...]
        north_ref[...] = inner[...]


def mix_row(which, row, rows, field, state_ref, south_ref, north_ref, west_in, east_in, coef_ref, right_ref, slot):
    col_count = state_ref.shape[2]
    chunks = col_count // LANES
    lane = lax.broadcasted_iota(jnp.int32, (1, LANES), 1)
    levels = slice(field * PAD, (field + 1) * PAD)

    def piece(chunk):
        return slice(chunk * LANES, (chunk + 1) * LANES)

    west_lane = column_lane(which, rows, field, 1, row)
    east_lane = column_lane(which, rows, field, 0, row)
    centers = [state_ref[row, levels, piece(c)] for c in range(chunks)]
    to_left = [pltpu.roll(c, LANES - 1, 1) for c in centers]
    to_right = [pltpu.roll(c, 1, 1) for c in centers]
    to_right.append(pltpu.roll(west_in[...], LANES - west_lane, 1))
    to_left.append(pltpu.roll(east_in[...], LANES - 1 - east_lane, 1))
    for c in range(chunks):
        south = south_ref[levels, piece(c)]
        north = north_ref[levels, piece(c)]
        east = jnp.where(lane == LANES - 1, to_left[c + 1], to_left[c])
        west = jnp.where(lane == 0, to_right[c - 1], to_right[c])

        def coef(kind):
            return coef_ref[row, kind : kind + 1, piece(c)]

        mixed = (
            coef(0) * centers[c]
            + coef(1) * east
            + coef(2) * west
            + coef(3) * north
            + coef(4) * south
        )
        high, low = split_two(mixed)
        right_ref[slot, 0:PAD, piece(c)] = high
        right_ref[slot, PAD : 2 * PAD, piece(c)] = low
        right_ref[slot, 2 * PAD : 3 * PAD, piece(c)] = high


def sweep_rows(which, rows, units, state_ref, south_ref, north_ref, west_in, east_in, coef_ref, matrix_ref, right_ref, emit):
    slots = right_ref.shape[0]
    right_ref[:, 3 * PAD :, :] = jnp.zeros((slots,) + (256 - 3 * PAD, right_ref.shape[2]), BF)

    def product(number):
        row, field = units[number]
        emit(number, row, field, mm(matrix_ref[field, row], right_ref[number % slots]))

    for number, (row, field) in enumerate(units):
        south = state_ref.at[row - 1] if row > 0 else south_ref
        north = state_ref.at[row + 1] if row < rows - 1 else north_ref
        mix_row(which, row, rows, field, state_ref, south, north, west_in, east_in, coef_ref, right_ref, number % slots)
        if number > 0:
            product(number - 1)
    product(len(units) - 1)


def diffuse(which, flags, state, other, received, mirror, coef, matrix, *far_cols):
    rows = coef.shape[0]
    col_count = state.shape[2]

    def kernel(flag_ref, state_ref, other_ref, edge_in, west_in, east_in, mirror_ref, coef_ref, matrix_ref, *refs):
        out_ref, edge_ref, cols_ref, south_ref, north_ref, outer_ref, right_ref = refs[-7:]
        is_upper = flag_ref[which] > 0
        if state.shape[0] > rows:
            state_ref = state_ref.at[pl.ds(jnp.where(is_upper, rows, 0), rows)]
            inner = other_ref.at[jnp.where(is_upper, rows - 1, rows)]
        else:
            inner = other_ref.at[jnp.where(is_upper, rows - 1, 0)]
        receive_row(which, flag_ref, edge_in, mirror_ref, outer_ref)
        neighbour_rows(is_upper, inner, outer_ref, south_ref, north_ref)

        def emit(number, row, field, result):
            out_ref[row, field * PAD : (field + 1) * PAD] = result

        units = [(row, field) for row in range(rows) for field in range(2)]
        sweep_rows(which, rows, units, state_ref, south_ref, north_ref, west_in, east_in, coef_ref, matrix_ref, right_ref, emit)
        write_edge(is_upper, out_ref, edge_ref)
        old_cols = refs[0][...] if which == NEAR else jnp.zeros((PAD, LANES), F32)
        cols_ref[...] = columns_of(which, out_ref, old_cols)

    return pl.pallas_call(
        kernel,
        in_specs=in_place(8 + len(far_cols)),
        out_shape=half_shapes(2 * rows, col_count),
        scratch_shapes=[pltpu.VMEM((2 * PAD, col_count), F32)] * 3
        + [pltpu.VMEM((4, 256, col_count), BF)],
        compiler_params=pltpu.CompilerParams(vmem_limit_bytes=16 * MIB),
        cost_estimate=pl.CostEstimate(
            flops=3_000_000_000, bytes_accessed=8_000_000, transcendentals=0
        ),
        name="diffusion_" + ("near", "far")[which],
    )(flags, state, other, *received, mirror, coef, matrix, *far_cols)


def output_layout(results):
    return jnp.swapaxes(jnp.stack(results), 0, 1)[:LEVELS]


def store_block(out_ref, stage_ref, sem, at, field):
    rows = stage_ref.shape[2]
    copy = pltpu.make_async_copy(
        stage_ref.at[field],
        out_ref.at[pl.ds(field * LEVELS, LEVELS), pl.ds(at, rows), :],
        sem.at[field],
    )
    copy.start()
    return copy


def last_inner(flags, near, far, near_edge, near_sides, far_sides, mirror, near_fixed, far_fixed, mask):
    rows, _, col_count = near.shape

    def kernel(flag_ref, near_ref, far_ref, edge_in, near_west, near_east, far_west, far_east, mirror_ref, near_coef, near_matrix, far_coef, far_matrix, mask_ref, out_ref, done_ref, south_ref, north_ref, outer_ref, right_ref, stage_ref, sem, kept_ref):
        is_upper = flag_ref[NEAR] > 0
        at = pl.multiple_of(jnp.where(is_upper, rows, 0), 8)
        wet = mask_ref[pl.ds(at, rows), :].astype(F32)
        far_at = pl.multiple_of(rows - at, 8)
        far_wet = mask_ref[pl.ds(far_at, rows), :].astype(F32)
        last = rows - 1
        far_inner = far_ref.at[jnp.where(is_upper, last, 0)]
        receive_row(NEAR, flag_ref, edge_in, mirror_ref, outer_ref)
        neighbour_rows(is_upper, far_inner, outer_ref, south_ref, north_ref)
        copies = []
        for field in range(2):
            results = []

            def emit(number, row, field, result):
                results.append(result * wet[row : row + 1])

            units = [(row, field) for row in range(rows)]
            sweep_rows(NEAR, rows, units, near_ref, south_ref, north_ref, near_west, near_east, near_coef, near_matrix, right_ref, emit)
            stage_ref[field] = output_layout(results)
            copies.append(store_block(out_ref, stage_ref, sem, at, field))
        edge = jnp.where(is_upper, last, 0)
        near_inner = near_ref.at[jnp.where(is_upper, 0, last)]

        @pl.when(is_upper)
        def _():
            south_ref[...] = far_ref[last - 1]
            north_ref[...] = near_inner[...]

        @pl.when(jnp.logical_not(is_upper))
        def _():
            south_ref[...] = near_inner[...]
            north_ref[...] = far_ref[1]

        def keep(number, row, field, result):
            kept_ref[row, field * PAD : (field + 1) * PAD] = result * far_wet[row : row + 1]

        units = [(row, field) for row in range(1, last) for field in range(2)]
        sweep_rows(FAR, rows, units, far_ref, south_ref, north_ref, far_west, far_east, far_coef, far_matrix, right_ref, keep)
        edge_wet = jnp.where(is_upper, far_wet[last:], far_wet[0:1])
        for field in range(2):
            mix_row(FAR, edge, rows, field, far_ref, south_ref, north_ref, far_west, far_east, far_coef, right_ref, field)
        for field in range(2):
            result = mm(far_matrix[field, edge], right_ref[field])
            kept_ref[edge, field * PAD : (field + 1) * PAD] = result * edge_wet
        for field in range(2):
            levels = slice(field * PAD, (field + 1) * PAD)
            done_ref[field] = output_layout([kept_ref[row, levels] for row in range(rows)])
        for copy in copies:
            copy.wait()

    return pl.pallas_call(
        kernel,
        in_specs=in_place(13),
        out_specs=[pl.BlockSpec(memory_space=pl.ANY), pl.BlockSpec(memory_space=pltpu.VMEM)],
        out_shape=(
            jax.ShapeDtypeStruct((2 * LEVELS, 2 * rows, col_count), F32),
            jax.ShapeDtypeStruct((2, LEVELS, rows, col_count), F32),
        ),
        scratch_shapes=[pltpu.VMEM((2 * PAD, col_count), F32)] * 3
        + [
            pltpu.VMEM((4, 256, col_count), BF),
            pltpu.VMEM((2, LEVELS, rows, col_count), F32),
            pltpu.SemaphoreType.DMA((2,)),
            pltpu.VMEM((rows, 2 * PAD, col_count), F32),
        ],
        compiler_params=pltpu.CompilerParams(vmem_limit_bytes=22 * MIB),
        cost_estimate=pl.CostEstimate(
            flops=6_000_000_000, bytes_accessed=16_000_000, transcendentals=0
        ),
        name="last_inner",
    )(flags, near, far, near_edge, *near_sides, *far_sides, mirror, *near_fixed, *far_fixed, mask)


def last_outer(flags, far, far_edge, far_sides, mirror, far_fixed, mask, done, target):
    rows, _, col_count = far.shape

    def kernel(flag_ref, far_ref, edge_in, west_in, east_in, mirror_ref, coef_ref, matrix_ref, mask_ref, done_ref, target_ref, out_ref, south_ref, north_ref, outer_ref, right_ref, stage_ref, sem):
        is_upper = flag_ref[FAR] > 0
        at = pl.multiple_of(jnp.where(is_upper, rows, 0), 8)
        wet = mask_ref[pl.ds(at, rows), :].astype(F32)
        last = rows - 1
        row = jnp.where(is_upper, last, 0)
        row_wet = jnp.where(is_upper, wet[last:], wet[0:1])
        receive_row(FAR, flag_ref, edge_in, mirror_ref, outer_ref)
        neighbour_rows(is_upper, far_ref.at[jnp.where(is_upper, last - 1, 1)], outer_ref, south_ref, north_ref)
        right_ref[:, 3 * PAD :, :] = jnp.zeros((2, 256 - 3 * PAD, col_count), BF)
        for field in range(2):
            mix_row(FAR, row, rows, field, far_ref, south_ref, north_ref, west_in, east_in, coef_ref, right_ref, field)
        copies = []
        here = lax.broadcasted_iota(jnp.int32, (rows, 1), 0) == row
        for field in range(2):
            outer_ref[0:PAD] = mm(matrix_ref[field, row], right_ref[field]) * row_wet
            for level in range(LEVELS):
                stage_ref[field, level] = jnp.where(
                    here, outer_ref[level : level + 1, :], done_ref[field, level]
                )
            copies.append(store_block(out_ref, stage_ref, sem, at, field))
        for copy in copies:
            copy.wait()

    operands = [flags, far, far_edge, *far_sides, mirror, *far_fixed, mask, done, target]
    return pl.pallas_call(
        kernel,
        in_specs=in_place(9) + [pl.BlockSpec(memory_space=pl.ANY)],
        out_specs=pl.BlockSpec(memory_space=pl.ANY),
        out_shape=jax.ShapeDtypeStruct((2 * LEVELS, 2 * rows, col_count), F32),
        input_output_aliases={len(operands) - 1: 0},
        scratch_shapes=[pltpu.VMEM((2 * PAD, col_count), F32)] * 3
        + [
            pltpu.VMEM((2, 256, col_count), BF),
            pltpu.VMEM((2, LEVELS, rows, col_count), F32),
            pltpu.SemaphoreType.DMA((2,)),
        ],
        compiler_params=pltpu.CompilerParams(vmem_limit_bytes=20 * MIB),
        name="last_outer",
    )(*operands)


def mixing_matrices(vinv):
    turned = jnp.transpose(vinv, (1, 0, 3, 2))
    turned = jnp.pad(turned, ((0, 0), (0, 0), (0, PAD - LEVELS), (0, PAD - LEVELS)))
    high = lax.reduce_precision(turned, 8, 7)
    low = (turned - high).astype(BF)
    high = high.astype(BF)
    rest = jnp.zeros(high.shape[:3] + (256 - 3 * PAD,), BF)
    return jnp.concatenate([high, high, low, rest], axis=3)


def body(
    argo_value,
    argo_owner,
    argo_cell,
    alt_value,
    alt_owner,
    alt_cell,
    alt_profile,
    land_mask,
    coef_east,
    coef_north,
    mirror,
    vinv,
):
    row_count, col_count = land_mask.shape
    count_ja = lax.axis_size("ja")
    count_ia = lax.axis_size("ia")
    devices = count_ja * count_ia
    capacity = round_up(3 * argo_value.shape[0] // devices, 8)
    group = round_up(capacity // 4, 8)
    message = send_tables(
        devices,
        capacity,
        group,
        row_count,
        col_count,
        (
            argo_value.T,
            argo_owner.reshape(1, -1),
            argo_cell.reshape(1, -1),
            alt_value,
            alt_cell,
            alt_owner.reshape(1, -1),
        ),
    )
    message, ja_index = lax.optimization_barrier((message, lax.axis_index("ja")))
    message = lax.all_to_all(message, ("ja", "ia"), split_axis=0, concat_axis=0, tiled=True)

    ia_index = lax.axis_index("ia")
    is_top = (ja_index == count_ja - 1).astype(jnp.int32)
    parity = ja_index % 2
    flags = jnp.stack([1 - parity, parity, is_top]).astype(jnp.int32)
    fold_index = mirror - (count_ia - 1 - ia_index) * col_count
    mirror_lane = jnp.broadcast_to((fold_index % LANES)[None, :], (8, col_count))
    matrices = mixing_matrices(vinv)
    profile = jnp.pad(alt_profile.reshape(2, LEVELS, 1), ((0, 0), (0, PAD - LEVELS), (0, 0)))
    profile = profile.reshape(2 * PAD, 1)
    alt_capacity = max(2, 3 * alt_value.shape[0] // devices)
    coast = (land_mask, coef_north, coef_east)
    rows = row_count // 2
    lower = [matrices[:, :rows], matrices[:, rows:]]
    odd_device = parity == 1
    half_matrices = [
        jnp.where(odd_device, lower[0], lower[1]),
        jnp.where(odd_device, lower[1], lower[0]),
    ]

    ring_east = [(i, (i + 1) % count_ia) for i in range(count_ia)]
    ring_west = [((i + 1) % count_ia, i) for i in range(count_ia)]
    even_swap = []
    odd_swap = []
    for ja in range(count_ja):
        for ia in range(count_ia):
            here = ja * count_ia + ia
            even_swap.append((here, (ja ^ 1) * count_ia + ia))
            if ja == count_ja - 1:
                odd_swap.append((here, ja * count_ia + count_ia - 1 - ia))
            elif ja > 0:
                odd_swap.append((here, (((ja - 1) ^ 1) + 1) * count_ia + ia))
    swaps = (even_swap, odd_swap)

    def swap(which, edge):
        return lax.ppermute(edge, ("ja", "ia"), swaps[which])

    def pass_columns(cols):
        return lax.ppermute(cols, "ia", ring_east), lax.ppermute(cols, "ia", ring_west)

    near_edge, *prepared = first_forcing(
        capacity, alt_capacity, group, flags, message, profile, coast
    )
    near_edge = swap(NEAR, near_edge)
    state, far_edge, cols = rest_forcing(flags, profile, coast, prepared)
    near = far = state
    sides = pass_columns(cols)
    far_edge = swap(FAR, far_edge)
    near_coef = edge_weights(NEAR, flags, coast, (near_edge, *sides), mirror_lane)
    far_coef = edge_weights(FAR, flags, coast, (far_edge, *sides), mirror_lane)
    near_fixed = (mirror_lane, near_coef, half_matrices[NEAR])
    far_fixed = (mirror_lane, far_coef, half_matrices[FAR])
    for sweep in range(ITERS - 1):
        new_near, new_edge, cols = diffuse(
            NEAR, flags, near, far, (near_edge, *sides), *near_fixed, cols
        )
        near_edge = swap(NEAR, new_edge)
        sides = pass_columns(cols)
        far, new_edge, cols = diffuse(FAR, flags, far, near, (far_edge, *sides), *far_fixed)
        far_edge = swap(FAR, new_edge)
        near = new_near
    last_sides = pass_columns(cols)
    output, done = last_inner(
        flags, near, far, near_edge, sides, last_sides, mirror_lane, near_fixed[1:], far_fixed[1:], land_mask
    )
    return last_outer(
        flags, far, far_edge, last_sides, mirror_lane, far_fixed[1:], land_mask, done, output
    )


def solution(mesh):
    in_specs = (
        P(("ja", "ia"), None),
        P(("ja", "ia"), None),
        P(("ja", "ia")),
        P(("ja", "ia")),
        P(("ja", "ia"), None),
        P(("ja", "ia")),
        P(),
        P("ja", "ia"),
        P("ja", "ia"),
        P("ja", "ia"),
        P("ia"),
        P("ja", None, None, None),
    )
    out_specs = P(None, "ja", "ia")
    return jax.shard_map(body, mesh=mesh, in_specs=in_specs, out_specs=out_specs, check_vma=False)
```

```python
import math

import jax
import jax.numpy as jnp
from jax import lax
from jax.experimental import pallas as pl
from jax.experimental.pallas import tpu as pltpu
from jax.sharding import PartitionSpec as P

ITERS = 3
LEVELS = 75
PAD = 80
LANES = 128
NEAR, FAR, TOP = 0, 1, 2
BF = jnp.bfloat16
F32 = jnp.float32
MIB = 1024 * 1024


def round_up(value, unit):
    return (value + unit - 1) // unit * unit


def split_two(value):
    high = value.astype(BF)
    low = (value - high.astype(F32)).astype(BF)
    return high, low


def mm(left, right):
    return jnp.dot(left, right, preferred_element_type=F32)


def as_column(row):
    return jnp.broadcast_to(row, (8, row.shape[1])).T[:, 0:1]


def slot_ranks(owner_row, cell_row, devices, col_count, row_count, capacity, spread):
    count = owner_row.shape[1]
    owner = owner_row.astype(F32)
    inside = cell_row // col_count
    order = lax.broadcasted_iota(jnp.int32, (1, count), 1).astype(F32)
    key = (owner * float(row_count) + inside.astype(F32)) * float(count) + order
    key_col = as_column(key)
    device = lax.broadcasted_iota(jnp.int32, (devices, 1), 0)
    mine = device == owner_row
    totals = jnp.sum(jnp.where(mine, 1.0, 0.0), axis=1, keepdims=True)
    rank = -jnp.sum(jnp.where(device < owner_row, totals, 0.0), axis=0, keepdims=True)
    for start in range(0, count, 128):
        before = jnp.where(key_col[start : start + 128] < key, 1.0, 0.0)
        rank = rank + jnp.sum(before, axis=0, keepdims=True)
    if spread:
        total = jnp.sum(jnp.where(mine, totals, 0.0), axis=0, keepdims=True)
        offset = owner * 1024.0
        goal = (inside * capacity // row_count).astype(F32) - rank + offset
        goal_col = as_column(goal)
        shift = offset
        for start in range(0, count, 128):
            within = key_col[start : start + 128] <= key
            reached = jnp.where(within, goal_col[start : start + 128], 0.0)
            shift = jnp.maximum(shift, jnp.max(reached, axis=0, keepdims=True))
        rank = rank + jnp.minimum(shift - offset, float(capacity) - total)
    return rank


def table_kernel(
    devices,
    capacity,
    group,
    row_count,
    col_count,
    value_ref,
    owner_ref,
    cell_ref,
    alt_value_ref,
    alt_cell_ref,
    alt_owner_ref,
    message_ref,
    level_ref,
    side_ref,
    hi_ref,
    lo_ref,
    alt_all_ref,
    rank_hot_ref,
    alt_rank_hot_ref,
):
    index = pl.program_id(0)
    n_obs = owner_ref.shape[1]
    n_alt = alt_owner_ref.shape[1]

    @pl.when(index == 0)
    def _():
        slot = lax.broadcasted_iota(jnp.int32, (capacity, 1), 0).astype(F32)
        alt_cell = alt_cell_ref[...].reshape(1, n_alt)
        rank = slot_ranks(
            owner_ref[...], cell_ref[...], devices, col_count, row_count, capacity, True
        )
        rank_hot_ref[...] = jnp.where(slot == rank, 1.0, 0.0).astype(BF)
        rank = slot_ranks(
            alt_owner_ref[...], alt_cell, devices, col_count, row_count, capacity, False
        )
        alt_rank_hot_ref[...] = jnp.where(slot == rank, 1.0, 0.0).astype(BF)
        level_ref[...] = jnp.zeros(level_ref.shape, F32)
        level_ref[0:75, :] = value_ref[0:75, :]
        level_ref[75:76, :] = cell_ref[...].astype(F32) + 1.0
        level_ref[80:128, :] = value_ref[75:123, :]
        for lane_group in range(4):
            level_ref[128 + 32 * lane_group : 155 + 32 * lane_group, :] = value_ref[123:150, :]
        high, low = split_two(level_ref[...].T)
        hi_ref[...] = high
        lo_ref[...] = low
        pair = jnp.concatenate(
            [alt_value_ref[...].reshape(1, n_alt), alt_cell.astype(F32) + 1.0], axis=0
        )
        pair_high = pair.astype(BF).astype(F32)
        side_ref[...] = jnp.zeros(side_ref.shape, F32)
        side_ref[:, 0:8] = jnp.concatenate(
            [pair_high, pair - pair_high, jnp.zeros((4, n_alt), F32)], axis=0
        ).T
        alt_all_ref[...] = pltpu.roll(side_ref[...], 76, 1).astype(BF)

    per_step = message_ref.shape[0]
    chosen = []
    chosen_alt = []
    for member in range(per_step):
        device = index * per_step + member
        mask = jnp.where(owner_ref[...] == device, 1.0, 0.0).astype(BF)
        chosen.append(rank_hot_ref[...] * mask)
        mask = jnp.where(alt_owner_ref[...] == device, 1.0, 0.0).astype(BF)
        chosen_alt.append(alt_rank_hot_ref[...] * mask)
    chosen = jnp.concatenate(chosen, axis=0)
    chosen_alt = jnp.concatenate(chosen_alt, axis=0)
    table = mm(chosen, hi_ref[...]) + mm(chosen, lo_ref[...])
    lane = lax.broadcasted_iota(jnp.int32, (1, LANES), 1)
    extra = mm(chosen_alt, alt_all_ref[...])
    extra = jnp.where(lane < 78, extra + pltpu.roll(extra, LANES - 2, 1), 0.0)
    extra = jnp.where(lane >= 76, extra, 0.0)
    first = table[:, :LANES] + extra
    message_ref[:, 0:capacity] = first.reshape(per_step, capacity, LANES)
    rest = table[:, LANES:].reshape(per_step, capacity, LANES)
    total = jnp.zeros((per_step, group, LANES), F32)
    for lane_group in range(4):
        low_slot = lane_group * group
        if low_slot >= capacity:
            continue
        piece = rest[:, low_slot : low_slot + group]
        here = (lane // 32 == lane_group).reshape(1, 1, LANES)
        total = jnp.where(here, piece, total)
    message_ref[:, capacity : capacity + group] = total


def send_tables(devices, capacity, group, row_count, col_count, operands):
    n_obs = operands[1].shape[1]
    n_alt = operands[5].shape[1]
    per_step = max(1, 1536 // capacity)

    def kernel(*refs):
        table_kernel(devices, capacity, group, row_count, col_count, *refs)

    def whole(array):
        return pl.BlockSpec(array.shape, lambda s: (0,) * len(array.shape))

    return pl.pallas_call(
        kernel,
        grid=(devices // per_step,),
        in_specs=[whole(x) for x in operands],
        out_specs=pl.BlockSpec((per_step, capacity + group, LANES), lambda s: (s, 0, 0)),
        out_shape=jax.ShapeDtypeStruct((devices, capacity + group, LANES), F32),
        scratch_shapes=[
            pltpu.VMEM((2 * LANES, n_obs), F32),
            pltpu.VMEM((n_alt, LANES), F32),
            pltpu.VMEM((n_obs, 2 * LANES), BF),
            pltpu.VMEM((n_obs, 2 * LANES), BF),
            pltpu.VMEM((n_alt, LANES), BF),
            pltpu.VMEM((capacity, n_obs), BF),
            pltpu.VMEM((capacity, n_alt), BF),
        ],
        compiler_params=pltpu.CompilerParams(vmem_limit_bytes=56 * MIB),
        name="send_tables",
    )(*operands)


def column_lane(which, rows, field, east, row):
    return (4 * which + 2 * field + east) * rows + row


def columns_of(which, state_ref, cols):
    rows = state_ref.shape[0]
    lane = lax.broadcasted_iota(jnp.int32, (1, LANES), 1)
    for row in range(rows):
        for field in range(2):
            part = state_ref[row, field * PAD : (field + 1) * PAD, :]
            at = column_lane(which, rows, field, 0, row)
            cols = jnp.where(lane == at, pltpu.roll(part[:, :LANES], at, 1), cols)
            at = column_lane(which, rows, field, 1, row)
            cols = jnp.where(lane == at, pltpu.roll(part[:, -LANES:], at + 1, 1), cols)
    return cols


def pack_row(row_ref, edge_ref):
    edge_ref[0:LEVELS] = row_ref[0:LEVELS]
    edge_ref[LEVELS : 2 * LEVELS] = row_ref[PAD : PAD + LEVELS]
    edge_ref[2 * LEVELS : 2 * LEVELS + 2] = row_ref[LEVELS : LEVELS + 2]


def unpack_row(edge, row_ref, piece):
    row_ref[0:LEVELS, piece] = edge[0:LEVELS]
    row_ref[PAD : PAD + LEVELS, piece] = edge[LEVELS : 2 * LEVELS]
    for at in (LEVELS, PAD + LEVELS):
        row_ref[at : at + PAD - LEVELS, piece] = jnp.zeros((PAD - LEVELS, edge.shape[1]), F32)


def write_edge(is_upper, state_ref, edge_ref):
    pack_row(state_ref.at[jnp.where(is_upper, state_ref.shape[0] - 1, 0)], edge_ref)


def prepare(capacity, alt_capacity, group, col_count, message_ref, sea_ref, left_ref, hot_ref, rows_ref, bound_ref):
    row_count = sea_ref.shape[0]
    devices = message_ref.shape[0]
    block = min(32, devices)
    members = block * 8
    octets = capacity // 8
    alt_octets = (alt_capacity + 7) // 8
    per_group = group // 8
    shift = col_count.bit_length() - 1
    col_iota = lax.broadcasted_iota(jnp.int32, (1, col_count), 1)
    row_iota = lax.broadcasted_iota(jnp.int32, (row_count, 1), 0)

    def chunk(index, start):
        return message_ref[index * block : (index + 1) * block, start : start + 8, :].reshape(
            members, LANES
        )

    def hot_of(cell):
        return jnp.where(((cell - 1) & (col_count - 1)) == col_iota, 1.0, 0.0).astype(BF)

    def rows_of(cell):
        return lax.shift_right_arithmetic(cell - 1, shift)

    sea = jnp.zeros((row_count, col_count), F32)
    count = 0
    for index in range(devices // block):
        tails = [chunk(index, capacity + 8 * part).T for part in range(per_group)]
        for octet in range(octets):
            table = chunk(index, 8 * octet)
            turned = table.T
            tail = tails[octet % per_group]
            begin = 32 * (octet // per_group)
            levels = jnp.concatenate([turned, tail[begin : begin + 32]], axis=0)
            high, low = split_two(levels)
            left_ref[count, :, 0:members] = high
            left_ref[count, :, members : 2 * members] = low
            hot = hot_of(table[:, 75:76].astype(jnp.int32))
            hot_ref[count] = hot
            rows = rows_of(turned[75:76].astype(jnp.int32))
            rows_ref[count] = jnp.broadcast_to(rows, (8, members))
            bound_ref[2 * count] = jnp.min(jnp.where(rows >= 0, rows, row_count))
            bound_ref[2 * count + 1] = jnp.max(rows)
            count += 1
            if octet >= alt_octets:
                continue
            alt_hot = hot_of(table[:, 77:78].astype(jnp.int32))
            alt_rows = rows_of(turned[77:78].astype(jnp.int32))
            weighted = jnp.where(alt_rows == row_iota, turned[76:77], 0.0)
            high, low = split_two(weighted)
            product = mm(jnp.concatenate([high, low], axis=0), alt_hot)
            sea = sea + product[:row_count] + product[row_count:]
    sea_ref[...] = sea


def chosen_rows(number, here, row, span, left_ref, hot_ref):
    pieces = []
    for offset in range(span):
        mask = jnp.where(here == row + offset, 1.0, 0.0).astype(BF)
        pieces.append(left_ref[number] * jnp.concatenate([mask, mask], axis=1))
    hot = hot_ref[number]
    return mm(jnp.concatenate(pieces, axis=0), jnp.concatenate([hot, hot], axis=0))


def outer_forcing(row, is_upper, profile_ref, coast_refs, sea_ref, left_ref, hot_ref, rows_ref, bound_ref, edge_ref):
    row_count, col_count = sea_ref.shape
    last = row_count - 1
    profile = jnp.broadcast_to(profile_ref[...], (2 * PAD, LANES))
    sea = jnp.where(is_upper, sea_ref[last : last + 1, :], sea_ref[0:1, :])
    for start in range(0, col_count, LANES):
        edge_ref[:, start : start + LANES] = profile * sea[:, start : start + LANES]

    def step(number, carry):
        @pl.when((bound_ref[2 * number] <= row) & (row <= bound_ref[2 * number + 1]))
        def _():
            edge_ref[...] += chosen_rows(number, rows_ref[number][0:1], row, 1, left_ref, hot_ref)

        return carry

    lax.fori_loop(0, left_ref.shape[0], step, 0)
    for kind, coast_ref in enumerate(coast_refs):
        coast = jnp.where(is_upper, coast_ref[last : last + 1, :], coast_ref[0:1, :])
        edge_ref[LEVELS + kind : LEVELS + kind + 1, :] = coast.astype(F32)


def all_forcing(profile_ref, coast_refs, sea_ref, left_ref, hot_ref, rows_ref, bound_ref, state):
    row_count, _, col_count = state.shape
    count = left_ref.shape[0]
    for start in range(0, col_count, LANES):
        profile = jnp.broadcast_to(profile_ref[...], (2 * PAD, LANES))
        for row in range(row_count):
            state[row, :, start : start + LANES] = profile * sea_ref[row : row + 1, start : start + LANES]
    batch = math.gcd(count, 4)
    narrow, wide = 3, 6

    def step(number, carry):
        chunks = [number * batch + member for member in range(batch)]
        least = [bound_ref[2 * chunk] for chunk in chunks]
        extent = bound_ref[2 * chunks[0] + 1] - least[0]
        for i in range(1, batch):
            extent = jnp.maximum(extent, bound_ref[2 * chunks[i] + 1] - least[i])

        def add_runs(span, offset_rows, inner):
            for i, chunk in enumerate(chunks):
                begin = least[i] + offset_rows
                base = jnp.minimum(begin, row_count - span)
                here = rows_ref[chunk][0:1]
                here = jnp.where(here >= begin, here, -1)
                product = chosen_rows(chunk, here, base, span, left_ref, hot_ref)
                for offset in range(span):
                    state[base + offset] += product[2 * PAD * offset : 2 * PAD * (offset + 1)]
            return inner

        wanted = jnp.maximum(extent + 1, 0)
        full = lax.div(wanted, wide)
        rest = wanted - wide * full
        wide_turns = full + (rest > narrow).astype(jnp.int32)
        narrow_turns = ((rest > 0) & (rest <= narrow)).astype(jnp.int32)
        lax.fori_loop(0, wide_turns, lambda t, c: add_runs(wide, t * wide, c), 0)
        lax.fori_loop(0, narrow_turns, lambda t, c: add_runs(narrow, full * wide, c), 0)
        return carry

    lax.fori_loop(0, count // batch, step, 0)
    for kind, coast_ref in enumerate(coast_refs):
        coast = coast_ref[...].astype(F32)
        for row in range(row_count):
            state[row, LEVELS + kind : LEVELS + kind + 1, :] = coast[row : row + 1, :]


def half_shapes(row_count, col_count):
    return (
        jax.ShapeDtypeStruct((row_count // 2, 2 * PAD, col_count), F32),
        jax.ShapeDtypeStruct((2 * LEVELS + 2, col_count), F32),
        jax.ShapeDtypeStruct((PAD, LANES), F32),
    )


def in_place(count):
    return [pl.BlockSpec(memory_space=pltpu.SMEM)] + [pl.BlockSpec(memory_space=pltpu.VMEM)] * count


def first_forcing(capacity, alt_capacity, group, flags, message, profile, coast):
    row_count, col_count = coast[0].shape
    devices = message.shape[0]
    members = min(32, devices) * 8
    chunks = capacity // 8 * (devices // min(32, devices))

    def kernel(flag_ref, message_ref, profile_ref, wet, north, east, edge_ref, *refs):
        *outs, row_ref = refs
        prepare(capacity, alt_capacity, group, col_count, message_ref, *outs)
        is_upper = flag_ref[NEAR] > 0
        row = jnp.where(is_upper, row_count - 1, 0)
        outer_forcing(row, is_upper, profile_ref, (wet, north, east), *outs, row_ref)
        pack_row(row_ref, edge_ref)

    return pl.pallas_call(
        kernel,
        in_specs=in_place(5),
        out_shape=(
            half_shapes(row_count, col_count)[1],
            jax.ShapeDtypeStruct((row_count, col_count), F32),
            jax.ShapeDtypeStruct((chunks, 2 * PAD, 2 * members), BF),
            jax.ShapeDtypeStruct((chunks, members, col_count), BF),
            jax.ShapeDtypeStruct((chunks, 8, members), jnp.int32),
            jax.ShapeDtypeStruct((2 * chunks,), jnp.int32),
        ),
        out_specs=[pl.BlockSpec(memory_space=pltpu.VMEM)] * 5
        + [pl.BlockSpec(memory_space=pltpu.SMEM)],
        scratch_shapes=[pltpu.VMEM((2 * PAD, col_count), F32)],
        compiler_params=pltpu.CompilerParams(vmem_limit_bytes=24 * MIB),
        cost_estimate=pl.CostEstimate(
            flops=6_000_000_000, bytes_accessed=8_000_000, transcendentals=0
        ),
        name="forcing_first",
    )(flags, message, profile, *coast)


def rest_forcing(flags, profile, coast, prepared):
    row_count, col_count = coast[0].shape
    half = row_count // 2

    def kernel(flag_ref, profile_ref, wet, north, east, sea, left, hot, rows, bound, state, edge_ref, cols_ref):
        all_forcing(profile_ref, (wet, north, east), sea, left, hot, rows, bound, state)
        cols = jnp.zeros((PAD, LANES), F32)
        for which in (NEAR, FAR):
            first_row = jnp.where(flag_ref[which] > 0, half, 0)
            cols = columns_of(which, state.at[pl.ds(first_row, half)], cols)
        cols_ref[...] = cols
        write_edge(flag_ref[FAR] > 0, state, edge_ref)

    _, edge, cols = half_shapes(row_count, col_count)
    state = jax.ShapeDtypeStruct((row_count, 2 * PAD, col_count), F32)
    return pl.pallas_call(
        kernel,
        in_specs=in_place(8) + [pl.BlockSpec(memory_space=pltpu.SMEM)],
        out_shape=(state, edge, cols),
        compiler_params=pltpu.CompilerParams(vmem_limit_bytes=20 * MIB),
        cost_estimate=pl.CostEstimate(
            flops=6_000_000_000, bytes_accessed=8_000_000, transcendentals=0
        ),
        name="forcing_rest",
    )(flags, profile, *coast, *prepared)


def fold_row(row_ref, mirror_ref, piece, chunk, chunks, rows):
    index = jnp.broadcast_to(mirror_ref[0:1, piece(chunk)], (rows, LANES))
    return jnp.take_along_axis(row_ref[:, piece(chunks - 1 - chunk)], index, axis=1)


def weight_kernel(which, flag_ref, wet_ref, north_ref, east_ref, edge_in, west_in, east_in, mirror_ref, out_ref, fold_ref):
    row_count, col_count = wet_ref.shape
    rows = row_count // 2
    is_upper = flag_ref[which] > 0
    at = pl.multiple_of(jnp.where(is_upper, rows, 0), 8)
    wet = wet_ref[pl.ds(at, rows), :].astype(F32)
    north = north_ref[pl.ds(at, rows), :]
    east = east_ref[pl.ds(at, rows), :]
    chunks = col_count // LANES
    lane = lax.broadcasted_iota(jnp.int32, (1, col_count), 1)
    start = column_lane(which, rows, 0, 1, 0)
    west_cols = west_in[72:80, :].T[start : start + rows]
    start = column_lane(which, rows, 0, 0, 0)
    east_cols = east_in[72:80, :].T[start : start + rows]
    west_wet = jnp.where(lane == 0, west_cols[:, 3:4], pltpu.roll(wet, 1, 1))
    west_coef = jnp.where(lane == 0, west_cols[:, 5:6], pltpu.roll(east, 1, 1))
    east_wet = jnp.where(
        lane == col_count - 1, east_cols[:, 3:4], pltpu.roll(wet, col_count - 1, 1)
    )
    east_w = east * wet * east_wet
    west_w = west_coef * west_wet * wet

    def piece(c):
        return slice(c * LANES, (c + 1) * LANES)

    spare_ref = edge_in.at[2 * LEVELS - 6 : 2 * LEVELS + 2]
    if which == FAR:
        for c in range(chunks):
            fold_ref[:, piece(c)] = fold_row(spare_ref, mirror_ref, piece, c, chunks, 8)
    spare = spare_ref[...]
    last = rows - 1
    inner_wet = jnp.where(
        is_upper, wet_ref[rows - 1 : rows, :], wet_ref[rows : rows + 1, :]
    ).astype(F32)
    above = jnp.where(is_upper, spare[6:7], inner_wet)
    top_w = north[last:] * wet[last:] * above
    if which == FAR:
        fold = 0.5 * (north[last:] + fold_ref[7:8]) * wet[last:] * fold_ref[6:7]
        top_w = jnp.where(flag_ref[TOP] > 0, fold, top_w)
    below = jnp.where(is_upper, north_ref[rows - 1 : rows, :] * inner_wet, spare[7:8] * spare[6:7])
    between = north[:last] * wet[:last] * wet[1:]
    north_w = jnp.concatenate([between, top_w], axis=0)
    south_w = jnp.concatenate([below * wet[0:1], between], axis=0)
    center = 1.0 - (east_w + west_w + north_w + south_w)
    for kind, weight in enumerate((center, east_w, west_w, north_w, south_w)):
        for row in range(rows):
            out_ref[row, kind : kind + 1, :] = weight[row : row + 1]


def edge_weights(which, flags, coast, received, mirror):
    row_count, col_count = coast[0].shape

    def kernel(*refs):
        weight_kernel(which, *refs)

    return pl.pallas_call(
        kernel,
        in_specs=in_place(7),
        out_shape=jax.ShapeDtypeStruct((row_count // 2, 8, col_count), F32),
        scratch_shapes=[pltpu.VMEM((8, col_count), F32)],
        compiler_params=pltpu.CompilerParams(vmem_limit_bytes=16 * MIB),
        name="edge_weights",
    )(flags, *coast, *received, mirror)


def receive_row(which, flag_ref, edge_in, mirror_ref, row_ref):
    levels, col_count = edge_in.shape
    chunks = col_count // LANES
    is_top = flag_ref[TOP] > 0

    def piece(c):
        return slice(c * LANES, (c + 1) * LANES)

    def plain():
        for c in range(chunks):
            unpack_row(edge_in[:, piece(c)], row_ref, piece(c))

    if which == NEAR:
        plain()
        return

    @pl.when(jnp.logical_not(is_top))
    def _():
        plain()

    @pl.when(is_top)
    def _():
        for c in range(chunks):
            unpack_row(
                fold_row(edge_in, mirror_ref, piece, c, chunks, levels), row_ref, piece(c)
            )


def neighbour_rows(is_upper, inner, outer_ref, south_ref, north_ref):
    @pl.when(is_upper)
    def _():
        south_ref[...] = inner[...]
        north_ref[...] = outer_ref[...]

    @pl.when(jnp.logical_not(is_upper))
    def _():
        south_ref[...] = outer_ref[...]
        north_ref[...] = inner[...]


def mix_row(which, row, rows, field, state_ref, south_ref, north_ref, west_in, east_in, coef_ref, right_ref, slot):
    col_count = state_ref.shape[2]
    chunks = col_count // LANES
    lane = lax.broadcasted_iota(jnp.int32, (1, LANES), 1)
    levels = slice(field * PAD, (field + 1) * PAD)

    def piece(chunk):
        return slice(chunk * LANES, (chunk + 1) * LANES)

    west_lane = column_lane(which, rows, field, 1, row)
    east_lane = column_lane(which, rows, field, 0, row)
    centers = [state_ref[row, levels, piece(c)] for c in range(chunks)]
    to_left = [pltpu.roll(c, LANES - 1, 1) for c in centers]
    to_right = [pltpu.roll(c, 1, 1) for c in centers]
    to_right.append(pltpu.roll(west_in[...], LANES - west_lane, 1))
    to_left.append(pltpu.roll(east_in[...], LANES - 1 - east_lane, 1))
    for c in range(chunks):
        south = south_ref[levels, piece(c)]
        north = north_ref[levels, piece(c)]
        east = jnp.where(lane == LANES - 1, to_left[c + 1], to_left[c])
        west = jnp.where(lane == 0, to_right[c - 1], to_right[c])

        def coef(kind):
            return coef_ref[row, kind : kind + 1, piece(c)]

        mixed = (
            coef(0) * centers[c]
            + coef(1) * east
            + coef(2) * west
            + coef(3) * north
            + coef(4) * south
        )
        high, low = split_two(mixed)
        right_ref[slot, 0:PAD, piece(c)] = high
        right_ref[slot, PAD : 2 * PAD, piece(c)] = low
        right_ref[slot, 2 * PAD : 3 * PAD, piece(c)] = high


def sweep_rows(which, rows, units, state_ref, south_ref, north_ref, west_in, east_in, coef_ref, matrix_ref, right_ref, emit):
    slots = right_ref.shape[0]
    right_ref[:, 3 * PAD :, :] = jnp.zeros((slots,) + (256 - 3 * PAD, right_ref.shape[2]), BF)

    def product(number):
        row, field = units[number]
        emit(number, row, field, mm(matrix_ref[field, row], right_ref[number % slots]))

    for number, (row, field) in enumerate(units):
        south = state_ref.at[row - 1] if row > 0 else south_ref
        north = state_ref.at[row + 1] if row < rows - 1 else north_ref
        mix_row(which, row, rows, field, state_ref, south, north, west_in, east_in, coef_ref, right_ref, number % slots)
        if number > 0:
            product(number - 1)
    product(len(units) - 1)


def diffuse(which, flags, state, other, received, mirror, coef, matrix, *far_cols):
    rows = coef.shape[0]
    col_count = state.shape[2]

    def kernel(flag_ref, state_ref, other_ref, edge_in, west_in, east_in, mirror_ref, coef_ref, matrix_ref, *refs):
        out_ref, edge_ref, cols_ref, south_ref, north_ref, outer_ref, right_ref = refs[-7:]
        is_upper = flag_ref[which] > 0
        if state.shape[0] > rows:
            state_ref = state_ref.at[pl.ds(jnp.where(is_upper, rows, 0), rows)]
            inner = other_ref.at[jnp.where(is_upper, rows - 1, rows)]
        else:
            inner = other_ref.at[jnp.where(is_upper, rows - 1, 0)]
        receive_row(which, flag_ref, edge_in, mirror_ref, outer_ref)
        neighbour_rows(is_upper, inner, outer_ref, south_ref, north_ref)

        def emit(number, row, field, result):
            out_ref[row, field * PAD : (field + 1) * PAD] = result

        units = [(row, field) for row in range(rows) for field in range(2)]
        sweep_rows(which, rows, units, state_ref, south_ref, north_ref, west_in, east_in, coef_ref, matrix_ref, right_ref, emit)
        write_edge(is_upper, out_ref, edge_ref)
        old_cols = refs[0][...] if which == NEAR else jnp.zeros((PAD, LANES), F32)
        cols_ref[...] = columns_of(which, out_ref, old_cols)

    return pl.pallas_call(
        kernel,
        in_specs=in_place(8 + len(far_cols)),
        out_shape=half_shapes(2 * rows, col_count),
        scratch_shapes=[pltpu.VMEM((2 * PAD, col_count), F32)] * 3
        + [pltpu.VMEM((4, 256, col_count), BF)],
        compiler_params=pltpu.CompilerParams(vmem_limit_bytes=16 * MIB),
        cost_estimate=pl.CostEstimate(
            flops=3_000_000_000, bytes_accessed=8_000_000, transcendentals=0
        ),
        name="diffusion_" + ("near", "far")[which],
    )(flags, state, other, *received, mirror, coef, matrix, *far_cols)


def output_layout(results):
    return jnp.swapaxes(jnp.stack(results), 0, 1)[:LEVELS]


def store_block(out_ref, stage_ref, sem, at, field):
    rows = stage_ref.shape[2]
    copy = pltpu.make_async_copy(
        stage_ref.at[field],
        out_ref.at[pl.ds(field * LEVELS, LEVELS), pl.ds(at, rows), :],
        sem.at[field],
    )
    copy.start()
    return copy


def last_inner(flags, near, far, near_edge, near_sides, far_sides, mirror, near_fixed, far_fixed, mask):
    rows, _, col_count = near.shape

    def kernel(flag_ref, near_ref, far_ref, edge_in, near_west, near_east, far_west, far_east, mirror_ref, near_coef, near_matrix, far_coef, far_matrix, mask_ref, out_ref, done_ref, south_ref, north_ref, outer_ref, right_ref, stage_ref, sem, kept_ref):
        is_upper = flag_ref[NEAR] > 0
        at = pl.multiple_of(jnp.where(is_upper, rows, 0), 8)
        wet = mask_ref[pl.ds(at, rows), :].astype(F32)
        far_at = pl.multiple_of(rows - at, 8)
        far_wet = mask_ref[pl.ds(far_at, rows), :].astype(F32)
        last = rows - 1
        far_inner = far_ref.at[jnp.where(is_upper, last, 0)]
        receive_row(NEAR, flag_ref, edge_in, mirror_ref, outer_ref)
        neighbour_rows(is_upper, far_inner, outer_ref, south_ref, north_ref)
        copies = []
        for field in range(2):
            results = []

            def emit(number, row, field, result):
                results.append(result * wet[row : row + 1])

            units = [(row, field) for row in range(rows)]
            sweep_rows(NEAR, rows, units, near_ref, south_ref, north_ref, near_west, near_east, near_coef, near_matrix, right_ref, emit)
            stage_ref[field] = output_layout(results)
            copies.append(store_block(out_ref, stage_ref, sem, at, field))
        edge = jnp.where(is_upper, last, 0)
        near_inner = near_ref.at[jnp.where(is_upper, 0, last)]

        @pl.when(is_upper)
        def _():
            south_ref[...] = far_ref[last - 1]
            north_ref[...] = near_inner[...]

        @pl.when(jnp.logical_not(is_upper))
        def _():
            south_ref[...] = near_inner[...]
            north_ref[...] = far_ref[1]

        def keep(number, row, field, result):
            kept_ref[row, field * PAD : (field + 1) * PAD] = result * far_wet[row : row + 1]

        units = [(row, field) for row in range(1, last) for field in range(2)]
        sweep_rows(FAR, rows, units, far_ref, south_ref, north_ref, far_west, far_east, far_coef, far_matrix, right_ref, keep)
        edge_wet = jnp.where(is_upper, far_wet[last:], far_wet[0:1])
        for field in range(2):
            mix_row(FAR, edge, rows, field, far_ref, south_ref, north_ref, far_west, far_east, far_coef, right_ref, field)
        for field in range(2):
            result = mm(far_matrix[field, edge], right_ref[field])
            kept_ref[edge, field * PAD : (field + 1) * PAD] = result * edge_wet
        for field in range(2):
            levels = slice(field * PAD, (field + 1) * PAD)
            done_ref[field] = output_layout([kept_ref[row, levels] for row in range(rows)])
        for copy in copies:
            copy.wait()

    return pl.pallas_call(
        kernel,
        in_specs=in_place(13),
        out_specs=[pl.BlockSpec(memory_space=pl.ANY), pl.BlockSpec(memory_space=pltpu.VMEM)],
        out_shape=(
            jax.ShapeDtypeStruct((2 * LEVELS, 2 * rows, col_count), F32),
            jax.ShapeDtypeStruct((2, LEVELS, rows, col_count), F32),
        ),
        scratch_shapes=[pltpu.VMEM((2 * PAD, col_count), F32)] * 3
        + [
            pltpu.VMEM((4, 256, col_count), BF),
            pltpu.VMEM((2, LEVELS, rows, col_count), F32),
            pltpu.SemaphoreType.DMA((2,)),
            pltpu.VMEM((rows, 2 * PAD, col_count), F32),
        ],
        compiler_params=pltpu.CompilerParams(vmem_limit_bytes=22 * MIB),
        cost_estimate=pl.CostEstimate(
            flops=6_000_000_000, bytes_accessed=16_000_000, transcendentals=0
        ),
        name="last_inner",
    )(flags, near, far, near_edge, *near_sides, *far_sides, mirror, *near_fixed, *far_fixed, mask)


def last_outer(flags, far, far_edge, far_sides, mirror, far_fixed, mask, done, target):
    rows, _, col_count = far.shape

    def kernel(flag_ref, far_ref, edge_in, west_in, east_in, mirror_ref, coef_ref, matrix_ref, mask_ref, done_ref, target_ref, out_ref, south_ref, north_ref, outer_ref, right_ref, stage_ref, sem):
        is_upper = flag_ref[FAR] > 0
        at = pl.multiple_of(jnp.where(is_upper, rows, 0), 8)
        wet = mask_ref[pl.ds(at, rows), :].astype(F32)
        last = rows - 1
        row = jnp.where(is_upper, last, 0)
        row_wet = jnp.where(is_upper, wet[last:], wet[0:1])
        receive_row(FAR, flag_ref, edge_in, mirror_ref, outer_ref)
        neighbour_rows(is_upper, far_ref.at[jnp.where(is_upper, last - 1, 1)], outer_ref, south_ref, north_ref)
        right_ref[:, 3 * PAD :, :] = jnp.zeros((2, 256 - 3 * PAD, col_count), BF)
        for field in range(2):
            mix_row(FAR, row, rows, field, far_ref, south_ref, north_ref, west_in, east_in, coef_ref, right_ref, field)
        copies = []
        here = lax.broadcasted_iota(jnp.int32, (rows, 1), 0) == row
        for field in range(2):
            outer_ref[0:PAD] = mm(matrix_ref[field, row], right_ref[field]) * row_wet
            for level in range(LEVELS):
                stage_ref[field, level] = jnp.where(
                    here, outer_ref[level : level + 1, :], done_ref[field, level]
                )
            copies.append(store_block(out_ref, stage_ref, sem, at, field))
        for copy in copies:
            copy.wait()

    operands = [flags, far, far_edge, *far_sides, mirror, *far_fixed, mask, done, target]
    return pl.pallas_call(
        kernel,
        in_specs=in_place(9) + [pl.BlockSpec(memory_space=pl.ANY)],
        out_specs=pl.BlockSpec(memory_space=pl.ANY),
        out_shape=jax.ShapeDtypeStruct((2 * LEVELS, 2 * rows, col_count), F32),
        input_output_aliases={len(operands) - 1: 0},
        scratch_shapes=[pltpu.VMEM((2 * PAD, col_count), F32)] * 3
        + [
            pltpu.VMEM((2, 256, col_count), BF),
            pltpu.VMEM((2, LEVELS, rows, col_count), F32),
            pltpu.SemaphoreType.DMA((2,)),
        ],
        compiler_params=pltpu.CompilerParams(vmem_limit_bytes=20 * MIB),
        name="last_outer",
    )(*operands)


def mixing_matrices(vinv):
    turned = jnp.transpose(vinv, (1, 0, 3, 2))
    turned = jnp.pad(turned, ((0, 0), (0, 0), (0, PAD - LEVELS), (0, PAD - LEVELS)))
    high = lax.reduce_precision(turned, 8, 7)
    low = (turned - high).astype(BF)
    high = high.astype(BF)
    rest = jnp.zeros(high.shape[:3] + (256 - 3 * PAD,), BF)
    return jnp.concatenate([high, high, low, rest], axis=3)


def body(
    argo_value,
    argo_owner,
    argo_cell,
    alt_value,
    alt_owner,
    alt_cell,
    alt_profile,
    land_mask,
    coef_east,
    coef_north,
    mirror,
    vinv,
):
    row_count, col_count = land_mask.shape
    count_ja = lax.axis_size("ja")
    count_ia = lax.axis_size("ia")
    devices = count_ja * count_ia
    capacity = round_up(3 * argo_value.shape[0] // devices, 8)
    group = round_up(capacity // 4, 8)
    message = send_tables(
        devices,
        capacity,
        group,
        row_count,
        col_count,
        (
            argo_value.T,
            argo_owner.reshape(1, -1),
            argo_cell.reshape(1, -1),
            alt_value,
            alt_cell,
            alt_owner.reshape(1, -1),
        ),
    )
    message, ja_index = lax.optimization_barrier((message, lax.axis_index("ja")))
    message = lax.all_to_all(message, ("ja", "ia"), split_axis=0, concat_axis=0, tiled=True)

    ia_index = lax.axis_index("ia")
    is_top = (ja_index == count_ja - 1).astype(jnp.int32)
    parity = ja_index % 2
    flags = jnp.stack([1 - parity, parity, is_top]).astype(jnp.int32)
    fold_index = mirror - (count_ia - 1 - ia_index) * col_count
    mirror_lane = jnp.broadcast_to((fold_index % LANES)[None, :], (8, col_count))
    matrices = mixing_matrices(vinv)
    profile = jnp.pad(alt_profile.reshape(2, LEVELS, 1), ((0, 0), (0, PAD - LEVELS), (0, 0)))
    profile = profile.reshape(2 * PAD, 1)
    alt_capacity = max(2, 3 * alt_value.shape[0] // devices)
    coast = (land_mask, coef_north, coef_east)
    rows = row_count // 2
    lower = [matrices[:, :rows], matrices[:, rows:]]
    odd_device = parity == 1
    half_matrices = [
        jnp.where(odd_device, lower[0], lower[1]),
        jnp.where(odd_device, lower[1], lower[0]),
    ]

    ring_east = [(i, (i + 1) % count_ia) for i in range(count_ia)]
    ring_west = [((i + 1) % count_ia, i) for i in range(count_ia)]
    even_swap = []
    odd_swap = []
    for ja in range(count_ja):
        for ia in range(count_ia):
            here = ja * count_ia + ia
            even_swap.append((here, (ja ^ 1) * count_ia + ia))
            if ja == count_ja - 1:
                odd_swap.append((here, ja * count_ia + count_ia - 1 - ia))
            elif ja > 0:
                odd_swap.append((here, (((ja - 1) ^ 1) + 1) * count_ia + ia))
    swaps = (even_swap, odd_swap)

    def swap(which, edge):
        return lax.ppermute(edge, ("ja", "ia"), swaps[which])

    def pass_columns(cols):
        return lax.ppermute(cols, "ia", ring_east), lax.ppermute(cols, "ia", ring_west)

    near_edge, *prepared = first_forcing(
        capacity, alt_capacity, group, flags, message, profile, coast
    )
    near_edge = swap(NEAR, near_edge)
    state, far_edge, cols = rest_forcing(flags, profile, coast, prepared)
    near = far = state
    sides = pass_columns(cols)
    far_edge = swap(FAR, far_edge)
    near_coef = edge_weights(NEAR, flags, coast, (near_edge, *sides), mirror_lane)
    far_coef = edge_weights(FAR, flags, coast, (far_edge, *sides), mirror_lane)
    near_fixed = (mirror_lane, near_coef, half_matrices[NEAR])
    far_fixed = (mirror_lane, far_coef, half_matrices[FAR])
    for sweep in range(ITERS - 1):
        new_near, new_edge, cols = diffuse(
            NEAR, flags, near, far, (near_edge, *sides), *near_fixed, cols
        )
        near_edge = swap(NEAR, new_edge)
        sides = pass_columns(cols)
        far, new_edge, cols = diffuse(FAR, flags, far, near, (far_edge, *sides), *far_fixed)
        far_edge = swap(FAR, new_edge)
        near = new_near
    last_sides = pass_columns(cols)
    output, done = last_inner(
        flags, near, far, near_edge, sides, last_sides, mirror_lane, near_fixed[1:], far_fixed[1:], land_mask
    )
    return last_outer(
        flags, far, far_edge, last_sides, mirror_lane, far_fixed[1:], land_mask, done, output
    )


def solution(mesh):
    in_specs = (
        P(("ja", "ia"), None),
        P(("ja", "ia"), None),
        P(("ja", "ia")),
        P(("ja", "ia")),
        P(("ja", "ia"), None),
        P(("ja", "ia")),
        P(),
        P("ja", "ia"),
        P("ja", "ia"),
        P("ja", "ia"),
        P("ia"),
        P("ja", None, None, None),
    )
    out_specs = P(None, "ja", "ia")
    return jax.shard_map(body, mesh=mesh, in_specs=in_specs, out_specs=out_specs, check_vma=False)
```

```python
import math

import jax
import jax.numpy as jnp
from jax import lax
from jax.experimental import pallas as pl
from jax.experimental.pallas import tpu as pltpu
from jax.sharding import PartitionSpec as P

ITERS = 3
LEVELS = 75
PAD = 80
LANES = 128
NEAR, FAR, TOP = 0, 1, 2
BF = jnp.bfloat16
F32 = jnp.float32
MIB = 1024 * 1024


def round_up(value, unit):
    return (value + unit - 1) // unit * unit


def split_two(value):
    high = value.astype(BF)
    low = (value - high.astype(F32)).astype(BF)
    return high, low


def mm(left, right):
    return jnp.dot(left, right, preferred_element_type=F32)


def as_column(row):
    return jnp.broadcast_to(row, (8, row.shape[1])).T[:, 0:1]


def slot_ranks(owner_row, cell_row, devices, col_count, row_count, capacity):
    count = owner_row.shape[1]
    owner = owner_row.astype(F32)
    inside = cell_row // col_count
    order = lax.broadcasted_iota(jnp.int32, (1, count), 1).astype(F32)
    key = (owner * float(row_count) + inside.astype(F32)) * float(count) + order
    key_col = as_column(key)
    device = lax.broadcasted_iota(jnp.int32, (devices, 1), 0)
    mine = device == owner_row
    totals = jnp.sum(jnp.where(mine, 1.0, 0.0), axis=1, keepdims=True)
    rank = -jnp.sum(jnp.where(device < owner_row, totals, 0.0), axis=0, keepdims=True)
    for start in range(0, count, 128):
        before = jnp.where(key_col[start : start + 128] < key, 1.0, 0.0)
        rank = rank + jnp.sum(before, axis=0, keepdims=True)
    total = jnp.sum(jnp.where(mine, totals, 0.0), axis=0, keepdims=True)
    offset = owner * 1024.0
    goal = (inside * capacity // row_count).astype(F32) - rank + offset
    goal_col = as_column(goal)
    shift = offset
    for start in range(0, count, 128):
        within = key_col[start : start + 128] <= key
        reached = jnp.where(within, goal_col[start : start + 128], 0.0)
        shift = jnp.maximum(shift, jnp.max(reached, axis=0, keepdims=True))
    rank = rank + jnp.minimum(shift - offset, float(capacity) - total)
    return rank


def table_kernel(
    devices,
    capacity,
    alt_capacity,
    group,
    row_count,
    col_count,
    value_ref,
    owner_ref,
    cell_ref,
    alt_value_ref,
    alt_cell_ref,
    alt_owner_ref,
    message_ref,
    level_ref,
    side_ref,
    hi_ref,
    lo_ref,
    alt_all_ref,
    rank_hot_ref,
    alt_rank_hot_ref,
):
    index = pl.program_id(0)
    n_obs = owner_ref.shape[1]
    n_alt = alt_owner_ref.shape[1]

    @pl.when(index == 0)
    def _():
        slot = lax.broadcasted_iota(jnp.int32, (capacity, 1), 0).astype(F32)
        alt_cell = alt_cell_ref[...].reshape(1, n_alt)
        rank = slot_ranks(
            owner_ref[...], cell_ref[...], devices, col_count, row_count, capacity
        )
        rank_hot_ref[...] = jnp.where(slot == rank, 1.0, 0.0).astype(BF)
        rank = slot_ranks(
            alt_owner_ref[...], alt_cell, devices, col_count, row_count, alt_capacity
        )
        alt_rank_hot_ref[...] = jnp.where(slot == rank, 1.0, 0.0).astype(BF)
        level_ref[...] = jnp.zeros(level_ref.shape, F32)
        level_ref[0:75, :] = value_ref[0:75, :]
        level_ref[75:76, :] = cell_ref[...].astype(F32) + 1.0
        level_ref[80:128, :] = value_ref[75:123, :]
        for lane_group in range(4):
            level_ref[128 + 32 * lane_group : 155 + 32 * lane_group, :] = value_ref[123:150, :]
        high, low = split_two(level_ref[...].T)
        hi_ref[...] = high
        lo_ref[...] = low
        pair = jnp.concatenate(
            [alt_value_ref[...].reshape(1, n_alt), alt_cell.astype(F32) + 1.0], axis=0
        )
        pair_high = pair.astype(BF).astype(F32)
        side_ref[...] = jnp.zeros(side_ref.shape, F32)
        side_ref[:, 0:8] = jnp.concatenate(
            [pair_high, pair - pair_high, jnp.zeros((4, n_alt), F32)], axis=0
        ).T
        alt_all_ref[...] = pltpu.roll(side_ref[...], 76, 1).astype(BF)

    per_step = message_ref.shape[0]
    chosen = []
    chosen_alt = []
    for member in range(per_step):
        device = index * per_step + member
        mask = jnp.where(owner_ref[...] == device, 1.0, 0.0).astype(BF)
        chosen.append(rank_hot_ref[...] * mask)
        mask = jnp.where(alt_owner_ref[...] == device, 1.0, 0.0).astype(BF)
        chosen_alt.append(alt_rank_hot_ref[...] * mask)
    chosen = jnp.concatenate(chosen, axis=0)
    chosen_alt = jnp.concatenate(chosen_alt, axis=0)
    table = mm(chosen, hi_ref[...]) + mm(chosen, lo_ref[...])
    lane = lax.broadcasted_iota(jnp.int32, (1, LANES), 1)
    extra = mm(chosen_alt, alt_all_ref[...])
    extra = jnp.where(lane < 78, extra + pltpu.roll(extra, LANES - 2, 1), 0.0)
    extra = jnp.where(lane >= 76, extra, 0.0)
    first = table[:, :LANES] + extra
    message_ref[:, 0:capacity] = first.reshape(per_step, capacity, LANES)
    rest = table[:, LANES:].reshape(per_step, capacity, LANES)
    total = jnp.zeros((per_step, group, LANES), F32)
    for lane_group in range(4):
        low_slot = lane_group * group
        if low_slot >= capacity:
            continue
        piece = rest[:, low_slot : low_slot + group]
        here = (lane // 32 == lane_group).reshape(1, 1, LANES)
        total = jnp.where(here, piece, total)
    message_ref[:, capacity : capacity + group] = total


def send_tables(devices, capacity, alt_capacity, group, row_count, col_count, operands):
    n_obs = operands[1].shape[1]
    n_alt = operands[5].shape[1]
    per_step = max(1, 1536 // capacity)

    def kernel(*refs):
        table_kernel(devices, capacity, alt_capacity, group, row_count, col_count, *refs)

    def whole(array):
        return pl.BlockSpec(array.shape, lambda s: (0,) * len(array.shape))

    return pl.pallas_call(
        kernel,
        grid=(devices // per_step,),
        in_specs=[whole(x) for x in operands],
        out_specs=pl.BlockSpec((per_step, capacity + group, LANES), lambda s: (s, 0, 0)),
        out_shape=jax.ShapeDtypeStruct((devices, capacity + group, LANES), F32),
        scratch_shapes=[
            pltpu.VMEM((2 * LANES, n_obs), F32),
            pltpu.VMEM((n_alt, LANES), F32),
            pltpu.VMEM((n_obs, 2 * LANES), BF),
            pltpu.VMEM((n_obs, 2 * LANES), BF),
            pltpu.VMEM((n_alt, LANES), BF),
            pltpu.VMEM((capacity, n_obs), BF),
            pltpu.VMEM((capacity, n_alt), BF),
        ],
        compiler_params=pltpu.CompilerParams(vmem_limit_bytes=56 * MIB),
        name="send_tables",
    )(*operands)


def column_lane(which, rows, field, east, row):
    return (4 * which + 2 * field + east) * rows + row


def columns_of(which, state_ref, cols):
    rows = state_ref.shape[0]
    lane = lax.broadcasted_iota(jnp.int32, (1, LANES), 1)
    for row in range(rows):
        for field in range(2):
            part = state_ref[row, field * PAD : (field + 1) * PAD, :]
            at = column_lane(which, rows, field, 0, row)
            cols = jnp.where(lane == at, pltpu.roll(part[:, :LANES], at, 1), cols)
            at = column_lane(which, rows, field, 1, row)
            cols = jnp.where(lane == at, pltpu.roll(part[:, -LANES:], at + 1, 1), cols)
    return cols


def pack_row(row_ref, edge_ref):
    edge_ref[0:LEVELS] = row_ref[0:LEVELS]
    edge_ref[LEVELS : 2 * LEVELS] = row_ref[PAD : PAD + LEVELS]
    edge_ref[2 * LEVELS : 2 * LEVELS + 2] = row_ref[LEVELS : LEVELS + 2]


def unpack_row(edge, row_ref, piece):
    row_ref[0:LEVELS, piece] = edge[0:LEVELS]
    row_ref[PAD : PAD + LEVELS, piece] = edge[LEVELS : 2 * LEVELS]
    for at in (LEVELS, PAD + LEVELS):
        row_ref[at : at + PAD - LEVELS, piece] = jnp.zeros((PAD - LEVELS, edge.shape[1]), F32)


def write_edge(is_upper, state_ref, edge_ref):
    pack_row(state_ref.at[jnp.where(is_upper, state_ref.shape[0] - 1, 0)], edge_ref)


def one_hot_columns(cell, col_count):
    col_iota = lax.broadcasted_iota(jnp.int32, (1, col_count), 1)
    cell = cell.astype(jnp.int32) - 1
    return jnp.where((cell & (col_count - 1)) == col_iota, 1.0, 0.0).astype(BF)


def grid_rows(cell, col_count):
    return lax.shift_right_arithmetic(cell.astype(jnp.int32) - 1, col_count.bit_length() - 1)


def slot_chunk(message_ref, index, start):
    block = min(32, message_ref.shape[0])
    return message_ref[index * block : (index + 1) * block, start : start + 8, :].reshape(
        block * 8, LANES
    )


def prepare(capacity, group, row_count, col_count, message_ref, left_ref, hot_ref, rows_ref, bound_ref, alt_ref, alt_bound_ref):
    devices = message_ref.shape[0]
    members = min(32, devices) * 8
    per_group = group // 8

    def bounds(ref, number, rows):
        ref[2 * number] = jnp.min(jnp.where(rows >= 0, rows, row_count))
        ref[2 * number + 1] = jnp.max(rows)

    count = 0
    for index in range(devices * 8 // members):
        tails = [
            slot_chunk(message_ref, index, capacity + 8 * part).T for part in range(per_group)
        ]
        for octet in range(capacity // 8):
            table = slot_chunk(message_ref, index, 8 * octet)
            turned = table.T
            tail = tails[octet % per_group]
            begin = 32 * (octet // per_group)
            levels = jnp.concatenate([turned, tail[begin : begin + 32]], axis=0)
            high, low = split_two(levels)
            left_ref[count, :, 0:members] = high
            left_ref[count, :, members : 2 * members] = low
            hot_ref[count] = one_hot_columns(table[:, 75:76], col_count)
            rows = grid_rows(turned[75:76], col_count)
            rows_ref[count] = jnp.broadcast_to(rows, (8, members))
            bounds(bound_ref, count, rows)
            alt_ref[count] = turned[72:80]
            bounds(alt_bound_ref, count, grid_rows(turned[77:78], col_count))
            count += 1


def alt_chunks(capacity, alt_capacity, devices):
    octets = capacity // 8
    blocks = devices // min(32, devices)
    used = (alt_capacity + 7) // 8
    return [(b * octets + o, b, o) for b in range(blocks) for o in range(used)]


def alt_product(chunk, message_ref, alt_ref, rows_wanted, col_count):
    number, index, octet = chunk
    table = slot_chunk(message_ref, index, 8 * octet)
    alt_hot = one_hot_columns(table[:, 77:78], col_count)
    rows = grid_rows(alt_ref[number, 5:6], col_count)
    weighted = jnp.where(rows == rows_wanted, alt_ref[number, 4:5], 0.0)
    count = weighted.shape[0]
    high, low = split_two(weighted)
    product = mm(jnp.concatenate([high, low], axis=0), alt_hot)
    return product[:count] + product[count:]


def row_sea_level(row, chunks, message_ref, alt_ref, alt_bound_ref, sea_ref):
    count, col_count = sea_ref.shape
    wanted = jnp.zeros((count, 1), jnp.int32) + row
    sea_ref[...] = jnp.zeros(sea_ref.shape, F32)
    for chunk in chunks:
        number = chunk[0]

        @pl.when((alt_bound_ref[2 * number] <= row) & (row <= alt_bound_ref[2 * number + 1]))
        def _():
            sea_ref[...] += alt_product(chunk, message_ref, alt_ref, wanted, col_count)


def sea_level(chunks, message_ref, alt_ref, sea_ref):
    row_count, col_count = sea_ref.shape
    wanted = lax.broadcasted_iota(jnp.int32, (row_count, 1), 0)
    sea = jnp.zeros((row_count, col_count), F32)
    for chunk in chunks:
        sea = sea + alt_product(chunk, message_ref, alt_ref, wanted, col_count)
    sea_ref[...] = sea


def chosen_rows(number, here, row, span, left_ref, hot_ref):
    pieces = []
    for offset in range(span):
        mask = jnp.where(here == row + offset, 1.0, 0.0).astype(BF)
        pieces.append(left_ref[number] * jnp.concatenate([mask, mask], axis=1))
    hot = hot_ref[number]
    return mm(jnp.concatenate(pieces, axis=0), jnp.concatenate([hot, hot], axis=0))


def outer_forcing(row, is_upper, profile_ref, coast_refs, sea_ref, left_ref, hot_ref, rows_ref, bound_ref, edge_ref):
    col_count = sea_ref.shape[1]
    last = coast_refs[0].shape[0] - 1
    profile = jnp.broadcast_to(profile_ref[...], (2 * PAD, LANES))
    for start in range(0, col_count, LANES):
        edge_ref[:, start : start + LANES] = profile * sea_ref[0:1, start : start + LANES]

    def step(number, carry):
        @pl.when((bound_ref[2 * number] <= row) & (row <= bound_ref[2 * number + 1]))
        def _():
            edge_ref[...] += chosen_rows(number, rows_ref[number][0:1], row, 1, left_ref, hot_ref)

        return carry

    lax.fori_loop(0, left_ref.shape[0], step, 0)
    for kind, coast_ref in enumerate(coast_refs):
        coast = jnp.where(is_upper, coast_ref[last : last + 1, :], coast_ref[0:1, :])
        edge_ref[LEVELS + kind : LEVELS + kind + 1, :] = coast.astype(F32)


def all_forcing(profile_ref, coast_refs, sea_ref, left_ref, hot_ref, rows_ref, bound_ref, state):
    row_count, _, col_count = state.shape
    count = left_ref.shape[0]
    for start in range(0, col_count, LANES):
        profile = jnp.broadcast_to(profile_ref[...], (2 * PAD, LANES))
        for row in range(row_count):
            state[row, :, start : start + LANES] = profile * sea_ref[row : row + 1, start : start + LANES]
    batch = math.gcd(count, 4)
    narrow, wide = 3, 6

    def step(number, carry):
        chunks = [number * batch + member for member in range(batch)]
        least = [bound_ref[2 * chunk] for chunk in chunks]
        extent = bound_ref[2 * chunks[0] + 1] - least[0]
        for i in range(1, batch):
            extent = jnp.maximum(extent, bound_ref[2 * chunks[i] + 1] - least[i])

        def add_runs(span, offset_rows, inner):
            for i, chunk in enumerate(chunks):
                begin = least[i] + offset_rows
                base = jnp.minimum(begin, row_count - span)
                here = rows_ref[chunk][0:1]
                here = jnp.where(here >= begin, here, -1)
                product = chosen_rows(chunk, here, base, span, left_ref, hot_ref)
                for offset in range(span):
                    state[base + offset] += product[2 * PAD * offset : 2 * PAD * (offset + 1)]
            return inner

        wanted = jnp.maximum(extent + 1, 0)
        full = lax.div(wanted, wide)
        rest = wanted - wide * full
        wide_turns = full + (rest > narrow).astype(jnp.int32)
        narrow_turns = ((rest > 0) & (rest <= narrow)).astype(jnp.int32)
        lax.fori_loop(0, wide_turns, lambda t, c: add_runs(wide, t * wide, c), 0)
        lax.fori_loop(0, narrow_turns, lambda t, c: add_runs(narrow, full * wide, c), 0)
        return carry

    lax.fori_loop(0, count // batch, step, 0)
    for kind, coast_ref in enumerate(coast_refs):
        coast = coast_ref[...].astype(F32)
        for row in range(row_count):
            state[row, LEVELS + kind : LEVELS + kind + 1, :] = coast[row : row + 1, :]


def half_shapes(row_count, col_count):
    return (
        jax.ShapeDtypeStruct((row_count // 2, 2 * PAD, col_count), F32),
        jax.ShapeDtypeStruct((2 * LEVELS + 2, col_count), F32),
        jax.ShapeDtypeStruct((PAD, LANES), F32),
    )


def in_place(count):
    return [pl.BlockSpec(memory_space=pltpu.SMEM)] + [pl.BlockSpec(memory_space=pltpu.VMEM)] * count


def first_forcing(capacity, alt_capacity, group, flags, message, profile, coast):
    row_count, col_count = coast[0].shape
    devices = message.shape[0]
    members = min(32, devices) * 8
    chunks = capacity // 8 * (devices // min(32, devices))

    def kernel(flag_ref, message_ref, profile_ref, wet, north, east, edge_ref, left, hot, rows, bound, alt, alt_bound, row_ref, sea_ref):
        prepare(capacity, group, row_count, col_count, message_ref, left, hot, rows, bound, alt, alt_bound)
        is_upper = flag_ref[NEAR] > 0
        row = jnp.where(is_upper, row_count - 1, 0)
        row_sea_level(row, alt_chunks(capacity, alt_capacity, devices), message_ref, alt, alt_bound, sea_ref)
        outer_forcing(row, is_upper, profile_ref, (wet, north, east), sea_ref, left, hot, rows, bound, row_ref)
        pack_row(row_ref, edge_ref)

    in_vmem = pl.BlockSpec(memory_space=pltpu.VMEM)
    in_smem = pl.BlockSpec(memory_space=pltpu.SMEM)
    return pl.pallas_call(
        kernel,
        in_specs=in_place(5),
        out_shape=(
            half_shapes(row_count, col_count)[1],
            jax.ShapeDtypeStruct((chunks, 2 * PAD, 2 * members), BF),
            jax.ShapeDtypeStruct((chunks, members, col_count), BF),
            jax.ShapeDtypeStruct((chunks, 8, members), jnp.int32),
            jax.ShapeDtypeStruct((2 * chunks,), jnp.int32),
            jax.ShapeDtypeStruct((chunks, 8, members), F32),
            jax.ShapeDtypeStruct((2 * chunks,), jnp.int32),
        ),
        out_specs=[in_vmem] * 4 + [in_smem, in_vmem, in_smem],
        scratch_shapes=[
            pltpu.VMEM((2 * PAD, col_count), F32),
            pltpu.VMEM((8, col_count), F32),
        ],
        compiler_params=pltpu.CompilerParams(vmem_limit_bytes=24 * MIB),
        cost_estimate=pl.CostEstimate(
            flops=6_000_000_000, bytes_accessed=8_000_000, transcendentals=0
        ),
        name="forcing_first",
    )(flags, message, profile, *coast)


def rest_forcing(capacity, alt_capacity, flags, message, profile, coast, left, hot, rows, bound, alt):
    row_count, col_count = coast[0].shape
    half = row_count // 2
    devices = message.shape[0]

    def kernel(flag_ref, message_ref, profile_ref, wet, north, east, left, hot, rows, alt, bound, state, edge_ref, cols_ref, sea_ref):
        sea_level(alt_chunks(capacity, alt_capacity, devices), message_ref, alt, sea_ref)
        all_forcing(profile_ref, (wet, north, east), sea_ref, left, hot, rows, bound, state)
        cols = jnp.zeros((PAD, LANES), F32)
        for which in (NEAR, FAR):
            first_row = jnp.where(flag_ref[which] > 0, half, 0)
            cols = columns_of(which, state.at[pl.ds(first_row, half)], cols)
        cols_ref[...] = cols
        write_edge(flag_ref[FAR] > 0, state, edge_ref)

    _, edge, cols = half_shapes(row_count, col_count)
    state = jax.ShapeDtypeStruct((row_count, 2 * PAD, col_count), F32)
    return pl.pallas_call(
        kernel,
        in_specs=in_place(9) + [pl.BlockSpec(memory_space=pltpu.SMEM)],
        out_shape=(state, edge, cols),
        scratch_shapes=[pltpu.VMEM((row_count, col_count), F32)],
        compiler_params=pltpu.CompilerParams(vmem_limit_bytes=20 * MIB),
        cost_estimate=pl.CostEstimate(
            flops=6_000_000_000, bytes_accessed=8_000_000, transcendentals=0
        ),
        name="forcing_rest",
    )(flags, message, profile, *coast, left, hot, rows, alt, bound)


def fold_row(row_ref, mirror_ref, piece, chunk, chunks, rows):
    index = jnp.broadcast_to(mirror_ref[0:1, piece(chunk)], (rows, LANES))
    return jnp.take_along_axis(row_ref[:, piece(chunks - 1 - chunk)], index, axis=1)


def weight_kernel(which, flag_ref, wet_ref, north_ref, east_ref, edge_in, west_in, east_in, mirror_ref, out_ref, fold_ref):
    row_count, col_count = wet_ref.shape
    rows = row_count // 2
    is_upper = flag_ref[which] > 0
    at = pl.multiple_of(jnp.where(is_upper, rows, 0), 8)
    wet = wet_ref[pl.ds(at, rows), :].astype(F32)
    north = north_ref[pl.ds(at, rows), :]
    east = east_ref[pl.ds(at, rows), :]
    chunks = col_count // LANES
    lane = lax.broadcasted_iota(jnp.int32, (1, col_count), 1)
    start = column_lane(which, rows, 0, 1, 0)
    west_cols = west_in[72:80, :].T[start : start + rows]
    start = column_lane(which, rows, 0, 0, 0)
    east_cols = east_in[72:80, :].T[start : start + rows]
    west_wet = jnp.where(lane == 0, west_cols[:, 3:4], pltpu.roll(wet, 1, 1))
    west_coef = jnp.where(lane == 0, west_cols[:, 5:6], pltpu.roll(east, 1, 1))
    east_wet = jnp.where(
        lane == col_count - 1, east_cols[:, 3:4], pltpu.roll(wet, col_count - 1, 1)
    )
    east_w = east * wet * east_wet
    west_w = west_coef * west_wet * wet

    def piece(c):
        return slice(c * LANES, (c + 1) * LANES)

    spare_ref = edge_in.at[2 * LEVELS - 6 : 2 * LEVELS + 2]
    if which == FAR:
        for c in range(chunks):
            fold_ref[:, piece(c)] = fold_row(spare_ref, mirror_ref, piece, c, chunks, 8)
    spare = spare_ref[...]
    last = rows - 1
    inner_wet = jnp.where(
        is_upper, wet_ref[rows - 1 : rows, :], wet_ref[rows : rows + 1, :]
    ).astype(F32)
    above = jnp.where(is_upper, spare[6:7], inner_wet)
    top_w = north[last:] * wet[last:] * above
    if which == FAR:
        fold = 0.5 * (north[last:] + fold_ref[7:8]) * wet[last:] * fold_ref[6:7]
        top_w = jnp.where(flag_ref[TOP] > 0, fold, top_w)
    below = jnp.where(is_upper, north_ref[rows - 1 : rows, :] * inner_wet, spare[7:8] * spare[6:7])
    between = north[:last] * wet[:last] * wet[1:]
    north_w = jnp.concatenate([between, top_w], axis=0)
    south_w = jnp.concatenate([below * wet[0:1], between], axis=0)
    center = 1.0 - (east_w + west_w + north_w + south_w)
    for kind, weight in enumerate((center, east_w, west_w, north_w, south_w)):
        for row in range(rows):
            out_ref[row, kind : kind + 1, :] = weight[row : row + 1]


def edge_weights(which, flags, coast, received, mirror):
    row_count, col_count = coast[0].shape

    def kernel(*refs):
        weight_kernel(which, *refs)

    return pl.pallas_call(
        kernel,
        in_specs=in_place(7),
        out_shape=jax.ShapeDtypeStruct((row_count // 2, 8, col_count), F32),
        scratch_shapes=[pltpu.VMEM((8, col_count), F32)],
        compiler_params=pltpu.CompilerParams(vmem_limit_bytes=16 * MIB),
        name="edge_weights",
    )(flags, *coast, *received, mirror)


def receive_row(which, flag_ref, edge_in, mirror_ref, row_ref):
    levels, col_count = edge_in.shape
    chunks = col_count // LANES
    is_top = flag_ref[TOP] > 0

    def piece(c):
        return slice(c * LANES, (c + 1) * LANES)

    def plain():
        for c in range(chunks):
            unpack_row(edge_in[:, piece(c)], row_ref, piece(c))

    if which == NEAR:
        plain()
        return

    @pl.when(jnp.logical_not(is_top))
    def _():
        plain()

    @pl.when(is_top)
    def _():
        for c in range(chunks):
            unpack_row(
                fold_row(edge_in, mirror_ref, piece, c, chunks, levels), row_ref, piece(c)
            )


def neighbour_rows(is_upper, inner, outer_ref, south_ref, north_ref):
    @pl.when(is_upper)
    def _():
        south_ref[...] = inner[...]
        north_ref[...] = outer_ref[...]

    @pl.when(jnp.logical_not(is_upper))
    def _():
        south_ref[...] = outer_ref[...]
        north_ref[...] = inner[...]


def mix_row(which, row, rows, field, state_ref, south_ref, north_ref, west_in, east_in, coef_ref, right_ref, slot):
    col_count = state_ref.shape[2]
    chunks = col_count // LANES
    lane = lax.broadcasted_iota(jnp.int32, (1, LANES), 1)
    levels = slice(field * PAD, (field + 1) * PAD)

    def piece(chunk):
        return slice(chunk * LANES, (chunk + 1) * LANES)

    west_lane = column_lane(which, rows, field, 1, row)
    east_lane = column_lane(which, rows, field, 0, row)
    centers = [state_ref[row, levels, piece(c)] for c in range(chunks)]
    to_left = [pltpu.roll(c, LANES - 1, 1) for c in centers]
    to_right = [pltpu.roll(c, 1, 1) for c in centers]
    to_right.append(pltpu.roll(west_in[...], LANES - west_lane, 1))
    to_left.append(pltpu.roll(east_in[...], LANES - 1 - east_lane, 1))
    for c in range(chunks):
        south = south_ref[levels, piece(c)]
        north = north_ref[levels, piece(c)]
        east = jnp.where(lane == LANES - 1, to_left[c + 1], to_left[c])
        west = jnp.where(lane == 0, to_right[c - 1], to_right[c])

        def coef(kind):
            return coef_ref[row, kind : kind + 1, piece(c)]

        mixed = (
            coef(0) * centers[c]
            + coef(1) * east
            + coef(2) * west
            + coef(3) * north
            + coef(4) * south
        )
        high, low = split_two(mixed)
        right_ref[slot, 0:PAD, piece(c)] = high
        right_ref[slot, PAD : 2 * PAD, piece(c)] = low
        right_ref[slot, 2 * PAD : 3 * PAD, piece(c)] = high


def sweep_rows(which, rows, units, state_ref, south_ref, north_ref, west_in, east_in, coef_ref, matrix_ref, right_ref, emit):
    slots = right_ref.shape[0]
    right_ref[:, 3 * PAD :, :] = jnp.zeros((slots,) + (256 - 3 * PAD, right_ref.shape[2]), BF)

    def product(number):
        row, field = units[number]
        emit(number, row, field, mm(matrix_ref[field, row], right_ref[number % slots]))

    for number, (row, field) in enumerate(units):
        south = state_ref.at[row - 1] if row > 0 else south_ref
        north = state_ref.at[row + 1] if row < rows - 1 else north_ref
        mix_row(which, row, rows, field, state_ref, south, north, west_in, east_in, coef_ref, right_ref, number % slots)
        if number > 0:
            product(number - 1)
    product(len(units) - 1)


def diffuse(which, flags, state, other, received, mirror, coef, matrix, *far_cols):
    rows = coef.shape[0]
    col_count = state.shape[2]

    def kernel(flag_ref, state_ref, other_ref, edge_in, west_in, east_in, mirror_ref, coef_ref, matrix_ref, *refs):
        out_ref, edge_ref, cols_ref, south_ref, north_ref, outer_ref, right_ref = refs[-7:]
        is_upper = flag_ref[which] > 0
        if state.shape[0] > rows:
            state_ref = state_ref.at[pl.ds(jnp.where(is_upper, rows, 0), rows)]
            inner = other_ref.at[jnp.where(is_upper, rows - 1, rows)]
        else:
            inner = other_ref.at[jnp.where(is_upper, rows - 1, 0)]
        receive_row(which, flag_ref, edge_in, mirror_ref, outer_ref)
        neighbour_rows(is_upper, inner, outer_ref, south_ref, north_ref)

        def emit(number, row, field, result):
            out_ref[row, field * PAD : (field + 1) * PAD] = result

        units = [(row, field) for row in range(rows) for field in range(2)]
        sweep_rows(which, rows, units, state_ref, south_ref, north_ref, west_in, east_in, coef_ref, matrix_ref, right_ref, emit)
        write_edge(is_upper, out_ref, edge_ref)
        old_cols = refs[0][...] if which == NEAR else jnp.zeros((PAD, LANES), F32)
        cols_ref[...] = columns_of(which, out_ref, old_cols)

    return pl.pallas_call(
        kernel,
        in_specs=in_place(8 + len(far_cols)),
        out_shape=half_shapes(2 * rows, col_count),
        scratch_shapes=[pltpu.VMEM((2 * PAD, col_count), F32)] * 3
        + [pltpu.VMEM((4, 256, col_count), BF)],
        compiler_params=pltpu.CompilerParams(vmem_limit_bytes=16 * MIB),
        cost_estimate=pl.CostEstimate(
            flops=3_000_000_000, bytes_accessed=8_000_000, transcendentals=0
        ),
        name="diffusion_" + ("near", "far")[which],
    )(flags, state, other, *received, mirror, coef, matrix, *far_cols)


def output_layout(results):
    return jnp.swapaxes(jnp.stack(results), 0, 1)[:LEVELS]


def store_block(out_ref, stage_ref, sem, at, field):
    rows = stage_ref.shape[2]
    copy = pltpu.make_async_copy(
        stage_ref.at[field],
        out_ref.at[pl.ds(field * LEVELS, LEVELS), pl.ds(at, rows), :],
        sem.at[field],
    )
    copy.start()
    return copy


def last_inner(flags, near, far, near_edge, near_sides, far_sides, mirror, near_fixed, far_fixed, mask):
    rows, _, col_count = near.shape

    def kernel(flag_ref, near_ref, far_ref, edge_in, near_west, near_east, far_west, far_east, mirror_ref, near_coef, near_matrix, far_coef, far_matrix, mask_ref, out_ref, done_ref, south_ref, north_ref, outer_ref, right_ref, stage_ref, sem, kept_ref):
        is_upper = flag_ref[NEAR] > 0
        at = pl.multiple_of(jnp.where(is_upper, rows, 0), 8)
        wet = mask_ref[pl.ds(at, rows), :].astype(F32)
        far_at = pl.multiple_of(rows - at, 8)
        far_wet = mask_ref[pl.ds(far_at, rows), :].astype(F32)
        last = rows - 1
        far_inner = far_ref.at[jnp.where(is_upper, last, 0)]
        receive_row(NEAR, flag_ref, edge_in, mirror_ref, outer_ref)
        neighbour_rows(is_upper, far_inner, outer_ref, south_ref, north_ref)
        copies = []
        for field in range(2):
            results = []

            def emit(number, row, field, result):
                results.append(result * wet[row : row + 1])

            units = [(row, field) for row in range(rows)]
            sweep_rows(NEAR, rows, units, near_ref, south_ref, north_ref, near_west, near_east, near_coef, near_matrix, right_ref, emit)
            stage_ref[field] = output_layout(results)
            copies.append(store_block(out_ref, stage_ref, sem, at, field))
        edge = jnp.where(is_upper, last, 0)
        near_inner = near_ref.at[jnp.where(is_upper, 0, last)]

        @pl.when(is_upper)
        def _():
            south_ref[...] = far_ref[last - 1]
            north_ref[...] = near_inner[...]

        @pl.when(jnp.logical_not(is_upper))
        def _():
            south_ref[...] = near_inner[...]
            north_ref[...] = far_ref[1]

        def keep(number, row, field, result):
            kept_ref[row, field * PAD : (field + 1) * PAD] = result * far_wet[row : row + 1]

        units = [(row, field) for row in range(1, last) for field in range(2)]
        sweep_rows(FAR, rows, units, far_ref, south_ref, north_ref, far_west, far_east, far_coef, far_matrix, right_ref, keep)
        edge_wet = jnp.where(is_upper, far_wet[last:], far_wet[0:1])
        for field in range(2):
            mix_row(FAR, edge, rows, field, far_ref, south_ref, north_ref, far_west, far_east, far_coef, right_ref, field)
        for field in range(2):
            result = mm(far_matrix[field, edge], right_ref[field])
            kept_ref[edge, field * PAD : (field + 1) * PAD] = result * edge_wet
        for field in range(2):
            levels = slice(field * PAD, (field + 1) * PAD)
            done_ref[field] = output_layout([kept_ref[row, levels] for row in range(rows)])
        for copy in copies:
            copy.wait()

    return pl.pallas_call(
        kernel,
        in_specs=in_place(13),
        out_specs=[pl.BlockSpec(memory_space=pl.ANY), pl.BlockSpec(memory_space=pltpu.VMEM)],
        out_shape=(
            jax.ShapeDtypeStruct((2 * LEVELS, 2 * rows, col_count), F32),
            jax.ShapeDtypeStruct((2, LEVELS, rows, col_count), F32),
        ),
        scratch_shapes=[pltpu.VMEM((2 * PAD, col_count), F32)] * 3
        + [
            pltpu.VMEM((4, 256, col_count), BF),
            pltpu.VMEM((2, LEVELS, rows, col_count), F32),
            pltpu.SemaphoreType.DMA((2,)),
            pltpu.VMEM((rows, 2 * PAD, col_count), F32),
        ],
        compiler_params=pltpu.CompilerParams(vmem_limit_bytes=22 * MIB),
        cost_estimate=pl.CostEstimate(
            flops=6_000_000_000, bytes_accessed=16_000_000, transcendentals=0
        ),
        name="last_inner",
    )(flags, near, far, near_edge, *near_sides, *far_sides, mirror, *near_fixed, *far_fixed, mask)


def last_outer(flags, far, far_edge, far_sides, mirror, far_fixed, mask, done, target):
    rows, _, col_count = far.shape

    def kernel(flag_ref, far_ref, edge_in, west_in, east_in, mirror_ref, coef_ref, matrix_ref, mask_ref, done_ref, target_ref, out_ref, south_ref, north_ref, outer_ref, right_ref, stage_ref, sem):
        is_upper = flag_ref[FAR] > 0
        at = pl.multiple_of(jnp.where(is_upper, rows, 0), 8)
        wet = mask_ref[pl.ds(at, rows), :].astype(F32)
        last = rows - 1
        row = jnp.where(is_upper, last, 0)
        row_wet = jnp.where(is_upper, wet[last:], wet[0:1])
        receive_row(FAR, flag_ref, edge_in, mirror_ref, outer_ref)
        neighbour_rows(is_upper, far_ref.at[jnp.where(is_upper, last - 1, 1)], outer_ref, south_ref, north_ref)
        right_ref[:, 3 * PAD :, :] = jnp.zeros((2, 256 - 3 * PAD, col_count), BF)
        for field in range(2):
            mix_row(FAR, row, rows, field, far_ref, south_ref, north_ref, west_in, east_in, coef_ref, right_ref, field)
        copies = []
        here = lax.broadcasted_iota(jnp.int32, (rows, 1), 0) == row
        for field in range(2):
            outer_ref[0:PAD] = mm(matrix_ref[field, row], right_ref[field]) * row_wet
            for level in range(LEVELS):
                stage_ref[field, level] = jnp.where(
                    here, outer_ref[level : level + 1, :], done_ref[field, level]
                )
            copies.append(store_block(out_ref, stage_ref, sem, at, field))
        for copy in copies:
            copy.wait()

    operands = [flags, far, far_edge, *far_sides, mirror, *far_fixed, mask, done, target]
    return pl.pallas_call(
        kernel,
        in_specs=in_place(9) + [pl.BlockSpec(memory_space=pl.ANY)],
        out_specs=pl.BlockSpec(memory_space=pl.ANY),
        out_shape=jax.ShapeDtypeStruct((2 * LEVELS, 2 * rows, col_count), F32),
        input_output_aliases={len(operands) - 1: 0},
        scratch_shapes=[pltpu.VMEM((2 * PAD, col_count), F32)] * 3
        + [
            pltpu.VMEM((2, 256, col_count), BF),
            pltpu.VMEM((2, LEVELS, rows, col_count), F32),
            pltpu.SemaphoreType.DMA((2,)),
        ],
        compiler_params=pltpu.CompilerParams(vmem_limit_bytes=20 * MIB),
        name="last_outer",
    )(*operands)


def mixing_matrices(vinv):
    turned = jnp.transpose(vinv, (1, 0, 3, 2))
    turned = jnp.pad(turned, ((0, 0), (0, 0), (0, PAD - LEVELS), (0, PAD - LEVELS)))
    high = lax.reduce_precision(turned, 8, 7)
    low = (turned - high).astype(BF)
    high = high.astype(BF)
    rest = jnp.zeros(high.shape[:3] + (256 - 3 * PAD,), BF)
    return jnp.concatenate([high, high, low, rest], axis=3)


def body(
    argo_value,
    argo_owner,
    argo_cell,
    alt_value,
    alt_owner,
    alt_cell,
    alt_profile,
    land_mask,
    coef_east,
    coef_north,
    mirror,
    vinv,
):
    row_count, col_count = land_mask.shape
    count_ja = lax.axis_size("ja")
    count_ia = lax.axis_size("ia")
    devices = count_ja * count_ia
    capacity = round_up(3 * argo_value.shape[0] // devices, 8)
    group = round_up(capacity // 4, 8)
    alt_capacity = max(2, 3 * alt_value.shape[0] // devices)
    message = send_tables(
        devices,
        capacity,
        alt_capacity,
        group,
        row_count,
        col_count,
        (
            argo_value.T,
            argo_owner.reshape(1, -1),
            argo_cell.reshape(1, -1),
            alt_value,
            alt_cell,
            alt_owner.reshape(1, -1),
        ),
    )
    message, ja_index = lax.optimization_barrier((message, lax.axis_index("ja")))
    message = lax.all_to_all(message, ("ja", "ia"), split_axis=0, concat_axis=0, tiled=True)

    ia_index = lax.axis_index("ia")
    is_top = (ja_index == count_ja - 1).astype(jnp.int32)
    parity = ja_index % 2
    flags = jnp.stack([1 - parity, parity, is_top]).astype(jnp.int32)
    fold_index = mirror - (count_ia - 1 - ia_index) * col_count
    mirror_lane = jnp.broadcast_to((fold_index % LANES)[None, :], (8, col_count))
    matrices = mixing_matrices(vinv)
    profile = jnp.pad(alt_profile.reshape(2, LEVELS, 1), ((0, 0), (0, PAD - LEVELS), (0, 0)))
    profile = profile.reshape(2 * PAD, 1)
    coast = (land_mask, coef_north, coef_east)
    rows = row_count // 2
    lower = [matrices[:, :rows], matrices[:, rows:]]
    odd_device = parity == 1
    half_matrices = [
        jnp.where(odd_device, lower[0], lower[1]),
        jnp.where(odd_device, lower[1], lower[0]),
    ]

    ring_east = [(i, (i + 1) % count_ia) for i in range(count_ia)]
    ring_west = [((i + 1) % count_ia, i) for i in range(count_ia)]
    even_swap = []
    odd_swap = []
    for ja in range(count_ja):
        for ia in range(count_ia):
            here = ja * count_ia + ia
            even_swap.append((here, (ja ^ 1) * count_ia + ia))
            if ja == count_ja - 1:
                odd_swap.append((here, ja * count_ia + count_ia - 1 - ia))
            elif ja > 0:
                odd_swap.append((here, (((ja - 1) ^ 1) + 1) * count_ia + ia))
    swaps = (even_swap, odd_swap)

    def swap(which, edge):
        return lax.ppermute(edge, ("ja", "ia"), swaps[which])

    def pass_columns(cols):
        return lax.ppermute(cols, "ia", ring_east), lax.ppermute(cols, "ia", ring_west)

    near_edge, *prepared = first_forcing(
        capacity, alt_capacity, group, flags, message, profile, coast
    )
    near_edge = swap(NEAR, near_edge)
    state, far_edge, cols = rest_forcing(
        capacity, alt_capacity, flags, message, profile, coast, *prepared[:5]
    )
    near = far = state
    sides = pass_columns(cols)
    far_edge = swap(FAR, far_edge)
    near_coef = edge_weights(NEAR, flags, coast, (near_edge, *sides), mirror_lane)
    far_coef = edge_weights(FAR, flags, coast, (far_edge, *sides), mirror_lane)
    near_fixed = (mirror_lane, near_coef, half_matrices[NEAR])
    far_fixed = (mirror_lane, far_coef, half_matrices[FAR])
    for sweep in range(ITERS - 1):
        new_near, new_edge, cols = diffuse(
            NEAR, flags, near, far, (near_edge, *sides), *near_fixed, cols
        )
        near_edge = swap(NEAR, new_edge)
        sides = pass_columns(cols)
        far, new_edge, cols = diffuse(FAR, flags, far, near, (far_edge, *sides), *far_fixed)
        far_edge = swap(FAR, new_edge)
        near = new_near
    last_sides = pass_columns(cols)
    output, done = last_inner(
        flags, near, far, near_edge, sides, last_sides, mirror_lane, near_fixed[1:], far_fixed[1:], land_mask
    )
    return last_outer(
        flags, far, far_edge, last_sides, mirror_lane, far_fixed[1:], land_mask, done, output
    )


def solution(mesh):
    in_specs = (
        P(("ja", "ia"), None),
        P(("ja", "ia"), None),
        P(("ja", "ia")),
        P(("ja", "ia")),
        P(("ja", "ia"), None),
        P(("ja", "ia")),
        P(),
        P("ja", "ia"),
        P("ja", "ia"),
        P("ja", "ia"),
        P("ia"),
        P("ja", None, None, None),
    )
    out_specs = P(None, "ja", "ia")
    return jax.shard_map(body, mesh=mesh, in_specs=in_specs, out_specs=out_specs, check_vma=False)
```

```python
import math

import jax
import jax.numpy as jnp
from jax import lax
from jax.experimental import pallas as pl
from jax.experimental.pallas import tpu as pltpu
from jax.sharding import PartitionSpec as P

ITERS = 3
LEVELS = 75
PAD = 80
LANES = 128
NEAR, FAR, TOP = 0, 1, 2
BF = jnp.bfloat16
F32 = jnp.float32
MIB = 1024 * 1024


def round_up(value, unit):
    return (value + unit - 1) // unit * unit


def split_two(value):
    high = value.astype(BF)
    low = (value - high.astype(F32)).astype(BF)
    return high, low


def mm(left, right):
    return jnp.dot(left, right, preferred_element_type=F32)


def as_column(row):
    return jnp.broadcast_to(row, (8, row.shape[1])).T[:, 0:1]


def slot_ranks(owner_row, cell_row, devices, col_count, row_count, capacity, spread):
    count = owner_row.shape[1]
    owner = owner_row.astype(F32)
    inside = cell_row // col_count
    order = lax.broadcasted_iota(jnp.int32, (1, count), 1).astype(F32)
    key = (owner * float(row_count) + inside.astype(F32)) * float(count) + order
    key_col = as_column(key)
    device = lax.broadcasted_iota(jnp.int32, (devices, 1), 0)
    mine = device == owner_row
    totals = jnp.sum(jnp.where(mine, 1.0, 0.0), axis=1, keepdims=True)
    rank = -jnp.sum(jnp.where(device < owner_row, totals, 0.0), axis=0, keepdims=True)
    for start in range(0, count, 128):
        before = jnp.where(key_col[start : start + 128] < key, 1.0, 0.0)
        rank = rank + jnp.sum(before, axis=0, keepdims=True)
    if spread:
        total = jnp.sum(jnp.where(mine, totals, 0.0), axis=0, keepdims=True)
        offset = owner * 1024.0
        goal = (inside * capacity // row_count).astype(F32) - rank + offset
        goal_col = as_column(goal)
        shift = offset
        for start in range(0, count, 128):
            within = key_col[start : start + 128] <= key
            reached = jnp.where(within, goal_col[start : start + 128], 0.0)
            shift = jnp.maximum(shift, jnp.max(reached, axis=0, keepdims=True))
        rank = rank + jnp.minimum(shift - offset, float(capacity) - total)
    return rank


def table_kernel(
    devices,
    capacity,
    group,
    row_count,
    col_count,
    value_ref,
    owner_ref,
    cell_ref,
    alt_value_ref,
    alt_cell_ref,
    alt_owner_ref,
    message_ref,
    level_ref,
    side_ref,
    hi_ref,
    lo_ref,
    alt_all_ref,
    rank_hot_ref,
    alt_rank_hot_ref,
):
    index = pl.program_id(0)
    n_obs = owner_ref.shape[1]
    n_alt = alt_owner_ref.shape[1]

    @pl.when(index == 0)
    def _():
        slot = lax.broadcasted_iota(jnp.int32, (capacity, 1), 0).astype(F32)
        alt_cell = alt_cell_ref[...].reshape(1, n_alt)
        rank = slot_ranks(
            owner_ref[...], cell_ref[...], devices, col_count, row_count, capacity, True
        )
        rank_hot_ref[...] = jnp.where(slot == rank, 1.0, 0.0).astype(BF)
        rank = slot_ranks(
            alt_owner_ref[...], alt_cell, devices, col_count, row_count, capacity, False
        )
        alt_rank_hot_ref[...] = jnp.where(slot == rank, 1.0, 0.0).astype(BF)
        level_ref[...] = jnp.zeros(level_ref.shape, F32)
        level_ref[0:75, :] = value_ref[0:75, :]
        level_ref[75:76, :] = cell_ref[...].astype(F32) + 1.0
        level_ref[80:128, :] = value_ref[75:123, :]
        for lane_group in range(4):
            level_ref[128 + 32 * lane_group : 155 + 32 * lane_group, :] = value_ref[123:150, :]
        high, low = split_two(level_ref[...].T)
        hi_ref[...] = high
        lo_ref[...] = low
        pair = jnp.concatenate(
            [alt_value_ref[...].reshape(1, n_alt), alt_cell.astype(F32) + 1.0], axis=0
        )
        pair_high = pair.astype(BF).astype(F32)
        side_ref[...] = jnp.zeros(side_ref.shape, F32)
        side_ref[:, 0:8] = jnp.concatenate(
            [pair_high, pair - pair_high, jnp.zeros((4, n_alt), F32)], axis=0
        ).T
        alt_all_ref[...] = pltpu.roll(side_ref[...], 76, 1).astype(BF)

    per_step = message_ref.shape[0]
    chosen = []
    chosen_alt = []
    for member in range(per_step):
        device = index * per_step + member
        mask = jnp.where(owner_ref[...] == device, 1.0, 0.0).astype(BF)
        chosen.append(rank_hot_ref[...] * mask)
        mask = jnp.where(alt_owner_ref[...] == device, 1.0, 0.0).astype(BF)
        chosen_alt.append(alt_rank_hot_ref[...] * mask)
    chosen = jnp.concatenate(chosen, axis=0)
    chosen_alt = jnp.concatenate(chosen_alt, axis=0)
    table = mm(chosen, hi_ref[...]) + mm(chosen, lo_ref[...])
    lane = lax.broadcasted_iota(jnp.int32, (1, LANES), 1)
    extra = mm(chosen_alt, alt_all_ref[...])
    extra = jnp.where(lane < 78, extra + pltpu.roll(extra, LANES - 2, 1), 0.0)
    extra = jnp.where(lane >= 76, extra, 0.0)
    first = table[:, :LANES] + extra
    message_ref[:, 0:capacity] = first.reshape(per_step, capacity, LANES)
    rest = table[:, LANES:].reshape(per_step, capacity, LANES)
    total = jnp.zeros((per_step, group, LANES), F32)
    for lane_group in range(4):
        low_slot = lane_group * group
        if low_slot >= capacity:
            continue
        piece = rest[:, low_slot : low_slot + group]
        here = (lane // 32 == lane_group).reshape(1, 1, LANES)
        total = jnp.where(here, piece, total)
    message_ref[:, capacity : capacity + group] = total


def send_tables(devices, capacity, group, row_count, col_count, operands):
    n_obs = operands[1].shape[1]
    n_alt = operands[5].shape[1]
    per_step = max(1, 1536 // capacity)

    def kernel(*refs):
        table_kernel(devices, capacity, group, row_count, col_count, *refs)

    def whole(array):
        return pl.BlockSpec(array.shape, lambda s: (0,) * len(array.shape))

    return pl.pallas_call(
        kernel,
        grid=(devices // per_step,),
        in_specs=[whole(x) for x in operands],
        out_specs=pl.BlockSpec((per_step, capacity + group, LANES), lambda s: (s, 0, 0)),
        out_shape=jax.ShapeDtypeStruct((devices, capacity + group, LANES), F32),
        scratch_shapes=[
            pltpu.VMEM((2 * LANES, n_obs), F32),
            pltpu.VMEM((n_alt, LANES), F32),
            pltpu.VMEM((n_obs, 2 * LANES), BF),
            pltpu.VMEM((n_obs, 2 * LANES), BF),
            pltpu.VMEM((n_alt, LANES), BF),
            pltpu.VMEM((capacity, n_obs), BF),
            pltpu.VMEM((capacity, n_alt), BF),
        ],
        compiler_params=pltpu.CompilerParams(vmem_limit_bytes=56 * MIB),
        name="send_tables",
    )(*operands)


def column_lane(which, rows, field, east, row):
    return (4 * which + 2 * field + east) * rows + row


def columns_of(which, state_ref, cols):
    rows = state_ref.shape[0]
    lane = lax.broadcasted_iota(jnp.int32, (1, LANES), 1)
    for row in range(rows):
        for field in range(2):
            part = state_ref[row, field * PAD : (field + 1) * PAD, :]
            at = column_lane(which, rows, field, 0, row)
            cols = jnp.where(lane == at, pltpu.roll(part[:, :LANES], at, 1), cols)
            at = column_lane(which, rows, field, 1, row)
            cols = jnp.where(lane == at, pltpu.roll(part[:, -LANES:], at + 1, 1), cols)
    return cols


def pack_row(row_ref, edge_ref):
    edge_ref[0:LEVELS] = row_ref[0:LEVELS]
    edge_ref[LEVELS : 2 * LEVELS] = row_ref[PAD : PAD + LEVELS]
    edge_ref[2 * LEVELS : 2 * LEVELS + 2] = row_ref[LEVELS : LEVELS + 2]


def unpack_row(edge, row_ref, piece):
    row_ref[0:LEVELS, piece] = edge[0:LEVELS]
    row_ref[PAD : PAD + LEVELS, piece] = edge[LEVELS : 2 * LEVELS]
    for at in (LEVELS, PAD + LEVELS):
        row_ref[at : at + PAD - LEVELS, piece] = jnp.zeros((PAD - LEVELS, edge.shape[1]), F32)


def write_edge(is_upper, state_ref, edge_ref):
    pack_row(state_ref.at[jnp.where(is_upper, state_ref.shape[0] - 1, 0)], edge_ref)


def prepare(capacity, alt_capacity, group, col_count, message_ref, sea_ref, left_ref, hot_ref, rows_ref, bound_ref):
    row_count = sea_ref.shape[0]
    devices = message_ref.shape[0]
    block = min(32, devices)
    members = block * 8
    octets = capacity // 8
    alt_octets = (alt_capacity + 7) // 8
    per_group = group // 8
    shift = col_count.bit_length() - 1
    col_iota = lax.broadcasted_iota(jnp.int32, (1, col_count), 1)
    row_iota = lax.broadcasted_iota(jnp.int32, (row_count, 1), 0)

    def chunk(index, start):
        return message_ref[index * block : (index + 1) * block, start : start + 8, :].reshape(
            members, LANES
        )

    def hot_of(cell):
        return jnp.where(((cell - 1) & (col_count - 1)) == col_iota, 1.0, 0.0).astype(BF)

    def rows_of(cell):
        return lax.shift_right_arithmetic(cell - 1, shift)

    sea = jnp.zeros((row_count, col_count), F32)
    all_rows = []
    count = 0
    for index in range(devices // block):
        tails = [chunk(index, capacity + 8 * part).T for part in range(per_group)]
        for octet in range(octets):
            table = chunk(index, 8 * octet)
            turned = table.T
            tail = tails[octet % per_group]
            begin = 32 * (octet // per_group)
            levels = jnp.concatenate([turned, tail[begin : begin + 32]], axis=0)
            high, low = split_two(levels)
            left_ref[count, :, 0:members] = high
            left_ref[count, :, members : 2 * members] = low
            hot = hot_of(table[:, 75:76].astype(jnp.int32))
            hot_ref[count] = hot
            rows = rows_of(turned[75:76].astype(jnp.int32))
            rows_ref[count] = jnp.broadcast_to(rows, (8, members))
            all_rows.append(rows.astype(F32))
            count += 1
            if octet >= alt_octets:
                continue
            alt_hot = hot_of(table[:, 77:78].astype(jnp.int32))
            alt_rows = rows_of(turned[77:78].astype(jnp.int32))
            weighted = jnp.where(alt_rows == row_iota, turned[76:77], 0.0)
            high, low = split_two(weighted)
            product = mm(jnp.concatenate([high, low], axis=0), alt_hot)
            sea = sea + product[:row_count] + product[row_count:]
    sea_ref[...] = sea
    all_rows = jnp.concatenate(all_rows, axis=0)
    least = jnp.where(all_rows >= 0.0, all_rows, float(row_count))
    least = jnp.min(least, axis=1, keepdims=True).astype(jnp.int32)
    most = jnp.max(all_rows, axis=1, keepdims=True).astype(jnp.int32)
    for number in range(count):
        bound_ref[2 * number] = least[number, 0]
        bound_ref[2 * number + 1] = most[number, 0]


def chosen_rows(number, here, row, span, left_ref, hot_ref):
    pieces = []
    for offset in range(span):
        mask = jnp.where(here == row + offset, 1.0, 0.0).astype(BF)
        pieces.append(left_ref[number] * jnp.concatenate([mask, mask], axis=1))
    hot = hot_ref[number]
    return mm(jnp.concatenate(pieces, axis=0), jnp.concatenate([hot, hot], axis=0))


def outer_forcing(row, is_upper, profile_ref, coast_refs, sea_ref, left_ref, hot_ref, rows_ref, bound_ref, edge_ref):
    row_count, col_count = sea_ref.shape
    last = row_count - 1
    profile = jnp.broadcast_to(profile_ref[...], (2 * PAD, LANES))
    sea = jnp.where(is_upper, sea_ref[last : last + 1, :], sea_ref[0:1, :])
    for start in range(0, col_count, LANES):
        edge_ref[:, start : start + LANES] = profile * sea[:, start : start + LANES]

    def step(number, carry):
        @pl.when((bound_ref[2 * number] <= row) & (row <= bound_ref[2 * number + 1]))
        def _():
            edge_ref[...] += chosen_rows(number, rows_ref[number][0:1], row, 1, left_ref, hot_ref)

        return carry

    lax.fori_loop(0, left_ref.shape[0], step, 0)
    for kind, coast_ref in enumerate(coast_refs):
        coast = jnp.where(is_upper, coast_ref[last : last + 1, :], coast_ref[0:1, :])
        edge_ref[LEVELS + kind : LEVELS + kind + 1, :] = coast.astype(F32)


def all_forcing(profile_ref, coast_refs, sea_ref, left_ref, hot_ref, rows_ref, bound_ref, state):
    row_count, _, col_count = state.shape
    count = left_ref.shape[0]
    for start in range(0, col_count, LANES):
        profile = jnp.broadcast_to(profile_ref[...], (2 * PAD, LANES))
        for row in range(row_count):
            state[row, :, start : start + LANES] = profile * sea_ref[row : row + 1, start : start + LANES]
    batch = math.gcd(count, 4)
    narrow, wide = 3, 6

    def step(number, carry):
        chunks = [number * batch + member for member in range(batch)]
        least = [bound_ref[2 * chunk] for chunk in chunks]
        extent = bound_ref[2 * chunks[0] + 1] - least[0]
        for i in range(1, batch):
            extent = jnp.maximum(extent, bound_ref[2 * chunks[i] + 1] - least[i])

        def add_runs(span, offset_rows, inner):
            for i, chunk in enumerate(chunks):
                begin = least[i] + offset_rows
                base = jnp.minimum(begin, row_count - span)
                here = rows_ref[chunk][0:1]
                here = jnp.where(here >= begin, here, -1)
                product = chosen_rows(chunk, here, base, span, left_ref, hot_ref)
                for offset in range(span):
                    state[base + offset] += product[2 * PAD * offset : 2 * PAD * (offset + 1)]
            return inner

        wanted = jnp.maximum(extent + 1, 0)
        full = lax.div(wanted, wide)
        rest = wanted - wide * full
        wide_turns = full + (rest > narrow).astype(jnp.int32)
        narrow_turns = ((rest > 0) & (rest <= narrow)).astype(jnp.int32)
        lax.fori_loop(0, wide_turns, lambda t, c: add_runs(wide, t * wide, c), 0)
        lax.fori_loop(0, narrow_turns, lambda t, c: add_runs(narrow, full * wide, c), 0)
        return carry

    lax.fori_loop(0, count // batch, step, 0)
    for kind, coast_ref in enumerate(coast_refs):
        coast = coast_ref[...].astype(F32)
        for row in range(row_count):
            state[row, LEVELS + kind : LEVELS + kind + 1, :] = coast[row : row + 1, :]


def half_shapes(row_count, col_count):
    return (
        jax.ShapeDtypeStruct((row_count // 2, 2 * PAD, col_count), F32),
        jax.ShapeDtypeStruct((2 * LEVELS + 2, col_count), F32),
        jax.ShapeDtypeStruct((PAD, LANES), F32),
    )


def in_place(count):
    return [pl.BlockSpec(memory_space=pltpu.SMEM)] + [pl.BlockSpec(memory_space=pltpu.VMEM)] * count


def first_forcing(capacity, alt_capacity, group, flags, message, profile, coast):
    row_count, col_count = coast[0].shape
    devices = message.shape[0]
    members = min(32, devices) * 8
    chunks = capacity // 8 * (devices // min(32, devices))

    def kernel(flag_ref, message_ref, profile_ref, wet, north, east, edge_ref, *refs):
        *outs, row_ref = refs
        prepare(capacity, alt_capacity, group, col_count, message_ref, *outs)
        is_upper = flag_ref[NEAR] > 0
        row = jnp.where(is_upper, row_count - 1, 0)
        outer_forcing(row, is_upper, profile_ref, (wet, north, east), *outs, row_ref)
        pack_row(row_ref, edge_ref)

    return pl.pallas_call(
        kernel,
        in_specs=in_place(5),
        out_shape=(
            half_shapes(row_count, col_count)[1],
            jax.ShapeDtypeStruct((row_count, col_count), F32),
            jax.ShapeDtypeStruct((chunks, 2 * PAD, 2 * members), BF),
            jax.ShapeDtypeStruct((chunks, members, col_count), BF),
            jax.ShapeDtypeStruct((chunks, 8, members), jnp.int32),
            jax.ShapeDtypeStruct((2 * chunks,), jnp.int32),
        ),
        out_specs=[pl.BlockSpec(memory_space=pltpu.VMEM)] * 5
        + [pl.BlockSpec(memory_space=pltpu.SMEM)],
        scratch_shapes=[pltpu.VMEM((2 * PAD, col_count), F32)],
        compiler_params=pltpu.CompilerParams(vmem_limit_bytes=24 * MIB),
        cost_estimate=pl.CostEstimate(
            flops=6_000_000_000, bytes_accessed=8_000_000, transcendentals=0
        ),
        name="forcing_first",
    )(flags, message, profile, *coast)


def rest_forcing(flags, profile, coast, prepared):
    row_count, col_count = coast[0].shape
    half = row_count // 2

    def kernel(flag_ref, profile_ref, wet, north, east, sea, left, hot, rows, bound, state, edge_ref, cols_ref):
        all_forcing(profile_ref, (wet, north, east), sea, left, hot, rows, bound, state)
        cols = jnp.zeros((PAD, LANES), F32)
        for which in (NEAR, FAR):
            first_row = jnp.where(flag_ref[which] > 0, half, 0)
            cols = columns_of(which, state.at[pl.ds(first_row, half)], cols)
        cols_ref[...] = cols
        write_edge(flag_ref[FAR] > 0, state, edge_ref)

    _, edge, cols = half_shapes(row_count, col_count)
    state = jax.ShapeDtypeStruct((row_count, 2 * PAD, col_count), F32)
    return pl.pallas_call(
        kernel,
        in_specs=in_place(8) + [pl.BlockSpec(memory_space=pltpu.SMEM)],
        out_shape=(state, edge, cols),
        compiler_params=pltpu.CompilerParams(vmem_limit_bytes=20 * MIB),
        cost_estimate=pl.CostEstimate(
            flops=6_000_000_000, bytes_accessed=8_000_000, transcendentals=0
        ),
        name="forcing_rest",
    )(flags, profile, *coast, *prepared)


def fold_row(row_ref, mirror_ref, piece, chunk, chunks, rows):
    index = jnp.broadcast_to(mirror_ref[0:1, piece(chunk)], (rows, LANES))
    return jnp.take_along_axis(row_ref[:, piece(chunks - 1 - chunk)], index, axis=1)


def weight_kernel(which, flag_ref, wet_ref, north_ref, east_ref, edge_in, west_in, east_in, mirror_ref, out_ref, fold_ref):
    row_count, col_count = wet_ref.shape
    rows = row_count // 2
    is_upper = flag_ref[which] > 0
    at = pl.multiple_of(jnp.where(is_upper, rows, 0), 8)
    wet = wet_ref[pl.ds(at, rows), :].astype(F32)
    north = north_ref[pl.ds(at, rows), :]
    east = east_ref[pl.ds(at, rows), :]
    chunks = col_count // LANES
    lane = lax.broadcasted_iota(jnp.int32, (1, col_count), 1)
    start = column_lane(which, rows, 0, 1, 0)
    west_cols = west_in[72:80, :].T[start : start + rows]
    start = column_lane(which, rows, 0, 0, 0)
    east_cols = east_in[72:80, :].T[start : start + rows]
    west_wet = jnp.where(lane == 0, west_cols[:, 3:4], pltpu.roll(wet, 1, 1))
    west_coef = jnp.where(lane == 0, west_cols[:, 5:6], pltpu.roll(east, 1, 1))
    east_wet = jnp.where(
        lane == col_count - 1, east_cols[:, 3:4], pltpu.roll(wet, col_count - 1, 1)
    )
    east_w = east * wet * east_wet
    west_w = west_coef * west_wet * wet

    def piece(c):
        return slice(c * LANES, (c + 1) * LANES)

    spare_ref = edge_in.at[2 * LEVELS - 6 : 2 * LEVELS + 2]
    if which == FAR:
        for c in range(chunks):
            fold_ref[:, piece(c)] = fold_row(spare_ref, mirror_ref, piece, c, chunks, 8)
    spare = spare_ref[...]
    last = rows - 1
    inner_wet = jnp.where(
        is_upper, wet_ref[rows - 1 : rows, :], wet_ref[rows : rows + 1, :]
    ).astype(F32)
    above = jnp.where(is_upper, spare[6:7], inner_wet)
    top_w = north[last:] * wet[last:] * above
    if which == FAR:
        fold = 0.5 * (north[last:] + fold_ref[7:8]) * wet[last:] * fold_ref[6:7]
        top_w = jnp.where(flag_ref[TOP] > 0, fold, top_w)
    below = jnp.where(is_upper, north_ref[rows - 1 : rows, :] * inner_wet, spare[7:8] * spare[6:7])
    between = north[:last] * wet[:last] * wet[1:]
    north_w = jnp.concatenate([between, top_w], axis=0)
    south_w = jnp.concatenate([below * wet[0:1], between], axis=0)
    center = 1.0 - (east_w + west_w + north_w + south_w)
    for kind, weight in enumerate((center, east_w, west_w, north_w, south_w)):
        for row in range(rows):
            out_ref[row, kind : kind + 1, :] = weight[row : row + 1]


def edge_weights(which, flags, coast, received, mirror):
    row_count, col_count = coast[0].shape

    def kernel(*refs):
        weight_kernel(which, *refs)

    return pl.pallas_call(
        kernel,
        in_specs=in_place(7),
        out_shape=jax.ShapeDtypeStruct((row_count // 2, 8, col_count), F32),
        scratch_shapes=[pltpu.VMEM((8, col_count), F32)],
        compiler_params=pltpu.CompilerParams(vmem_limit_bytes=16 * MIB),
        name="edge_weights",
    )(flags, *coast, *received, mirror)


def receive_row(which, flag_ref, edge_in, mirror_ref, row_ref):
    levels, col_count = edge_in.shape
    chunks = col_count // LANES
    is_top = flag_ref[TOP] > 0

    def piece(c):
        return slice(c * LANES, (c + 1) * LANES)

    def plain():
        for c in range(chunks):
            unpack_row(edge_in[:, piece(c)], row_ref, piece(c))

    if which == NEAR:
        plain()
        return

    @pl.when(jnp.logical_not(is_top))
    def _():
        plain()

    @pl.when(is_top)
    def _():
        for c in range(chunks):
            unpack_row(
                fold_row(edge_in, mirror_ref, piece, c, chunks, levels), row_ref, piece(c)
            )


def neighbour_rows(is_upper, inner, outer_ref, south_ref, north_ref):
    @pl.when(is_upper)
    def _():
        south_ref[...] = inner[...]
        north_ref[...] = outer_ref[...]

    @pl.when(jnp.logical_not(is_upper))
    def _():
        south_ref[...] = outer_ref[...]
        north_ref[...] = inner[...]


def mix_row(which, row, rows, field, state_ref, south_ref, north_ref, west_in, east_in, coef_ref, right_ref, slot):
    col_count = state_ref.shape[2]
    chunks = col_count // LANES
    lane = lax.broadcasted_iota(jnp.int32, (1, LANES), 1)
    levels = slice(field * PAD, (field + 1) * PAD)

    def piece(chunk):
        return slice(chunk * LANES, (chunk + 1) * LANES)

    west_lane = column_lane(which, rows, field, 1, row)
    east_lane = column_lane(which, rows, field, 0, row)
    centers = [state_ref[row, levels, piece(c)] for c in range(chunks)]
    to_left = [pltpu.roll(c, LANES - 1, 1) for c in centers]
    to_right = [pltpu.roll(c, 1, 1) for c in centers]
    to_right.append(pltpu.roll(west_in[...], LANES - west_lane, 1))
    to_left.append(pltpu.roll(east_in[...], LANES - 1 - east_lane, 1))
    for c in range(chunks):
        south = south_ref[levels, piece(c)]
        north = north_ref[levels, piece(c)]
        east = jnp.where(lane == LANES - 1, to_left[c + 1], to_left[c])
        west = jnp.where(lane == 0, to_right[c - 1], to_right[c])

        def coef(kind):
            return coef_ref[row, kind : kind + 1, piece(c)]

        mixed = (
            coef(0) * centers[c]
            + coef(1) * east
            + coef(2) * west
            + coef(3) * north
            + coef(4) * south
        )
        high, low = split_two(mixed)
        right_ref[slot, 0:PAD, piece(c)] = high
        right_ref[slot, PAD : 2 * PAD, piece(c)] = low
        right_ref[slot, 2 * PAD : 3 * PAD, piece(c)] = high


def sweep_rows(which, rows, units, state_ref, south_ref, north_ref, west_in, east_in, coef_ref, matrix_ref, right_ref, emit):
    slots = right_ref.shape[0]
    right_ref[:, 3 * PAD :, :] = jnp.zeros((slots,) + (256 - 3 * PAD, right_ref.shape[2]), BF)

    def product(number):
        row, field = units[number]
        emit(number, row, field, mm(matrix_ref[field, row], right_ref[number % slots]))

    for number, (row, field) in enumerate(units):
        south = state_ref.at[row - 1] if row > 0 else south_ref
        north = state_ref.at[row + 1] if row < rows - 1 else north_ref
        mix_row(which, row, rows, field, state_ref, south, north, west_in, east_in, coef_ref, right_ref, number % slots)
        if number > 0:
            product(number - 1)
    product(len(units) - 1)


def diffuse(which, flags, state, other, received, mirror, coef, matrix, *far_cols):
    rows = coef.shape[0]
    col_count = state.shape[2]

    def kernel(flag_ref, state_ref, other_ref, edge_in, west_in, east_in, mirror_ref, coef_ref, matrix_ref, *refs):
        out_ref, edge_ref, cols_ref, south_ref, north_ref, outer_ref, right_ref = refs[-7:]
        is_upper = flag_ref[which] > 0
        if state.shape[0] > rows:
            state_ref = state_ref.at[pl.ds(jnp.where(is_upper, rows, 0), rows)]
            inner = other_ref.at[jnp.where(is_upper, rows - 1, rows)]
        else:
            inner = other_ref.at[jnp.where(is_upper, rows - 1, 0)]
        receive_row(which, flag_ref, edge_in, mirror_ref, outer_ref)
        neighbour_rows(is_upper, inner, outer_ref, south_ref, north_ref)

        def emit(number, row, field, result):
            out_ref[row, field * PAD : (field + 1) * PAD] = result

        units = [(row, field) for row in range(rows) for field in range(2)]
        sweep_rows(which, rows, units, state_ref, south_ref, north_ref, west_in, east_in, coef_ref, matrix_ref, right_ref, emit)
        write_edge(is_upper, out_ref, edge_ref)
        old_cols = refs[0][...] if which == NEAR else jnp.zeros((PAD, LANES), F32)
        cols_ref[...] = columns_of(which, out_ref, old_cols)

    return pl.pallas_call(
        kernel,
        in_specs=in_place(8 + len(far_cols)),
        out_shape=half_shapes(2 * rows, col_count),
        scratch_shapes=[pltpu.VMEM((2 * PAD, col_count), F32)] * 3
        + [pltpu.VMEM((4, 256, col_count), BF)],
        compiler_params=pltpu.CompilerParams(vmem_limit_bytes=16 * MIB),
        cost_estimate=pl.CostEstimate(
            flops=3_000_000_000, bytes_accessed=8_000_000, transcendentals=0
        ),
        name="diffusion_" + ("near", "far")[which],
    )(flags, state, other, *received, mirror, coef, matrix, *far_cols)


def output_layout(results):
    return jnp.swapaxes(jnp.stack(results), 0, 1)[:LEVELS]


def store_block(out_ref, stage_ref, sem, at, field):
    rows = stage_ref.shape[2]
    copy = pltpu.make_async_copy(
        stage_ref.at[field],
        out_ref.at[pl.ds(field * LEVELS, LEVELS), pl.ds(at, rows), :],
        sem.at[field],
    )
    copy.start()
    return copy


def last_inner(flags, near, far, near_edge, near_sides, far_sides, mirror, near_fixed, far_fixed, mask):
    rows, _, col_count = near.shape

    def kernel(flag_ref, near_ref, far_ref, edge_in, near_west, near_east, far_west, far_east, mirror_ref, near_coef, near_matrix, far_coef, far_matrix, mask_ref, out_ref, done_ref, south_ref, north_ref, outer_ref, right_ref, stage_ref, sem, kept_ref):
        is_upper = flag_ref[NEAR] > 0
        at = pl.multiple_of(jnp.where(is_upper, rows, 0), 8)
        wet = mask_ref[pl.ds(at, rows), :].astype(F32)
        far_at = pl.multiple_of(rows - at, 8)
        far_wet = mask_ref[pl.ds(far_at, rows), :].astype(F32)
        last = rows - 1
        far_inner = far_ref.at[jnp.where(is_upper, last, 0)]
        receive_row(NEAR, flag_ref, edge_in, mirror_ref, outer_ref)
        neighbour_rows(is_upper, far_inner, outer_ref, south_ref, north_ref)
        copies = []
        for field in range(2):
            results = []

            def emit(number, row, field, result):
                results.append(result * wet[row : row + 1])

            units = [(row, field) for row in range(rows)]
            sweep_rows(NEAR, rows, units, near_ref, south_ref, north_ref, near_west, near_east, near_coef, near_matrix, right_ref, emit)
            stage_ref[field] = output_layout(results)
            copies.append(store_block(out_ref, stage_ref, sem, at, field))
        edge = jnp.where(is_upper, last, 0)
        near_inner = near_ref.at[jnp.where(is_upper, 0, last)]

        @pl.when(is_upper)
        def _():
            south_ref[...] = far_ref[last - 1]
            north_ref[...] = near_inner[...]

        @pl.when(jnp.logical_not(is_upper))
        def _():
            south_ref[...] = near_inner[...]
            north_ref[...] = far_ref[1]

        def keep(number, row, field, result):
            kept_ref[row, field * PAD : (field + 1) * PAD] = result * far_wet[row : row + 1]

        units = [(row, field) for row in range(1, last) for field in range(2)]
        sweep_rows(FAR, rows, units, far_ref, south_ref, north_ref, far_west, far_east, far_coef, far_matrix, right_ref, keep)
        edge_wet = jnp.where(is_upper, far_wet[last:], far_wet[0:1])
        for field in range(2):
            mix_row(FAR, edge, rows, field, far_ref, south_ref, north_ref, far_west, far_east, far_coef, right_ref, field)
        for field in range(2):
            result = mm(far_matrix[field, edge], right_ref[field])
            kept_ref[edge, field * PAD : (field + 1) * PAD] = result * edge_wet
        for field in range(2):
            levels = slice(field * PAD, (field + 1) * PAD)
            done_ref[field] = output_layout([kept_ref[row, levels] for row in range(rows)])
        for copy in copies:
            copy.wait()

    return pl.pallas_call(
        kernel,
        in_specs=in_place(13),
        out_specs=[pl.BlockSpec(memory_space=pl.ANY), pl.BlockSpec(memory_space=pltpu.VMEM)],
        out_shape=(
            jax.ShapeDtypeStruct((2 * LEVELS, 2 * rows, col_count), F32),
            jax.ShapeDtypeStruct((2, LEVELS, rows, col_count), F32),
        ),
        scratch_shapes=[pltpu.VMEM((2 * PAD, col_count), F32)] * 3
        + [
            pltpu.VMEM((4, 256, col_count), BF),
            pltpu.VMEM((2, LEVELS, rows, col_count), F32),
            pltpu.SemaphoreType.DMA((2,)),
            pltpu.VMEM((rows, 2 * PAD, col_count), F32),
        ],
        compiler_params=pltpu.CompilerParams(vmem_limit_bytes=22 * MIB),
        cost_estimate=pl.CostEstimate(
            flops=6_000_000_000, bytes_accessed=16_000_000, transcendentals=0
        ),
        name="last_inner",
    )(flags, near, far, near_edge, *near_sides, *far_sides, mirror, *near_fixed, *far_fixed, mask)


def last_outer(flags, far, far_edge, far_sides, mirror, far_fixed, mask, done, target):
    rows, _, col_count = far.shape

    def kernel(flag_ref, far_ref, edge_in, west_in, east_in, mirror_ref, coef_ref, matrix_ref, mask_ref, done_ref, target_ref, out_ref, south_ref, north_ref, outer_ref, right_ref, stage_ref, sem):
        is_upper = flag_ref[FAR] > 0
        at = pl.multiple_of(jnp.where(is_upper, rows, 0), 8)
        wet = mask_ref[pl.ds(at, rows), :].astype(F32)
        last = rows - 1
        row = jnp.where(is_upper, last, 0)
        row_wet = jnp.where(is_upper, wet[last:], wet[0:1])
        receive_row(FAR, flag_ref, edge_in, mirror_ref, outer_ref)
        neighbour_rows(is_upper, far_ref.at[jnp.where(is_upper, last - 1, 1)], outer_ref, south_ref, north_ref)
        right_ref[:, 3 * PAD :, :] = jnp.zeros((2, 256 - 3 * PAD, col_count), BF)
        for field in range(2):
            mix_row(FAR, row, rows, field, far_ref, south_ref, north_ref, west_in, east_in, coef_ref, right_ref, field)
        copies = []
        here = lax.broadcasted_iota(jnp.int32, (rows, 1), 0) == row
        for field in range(2):
            outer_ref[0:PAD] = mm(matrix_ref[field, row], right_ref[field]) * row_wet
            for level in range(LEVELS):
                stage_ref[field, level] = jnp.where(
                    here, outer_ref[level : level + 1, :], done_ref[field, level]
                )
            copies.append(store_block(out_ref, stage_ref, sem, at, field))
        for copy in copies:
            copy.wait()

    operands = [flags, far, far_edge, *far_sides, mirror, *far_fixed, mask, done, target]
    return pl.pallas_call(
        kernel,
        in_specs=in_place(9) + [pl.BlockSpec(memory_space=pl.ANY)],
        out_specs=pl.BlockSpec(memory_space=pl.ANY),
        out_shape=jax.ShapeDtypeStruct((2 * LEVELS, 2 * rows, col_count), F32),
        input_output_aliases={len(operands) - 1: 0},
        scratch_shapes=[pltpu.VMEM((2 * PAD, col_count), F32)] * 3
        + [
            pltpu.VMEM((2, 256, col_count), BF),
            pltpu.VMEM((2, LEVELS, rows, col_count), F32),
            pltpu.SemaphoreType.DMA((2,)),
        ],
        compiler_params=pltpu.CompilerParams(vmem_limit_bytes=20 * MIB),
        name="last_outer",
    )(*operands)


def mixing_matrices(vinv):
    turned = jnp.transpose(vinv, (1, 0, 3, 2))
    turned = jnp.pad(turned, ((0, 0), (0, 0), (0, PAD - LEVELS), (0, PAD - LEVELS)))
    high = lax.reduce_precision(turned, 8, 7)
    low = (turned - high).astype(BF)
    high = high.astype(BF)
    rest = jnp.zeros(high.shape[:3] + (256 - 3 * PAD,), BF)
    return jnp.concatenate([high, high, low, rest], axis=3)


def body(
    argo_value,
    argo_owner,
    argo_cell,
    alt_value,
    alt_owner,
    alt_cell,
    alt_profile,
    land_mask,
    coef_east,
    coef_north,
    mirror,
    vinv,
):
    row_count, col_count = land_mask.shape
    count_ja = lax.axis_size("ja")
    count_ia = lax.axis_size("ia")
    devices = count_ja * count_ia
    capacity = round_up(3 * argo_value.shape[0] // devices, 8)
    group = round_up(capacity // 4, 8)
    message = send_tables(
        devices,
        capacity,
        group,
        row_count,
        col_count,
        (
            argo_value.T,
            argo_owner.reshape(1, -1),
            argo_cell.reshape(1, -1),
            alt_value,
            alt_cell,
            alt_owner.reshape(1, -1),
        ),
    )
    message, ja_index = lax.optimization_barrier((message, lax.axis_index("ja")))
    message = lax.all_to_all(message, ("ja", "ia"), split_axis=0, concat_axis=0, tiled=True)

    ia_index = lax.axis_index("ia")
    is_top = (ja_index == count_ja - 1).astype(jnp.int32)
    parity = ja_index % 2
    flags = jnp.stack([1 - parity, parity, is_top]).astype(jnp.int32)
    fold_index = mirror - (count_ia - 1 - ia_index) * col_count
    mirror_lane = jnp.broadcast_to((fold_index % LANES)[None, :], (8, col_count))
    matrices = mixing_matrices(vinv)
    profile = jnp.pad(alt_profile.reshape(2, LEVELS, 1), ((0, 0), (0, PAD - LEVELS), (0, 0)))
    profile = profile.reshape(2 * PAD, 1)
    alt_capacity = max(2, 3 * alt_value.shape[0] // devices)
    coast = (land_mask, coef_north, coef_east)
    rows = row_count // 2
    lower = [matrices[:, :rows], matrices[:, rows:]]
    odd_device = parity == 1
    half_matrices = [
        jnp.where(odd_device, lower[0], lower[1]),
        jnp.where(odd_device, lower[1], lower[0]),
    ]

    ring_east = [(i, (i + 1) % count_ia) for i in range(count_ia)]
    ring_west = [((i + 1) % count_ia, i) for i in range(count_ia)]
    even_swap = []
    odd_swap = []
    for ja in range(count_ja):
        for ia in range(count_ia):
            here = ja * count_ia + ia
            even_swap.append((here, (ja ^ 1) * count_ia + ia))
            if ja == count_ja - 1:
                odd_swap.append((here, ja * count_ia + count_ia - 1 - ia))
            elif ja > 0:
                odd_swap.append((here, (((ja - 1) ^ 1) + 1) * count_ia + ia))
    swaps = (even_swap, odd_swap)

    def swap(which, edge):
        return lax.ppermute(edge, ("ja", "ia"), swaps[which])

    def pass_columns(cols):
        return lax.ppermute(cols, "ia", ring_east), lax.ppermute(cols, "ia", ring_west)

    near_edge, *prepared = first_forcing(
        capacity, alt_capacity, group, flags, message, profile, coast
    )
    near_edge = swap(NEAR, near_edge)
    state, far_edge, cols = rest_forcing(flags, profile, coast, prepared)
    near = far = state
    sides = pass_columns(cols)
    far_edge = swap(FAR, far_edge)
    near_coef = edge_weights(NEAR, flags, coast, (near_edge, *sides), mirror_lane)
    far_coef = edge_weights(FAR, flags, coast, (far_edge, *sides), mirror_lane)
    near_fixed = (mirror_lane, near_coef, half_matrices[NEAR])
    far_fixed = (mirror_lane, far_coef, half_matrices[FAR])
    for sweep in range(ITERS - 1):
        new_near, new_edge, cols = diffuse(
            NEAR, flags, near, far, (near_edge, *sides), *near_fixed, cols
        )
        near_edge = swap(NEAR, new_edge)
        sides = pass_columns(cols)
        far, new_edge, cols = diffuse(FAR, flags, far, near, (far_edge, *sides), *far_fixed)
        far_edge = swap(FAR, new_edge)
        near = new_near
    last_sides = pass_columns(cols)
    output, done = last_inner(
        flags, near, far, near_edge, sides, last_sides, mirror_lane, near_fixed[1:], far_fixed[1:], land_mask
    )
    return last_outer(
        flags, far, far_edge, last_sides, mirror_lane, far_fixed[1:], land_mask, done, output
    )


def solution(mesh):
    in_specs = (
        P(("ja", "ia"), None),
        P(("ja", "ia"), None),
        P(("ja", "ia")),
        P(("ja", "ia")),
        P(("ja", "ia"), None),
        P(("ja", "ia")),
        P(),
        P("ja", "ia"),
        P("ja", "ia"),
        P("ja", "ia"),
        P("ia"),
        P("ja", None, None, None),
    )
    out_specs = P(None, "ja", "ia")
    return jax.shard_map(body, mesh=mesh, in_specs=in_specs, out_specs=out_specs, check_vma=False)
```
